32 devices in a mesh: rep: 2 (over x), pop: 16 (over z, y, core).
Axes of the slice: x: 2, y: 2, z: 4, core: 2. Of those that a mesh axis runs over, the one named last changes fastest.
Arguments:
- pool_tokens: bfloat16 [32, 128, 1024], P(('rep', 'pop')), parts along dimension 0, may hold values from -6 to 6
- pool_targets: bfloat16 [32, 128, 2560], P(('rep', 'pop')), parts along dimension 0, may hold values from -3 to 3
- weight: bfloat16 [32, 1024, 640], P(('rep', 'pop')), parts along dimension 0, may hold values from -0.1875 to 0.1875
- first_moment: bfloat16 [32, 1024, 640], P(('rep', 'pop')), parts along dimension 0, may hold values from -0.75 to 0.75
- second_moment: bfloat16 [32, 1024, 640], P(('rep', 'pop')), parts along dimension 0, may hold values from 0.0009994507 to 0.0099487305
- winner: int32 [8], P('rep'), parts along dimension 0, may hold values from 0 to 3, as said below
- learn_rate: float32 [8], P('rep'), parts along dimension 0, may hold values from 0.01 to 0.05
- explore: float32 [8], P('rep'), parts along dimension 0, may hold values from 0.25 to 4
- task_weight: float32 [8, 8], P('rep'), parts along dimension 0, may hold values from 0.1 to 1
- tile_ids: int32 [8, 4], P('rep'), parts along dimension 0, may hold values from 0 to 15
- slot_task: int32 [8, 4], P('rep'), parts along dimension 0, may hold values from 0 to 7
- slot_tokens: int32 [8, 4], P('rep'), parts along dimension 0, may hold values from 1 to 128, 384 in all within a row
Outputs:
- new_weight: bfloat16 [32, 1024, 640], P(('rep', 'pop')), parts along dimension 0
- new_first: bfloat16 [32, 1024, 640], P(('rep', 'pop')), parts along dimension 0
- new_second: bfloat16 [32, 1024, 640], P(('rep', 'pop')), parts along dimension 0
- member_loss: float32 [8], P('rep'), parts along dimension 0
The draws below stay inside these ranges and needn't reach their ends.
There are 2 independent parts, one for each index of `rep`. The reference program is written for one: setup_inputs(seed, part) draws one part's arguments, and reference() takes and returns one part's arrays. A program takes and returns all parts, laid end to end along the dimension named above; each array names one. Nothing has to cross between parts.
Inputs may be any that keep to these rules, and one draw needn't show every extreme that they name: Exactly 1 member takes another member's state; every such winner keeps its own state, and every other member maps to itself.
All inputs are finite; a program needn't handle non-finite values.
Results may differ from the reference program's by a relative error of at most 0.003.
Values may be sent and summed in bfloat16 or wider, within the bound.
No kernel may reach another device: no remote copies, remote signals or barrier semaphores. Data moves between devices by JAX's collectives and lax.ppermute only.
A program may use at most 128 MiB of HBM per device.

```python
import math
import jax
import jax.numpy as jnp
import numpy as np
from jax import lax

DW = 1024
FFW = 2560
SHARDS = 4
TILE = 128
TASKS = 8
SLOTS = 4
FFS = 640
MEMBERS = 4
TILES = 16


def draw_winner(key, part):
    key = jax.random.fold_in(key, 11)
    key_order, key_pick = jax.random.split(key)
    inner = MEMBERS - 2
    scores = jax.random.randint(key_order, (inner,), 0, 1 << 20).astype(jnp.int32) * inner + jnp.arange(inner, dtype=jnp.int32)
    middle = (jnp.argsort(scores, stable=True).astype(jnp.int32) + 1).astype(jnp.int32)
    ends = jnp.array([0, MEMBERS - 1], dtype=jnp.int32)
    order = jnp.concatenate([middle, ends])
    quarter = MEMBERS // 4
    losers = order[:quarter]
    keepers = order[quarter:]
    picks = jax.random.randint(key_pick, (quarter,), 0, MEMBERS - quarter).astype(jnp.int32)
    chosen = keepers[picks]
    mapping = jnp.arange(MEMBERS, dtype=jnp.int32).at[losers].set(chosen.astype(jnp.int32))
    return mapping.astype(jnp.int32)


def touch_ends(values, own_key, least, high):
    dims = values.shape
    index_at = [jax.random.randint(jax.random.fold_in(own_key, axis), (), 0, dims[axis]) for axis in range(len(dims))]
    values = values.at[tuple(index_at)].set(least)
    longest = dims.index(max(dims))
    index_at[longest] = (index_at[longest] + 1) % dims[longest]
    return values.at[tuple(index_at)].set(high)


def steps_of(key, dims, cuts, smallest, top_value):
    def one(position, blocks):
        steps = jax.random.uniform(jax.random.fold_in(jax.random.fold_in(key, 6), position), (blocks,), jnp.float32, smallest / len(cuts), top_value / len(cuts))
        return jnp.repeat(jnp.exp(steps), dims[position] // blocks).reshape((-1,) + (1,) * (len(dims) - position - 1))

    loudness = one(*cuts[0])
    for cut in cuts[1:]:
        loudness = loudness * one(*cut)
    return loudness


def cumulative_ranks(amount, skew):
    loads = [(1 << 20) // math.isqrt(standing ** skew) + 1 for standing in range(1, amount + 1)]
    scale = 1 + sum(loads) // (1 << 30)
    return np.cumsum(np.array([max(1, weight // scale) for weight in loads]))


def skewed_ids(stream_key, shape, number_of, lean):
    table = cumulative_ranks(number_of, lean)
    ticket = jax.random.randint(jax.random.fold_in(stream_key, 1), shape, 0, int(table[number_of - 1]))
    rank = jnp.searchsorted(jnp.asarray(table, jnp.int32), ticket, side="right")
    return jax.random.permutation(jax.random.fold_in(stream_key, 2), number_of)[rank].astype(jnp.int32)


def profile(count, total, bound, skew):
    weights = [(1 << 20) // math.isqrt(rank ** skew) + 1 for rank in range(2, count + 1)]
    spare, given = total - bound - (count - 1), [1] * (count - 1)
    while spare > 0:
        candidates = [i for i in range(count - 1) if given[i] < bound]
        mass, budget = sum([weights[i] for i in candidates]), spare
        for i in candidates:
            extra = min(bound - given[i], max(1, budget * weights[i] // mass), spare)
            given[i] = given[i] + extra
            spare = spare - extra
    return np.array([bound] + given)


def uneven(stream_key, amount, total, bound, skew):
    if amount == 2:
        one = jax.random.randint(stream_key, (), max(1, total - bound), min(bound, total - 1) + 1)
        return jnp.stack([one, total - one])
    sizes = jnp.asarray(profile(amount, total, bound, skew), jnp.int32)
    twos = (amount - 1) // 2
    giver, taker = sizes[1:1 + 2 * twos:2], sizes[2:2 + 2 * twos:2]
    slack = jnp.minimum(giver - 1, bound - taker)
    moved = jax.random.randint(jax.random.fold_in(stream_key, 1), (twos,), 0, 1 << 20) % (slack + 1)
    sizes = sizes.at[1:1 + 2 * twos:2].set(giver - moved).at[2:2 + 2 * twos:2].set(taker + moved)
    return sizes[jax.random.permutation(jax.random.fold_in(stream_key, 2), amount)]


def bell_draw(key, dims, spread, bound, pieces=(), kind=jnp.bfloat16):
    entries = jax.random.normal(key, dims, jnp.float32) * spread
    if len(pieces) > 0:
        entries = steps_of(key, dims, pieces, -0.22, 0.18) * entries
    return jnp.clip(entries, min=-bound, max=bound).astype(kind)


def setup_inputs(seed: int = 0, part: int = 0) -> dict:
    keys = jax.random.split(jax.random.key(seed), 13)
    part_splits = jax.random.split(jax.random.fold_in(keys[12], part), 13)
    pool_tokens = bell_draw(part_splits[0], (TILES, TILE, DW), 1.0, 6.0, ((0, 16),))
    pool_targets = bell_draw(part_splits[1], (TILES, TILE, FFW), 0.5, 3.0, ((0, 16),))
    weight = bell_draw(part_splits[2], (MEMBERS * SHARDS, DW, FFS), DW ** -0.5, 0.1875, ((0, 16),))
    first_moment = bell_draw(part_splits[3], (MEMBERS * SHARDS, DW, FFS), 0.05, 0.75, ((0, 16),))
    second_moment = jnp.clip(jnp.exp(math.log(0.0099487305) - 2.2979944 * jax.random.uniform(part_splits[4], (MEMBERS * SHARDS, DW, FFS), jnp.float32) ** steps_of(part_splits[4], (MEMBERS * SHARDS, DW, FFS), ((0, 16),), -0.2, 0.2)), 0.0009994507, 0.0099487305).astype(jnp.bfloat16)
    winner = draw_winner(jax.random.fold_in(jax.random.fold_in(keys[12], part), 71), part)
    learn_rate = jnp.clip(jnp.exp(jax.random.uniform(part_splits[6], (MEMBERS,), jnp.float32, math.log(0.01), math.log(0.05))), 0.01, 0.05)
    explore = jnp.clip(jax.random.uniform(part_splits[7], (MEMBERS,), jnp.float32, 0.25, 4.0), 0.25, 4.0)
    task_weight = jnp.clip(jnp.exp(jax.random.uniform(part_splits[8], (MEMBERS, TASKS), jnp.float32, math.log(0.1), math.log(1.0))), 0.1, 1.0)
    tile_ids = touch_ends(skewed_ids(part_splits[9], (MEMBERS, SLOTS), TILES, 2), jax.random.fold_in(part_splits[9], 3), 0, TILES - 1).astype(jnp.int32)
    slot_task = touch_ends(jax.random.randint(part_splits[10], (MEMBERS, SLOTS), 0, TASKS), jax.random.fold_in(part_splits[10], 1), 0, TASKS - 1).astype(jnp.int32)
    slot_tokens = jax.vmap(lambda own: uneven(own, SLOTS, SLOTS * 96, TILE, 1))(jax.random.split(part_splits[11], MEMBERS)).reshape((MEMBERS, SLOTS)).astype(jnp.int32)
    return {"pool_tokens": pool_tokens, "pool_targets": pool_targets, "weight": weight, "first_moment": first_moment, "second_moment": second_moment, "winner": winner, "learn_rate": learn_rate, "explore": explore, "task_weight": task_weight, "tile_ids": tile_ids, "slot_task": slot_task, "slot_tokens": slot_tokens}


beta_one = 0.9
beta_two = 0.999
adam_eps = 1e-08
gelu_coef = 0.7978845608028654

def gelu_pair(pre):
    inner = jnp.tanh(gelu_coef * (pre + 0.044715 * pre * pre * pre))
    value = 0.5 * pre * (1.0 + inner)
    slope = 0.5 * (1.0 + inner) + 0.5 * pre * (1.0 - inner * inner) * gelu_coef * (1.0 + 3.0 * 0.044715 * pre * pre)
    return (value, slope)

def token_coef(member, winner, task_weight, slot_task, slot_tokens, tile):
    tasks_here = slot_task[member]
    lengths = slot_tokens[member]
    onehot = tasks_here[:, None] == jnp.arange(TASKS, dtype=jnp.int32)[None, :]
    counts = lax.optimization_barrier(jnp.sum(jnp.where(onehot, lengths[:, None], 0), axis=0))
    scale = task_weight[winner[member]] / jnp.maximum(counts, 1).astype(jnp.float32)
    per_slot = lax.optimization_barrier(jnp.sum(jnp.where(onehot, scale[None, :], jnp.float32(0.0)), axis=1))
    live = jnp.arange(tile, dtype=jnp.int32)[None, :] < lengths[:, None]
    return jnp.where(live, per_slot[:, None], jnp.float32(0.0)).reshape(-1)

def member_rate(member, winner, learn_rate, explore):
    source = winner[member]
    return learn_rate[source] * jnp.where(source != member, explore[member], jnp.float32(1.0))

def shard_step(inputs, targets, start_weight, start_first, start_second, coef, step_rate):
    pre = jnp.dot(inputs, start_weight, preferred_element_type=jnp.float32)
    hidden, slope = gelu_pair(pre)
    diff = hidden - targets.astype(jnp.float32)
    part = jnp.sum(coef[:, None] * diff * diff)
    delta = (2.0 * coef[:, None] * diff * slope).astype(jnp.bfloat16)
    grad = lax.dot_general(inputs, delta, (((0,), (0,)), ((), ())), preferred_element_type=jnp.float32)
    first = beta_one * start_first.astype(jnp.float32) + (1.0 - beta_one) * grad
    second = beta_two * start_second.astype(jnp.float32) + (1.0 - beta_two) * grad * grad
    updated = start_weight.astype(jnp.float32) - step_rate * first / (jnp.sqrt(second) + adam_eps)
    return (updated.astype(jnp.bfloat16), first.astype(jnp.bfloat16), second.astype(jnp.bfloat16), part)

def reference(pool_tokens, pool_targets, weight, first_moment, second_moment, winner, learn_rate, explore, task_weight, tile_ids, slot_task, slot_tokens):
    nodes = weight.shape[0]
    width = weight.shape[2]
    tile = pool_tokens.shape[1]

    def one_row(place):
        member = place // SHARDS
        shard = place % SHARDS
        source = winner[member] * SHARDS + shard
        chosen = tile_ids[member]
        inputs = jnp.take(pool_tokens, chosen, axis=0).reshape(-1, pool_tokens.shape[2])
        picked = jnp.take(pool_targets, chosen, axis=0)
        targets = lax.dynamic_slice_in_dim(picked, (shard * width).astype(jnp.int32), width, 2).reshape(-1, width)
        coef = token_coef(member, winner, task_weight, slot_task, slot_tokens, tile)
        step_rate = member_rate(member, winner, learn_rate, explore)
        return shard_step(inputs, targets, weight[source], first_moment[source], second_moment[source], coef, step_rate)
    new_weight, new_first, new_second, parts = lax.map(one_row, jnp.arange(nodes, dtype=jnp.int32))
    member_loss = lax.optimization_barrier(jnp.sum(parts.reshape(-1, SHARDS), axis=1))
    return (new_weight, new_first, new_second, member_loss)
```

```python
import functools

import jax
import jax.numpy as jnp
from jax import lax
from jax.experimental import pallas as pl
from jax.experimental.pallas import tpu as pltpu
from jax.sharding import PartitionSpec as P

SHARDS = 4
TASKS = 8
PLANES = 4


beta_one = 0.9
beta_two = 0.999
adam_eps = 1e-08
gelu_coef = 0.7978845608028654

SMEM = pl.BlockSpec(memory_space=pltpu.SMEM)
VMEM = pl.BlockSpec(memory_space=pltpu.VMEM)
ANY = pl.BlockSpec(memory_space=pl.ANY)


def gelu_pair(pre):
    inner = jnp.tanh(gelu_coef * (pre + 0.044715 * pre * pre * pre))
    value = 0.5 * pre * (1.0 + inner)
    slope = 0.5 * (1.0 + inner) + 0.5 * pre * (1.0 - inner * inner) * gelu_coef * (
        1.0 + 3.0 * 0.044715 * pre * pre
    )
    return (value, slope)


def for_sending(shard):

    def short(part):
        return part.astype(jnp.bfloat16) if part.dtype == jnp.float32 else part

    return jax.tree.map(short, shard)


def relayed(
    pool_tokens,
    pool_targets,
    weight,
    first_moment,
    second_moment,
    winner,
    learn_rate,
    explore,
    task_weight,
    tile_ids,
    slot_task,
    slot_tokens,
):
    nodes = lax.axis_size("pop")
    place = lax.axis_index("pop")
    member = place // SHARDS
    shard = place % SHARDS
    members = winner.shape[0]
    slots = tile_ids.shape[1]
    tile = pool_tokens.shape[1]
    depth = pool_tokens.shape[2]
    width = weight.shape[2]
    hidden_all = pool_targets.shape[2]
    reach = tile // nodes
    flat_state = (
        weight.reshape(nodes, -1),
        first_moment.reshape(nodes, -1),
        second_moment.reshape(nodes, -1),
    )
    spread = (
        lax.all_to_all(flat_state[0], "pop", split_axis=0, concat_axis=0, tiled=True),
        lax.all_to_all(flat_state[1], "pop", split_axis=0, concat_axis=0, tiled=True),
        lax.all_to_all(flat_state[2], "pop", split_axis=0, concat_axis=0, tiled=True),
    )
    source_rows = (winner[:, None] * SHARDS + jnp.arange(SHARDS, dtype=jnp.int32)[None, :]).reshape(
        -1
    )
    picked_state = tuple((jnp.take(piece, source_rows, axis=0) for piece in spread))
    returned = jax.tree.map(
        lambda part, own: part.astype(own.dtype),
        lax.all_to_all(for_sending(picked_state), "pop", split_axis=0, concat_axis=0, tiled=True),
        picked_state,
    )
    start_weight = returned[0].reshape(depth, width)
    start_first = returned[1].reshape(depth, width)
    start_second = returned[2].reshape(depth, width)
    relay_tokens, relay_targets = (
        lax.all_to_all(pool_tokens, "pop", split_axis=1, concat_axis=0, tiled=True),
        lax.all_to_all(pool_targets, "pop", split_axis=1, concat_axis=0, tiled=True),
    )
    flat_ids = tile_ids.reshape(-1)
    pick_tokens = jnp.take(relay_tokens, flat_ids, axis=0).reshape(members, 1, slots, reach, depth)
    send_tokens = jnp.broadcast_to(pick_tokens, (members, SHARDS, slots, reach, depth)).reshape(
        nodes, slots, reach, depth
    )
    pick_targets = jnp.take(relay_targets, flat_ids, axis=0).reshape(
        members, slots, reach, hidden_all
    )
    send_targets = jnp.broadcast_to(
        pick_targets[:, None], (members, SHARDS, slots, reach, hidden_all)
    ).reshape(nodes, slots, reach, hidden_all)
    got_tokens, got_targets = (
        lax.all_to_all(send_tokens, "pop", split_axis=0, concat_axis=2, tiled=True),
        lax.all_to_all(send_targets, "pop", split_axis=0, concat_axis=2, tiled=True),
    )
    targets = lax.dynamic_slice_in_dim(got_targets[0], shard * width, width, 2).reshape(
        slots * tile, width
    )
    inputs = got_tokens.reshape(slots * tile, depth)
    tasks_here = lax.dynamic_index_in_dim(slot_task, member, 0, keepdims=False)
    lengths = lax.dynamic_index_in_dim(slot_tokens, member, 0, keepdims=False)
    source_member = lax.dynamic_index_in_dim(winner, member, 0, keepdims=False)
    onehot = tasks_here[:, None] == jnp.arange(TASKS, dtype=jnp.int32)[None, :]
    counts = jnp.sum(jnp.where(onehot, lengths[:, None], 0), axis=0)
    weights_here = lax.dynamic_index_in_dim(task_weight, source_member, 0, keepdims=False)
    scale = weights_here / jnp.maximum(counts, 1).astype(jnp.float32)
    per_slot = jnp.sum(jnp.where(onehot, scale[None, :], jnp.float32(0.0)), axis=1)
    live = jnp.arange(tile, dtype=jnp.int32)[None, :] < lengths[:, None]
    coef = jnp.where(live, per_slot[:, None], jnp.float32(0.0)).reshape(-1)
    own_rate = lax.dynamic_index_in_dim(learn_rate, source_member, 0, keepdims=False)
    own_explore = lax.dynamic_index_in_dim(explore, member, 0, keepdims=False)
    step_rate = own_rate * jnp.where(source_member != member, own_explore, jnp.float32(1.0))
    pre = jnp.dot(inputs, start_weight, preferred_element_type=jnp.float32)
    hidden, slope = gelu_pair(pre)
    diff = hidden - targets.astype(jnp.float32)
    part = jnp.sum(coef[:, None] * diff * diff)
    delta = (2.0 * coef[:, None] * diff * slope).astype(jnp.bfloat16)
    grad = lax.dot_general(
        inputs, delta, (((0,), (0,)), ((), ())), preferred_element_type=jnp.float32
    )
    first = beta_one * start_first.astype(jnp.float32) + (1.0 - beta_one) * grad
    second = beta_two * start_second.astype(jnp.float32) + (1.0 - beta_two) * grad * grad
    updated = start_weight.astype(jnp.float32) - step_rate * first / (jnp.sqrt(second) + adam_eps)
    share = jnp.where(jnp.arange(members, dtype=jnp.int32) == member, part, jnp.float32(0.0))
    member_loss = lax.psum(share, "pop")
    return (
        updated.astype(jnp.bfloat16)[None],
        first.astype(jnp.bfloat16)[None],
        second.astype(jnp.bfloat16)[None],
        member_loss,
    )


def pack_kernel(where, tokens, targets, *parts):
    k = where[1]
    width = targets.shape[2] // SHARDS
    slim = tokens.shape[2] // SHARDS
    for j, part in enumerate(parts):
        q = k ^ j
        part[:, :width] = targets[0, :, pl.ds(pl.multiple_of(q * width, 128), width)]
        part[:, width:] = tokens[0, :, pl.ds(pl.multiple_of(q * slim, 128), slim)]


def pack(where, tokens, targets):
    tile = tokens.shape[1]
    row = (tokens.shape[2] + targets.shape[2]) // SHARDS
    return pl.pallas_call(
        pack_kernel,
        out_shape=[jax.ShapeDtypeStruct((tile, row), tokens.dtype)] * SHARDS,
        in_specs=[SMEM, VMEM, VMEM],
        out_specs=[VMEM] * SHARDS,
        name="pack_quarters",
    )(where, tokens, targets)


def from_pool(t, m, k):
    return lax.rem(t // SHARDS - m + 1 + PLANES, PLANES), lax.rem(t, SHARDS) ^ k


def forward_kernel(where, tile_ids, *refs):
    pool, (out, sem) = refs[: PLANES * SHARDS], refs[PLANES * SHARDS :]
    m, k = where[0], where[1]
    end = jnp.where(m <= 1, 0, PLANES - 1)
    slots = out.shape[0]
    for s in range(slots):
        r, j = from_pool(tile_ids[end, s], m, k)
        for i, ref in enumerate(pool):

            @pl.when((r == i // SHARDS) & (j == i % SHARDS))
            def _():
                pltpu.make_async_copy(ref, out.at[s], sem.at[s]).start()

    for s in range(slots):
        pltpu.make_async_copy(pool[0], out.at[s], sem.at[s]).wait()


def forward_slots(where, tile_ids, pool):
    slots = tile_ids.shape[1]
    return pl.pallas_call(
        forward_kernel,
        out_shape=jax.ShapeDtypeStruct((slots,) + pool[0].shape, pool[0].dtype),
        in_specs=[SMEM, SMEM] + [ANY] * len(pool),
        out_specs=ANY,
        scratch_shapes=[pltpu.SemaphoreType.DMA((slots,))],
        name="slots_for_end",
    )(where, tile_ids, *pool)


def own_kernel(where, tile_ids, *refs):
    pool = refs[: PLANES * SHARDS]
    handed, inputs, targets, sem = refs[PLANES * SHARDS :]
    m, k = where[0], where[1]
    slots, tile, row = handed.shape
    width = targets.shape[1]
    at_end = (m == 0) | (m == PLANES - 1)

    def copies(ref, s):
        rows = pl.ds(s * tile, tile)
        return (
            pltpu.make_async_copy(ref.at[:, pl.ds(0, width)], targets.at[rows], sem.at[0, s]),
            pltpu.make_async_copy(ref.at[:, pl.ds(width, row - width)], inputs.at[rows], sem.at[1, s]),
        )

    for s in range(slots):
        r, j = from_pool(tile_ids[m, s], m, k)

        @pl.when(at_end)
        def _():
            for copy in copies(handed.at[s], s):
                copy.start()

        for i, ref in enumerate(pool):

            @pl.when(jnp.logical_not(at_end) & (r == i // SHARDS) & (j == i % SHARDS))
            def _():
                for copy in copies(ref, s):
                    copy.start()

    for s in range(slots):
        for copy in copies(pool[0], s):
            copy.wait()


def own_slots(where, tile_ids, pool, handed, width):
    slots, tile, row = handed.shape
    return pl.pallas_call(
        own_kernel,
        out_shape=[
            jax.ShapeDtypeStruct((slots * tile, row - width), handed.dtype),
            jax.ShapeDtypeStruct((slots * tile, width), handed.dtype),
        ],
        in_specs=[SMEM, SMEM] + [ANY] * (len(pool) + 1),
        out_specs=[ANY, ANY],
        scratch_shapes=[pltpu.SemaphoreType.DMA((2, slots))],
        name="slots_for_own",
    )(where, tile_ids, *pool, handed)


def grad_kernel(
    where, winner, task_weight, slot_task, slot_tokens, in0, in1, in2, in3, targets, own_w, sent_w,
    grad, loss, w_buf, delta, sem,
):
    m, k, copied = where[0], where[1], where[2]

    @pl.when(copied == 1)
    def _():
        pltpu.make_async_copy(sent_w.at[0], w_buf, sem).start()

    @pl.when(copied == 0)
    def _():
        pltpu.make_async_copy(own_w.at[0], w_buf, sem).start()

    slots = slot_task.shape[1]
    rows = in0.shape[0]
    tile = rows // slots
    slim = in0.shape[1]
    ins = (in0, in1, in2, in3)
    pltpu.make_async_copy(own_w.at[0], w_buf, sem).wait()
    total = jnp.zeros((1, 1), jnp.float32)
    for s in range(slots):
        task = slot_task[m, s]
        count = jnp.int32(0)
        for o in range(slots):
            count = count + jnp.where(slot_task[m, o] == task, slot_tokens[m, o], 0)
        span = pl.ds(s * tile, tile)
        pre = None
        for j in range(SHARDS):
            at = pl.ds(pl.multiple_of((k ^ j) * slim, slim), slim)
            one = jnp.dot(ins[j][span, :], w_buf[at, :], preferred_element_type=jnp.float32)
            pre = one if pre is None else pre + one
        live = lax.broadcasted_iota(jnp.int32, pre.shape, 0) < slot_tokens[m, s]
        many = jnp.full(pre.shape, jnp.maximum(count, 1), jnp.int32).astype(jnp.float32)
        coef = jnp.where(live, task_weight[winner[m], task] / many, 0.0)
        hidden, slope = gelu_pair(pre)
        diff = hidden - targets[span, :].astype(jnp.float32)
        scaled = coef * diff
        total = total + jnp.sum(scaled * diff, keepdims=True)
        delta[span, :] = (2.0 * scaled * slope).astype(jnp.bfloat16)
    lane = lax.broadcasted_iota(jnp.int32, loss.shape, 1)
    loss[...] = jnp.where(lane == m, total, 0.0)
    for j in range(SHARDS):
        at = pl.ds(pl.multiple_of((k ^ j) * slim, slim), slim)
        grad[at, :] = lax.dot_general(
            ins[j][...], delta[...], (((0,), (0,)), ((), ())), preferred_element_type=jnp.float32
        )


def gradient(where, winner, task_weight, slot_task, slot_tokens, ins, targets, own_w, sent_w):
    rows, width = targets.shape
    depth = own_w.shape[1]
    return pl.pallas_call(
        grad_kernel,
        out_shape=[
            jax.ShapeDtypeStruct((depth, width), jnp.float32),
            jax.ShapeDtypeStruct((8, 128), jnp.float32),
        ],
        in_specs=[SMEM] * 5 + [VMEM] * 5 + [ANY] * 2,
        out_specs=[VMEM, VMEM],
        scratch_shapes=[
            pltpu.VMEM((depth, width), own_w.dtype),
            pltpu.VMEM((rows, width), jnp.bfloat16),
            pltpu.SemaphoreType.DMA,
        ],
        compiler_params=pltpu.CompilerParams(vmem_limit_bytes=40 * 1024 * 1024),
        name="forward_and_gradient",
    )(where, winner, task_weight, slot_task, slot_tokens, *ins, targets, own_w, sent_w)


def adam_kernel(
    where, winner, learn_rate, explore, grad, own_w, own_f, own_s, sent_w, sent_f, sent_s,
    new_w, new_f, new_s, w_buf, f_buf, s_buf, sem,
):
    m, copied = where[0], where[2]
    blocks = sem.shape[1]
    step = grad.shape[0] // blocks
    own, sent, bufs = (own_w, own_f, own_s), (sent_w, sent_f, sent_s), (w_buf, f_buf, s_buf)

    def copy(refs, i, b):
        at = pl.ds(b * step, step)
        return pltpu.make_async_copy(refs[i].at[0, at], bufs[i].at[at], sem.at[i, b])

    for b in range(blocks):
        for i in range(3):

            @pl.when(copied == 1)
            def _():
                copy(sent, i, b).start()

            @pl.when(copied == 0)
            def _():
                copy(own, i, b).start()

    rate = learn_rate[winner[m]] * jnp.where(winner[m] != m, explore[m], 1.0)
    for b in range(blocks):
        for i in range(3):
            copy(own, i, b).wait()
        at = pl.ds(b * step, step)
        g = grad[at, :]
        first = beta_one * f_buf[at, :].astype(jnp.float32) + (1.0 - beta_one) * g
        second = beta_two * s_buf[at, :].astype(jnp.float32) + (1.0 - beta_two) * g * g
        updated = w_buf[at, :].astype(jnp.float32) - rate * first / (jnp.sqrt(second) + adam_eps)
        new_w[0, at, :] = updated.astype(new_w.dtype)
        new_f[0, at, :] = first.astype(new_f.dtype)
        new_s[0, at, :] = second.astype(new_s.dtype)


def adam(where, winner, learn_rate, explore, grad, own, sent):
    depth, width = grad.shape
    blocks = 4
    return pl.pallas_call(
        adam_kernel,
        out_shape=[jax.ShapeDtypeStruct(x.shape, x.dtype) for x in own],
        in_specs=[SMEM] * 4 + [VMEM] + [ANY] * 6,
        out_specs=[VMEM] * 3,
        scratch_shapes=[pltpu.VMEM((depth, width), x.dtype) for x in own]
        + [pltpu.SemaphoreType.DMA((3, blocks))],
        compiler_params=pltpu.CompilerParams(vmem_limit_bytes=40 * 1024 * 1024),
        name="adam_update",
    )(where, winner, learn_rate, explore, grad, *own, *sent)


def in_plane(x, j):
    pairs = [(m * SHARDS + k, m * SHARDS + (k ^ j)) for m in range(PLANES) for k in range(SHARDS)]
    return lax.ppermute(x, "pop", pairs)


def along(x, hops):
    pairs = [(a * SHARDS + k, b * SHARDS + k) for a, b in hops for k in range(SHARDS)]
    return lax.ppermute(x, "pop", pairs)


ROUTES = (
    ((0, 1), (1, 2), (2, 3)),
    ((1, 0), (2, 1), (3, 2)),
    ((0, 2), (2, 0)),
    ((1, 3), (3, 1)),
    ((0, 3), (3, 0)),
)


def route_of(source, loser):
    table = [[0] * PLANES for _ in range(PLANES)]
    for number, hops in enumerate(ROUTES):
        for a, b in hops:
            table[a][b] = number
    return jnp.array(table, jnp.int32)[source, loser]


def exploit(x, routes):
    nodes = PLANES * SHARDS
    pairs = [
        (rep * nodes + a * SHARDS + k, rep * nodes + b * SHARDS + k)
        for rep, number in enumerate(routes)
        for a, b in ROUTES[number]
        for k in range(SHARDS)
    ]
    return lax.ppermute(x, ("rep", "pop"), pairs)


def direct(
    routes,
    where,
    pool_tokens,
    pool_targets,
    weight,
    first_moment,
    second_moment,
    winner,
    learn_rate,
    explore,
    task_weight,
    tile_ids,
    slot_task,
    slot_tokens,
):
    width = weight.shape[2]
    own = (weight, first_moment, second_moment)
    sent = tuple(exploit(x, routes) for x in own)
    parts = pack(where, pool_tokens, pool_targets)
    here = [parts[0]] + [in_plane(parts[j], j) for j in range(1, SHARDS)]
    below = [along(x, [(0, 1), (1, 2)]) for x in here]
    above = [along(x, [(3, 2), (2, 1)]) for x in here]
    place = where[0]
    far = [
        along(jnp.where(place == 1, b, a), [(1, 2), (2, 1)]) for a, b in zip(above, below)
    ]
    pool = [*below, *here, *above, *far]
    handed = along(forward_slots(where, tile_ids, pool), [(1, 0), (2, 3)])
    quarter, targets = own_slots(where, tile_ids, pool, handed, width)
    side = in_plane(quarter, 1)
    cross = in_plane(quarter, 2)
    ins = (quarter, side, cross, in_plane(cross, 1))
    grad, loss = gradient(
        where, winner, task_weight, slot_task, slot_tokens, ins, targets, weight, sent[0]
    )
    loss = loss + in_plane(loss, 1)
    loss = loss + in_plane(loss, 2)
    ring = [along(loss, [(m, (m + d) % PLANES) for m in range(PLANES)]) for d in range(1, PLANES)]
    loss = loss + ring[0] + ring[1] + ring[2]
    new = adam(where, winner, learn_rate, explore, grad, own, sent)
    return (*new, loss[0, :PLANES])


def per_device(*args):
    weight, winner = args[2], args[5]
    members = winner.shape[0]
    if members != PLANES or lax.axis_size("rep") != 2:
        return relayed(*args)
    place = lax.axis_index("pop")
    member, shard = place // SHARDS, place % SHARDS
    copies = winner != jnp.arange(members, dtype=jnp.int32)
    loser = jnp.argmax(copies).astype(jnp.int32)
    source = winner[loser]
    where = jnp.stack([member, shard, (member == loser).astype(jnp.int32)]).astype(jnp.int32)
    route = route_of(source, loser)
    reps = lax.axis_size("rep")
    rep = lax.axis_index("rep")
    other = lax.ppermute(jnp.full((8, 128), route), "rep", [(r, reps - 1 - r) for r in range(reps)])
    other = other[0, 0]
    index = jnp.where(rep == 0, route * len(ROUTES) + other, other * len(ROUTES) + route)
    branches = [
        functools.partial(direct, (a, b)) for a in range(len(ROUTES)) for b in range(len(ROUTES))
    ]
    return lax.switch(index, branches, where, *args)


def solution(mesh):
    in_specs = (
        P(("rep", "pop"), None, None),
        P(("rep", "pop"), None, None),
        P(("rep", "pop"), None, None),
        P(("rep", "pop"), None, None),
        P(("rep", "pop"), None, None),
        P("rep"),
        P("rep"),
        P("rep"),
        P("rep", None),
        P("rep", None),
        P("rep", None),
        P("rep", None),
    )
    out_specs = (
        P(("rep", "pop"), None, None),
        P(("rep", "pop"), None, None),
        P(("rep", "pop"), None, None),
        P("rep"),
    )
    return jax.shard_map(
        per_device, mesh=mesh, in_specs=in_specs, out_specs=out_specs, check_vma=False
    )
```

```python
import functools

import jax
import jax.numpy as jnp
from jax import lax
from jax.experimental import pallas as pl
from jax.experimental.pallas import tpu as pltpu
from jax.sharding import PartitionSpec as P

SHARDS = 4
TASKS = 8
PLANES = 4


beta_one = 0.9
beta_two = 0.999
adam_eps = 1e-08
gelu_coef = 0.7978845608028654

SMEM = pl.BlockSpec(memory_space=pltpu.SMEM)
VMEM = pl.BlockSpec(memory_space=pltpu.VMEM)
ANY = pl.BlockSpec(memory_space=pl.ANY)


def gelu_pair(pre):
    inner = jnp.tanh(gelu_coef * (pre + 0.044715 * pre * pre * pre))
    value = 0.5 * pre * (1.0 + inner)
    slope = 0.5 * (1.0 + inner) + 0.5 * pre * (1.0 - inner * inner) * gelu_coef * (
        1.0 + 3.0 * 0.044715 * pre * pre
    )
    return (value, slope)


def for_sending(shard):

    def short(part):
        return part.astype(jnp.bfloat16) if part.dtype == jnp.float32 else part

    return jax.tree.map(short, shard)


def relayed(
    pool_tokens,
    pool_targets,
    weight,
    first_moment,
    second_moment,
    winner,
    learn_rate,
    explore,
    task_weight,
    tile_ids,
    slot_task,
    slot_tokens,
):
    nodes = lax.axis_size("pop")
    place = lax.axis_index("pop")
    member = place // SHARDS
    shard = place % SHARDS
    members = winner.shape[0]
    slots = tile_ids.shape[1]
    tile = pool_tokens.shape[1]
    depth = pool_tokens.shape[2]
    width = weight.shape[2]
    hidden_all = pool_targets.shape[2]
    reach = tile // nodes
    flat_state = (
        weight.reshape(nodes, -1),
        first_moment.reshape(nodes, -1),
        second_moment.reshape(nodes, -1),
    )
    spread = (
        lax.all_to_all(flat_state[0], "pop", split_axis=0, concat_axis=0, tiled=True),
        lax.all_to_all(flat_state[1], "pop", split_axis=0, concat_axis=0, tiled=True),
        lax.all_to_all(flat_state[2], "pop", split_axis=0, concat_axis=0, tiled=True),
    )
    source_rows = (winner[:, None] * SHARDS + jnp.arange(SHARDS, dtype=jnp.int32)[None, :]).reshape(
        -1
    )
    picked_state = tuple((jnp.take(piece, source_rows, axis=0) for piece in spread))
    returned = jax.tree.map(
        lambda part, own: part.astype(own.dtype),
        lax.all_to_all(for_sending(picked_state), "pop", split_axis=0, concat_axis=0, tiled=True),
        picked_state,
    )
    start_weight = returned[0].reshape(depth, width)
    start_first = returned[1].reshape(depth, width)
    start_second = returned[2].reshape(depth, width)
    relay_tokens, relay_targets = (
        lax.all_to_all(pool_tokens, "pop", split_axis=1, concat_axis=0, tiled=True),
        lax.all_to_all(pool_targets, "pop", split_axis=1, concat_axis=0, tiled=True),
    )
    flat_ids = tile_ids.reshape(-1)
    pick_tokens = jnp.take(relay_tokens, flat_ids, axis=0).reshape(members, 1, slots, reach, depth)
    send_tokens = jnp.broadcast_to(pick_tokens, (members, SHARDS, slots, reach, depth)).reshape(
        nodes, slots, reach, depth
    )
    pick_targets = jnp.take(relay_targets, flat_ids, axis=0).reshape(
        members, slots, reach, hidden_all
    )
    send_targets = jnp.broadcast_to(
        pick_targets[:, None], (members, SHARDS, slots, reach, hidden_all)
    ).reshape(nodes, slots, reach, hidden_all)
    got_tokens, got_targets = (
        lax.all_to_all(send_tokens, "pop", split_axis=0, concat_axis=2, tiled=True),
        lax.all_to_all(send_targets, "pop", split_axis=0, concat_axis=2, tiled=True),
    )
    targets = lax.dynamic_slice_in_dim(got_targets[0], shard * width, width, 2).reshape(
        slots * tile, width
    )
    inputs = got_tokens.reshape(slots * tile, depth)
    tasks_here = lax.dynamic_index_in_dim(slot_task, member, 0, keepdims=False)
    lengths = lax.dynamic_index_in_dim(slot_tokens, member, 0, keepdims=False)
    source_member = lax.dynamic_index_in_dim(winner, member, 0, keepdims=False)
    onehot = tasks_here[:, None] == jnp.arange(TASKS, dtype=jnp.int32)[None, :]
    counts = jnp.sum(jnp.where(onehot, lengths[:, None], 0), axis=0)
    weights_here = lax.dynamic_index_in_dim(task_weight, source_member, 0, keepdims=False)
    scale = weights_here / jnp.maximum(counts, 1).astype(jnp.float32)
    per_slot = jnp.sum(jnp.where(onehot, scale[None, :], jnp.float32(0.0)), axis=1)
    live = jnp.arange(tile, dtype=jnp.int32)[None, :] < lengths[:, None]
    coef = jnp.where(live, per_slot[:, None], jnp.float32(0.0)).reshape(-1)
    own_rate = lax.dynamic_index_in_dim(learn_rate, source_member, 0, keepdims=False)
    own_explore = lax.dynamic_index_in_dim(explore, member, 0, keepdims=False)
    step_rate = own_rate * jnp.where(source_member != member, own_explore, jnp.float32(1.0))
    pre = jnp.dot(inputs, start_weight, preferred_element_type=jnp.float32)
    hidden, slope = gelu_pair(pre)
    diff = hidden - targets.astype(jnp.float32)
    part = jnp.sum(coef[:, None] * diff * diff)
    delta = (2.0 * coef[:, None] * diff * slope).astype(jnp.bfloat16)
    grad = lax.dot_general(
        inputs, delta, (((0,), (0,)), ((), ())), preferred_element_type=jnp.float32
    )
    first = beta_one * start_first.astype(jnp.float32) + (1.0 - beta_one) * grad
    second = beta_two * start_second.astype(jnp.float32) + (1.0 - beta_two) * grad * grad
    updated = start_weight.astype(jnp.float32) - step_rate * first / (jnp.sqrt(second) + adam_eps)
    share = jnp.where(jnp.arange(members, dtype=jnp.int32) == member, part, jnp.float32(0.0))
    member_loss = lax.psum(share, "pop")
    return (
        updated.astype(jnp.bfloat16)[None],
        first.astype(jnp.bfloat16)[None],
        second.astype(jnp.bfloat16)[None],
        member_loss,
    )


ROUTES = (
    ((0, 1), (1, 2), (2, 3)),
    ((1, 0), (2, 1), (3, 2)),
    ((0, 2),),
    ((2, 0),),
    ((1, 3),),
    ((3, 1),),
    ((0, 3), (3, 0)),
)
ENDS = ((0, 1), (1, 0), (2, 3), (3, 2))
MIDDLE = ((1, 2), (2, 1))


def cuts(route):
    steps = set()
    for a, b in ROUTES[route]:
        up = 1 if b > a else -1
        steps |= {(c, c + up) for c in range(a, b, up)}
    return steps


def position():
    place = lax.axis_index("pop")
    return place // SHARDS, lax.rem(place, SHARDS)


def copied_from(winner):
    loser, source = jnp.int32(0), jnp.int32(0)
    for m in range(PLANES):
        taken = winner[m] != m
        loser = jnp.where(taken, m, loser)
        source = jnp.where(taken, winner[m], source)
    return loser, source


def route_kernel(winner, code):
    loser, source = copied_from(winner)
    route = jnp.int32(0)
    for number, hops in enumerate(ROUTES):
        for a, b in hops:
            route = jnp.where((source == a) & (loser == b), number, route)
    scale = jnp.where(lax.axis_index("rep") == 0, len(ROUTES), 1)
    code[...] = jnp.full(code.shape, route * scale, jnp.int32)


def route_code(winner):
    return pl.pallas_call(
        route_kernel,
        out_shape=jax.ShapeDtypeStruct((8, 128), jnp.int32),
        in_specs=[SMEM],
        out_specs=VMEM,
        name="route_code",
    )(winner)


def pack_kernel(tokens, targets, *parts):
    _, k = position()
    width = targets.shape[2] // SHARDS
    slim = tokens.shape[2] // SHARDS
    for j, part in enumerate(parts):
        q = k ^ j
        part[:, :width] = targets[0, :, pl.ds(pl.multiple_of(q * width, 128), width)]
        part[:, width:] = tokens[0, :, pl.ds(pl.multiple_of(q * slim, 128), slim)]


def pack(tokens, targets):
    tile = tokens.shape[1]
    row = (tokens.shape[2] + targets.shape[2]) // SHARDS
    return pl.pallas_call(
        pack_kernel,
        out_shape=[jax.ShapeDtypeStruct((tile, row), tokens.dtype)] * SHARDS,
        in_specs=[VMEM, VMEM],
        out_specs=[VMEM] * SHARDS,
        name="pack_quarters",
    )(tokens, targets)


def copy_rows(ref, start, out, at, columns=slice(None)):
    tile, step = ref.shape[0] if start is None else out.shape[0], 16

    def body(i, _):
        rows = pl.multiple_of(i * step, step)
        out[pl.ds(pl.multiple_of(at + rows, step), step), :] = ref[pl.ds(rows, step), columns]
        return 0

    lax.fori_loop(0, tile // step, body, 0, unroll=4)


def in_pool(t, m, k):
    ahead = t // SHARDS - m
    ahead = jnp.where(m == 1, ahead, -ahead)
    group = jnp.where(ahead == 0, 0, jnp.where(ahead == -1, 1, ahead + 1))
    return group * SHARDS + (lax.rem(t, SHARDS) ^ k)


def pick_for_end_kernel(tile_ids, *refs):
    pool, out = refs[:-1], refs[-1]
    m, k = position()
    end = jnp.where(m <= 1, 0, PLANES - 1)
    tile = pool[0].shape[0]

    def slot(s, _):
        which = in_pool(tile_ids[end, s], m, k)
        for i, ref in enumerate(pool):

            @pl.when(which == i)
            def _():
                copy_rows(ref, None, out, s * tile)

        return 0

    lax.fori_loop(0, tile_ids.shape[1], slot, 0)


def pick_for_end(tile_ids, pool):
    slots = tile_ids.shape[1]
    tile, row = pool[0].shape
    return pl.pallas_call(
        pick_for_end_kernel,
        out_shape=jax.ShapeDtypeStruct((slots * tile, row), pool[0].dtype),
        in_specs=[SMEM] + [VMEM] * len(pool),
        out_specs=VMEM,
        compiler_params=pltpu.CompilerParams(vmem_limit_bytes=40 * 1024 * 1024),
        name="pick_for_end",
    )(tile_ids, *pool)


def pick_own_kernel(tile_ids, *refs):
    pool, (handed, quarter, targets) = refs[:-3], refs[-3:]
    m, k = position()
    tile = pool[0].shape[0]
    width = targets.shape[1]
    at_end = (m == 0) | (m == PLANES - 1)

    @pl.when(at_end)
    def _():
        copy_rows(handed, None, targets, 0, slice(0, width))
        copy_rows(handed, None, quarter, 0, slice(width, None))

    def slot(s, _):
        which = jnp.where(at_end, -1, in_pool(tile_ids[m, s], m, k))
        for i, ref in enumerate(pool):

            @pl.when(which == i)
            def _():
                copy_rows(ref, None, targets, s * tile, slice(0, width))
                copy_rows(ref, None, quarter, s * tile, slice(width, None))

        return 0

    lax.fori_loop(0, tile_ids.shape[1], slot, 0)


def pick_own(tile_ids, pool, handed, width):
    rows, row = handed.shape
    return pl.pallas_call(
        pick_own_kernel,
        out_shape=[
            jax.ShapeDtypeStruct((rows, row - width), handed.dtype),
            jax.ShapeDtypeStruct((rows, width), handed.dtype),
        ],
        in_specs=[SMEM] + [VMEM] * (len(pool) + 1),
        out_specs=[VMEM, VMEM],
        compiler_params=pltpu.CompilerParams(vmem_limit_bytes=40 * 1024 * 1024),
        name="pick_own",
    )(tile_ids, *pool, handed)


def grad_kernel(
    winner, task_weight, slot_task, slot_tokens, in0, in1, in2, in3, targets, own_w, sent_a, sent_b,
    grad, loss, w_buf, delta, sem,
):
    m, k = position()
    half = sent_a.shape[0]

    @pl.when(winner[m] != m)
    def _():
        pltpu.make_async_copy(sent_a, w_buf.at[pl.ds(0, half)], sem.at[0]).start()
        pltpu.make_async_copy(sent_b, w_buf.at[pl.ds(half, half)], sem.at[1]).start()

    @pl.when(winner[m] == m)
    def _():
        for h in range(2):
            at = pl.ds(h * half, half)
            pltpu.make_async_copy(own_w.at[0, at], w_buf.at[at], sem.at[h]).start()

    slots = slot_task.shape[1]
    tile = in0.shape[0] // slots
    slim = in0.shape[1]
    ins = (in0, in1, in2, in3)
    for h in range(2):
        at = pl.ds(h * half, half)
        pltpu.make_async_copy(own_w.at[0, at], w_buf.at[at], sem.at[h]).wait()

    def slot(s, total):
        task = slot_task[m, s]
        count = jnp.int32(0)
        for o in range(slots):
            count = count + jnp.where(slot_task[m, o] == task, slot_tokens[m, o], 0)
        span = pl.ds(pl.multiple_of(s * tile, tile), tile)
        pre = None
        for j in range(SHARDS):
            at = pl.ds(pl.multiple_of((k ^ j) * slim, slim), slim)
            one = jnp.dot(ins[j][span, :], w_buf[at, :], preferred_element_type=jnp.float32)
            pre = one if pre is None else pre + one
        live = lax.broadcasted_iota(jnp.int32, pre.shape, 0) < slot_tokens[m, s]
        many = jnp.full(pre.shape, jnp.maximum(count, 1), jnp.int32).astype(jnp.float32)
        coef = jnp.where(live, task_weight[winner[m], task] / many, 0.0)
        hidden, slope = gelu_pair(pre)
        diff = hidden - targets[span, :].astype(jnp.float32)
        scaled = coef * diff
        delta[span, :] = (2.0 * scaled * slope).astype(jnp.bfloat16)
        return total + jnp.sum(scaled * diff, keepdims=True)

    total = lax.fori_loop(0, slots, slot, jnp.zeros((1, 1), jnp.float32))
    lane = lax.broadcasted_iota(jnp.int32, loss.shape, 1)
    loss[...] = jnp.where(lane == m, total, 0.0)
    for j in range(SHARDS):
        at = pl.ds(pl.multiple_of((k ^ j) * slim, slim), slim)
        grad[at, :] = lax.dot_general(
            ins[j][...], delta[...], (((0,), (0,)), ((), ())), preferred_element_type=jnp.float32
        )


def gradient(winner, task_weight, slot_task, slot_tokens, ins, targets, own_w, sent):
    rows, width = targets.shape
    depth = own_w.shape[1]
    return pl.pallas_call(
        grad_kernel,
        out_shape=[
            jax.ShapeDtypeStruct((depth, width), jnp.float32),
            jax.ShapeDtypeStruct((8, 128), jnp.float32),
        ],
        in_specs=[SMEM] * 4 + [VMEM] * 5 + [ANY] * 3,
        out_specs=[VMEM, VMEM],
        scratch_shapes=[
            pltpu.VMEM((depth, width), own_w.dtype),
            pltpu.VMEM((rows, width), jnp.bfloat16),
            pltpu.SemaphoreType.DMA((2,)),
        ],
        compiler_params=pltpu.CompilerParams(vmem_limit_bytes=40 * 1024 * 1024),
        name="forward_and_gradient",
    )(winner, task_weight, slot_task, slot_tokens, *ins, targets, own_w, *sent)


def adam_kernel(half, winner, learn_rate, explore, grad, *refs):
    own, sent, refs = refs[:3], refs[3:6], refs[6:]
    new, bufs, outs, (in_sem, out_sem) = refs[-11:-8], refs[-8:-5], refs[-5:-2], refs[-2:]
    m, _ = position()
    blocks = in_sem.shape[1]
    rows = bufs[0].shape[0]
    step = rows // blocks
    here = half * rows

    def copy(i, b, taken):
        at = pl.ds(b * step, step)
        ref = sent[i].at[at] if taken else own[i].at[0, pl.ds(here + b * step, step)]
        return pltpu.make_async_copy(ref, bufs[i].at[at], in_sem.at[i, b])

    def result(i, b):
        return pltpu.make_async_copy(
            outs[i].at[pl.ds(b * step, step)],
            new[i].at[0, pl.ds(here + b * step, step)],
            out_sem.at[i, b],
        )

    @pl.when(winner[m] != m)
    def _():
        for b in range(blocks):
            for i in range(3):
                copy(i, b, True).start()

    @pl.when(winner[m] == m)
    def _():
        for b in range(blocks):
            for i in range(3):
                copy(i, b, False).start()

    rate = learn_rate[winner[m]] * jnp.where(winner[m] != m, explore[m], 1.0)
    for b in range(blocks):
        for i in range(3):
            copy(i, b, False).wait()

        def body(n, _):
            at = pl.ds(pl.multiple_of(b * step + n * 16, 16), 16)
            g = grad[pl.ds(pl.multiple_of(here + b * step + n * 16, 16), 16), :]
            first = beta_one * bufs[1][at, :].astype(jnp.float32) + (1.0 - beta_one) * g
            second = beta_two * bufs[2][at, :].astype(jnp.float32) + (1.0 - beta_two) * g * g
            start = bufs[0][at, :].astype(jnp.float32)
            updated = start - rate * first / (jnp.sqrt(second) + adam_eps)
            outs[0][at, :] = updated.astype(outs[0].dtype)
            outs[1][at, :] = first.astype(outs[1].dtype)
            outs[2][at, :] = second.astype(outs[2].dtype)
            return 0

        lax.fori_loop(0, step // 16, body, 0, unroll=2)
        for i in range(3):
            result(i, b).start()
    for b in range(blocks):
        for i in range(3):
            result(i, b).wait()


def adam(half, winner, learn_rate, explore, grad, own, sent, begun=()):
    rows, width = sent[0].shape
    blocks = 2
    return pl.pallas_call(
        functools.partial(adam_kernel, half),
        out_shape=[jax.ShapeDtypeStruct(x.shape, x.dtype) for x in own],
        in_specs=[SMEM] * 3 + [VMEM] + [ANY] * (6 + len(begun)),
        out_specs=[ANY] * 3,
        scratch_shapes=[pltpu.VMEM((rows, width), x.dtype) for x in own] * 2
        + [pltpu.SemaphoreType.DMA((3, blocks))] * 2,
        input_output_aliases={10 + i: i for i in range(len(begun))},
        compiler_params=pltpu.CompilerParams(vmem_limit_bytes=40 * 1024 * 1024),
        name="adam_half",
    )(winner, learn_rate, explore, grad, *own, *sent, *begun)


def in_plane(x, j):
    pairs = [(m * SHARDS + k, m * SHARDS + (k ^ j)) for m in range(PLANES) for k in range(SHARDS)]
    return lax.ppermute(x, "pop", pairs)


def along(x, hops):
    idle = [m for m in range(PLANES) if all(m not in hop for hop in hops)]
    pairs = [(a * SHARDS + k, b * SHARDS + k) for a, b in hops for k in range(SHARDS)]
    pairs += [(m * SHARDS + k, m * SHARDS + (k ^ 1)) for m in idle for k in range(SHARDS)]
    return lax.ppermute(x, "pop", pairs)


def beside(x):
    return lax.ppermute(x, "rep", [(0, 1), (1, 0)])


def exploit(x, routes):
    nodes = PLANES * SHARDS
    pairs = [
        (rep * nodes + a * SHARDS + k, rep * nodes + b * SHARDS + k)
        for rep, number in enumerate(routes)
        for a, b in ROUTES[number]
        for k in range(SHARDS)
    ]
    return lax.ppermute(x, ("rep", "pop"), pairs)


def direct(
    routes,
    here,
    guest_weight,
    weight,
    first_moment,
    second_moment,
    winner,
    learn_rate,
    explore,
    task_weight,
    tile_ids,
    slot_task,
    slot_tokens,
):
    half, width = weight.shape[1] // 2, weight.shape[2]
    own = (weight, first_moment, second_moment)
    lower = [exploit(x[0, :half], routes) for x in own]
    if cuts(routes[0]) & cuts(routes[1]):
        upper = [exploit(x[0, half:], routes) for x in own]
    else:
        guests = [guest_weight] + [beside(x[0, half:]) for x in own[1:]]
        upper = [beside(exploit(x, routes[::-1])) for x in guests]
    near = [along(x, ENDS) for x in here]
    middle = [along(x, MIDDLE) for x in here]
    far = [along(x, MIDDLE) for x in near]
    pool = [*here, *near, *middle, *far]
    handed = along(pick_for_end(tile_ids, pool), ENDS)
    quarter, targets = pick_own(tile_ids, pool, handed, width)
    side = in_plane(quarter, 1)
    cross = in_plane(quarter, 2)
    ins = (quarter, side, cross, in_plane(cross, 1))
    grad, loss = gradient(
        winner, task_weight, slot_task, slot_tokens, ins, targets, weight, (lower[0], upper[0])
    )
    loss = loss + in_plane(loss, 1)
    loss = loss + in_plane(loss, 2)
    ring = [along(loss, [(m, (m + d) % PLANES) for m in range(PLANES)]) for d in range(1, PLANES)]
    loss = loss + ring[0] + ring[1] + ring[2]
    new = adam(0, winner, learn_rate, explore, grad, own, lower)
    new = adam(1, winner, learn_rate, explore, grad, own, upper, new)
    return (*new, loss[0, :PLANES])


def per_device(pool_tokens, pool_targets, weight, *args):
    members = args[2].shape[0]
    if members != PLANES or lax.axis_size("rep") != 2:
        return relayed(pool_tokens, pool_targets, weight, *args)
    code = route_code(args[2])
    index = (code + beside(code))[0, 0]
    parts = pack(pool_tokens, pool_targets)
    here = (parts[0], *(in_plane(parts[j], j) for j in range(1, SHARDS)))
    guest_weight = beside(weight[0, weight.shape[1] // 2 :])
    branches = [
        functools.partial(direct, (a, b)) for a in range(len(ROUTES)) for b in range(len(ROUTES))
    ]
    return lax.switch(index, branches, here, guest_weight, weight, *args)


def solution(mesh):
    in_specs = (
        P(("rep", "pop"), None, None),
        P(("rep", "pop"), None, None),
        P(("rep", "pop"), None, None),
        P(("rep", "pop"), None, None),
        P(("rep", "pop"), None, None),
        P("rep"),
        P("rep"),
        P("rep"),
        P("rep", None),
        P("rep", None),
        P("rep", None),
        P("rep", None),
    )
    out_specs = (
        P(("rep", "pop"), None, None),
        P(("rep", "pop"), None, None),
        P(("rep", "pop"), None, None),
        P("rep"),
    )
    return jax.shard_map(
        per_device, mesh=mesh, in_specs=in_specs, out_specs=out_specs, check_vma=False
    )
```

```python
import functools

import jax
import jax.numpy as jnp
from jax import lax
from jax.experimental import pallas as pl
from jax.experimental.pallas import tpu as pltpu
from jax.sharding import PartitionSpec as P

SHARDS = 4
TASKS = 8
PLANES = 4


beta_one = 0.9
beta_two = 0.999
adam_eps = 1e-08
gelu_coef = 0.7978845608028654

SMEM = pl.BlockSpec(memory_space=pltpu.SMEM)
VMEM = pl.BlockSpec(memory_space=pltpu.VMEM)
ANY = pl.BlockSpec(memory_space=pl.ANY)


def gelu_pair(pre):
    inner = jnp.tanh(gelu_coef * (pre + 0.044715 * pre * pre * pre))
    value = 0.5 * pre * (1.0 + inner)
    slope = 0.5 * (1.0 + inner) + 0.5 * pre * (1.0 - inner * inner) * gelu_coef * (
        1.0 + 3.0 * 0.044715 * pre * pre
    )
    return (value, slope)


def for_sending(shard):

    def short(part):
        return part.astype(jnp.bfloat16) if part.dtype == jnp.float32 else part

    return jax.tree.map(short, shard)


def relayed(
    pool_tokens,
    pool_targets,
    weight,
    first_moment,
    second_moment,
    winner,
    learn_rate,
    explore,
    task_weight,
    tile_ids,
    slot_task,
    slot_tokens,
):
    nodes = lax.axis_size("pop")
    place = lax.axis_index("pop")
    member = place // SHARDS
    shard = place % SHARDS
    members = winner.shape[0]
    slots = tile_ids.shape[1]
    tile = pool_tokens.shape[1]
    depth = pool_tokens.shape[2]
    width = weight.shape[2]
    hidden_all = pool_targets.shape[2]
    reach = tile // nodes
    flat_state = (
        weight.reshape(nodes, -1),
        first_moment.reshape(nodes, -1),
        second_moment.reshape(nodes, -1),
    )
    spread = (
        lax.all_to_all(flat_state[0], "pop", split_axis=0, concat_axis=0, tiled=True),
        lax.all_to_all(flat_state[1], "pop", split_axis=0, concat_axis=0, tiled=True),
        lax.all_to_all(flat_state[2], "pop", split_axis=0, concat_axis=0, tiled=True),
    )
    source_rows = (winner[:, None] * SHARDS + jnp.arange(SHARDS, dtype=jnp.int32)[None, :]).reshape(
        -1
    )
    picked_state = tuple((jnp.take(piece, source_rows, axis=0) for piece in spread))
    returned = jax.tree.map(
        lambda part, own: part.astype(own.dtype),
        lax.all_to_all(for_sending(picked_state), "pop", split_axis=0, concat_axis=0, tiled=True),
        picked_state,
    )
    start_weight = returned[0].reshape(depth, width)
    start_first = returned[1].reshape(depth, width)
    start_second = returned[2].reshape(depth, width)
    relay_tokens, relay_targets = (
        lax.all_to_all(pool_tokens, "pop", split_axis=1, concat_axis=0, tiled=True),
        lax.all_to_all(pool_targets, "pop", split_axis=1, concat_axis=0, tiled=True),
    )
    flat_ids = tile_ids.reshape(-1)
    pick_tokens = jnp.take(relay_tokens, flat_ids, axis=0).reshape(members, 1, slots, reach, depth)
    send_tokens = jnp.broadcast_to(pick_tokens, (members, SHARDS, slots, reach, depth)).reshape(
        nodes, slots, reach, depth
    )
    pick_targets = jnp.take(relay_targets, flat_ids, axis=0).reshape(
        members, slots, reach, hidden_all
    )
    send_targets = jnp.broadcast_to(
        pick_targets[:, None], (members, SHARDS, slots, reach, hidden_all)
    ).reshape(nodes, slots, reach, hidden_all)
    got_tokens, got_targets = (
        lax.all_to_all(send_tokens, "pop", split_axis=0, concat_axis=2, tiled=True),
        lax.all_to_all(send_targets, "pop", split_axis=0, concat_axis=2, tiled=True),
    )
    targets = lax.dynamic_slice_in_dim(got_targets[0], shard * width, width, 2).reshape(
        slots * tile, width
    )
    inputs = got_tokens.reshape(slots * tile, depth)
    tasks_here = lax.dynamic_index_in_dim(slot_task, member, 0, keepdims=False)
    lengths = lax.dynamic_index_in_dim(slot_tokens, member, 0, keepdims=False)
    source_member = lax.dynamic_index_in_dim(winner, member, 0, keepdims=False)
    onehot = tasks_here[:, None] == jnp.arange(TASKS, dtype=jnp.int32)[None, :]
    counts = jnp.sum(jnp.where(onehot, lengths[:, None], 0), axis=0)
    weights_here = lax.dynamic_index_in_dim(task_weight, source_member, 0, keepdims=False)
    scale = weights_here / jnp.maximum(counts, 1).astype(jnp.float32)
    per_slot = jnp.sum(jnp.where(onehot, scale[None, :], jnp.float32(0.0)), axis=1)
    live = jnp.arange(tile, dtype=jnp.int32)[None, :] < lengths[:, None]
    coef = jnp.where(live, per_slot[:, None], jnp.float32(0.0)).reshape(-1)
    own_rate = lax.dynamic_index_in_dim(learn_rate, source_member, 0, keepdims=False)
    own_explore = lax.dynamic_index_in_dim(explore, member, 0, keepdims=False)
    step_rate = own_rate * jnp.where(source_member != member, own_explore, jnp.float32(1.0))
    pre = jnp.dot(inputs, start_weight, preferred_element_type=jnp.float32)
    hidden, slope = gelu_pair(pre)
    diff = hidden - targets.astype(jnp.float32)
    part = jnp.sum(coef[:, None] * diff * diff)
    delta = (2.0 * coef[:, None] * diff * slope).astype(jnp.bfloat16)
    grad = lax.dot_general(
        inputs, delta, (((0,), (0,)), ((), ())), preferred_element_type=jnp.float32
    )
    first = beta_one * start_first.astype(jnp.float32) + (1.0 - beta_one) * grad
    second = beta_two * start_second.astype(jnp.float32) + (1.0 - beta_two) * grad * grad
    updated = start_weight.astype(jnp.float32) - step_rate * first / (jnp.sqrt(second) + adam_eps)
    share = jnp.where(jnp.arange(members, dtype=jnp.int32) == member, part, jnp.float32(0.0))
    member_loss = lax.psum(share, "pop")
    return (
        updated.astype(jnp.bfloat16)[None],
        first.astype(jnp.bfloat16)[None],
        second.astype(jnp.bfloat16)[None],
        member_loss,
    )


ROUTES = (
    ((0, 1), (1, 2), (2, 3)),
    ((1, 0), (2, 1), (3, 2)),
    ((0, 2),),
    ((2, 0),),
    ((1, 3),),
    ((3, 1),),
)
RING = tuple((m, (m + 1) % PLANES) for m in range(PLANES))
ENDS = ((0, 1), (1, 0), (2, 3), (3, 2))
MIDDLE = ((1, 2), (2, 1))


def cuts(route):
    steps = set()
    for a, b in ROUTES[route]:
        up = 1 if b > a else -1
        steps |= {(c, c + up) for c in range(a, b, up)}
    return steps


def position():
    place = lax.axis_index("pop")
    return place // SHARDS, lax.rem(place, SHARDS)


def copied_from(winner):
    loser, source = jnp.int32(0), jnp.int32(0)
    for m in range(PLANES):
        taken = winner[m] != m
        loser = jnp.where(taken, m, loser)
        source = jnp.where(taken, winner[m], source)
    return loser, source


def route_kernel(winner, code):
    loser, source = copied_from(winner)
    scale = jnp.where(lax.axis_index("rep") == 0, len(ROUTES), 1)
    value = jnp.int32(len(ROUTES) ** 2)
    for number, hops in enumerate(ROUTES):
        for a, b in hops:
            value = jnp.where((source == a) & (loser == b), number * scale, value)
    code[...] = jnp.full(code.shape, value, jnp.int32)


def route_code(winner):
    return pl.pallas_call(
        route_kernel,
        out_shape=jax.ShapeDtypeStruct((8, 128), jnp.int32),
        in_specs=[SMEM],
        out_specs=VMEM,
        name="route_code",
    )(winner)


def pack_kernel(code, tokens, targets, *parts):
    _, k = position()
    width = targets.shape[2] // SHARDS
    slim = tokens.shape[2] // SHARDS
    for j, part in enumerate(parts):
        q = k ^ j
        part[:, :width] = targets[0, :, pl.ds(pl.multiple_of(q * width, 128), width)]
        part[:, width:] = tokens[0, :, pl.ds(pl.multiple_of(q * slim, 128), slim)]


def pack(code, tokens, targets):
    tile = tokens.shape[1]
    row = (tokens.shape[2] + targets.shape[2]) // SHARDS
    return pl.pallas_call(
        pack_kernel,
        out_shape=[jax.ShapeDtypeStruct((tile, row), tokens.dtype)] * SHARDS,
        in_specs=[VMEM] * 3,
        out_specs=[VMEM] * SHARDS,
        name="pack_quarters",
    )(code, tokens, targets)


def copy_rows(ref, start, out, at, count, columns=slice(None)):
    step = 16

    def body(i, _):
        rows = pl.ds(pl.multiple_of(at + i * step, step), step)
        out[rows, :] = ref[pl.ds(start + i * step, step), columns]
        return 0

    lax.fori_loop(0, count // step, body, 0, unroll=4)


def split_kernel(one, two, three, *halves):
    count = one.shape[0] // 2
    for h, half in enumerate(halves):
        for n, part in enumerate((one, two, three)):
            copy_rows(part, h * count, half, n * count, count)


def split_rows(parts):
    tile, row = parts[0].shape
    half = jax.ShapeDtypeStruct((len(parts) * tile // 2, row), parts[0].dtype)
    return pl.pallas_call(
        split_kernel,
        out_shape=[half, half],
        in_specs=[VMEM] * len(parts),
        out_specs=[VMEM, VMEM],
        name="split_rows",
    )(*parts)


def in_pool(t, m, k):
    ahead = t // SHARDS - m
    ahead = jnp.where(m == 1, ahead, -ahead)
    group = jnp.where(ahead == 0, 0, jnp.where(ahead == -1, 1, ahead + 1))
    return group * SHARDS + (lax.rem(t, SHARDS) ^ k)


def piece(pool, which, h):
    group, j = divmod(which, SHARDS)
    whole, halves = pool[group]
    rows = whole.shape[0] // 2
    return (whole, h * rows, rows) if j == 0 else (halves[h], (j - 1) * rows, rows)


def grouped(refs, halves):
    size = 1 + len(halves)
    pool = []
    for g in range(PLANES):
        group = refs[g * size : (g + 1) * size]
        pool.append((group[0], dict(zip(halves, group[1:]))))
    return pool, refs[PLANES * size :]


def pick_for_end_kernel(h, tile_ids, *refs):
    pool, (out,) = grouped(refs, (h,))
    m, k = position()
    end = jnp.where(m <= 1, 0, PLANES - 1)

    def slot(s, _):
        place = in_pool(tile_ids[end, s], m, k)
        for which in range(PLANES * SHARDS):
            ref, start, rows = piece(pool, which, h)

            @pl.when(place == which)
            def _():
                copy_rows(ref, start, out, s * rows, rows)

        return 0

    lax.fori_loop(0, tile_ids.shape[1], slot, 0)


def pick_for_end(h, tile_ids, pool):
    slots = tile_ids.shape[1]
    tile, row = pool[0][0].shape
    operands = [x for whole, halves in pool for x in (whole, halves[h])]
    return pl.pallas_call(
        functools.partial(pick_for_end_kernel, h),
        out_shape=jax.ShapeDtypeStruct((slots * tile // 2, row), operands[0].dtype),
        in_specs=[SMEM] + [VMEM] * len(operands),
        out_specs=VMEM,
        compiler_params=pltpu.CompilerParams(vmem_limit_bytes=32 * 1024 * 1024),
        name="pick_for_end",
    )(tile_ids, *operands)


def pick_own_kernel(tile_ids, *refs):
    pool, (handed_a, handed_b, quarter, targets) = grouped(refs, (0, 1))
    handed = (handed_a, handed_b)
    m, k = position()
    width = targets.shape[1]
    at_end = (m == 0) | (m == PLANES - 1)
    half = quarter.shape[0] // tile_ids.shape[1] // 2

    def slot(s, _):
        place = jnp.where(at_end, -1, in_pool(tile_ids[m, s], m, k))
        for h in range(2):
            at = (2 * s + h) * half

            @pl.when(at_end)
            def _():
                start = pl.multiple_of(s * half, half)
                copy_rows(handed[h], start, targets, at, half, slice(0, width))
                copy_rows(handed[h], start, quarter, at, half, slice(width, None))

            for which in range(PLANES * SHARDS):
                ref, start, rows = piece(pool, which, h)

                @pl.when(place == which)
                def _():
                    copy_rows(ref, start, targets, at, rows, slice(0, width))
                    copy_rows(ref, start, quarter, at, rows, slice(width, None))

        return 0

    lax.fori_loop(0, tile_ids.shape[1], slot, 0)


def pick_own(tile_ids, pool, handed, width):
    rows, row = handed[0].shape
    operands = [x for whole, halves in pool for x in (whole, *halves)]
    return pl.pallas_call(
        pick_own_kernel,
        out_shape=[
            jax.ShapeDtypeStruct((2 * rows, row - width), handed[0].dtype),
            jax.ShapeDtypeStruct((2 * rows, width), handed[0].dtype),
        ],
        in_specs=[SMEM] + [VMEM] * (len(operands) + 2),
        out_specs=[VMEM, VMEM],
        compiler_params=pltpu.CompilerParams(vmem_limit_bytes=32 * 1024 * 1024),
        name="pick_own",
    )(tile_ids, *operands, *handed)


def grad_kernel(
    winner, task_weight, slot_task, slot_tokens, in0, in1, in2, in3, targets, own_w, sent_a, sent_b,
    grad, loss, w_buf, delta, sem,
):
    m, k = position()
    cut = sent_a.shape[0]
    spans = (pl.ds(0, cut), pl.ds(cut, sent_b.shape[0]))

    @pl.when(winner[m] != m)
    def _():
        for h, sent in enumerate((sent_a, sent_b)):
            pltpu.make_async_copy(sent, w_buf.at[spans[h]], sem.at[h]).start()

    @pl.when(winner[m] == m)
    def _():
        for h, at in enumerate(spans):
            pltpu.make_async_copy(own_w.at[0, at], w_buf.at[at], sem.at[h]).start()

    slots = slot_task.shape[1]
    tile = in0.shape[0] // slots
    slim = in0.shape[1]
    ins = (in0, in1, in2, in3)
    for h, at in enumerate(spans):
        pltpu.make_async_copy(own_w.at[0, at], w_buf.at[at], sem.at[h]).wait()

    def slot(s, total):
        task = slot_task[m, s]
        count = jnp.int32(0)
        for o in range(slots):
            count = count + jnp.where(slot_task[m, o] == task, slot_tokens[m, o], 0)
        span = pl.ds(pl.multiple_of(s * tile, tile), tile)
        pre = None
        for j in range(SHARDS):
            at = pl.ds(pl.multiple_of((k ^ j) * slim, slim), slim)
            one = jnp.dot(ins[j][span, :], w_buf[at, :], preferred_element_type=jnp.float32)
            pre = one if pre is None else pre + one
        live = lax.broadcasted_iota(jnp.int32, pre.shape, 0) < slot_tokens[m, s]
        many = jnp.full(pre.shape, jnp.maximum(count, 1), jnp.int32).astype(jnp.float32)
        coef = jnp.where(live, task_weight[winner[m], task] / many, 0.0)
        hidden, slope = gelu_pair(pre)
        diff = hidden - targets[span, :].astype(jnp.float32)
        scaled = coef * diff
        delta[span, :] = (2.0 * scaled * slope).astype(jnp.bfloat16)
        return total + jnp.sum(scaled * diff, keepdims=True)

    total = lax.fori_loop(0, slots, slot, jnp.zeros((1, 1), jnp.float32))
    lane = lax.broadcasted_iota(jnp.int32, loss.shape, 1)
    loss[...] = jnp.where(lane == m, total, 0.0)
    for j in range(SHARDS):
        at = pl.ds(pl.multiple_of((k ^ j) * slim, slim), slim)
        grad[at, :] = lax.dot_general(
            ins[j][...], delta[...], (((0,), (0,)), ((), ())), preferred_element_type=jnp.float32
        )


def gradient(winner, task_weight, slot_task, slot_tokens, ins, targets, own_w, sent):
    rows, width = targets.shape
    depth = own_w.shape[1]
    return pl.pallas_call(
        grad_kernel,
        out_shape=[
            jax.ShapeDtypeStruct((depth, width), jnp.float32),
            jax.ShapeDtypeStruct((8, 128), jnp.float32),
        ],
        in_specs=[SMEM] * 4 + [VMEM] * 5 + [ANY] * 3,
        out_specs=[VMEM, VMEM],
        scratch_shapes=[
            pltpu.VMEM((depth, width), own_w.dtype),
            pltpu.VMEM((rows, width), jnp.bfloat16),
            pltpu.SemaphoreType.DMA((2,)),
        ],
        compiler_params=pltpu.CompilerParams(vmem_limit_bytes=32 * 1024 * 1024),
        name="forward_and_gradient",
    )(winner, task_weight, slot_task, slot_tokens, *ins, targets, own_w, *sent)


def adam_kernel(here, winner, learn_rate, explore, grad, *refs):
    own, sent, refs = refs[:3], refs[3:6], refs[6:]
    new, bufs, outs, (in_sem, out_sem) = refs[-11:-8], refs[-8:-5], refs[-5:-2], refs[-2:]
    m, _ = position()
    blocks = in_sem.shape[1]
    rows = bufs[0].shape[0]
    step = rows // blocks

    def copy(i, b, taken):
        at = pl.ds(b * step, step)
        ref = sent[i].at[at] if taken else own[i].at[0, pl.ds(here + b * step, step)]
        return pltpu.make_async_copy(ref, bufs[i].at[at], in_sem.at[i, b])

    def result(i, b):
        return pltpu.make_async_copy(
            outs[i].at[pl.ds(b * step, step)],
            new[i].at[0, pl.ds(here + b * step, step)],
            out_sem.at[i, b],
        )

    @pl.when(winner[m] != m)
    def _():
        for b in range(blocks):
            for i in range(3):
                copy(i, b, True).start()

    @pl.when(winner[m] == m)
    def _():
        for b in range(blocks):
            for i in range(3):
                copy(i, b, False).start()

    rate = learn_rate[winner[m]] * jnp.where(winner[m] != m, explore[m], 1.0)
    for b in range(blocks):
        for i in range(3):
            copy(i, b, False).wait()

        def body(n, _):
            at = pl.ds(pl.multiple_of(b * step + n * 16, 16), 16)
            g = grad[pl.ds(pl.multiple_of(here + b * step + n * 16, 16), 16), :]
            first = beta_one * bufs[1][at, :].astype(jnp.float32) + (1.0 - beta_one) * g
            second = beta_two * bufs[2][at, :].astype(jnp.float32) + (1.0 - beta_two) * g * g
            start = bufs[0][at, :].astype(jnp.float32)
            updated = start - rate * first / (jnp.sqrt(second) + adam_eps)
            outs[0][at, :] = updated.astype(outs[0].dtype)
            outs[1][at, :] = first.astype(outs[1].dtype)
            outs[2][at, :] = second.astype(outs[2].dtype)
            return 0

        lax.fori_loop(0, step // 16, body, 0, unroll=2)
        for i in range(3):
            result(i, b).start()
    for b in range(blocks):
        for i in range(3):
            result(i, b).wait()


def adam(here, winner, learn_rate, explore, grad, own, sent, begun=()):
    rows, width = sent[0].shape
    blocks = 2
    return pl.pallas_call(
        functools.partial(adam_kernel, here),
        out_shape=[jax.ShapeDtypeStruct(x.shape, x.dtype) for x in own],
        in_specs=[SMEM] * 3 + [VMEM] + [ANY] * (6 + len(begun)),
        out_specs=[ANY] * 3,
        scratch_shapes=[pltpu.VMEM((rows, width), x.dtype) for x in own] * 2
        + [pltpu.SemaphoreType.DMA((3, blocks))] * 2,
        input_output_aliases={10 + i: i for i in range(len(begun))},
        compiler_params=pltpu.CompilerParams(vmem_limit_bytes=32 * 1024 * 1024),
        name="adam_half",
    )(winner, learn_rate, explore, grad, *own, *sent, *begun)


def in_plane(x, j):
    pairs = [(m * SHARDS + k, m * SHARDS + (k ^ j)) for m in range(PLANES) for k in range(SHARDS)]
    return lax.ppermute(x, "pop", pairs)


def along(x, hops):
    idle = [m for m in range(PLANES) if all(m not in hop for hop in hops)]
    pairs = [(a * SHARDS + k, b * SHARDS + k) for a, b in hops for k in range(SHARDS)]
    pairs += [(m * SHARDS + k, m * SHARDS + (k ^ 1)) for m in idle for k in range(SHARDS)]
    return lax.ppermute(x, "pop", pairs)


def beside(x):
    return lax.ppermute(x, "rep", [(0, 1), (1, 0)])


def exploit(x, routes):
    nodes = PLANES * SHARDS
    pairs = [
        (rep * nodes + a * SHARDS + k, rep * nodes + b * SHARDS + k)
        for rep, number in enumerate(routes)
        for a, b in ROUTES[number]
        for k in range(SHARDS)
    ]
    return lax.ppermute(x, ("rep", "pop"), pairs)


def after(x, *others):
    return lax.optimization_barrier((x, *others))[0]


def tiles(here, tile_ids, width):
    near0, middle0, (here0, halves) = here
    near = [along(x, ENDS) for x in halves]
    far0 = along(near0, MIDDLE)
    middle = [along(x, MIDDLE) for x in halves]
    far = [along(x, MIDDLE) for x in near]
    pool = [(here0, halves), (near0, near), (middle0, middle), (far0, far)]
    handed = [along(pick_for_end(h, tile_ids, pool), ENDS) for h in range(2)]
    quarter, targets = pick_own(tile_ids, pool, handed, width)
    side = in_plane(quarter, 1)
    cross = in_plane(quarter, 2)
    return near, far, handed, (quarter, side, cross, in_plane(cross, 1)), targets


def finish(
    ins, targets, own, lower, upper, winner, learn_rate, explore, task_weight, slot_task, slot_tokens
):
    grad, loss = gradient(
        winner, task_weight, slot_task, slot_tokens, ins, targets, own[0], (lower[0], upper[0])
    )
    loss = loss + in_plane(loss, 1)
    loss = loss + in_plane(loss, 2)
    ring = [along(loss, [(m, (m + d) % PLANES) for m in range(PLANES)]) for d in range(1, PLANES)]
    loss = loss + ring[0] + ring[1] + ring[2]
    new = adam(0, winner, learn_rate, explore, grad, own, lower)
    new = adam(lower[0].shape[0], winner, learn_rate, explore, grad, own, upper, new)
    return (*new, loss[0, :PLANES])


def direct(
    routes,
    cut,
    here,
    weight,
    first_moment,
    second_moment,
    winner,
    learn_rate,
    explore,
    task_weight,
    tile_ids,
    slot_task,
    slot_tokens,
):
    own = (weight, first_moment, second_moment)
    near, far, handed, ins, targets = tiles(here, tile_ids, weight.shape[2])
    gates = (near[0], near[1], far[0])
    lower = [exploit(after(x[0, :cut], gate), routes) for x, gate in zip(own, gates)]
    if cuts(routes[0]) & cuts(routes[1]):
        upper = [exploit(after(x[0, cut:], gate), routes) for x, gate in zip(own, gates)]
    else:
        guests = [beside(x[0, cut:]) for x in own]
        guests = [exploit(after(x, gate), routes[::-1]) for x, gate in zip(guests, gates)]
        gates = (handed[0], ins[0], ins[0])
        upper = [beside(after(x, gate)) for x, gate in zip(guests, gates)]
    return finish(
        ins, targets, own, lower, upper, winner, learn_rate, explore, task_weight, slot_task, slot_tokens
    )


def around(
    cut,
    here,
    weight,
    first_moment,
    second_moment,
    winner,
    learn_rate,
    explore,
    task_weight,
    tile_ids,
    slot_task,
    slot_tokens,
):
    own = (weight, first_moment, second_moment)
    _, _, _, ins, targets = tiles(here, tile_ids, weight.shape[2])
    loser, source = copied_from(winner)
    hops = lax.rem(loser - source + PLANES, PLANES)
    passing, sent = own, own
    for hop in range(1, PLANES):
        passing = tuple(along(x, RING) for x in passing)
        sent = tuple(jnp.where(hops == hop, x, y) for x, y in zip(passing, sent))
    lower, upper = [x[0, :cut] for x in sent], [x[0, cut:] for x in sent]
    return finish(
        ins, targets, own, lower, upper, winner, learn_rate, explore, task_weight, slot_task, slot_tokens
    )


def choose(index, branches, *operands):
    if len(branches) == 1:
        return branches[0](*operands)
    half = len(branches) // 2
    return lax.cond(
        index < half,
        functools.partial(choose, index, branches[:half]),
        functools.partial(choose, index - half, branches[half:]),
        *operands,
    )


def per_device(pool_tokens, pool_targets, weight, *args):
    members = args[2].shape[0]
    if members != PLANES or lax.axis_size("rep") != 2:
        return relayed(pool_tokens, pool_targets, weight, *args)
    code = route_code(args[2])
    index = (code + beside(code))[0, 0]
    parts = pack(code, pool_tokens, pool_targets)
    near0, middle0 = along(parts[0], ENDS), along(parts[0], MIDDLE)
    halves = split_rows([in_plane(parts[j], j) for j in range(1, SHARDS)])
    cut = weight.shape[1] * 9 // 16
    branches = [
        functools.partial(direct, (a, b), cut) for a in range(len(ROUTES)) for b in range(len(ROUTES))
    ]
    branches.append(functools.partial(around, cut))
    here = (near0, middle0, (parts[0], halves))
    return choose(index, branches, here, weight, *args)


def solution(mesh):
    in_specs = (
        P(("rep", "pop"), None, None),
        P(("rep", "pop"), None, None),
        P(("rep", "pop"), None, None),
        P(("rep", "pop"), None, None),
        P(("rep", "pop"), None, None),
        P("rep"),
        P("rep"),
        P("rep"),
        P("rep", None),
        P("rep", None),
        P("rep", None),
        P("rep", None),
    )
    out_specs = (
        P(("rep", "pop"), None, None),
        P(("rep", "pop"), None, None),
        P(("rep", "pop"), None, None),
        P("rep"),
    )
    return jax.shard_map(
        per_device, mesh=mesh, in_specs=in_specs, out_specs=out_specs, check_vma=False
    )
```

```python
import functools

import jax
import jax.numpy as jnp
from jax import lax
from jax.experimental import pallas as pl
from jax.experimental.pallas import tpu as pltpu
from jax.sharding import PartitionSpec as P

SHARDS = 4
TASKS = 8
PLANES = 4


beta_one = 0.9
beta_two = 0.999
adam_eps = 1e-08
gelu_coef = 0.7978845608028654

SMEM = pl.BlockSpec(memory_space=pltpu.SMEM)
VMEM = pl.BlockSpec(memory_space=pltpu.VMEM)
ANY = pl.BlockSpec(memory_space=pl.ANY)


def gelu_pair(pre):
    inner = jnp.tanh(gelu_coef * (pre + 0.044715 * pre * pre * pre))
    value = 0.5 * pre * (1.0 + inner)
    slope = 0.5 * (1.0 + inner) + 0.5 * pre * (1.0 - inner * inner) * gelu_coef * (
        1.0 + 3.0 * 0.044715 * pre * pre
    )
    return (value, slope)


def for_sending(shard):

    def short(part):
        return part.astype(jnp.bfloat16) if part.dtype == jnp.float32 else part

    return jax.tree.map(short, shard)


def relayed(
    pool_tokens,
    pool_targets,
    weight,
    first_moment,
    second_moment,
    winner,
    learn_rate,
    explore,
    task_weight,
    tile_ids,
    slot_task,
    slot_tokens,
):
    nodes = lax.axis_size("pop")
    place = lax.axis_index("pop")
    member = place // SHARDS
    shard = place % SHARDS
    members = winner.shape[0]
    slots = tile_ids.shape[1]
    tile = pool_tokens.shape[1]
    depth = pool_tokens.shape[2]
    width = weight.shape[2]
    hidden_all = pool_targets.shape[2]
    reach = tile // nodes
    flat_state = (
        weight.reshape(nodes, -1),
        first_moment.reshape(nodes, -1),
        second_moment.reshape(nodes, -1),
    )
    spread = (
        lax.all_to_all(flat_state[0], "pop", split_axis=0, concat_axis=0, tiled=True),
        lax.all_to_all(flat_state[1], "pop", split_axis=0, concat_axis=0, tiled=True),
        lax.all_to_all(flat_state[2], "pop", split_axis=0, concat_axis=0, tiled=True),
    )
    source_rows = (winner[:, None] * SHARDS + jnp.arange(SHARDS, dtype=jnp.int32)[None, :]).reshape(
        -1
    )
    picked_state = tuple((jnp.take(piece, source_rows, axis=0) for piece in spread))
    returned = jax.tree.map(
        lambda part, own: part.astype(own.dtype),
        lax.all_to_all(for_sending(picked_state), "pop", split_axis=0, concat_axis=0, tiled=True),
        picked_state,
    )
    start_weight = returned[0].reshape(depth, width)
    start_first = returned[1].reshape(depth, width)
    start_second = returned[2].reshape(depth, width)
    relay_tokens, relay_targets = (
        lax.all_to_all(pool_tokens, "pop", split_axis=1, concat_axis=0, tiled=True),
        lax.all_to_all(pool_targets, "pop", split_axis=1, concat_axis=0, tiled=True),
    )
    flat_ids = tile_ids.reshape(-1)
    pick_tokens = jnp.take(relay_tokens, flat_ids, axis=0).reshape(members, 1, slots, reach, depth)
    send_tokens = jnp.broadcast_to(pick_tokens, (members, SHARDS, slots, reach, depth)).reshape(
        nodes, slots, reach, depth
    )
    pick_targets = jnp.take(relay_targets, flat_ids, axis=0).reshape(
        members, slots, reach, hidden_all
    )
    send_targets = jnp.broadcast_to(
        pick_targets[:, None], (members, SHARDS, slots, reach, hidden_all)
    ).reshape(nodes, slots, reach, hidden_all)
    got_tokens, got_targets = (
        lax.all_to_all(send_tokens, "pop", split_axis=0, concat_axis=2, tiled=True),
        lax.all_to_all(send_targets, "pop", split_axis=0, concat_axis=2, tiled=True),
    )
    targets = lax.dynamic_slice_in_dim(got_targets[0], shard * width, width, 2).reshape(
        slots * tile, width
    )
    inputs = got_tokens.reshape(slots * tile, depth)
    tasks_here = lax.dynamic_index_in_dim(slot_task, member, 0, keepdims=False)
    lengths = lax.dynamic_index_in_dim(slot_tokens, member, 0, keepdims=False)
    source_member = lax.dynamic_index_in_dim(winner, member, 0, keepdims=False)
    onehot = tasks_here[:, None] == jnp.arange(TASKS, dtype=jnp.int32)[None, :]
    counts = jnp.sum(jnp.where(onehot, lengths[:, None], 0), axis=0)
    weights_here = lax.dynamic_index_in_dim(task_weight, source_member, 0, keepdims=False)
    scale = weights_here / jnp.maximum(counts, 1).astype(jnp.float32)
    per_slot = jnp.sum(jnp.where(onehot, scale[None, :], jnp.float32(0.0)), axis=1)
    live = jnp.arange(tile, dtype=jnp.int32)[None, :] < lengths[:, None]
    coef = jnp.where(live, per_slot[:, None], jnp.float32(0.0)).reshape(-1)
    own_rate = lax.dynamic_index_in_dim(learn_rate, source_member, 0, keepdims=False)
    own_explore = lax.dynamic_index_in_dim(explore, member, 0, keepdims=False)
    step_rate = own_rate * jnp.where(source_member != member, own_explore, jnp.float32(1.0))
    pre = jnp.dot(inputs, start_weight, preferred_element_type=jnp.float32)
    hidden, slope = gelu_pair(pre)
    diff = hidden - targets.astype(jnp.float32)
    part = jnp.sum(coef[:, None] * diff * diff)
    delta = (2.0 * coef[:, None] * diff * slope).astype(jnp.bfloat16)
    grad = lax.dot_general(
        inputs, delta, (((0,), (0,)), ((), ())), preferred_element_type=jnp.float32
    )
    first = beta_one * start_first.astype(jnp.float32) + (1.0 - beta_one) * grad
    second = beta_two * start_second.astype(jnp.float32) + (1.0 - beta_two) * grad * grad
    updated = start_weight.astype(jnp.float32) - step_rate * first / (jnp.sqrt(second) + adam_eps)
    share = jnp.where(jnp.arange(members, dtype=jnp.int32) == member, part, jnp.float32(0.0))
    member_loss = lax.psum(share, "pop")
    return (
        updated.astype(jnp.bfloat16)[None],
        first.astype(jnp.bfloat16)[None],
        second.astype(jnp.bfloat16)[None],
        member_loss,
    )


ENDS = ((0, 1), (1, 0), (2, 3), (3, 2))
MIDDLE = ((1, 2), (2, 1))


def position():
    place = lax.axis_index("pop")
    return place // SHARDS, lax.rem(place, SHARDS)


def copied_from(winner):
    loser, source = jnp.int32(0), jnp.int32(0)
    for m in range(PLANES):
        taken = winner[m] != m
        loser = jnp.where(taken, m, loser)
        source = jnp.where(taken, winner[m], source)
    return loser, source


def route_kernel(winner, code):
    loser, source = copied_from(winner)
    code[...] = jnp.full(code.shape, source * PLANES + loser, jnp.int32)


def route_code(winner):
    return pl.pallas_call(
        route_kernel,
        out_shape=jax.ShapeDtypeStruct((8, 128), jnp.int32),
        in_specs=[SMEM],
        out_specs=VMEM,
        name="route_code",
    )(winner)


def routes(winner, other):
    loser, source = copied_from(winner)
    code = other[0, 0]
    source2, loser2 = lax.div(code, jnp.int32(PLANES)), lax.rem(code, jnp.int32(PLANES))
    upward = jnp.maximum(source, source2) < jnp.minimum(loser, loser2)
    downward = jnp.maximum(loser, loser2) < jnp.minimum(source, source2)
    return (source, loser), (source2, loser2), upward | downward


def last_kernel(winner, other, last):
    (a, b), (c, d), shared = routes(winner, other)
    most = jnp.maximum(jnp.abs(a - b), jnp.abs(c - d))
    last[0] = jnp.where(shared, 6, 3) + most - 1
    last[1] = shared.astype(jnp.int32)


def last_step(winner, other):
    return pl.pallas_call(
        last_kernel,
        out_shape=jax.ShapeDtypeStruct((2,), jnp.int32),
        in_specs=[SMEM, SMEM],
        out_specs=SMEM,
        name="last_step",
    )(winner, other)


def on_route(route, m, to):
    source, loser = route
    upward = (to == m + 1) & (source <= m) & (loser >= to)
    return upward | ((to == m - 1) & (source >= m) & (loser <= to))


def by_ends(route):
    source, loser = route
    return jnp.where(source < loser, loser - 1, loser + 1) == (loser ^ 1)


def stage_kernel(has_guest, has_last, step, winner, other, *refs):
    state, refs = refs[:3], refs[3:]
    guest = refs[0] if has_guest else None
    from_ends, from_middle = refs[has_guest : has_guest + 2] if has_last else (None, None)
    to_ends, to_middle, sem = refs[-3:]
    m, _ = position()
    mine, theirs, shared = routes(winner, other)
    t = step[0]
    half = to_ends.shape[0]
    array = jnp.where(shared, lax.div(t - 1, jnp.int32(2)), t - 1)
    start = pl.multiple_of(jnp.where(shared, lax.rem(t - 1, jnp.int32(2)), 0) * half, half)

    def fill(out, to, passed):
        own = on_route(mine, m, to)
        theirs_too = on_route(theirs, m, to) & jnp.logical_not(shared)
        send_own = own & (m == mine[0])
        send_guest = theirs_too & (m == theirs[0])
        for a, ref in enumerate(state):

            @pl.when(send_own & (array == a))
            def _():
                copy = pltpu.make_async_copy(ref.at[0, pl.ds(start, half)], out, sem)
                copy.start()
                copy.wait()

        if guest is not None:

            @pl.when(send_guest)
            def _():
                copy_rows(guest, 0, out, 0, half)

        if passed is not None:

            @pl.when((own & (m != mine[0])) | (theirs_too & (m != theirs[0])))
            def _():
                copy_rows(passed, 0, out, 0, half)

    fill(to_ends, m ^ 1, from_middle)
    fill(to_middle, jnp.where(m == 1, 2, jnp.where(m == 2, 1, -1)), from_ends)


def stage(step, winner, other, own, guest=None, last=()):
    half, width = own[0].shape[1] // 2, own[0].shape[2]
    guests = () if guest is None else (guest,)
    return pl.pallas_call(
        functools.partial(stage_kernel, len(guests), len(last) > 0),
        out_shape=[jax.ShapeDtypeStruct((half, width), own[0].dtype)] * 2,
        in_specs=[SMEM] * 3 + [ANY] * 3 + [VMEM] * (len(guests) + len(last)),
        out_specs=[VMEM, VMEM],
        scratch_shapes=[pltpu.SemaphoreType.DMA],
        name="stage_chunk",
    )(step, winner, other, *own, *guests, *last)


def arrived_kernel(winner, other, from_ends, from_middle, mine, theirs):
    own_route, other_route, _ = routes(winner, other)
    for route, out in ((own_route, mine), (other_route, theirs)):
        ends = by_ends(route)

        @pl.when(ends)
        def _():
            copy_rows(from_ends, 0, out, 0, out.shape[0])

        @pl.when(jnp.logical_not(ends))
        def _():
            copy_rows(from_middle, 0, out, 0, out.shape[0])


def arrived(winner, other, from_ends, from_middle):
    return pl.pallas_call(
        arrived_kernel,
        out_shape=[jax.ShapeDtypeStruct(from_ends.shape, from_ends.dtype)] * 2,
        in_specs=[SMEM] * 2 + [VMEM] * 2,
        out_specs=[VMEM, VMEM],
        name="arrived_chunk",
    )(winner, other, from_ends, from_middle)


def room(count, like):
    return pl.pallas_call(
        lambda out: None,
        out_shape=jax.ShapeDtypeStruct((count, *like.shape), like.dtype),
        out_specs=ANY,
        name="room_for_chunks",
    )()


def start_copies(winner, other, a, h, own, sent, out, sem):
    arrivals, late_arrivals, backs, late_backs = sent
    m, _ = position()
    (source, loser), _, shared = routes(winner, other)
    hops = jnp.abs(source - loser)
    taken = winner[m] != m
    half = out.shape[0]
    step = jnp.where(shared, 2 * a + h + hops, a + hops)
    direct = shared if h == 1 else True

    def copy(ref):
        return pltpu.make_async_copy(ref, out, sem)

    @pl.when(jnp.logical_not(taken))
    def _():
        copy(own.at[0, pl.ds(h * half, half)]).start()

    sides = ((arrivals, late_arrivals, direct),)
    if h == 1:
        sides += ((backs, late_backs, jnp.logical_not(shared)),)
    for early, late, here in sides:
        for n, ref in enumerate(early):

            @pl.when(taken & here & (step == n + 1))
            def _():
                copy(ref).start()

        @pl.when(taken & here & (step > len(early)))
        def _():
            copy(late.at[jnp.clip(step - len(early) - 1, 0, late.shape[0] - 1)]).start()

    return copy(own.at[0, pl.ds(h * half, half)])


def sent_refs(refs):
    return refs[0:3], refs[3], refs[4:7], refs[7]


def pack_kernel(code, tokens, targets, *parts):
    _, k = position()
    width = targets.shape[2] // SHARDS
    slim = tokens.shape[2] // SHARDS
    for j, part in enumerate(parts):
        q = k ^ j
        part[:, :width] = targets[0, :, pl.ds(pl.multiple_of(q * width, 128), width)]
        part[:, width:] = tokens[0, :, pl.ds(pl.multiple_of(q * slim, 128), slim)]


def pack(code, tokens, targets):
    tile = tokens.shape[1]
    row = (tokens.shape[2] + targets.shape[2]) // SHARDS
    return pl.pallas_call(
        pack_kernel,
        out_shape=[jax.ShapeDtypeStruct((tile, row), tokens.dtype)] * SHARDS,
        in_specs=[VMEM] * 3,
        out_specs=[VMEM] * SHARDS,
        name="pack_quarters",
    )(code, tokens, targets)


def copy_rows(ref, start, out, at, count, columns=slice(None)):
    step = 16

    def body(i, _):
        rows = pl.ds(pl.multiple_of(at + i * step, step), step)
        out[rows, :] = ref[pl.ds(start + i * step, step), columns]
        return 0

    lax.fori_loop(0, count // step, body, 0, unroll=4)


def split_kernel(one, two, three, *halves):
    count = one.shape[0] // 2
    for h, half in enumerate(halves):
        for n, part in enumerate((one, two, three)):
            copy_rows(part, h * count, half, n * count, count)


def split_rows(parts):
    tile, row = parts[0].shape
    half = jax.ShapeDtypeStruct((len(parts) * tile // 2, row), parts[0].dtype)
    return pl.pallas_call(
        split_kernel,
        out_shape=[half, half],
        in_specs=[VMEM] * len(parts),
        out_specs=[VMEM, VMEM],
        name="split_rows",
    )(*parts)


def in_pool(t, m, k):
    ahead = t // SHARDS - m
    ahead = jnp.where(m == 1, ahead, -ahead)
    group = jnp.where(ahead == 0, 0, jnp.where(ahead == -1, 1, ahead + 1))
    return group * SHARDS + (lax.rem(t, SHARDS) ^ k)


def piece(pool, which, h):
    group, j = divmod(which, SHARDS)
    whole, halves = pool[group]
    rows = whole.shape[0] // 2
    return (whole, h * rows, rows) if j == 0 else (halves[h], (j - 1) * rows, rows)


def grouped(refs, halves):
    size = 1 + len(halves)
    pool = []
    for g in range(PLANES):
        group = refs[g * size : (g + 1) * size]
        pool.append((group[0], dict(zip(halves, group[1:]))))
    return pool, refs[PLANES * size :]


def pick_for_end_kernel(h, tile_ids, *refs):
    pool, (out,) = grouped(refs, (h,))
    m, k = position()
    end = jnp.where(m <= 1, 0, PLANES - 1)

    def slot(s, _):
        place = in_pool(tile_ids[end, s], m, k)
        for which in range(PLANES * SHARDS):
            ref, start, rows = piece(pool, which, h)

            @pl.when(place == which)
            def _():
                copy_rows(ref, start, out, s * rows, rows)

        return 0

    lax.fori_loop(0, tile_ids.shape[1], slot, 0)


def pick_for_end(h, tile_ids, pool):
    slots = tile_ids.shape[1]
    tile, row = pool[0][0].shape
    operands = [x for whole, halves in pool for x in (whole, halves[h])]
    return pl.pallas_call(
        functools.partial(pick_for_end_kernel, h),
        out_shape=jax.ShapeDtypeStruct((slots * tile // 2, row), operands[0].dtype),
        in_specs=[SMEM] + [VMEM] * len(operands),
        out_specs=VMEM,
        compiler_params=pltpu.CompilerParams(vmem_limit_bytes=32 * 1024 * 1024),
        name="pick_for_end",
    )(tile_ids, *operands)


def pick_own_kernel(tile_ids, *refs):
    pool, (handed_a, handed_b, quarter, targets) = grouped(refs, (0, 1))
    handed = (handed_a, handed_b)
    m, k = position()
    width = targets.shape[1]
    at_end = (m == 0) | (m == PLANES - 1)
    half = quarter.shape[0] // tile_ids.shape[1] // 2

    def slot(s, _):
        place = jnp.where(at_end, -1, in_pool(tile_ids[m, s], m, k))
        for h in range(2):
            at = (2 * s + h) * half

            @pl.when(at_end)
            def _():
                start = pl.multiple_of(s * half, half)
                copy_rows(handed[h], start, targets, at, half, slice(0, width))
                copy_rows(handed[h], start, quarter, at, half, slice(width, None))

            for which in range(PLANES * SHARDS):
                ref, start, rows = piece(pool, which, h)

                @pl.when(place == which)
                def _():
                    copy_rows(ref, start, targets, at, rows, slice(0, width))
                    copy_rows(ref, start, quarter, at, rows, slice(width, None))

        return 0

    lax.fori_loop(0, tile_ids.shape[1], slot, 0)


def pick_own(tile_ids, pool, handed, width):
    rows, row = handed[0].shape
    operands = [x for whole, halves in pool for x in (whole, *halves)]
    return pl.pallas_call(
        pick_own_kernel,
        out_shape=[
            jax.ShapeDtypeStruct((2 * rows, row - width), handed[0].dtype),
            jax.ShapeDtypeStruct((2 * rows, width), handed[0].dtype),
        ],
        in_specs=[SMEM] + [VMEM] * (len(operands) + 2),
        out_specs=[VMEM, VMEM],
        compiler_params=pltpu.CompilerParams(vmem_limit_bytes=32 * 1024 * 1024),
        name="pick_own",
    )(tile_ids, *operands, *handed)


def grad_kernel(
    winner, other, task_weight, slot_task, slot_tokens, in0, in1, in2, in3, targets, own_w, *refs
):
    sent, (grad, loss, w_buf, delta, sem) = sent_refs(refs[:8]), refs[8:]
    m, k = position()
    half = w_buf.shape[0] // 2
    copies = [
        start_copies(winner, other, 0, h, own_w, sent, w_buf.at[pl.ds(h * half, half)], sem.at[h])
        for h in range(2)
    ]
    slots = slot_task.shape[1]
    tile = in0.shape[0] // slots
    slim = in0.shape[1]
    ins = (in0, in1, in2, in3)
    for copy in copies:
        copy.wait()

    def slot(s, total):
        task = slot_task[m, s]
        count = jnp.int32(0)
        for o in range(slots):
            count = count + jnp.where(slot_task[m, o] == task, slot_tokens[m, o], 0)
        span = pl.ds(pl.multiple_of(s * tile, tile), tile)
        pre = None
        for j in range(SHARDS):
            at = pl.ds(pl.multiple_of((k ^ j) * slim, slim), slim)
            one = jnp.dot(ins[j][span, :], w_buf[at, :], preferred_element_type=jnp.float32)
            pre = one if pre is None else pre + one
        live = lax.broadcasted_iota(jnp.int32, pre.shape, 0) < slot_tokens[m, s]
        many = jnp.full(pre.shape, jnp.maximum(count, 1), jnp.int32).astype(jnp.float32)
        coef = jnp.where(live, task_weight[winner[m], task] / many, 0.0)
        hidden, slope = gelu_pair(pre)
        diff = hidden - targets[span, :].astype(jnp.float32)
        scaled = coef * diff
        delta[span, :] = (2.0 * scaled * slope).astype(jnp.bfloat16)
        return total + jnp.sum(scaled * diff, keepdims=True)

    total = lax.fori_loop(0, slots, slot, jnp.zeros((1, 1), jnp.float32))
    lane = lax.broadcasted_iota(jnp.int32, loss.shape, 1)
    loss[...] = jnp.where(lane == m, total, 0.0)
    for j in range(SHARDS):
        at = pl.ds(pl.multiple_of((k ^ j) * slim, slim), slim)
        grad[at, :] = lax.dot_general(
            ins[j][...], delta[...], (((0,), (0,)), ((), ())), preferred_element_type=jnp.float32
        )


def gradient(winner, other, task_weight, slot_task, slot_tokens, ins, targets, own_w, sent):
    rows, width = targets.shape
    depth = own_w.shape[1]
    return pl.pallas_call(
        grad_kernel,
        out_shape=[
            jax.ShapeDtypeStruct((depth, width), jnp.float32),
            jax.ShapeDtypeStruct((8, 128), jnp.float32),
        ],
        in_specs=[SMEM] * 5 + [VMEM] * 5 + [ANY] * (1 + len(sent)),
        out_specs=[VMEM, VMEM],
        scratch_shapes=[
            pltpu.VMEM((depth, width), own_w.dtype),
            pltpu.VMEM((rows, width), jnp.bfloat16),
            pltpu.SemaphoreType.DMA((2,)),
        ],
        compiler_params=pltpu.CompilerParams(vmem_limit_bytes=32 * 1024 * 1024),
        name="forward_and_gradient",
    )(winner, other, task_weight, slot_task, slot_tokens, *ins, targets, own_w, *sent)


def adam_kernel(h, winner, other, learn_rate, explore, grad, *refs):
    own, sent, refs = refs[:3], sent_refs(refs[3:11]), refs[11:]
    new, bufs, outs, (in_sem, out_sem) = refs[-11:-8], refs[-8:-5], refs[-5:-2], refs[-2:]
    m, _ = position()
    blocks = out_sem.shape[1]
    rows = bufs[0].shape[0]
    step = rows // blocks
    here = h * rows

    def result(i, b):
        return pltpu.make_async_copy(
            outs[i].at[pl.ds(b * step, step)],
            new[i].at[0, pl.ds(here + b * step, step)],
            out_sem.at[i, b],
        )

    copies = [
        start_copies(winner, other, a, h, own[a], sent, bufs[a], in_sem.at[a]) for a in range(3)
    ]
    rate = learn_rate[winner[m]] * jnp.where(winner[m] != m, explore[m], 1.0)
    for copy in copies:
        copy.wait()
    for b in range(blocks):

        def body(n, _):
            at = pl.ds(pl.multiple_of(b * step + n * 16, 16), 16)
            g = grad[pl.ds(pl.multiple_of(here + b * step + n * 16, 16), 16), :]
            first = beta_one * bufs[1][at, :].astype(jnp.float32) + (1.0 - beta_one) * g
            second = beta_two * bufs[2][at, :].astype(jnp.float32) + (1.0 - beta_two) * g * g
            start = bufs[0][at, :].astype(jnp.float32)
            updated = start - rate * first / (jnp.sqrt(second) + adam_eps)
            outs[0][at, :] = updated.astype(outs[0].dtype)
            outs[1][at, :] = first.astype(outs[1].dtype)
            outs[2][at, :] = second.astype(outs[2].dtype)
            return 0

        lax.fori_loop(0, step // 16, body, 0, unroll=2)
        for i in range(3):
            result(i, b).start()
    for b in range(blocks):
        for i in range(3):
            result(i, b).wait()


def adam(h, winner, other, learn_rate, explore, grad, own, sent, begun=()):
    depth, width = grad.shape
    blocks = 2
    return pl.pallas_call(
        functools.partial(adam_kernel, h),
        out_shape=[jax.ShapeDtypeStruct(x.shape, x.dtype) for x in own],
        in_specs=[SMEM] * 4 + [VMEM] + [ANY] * (3 + len(sent) + len(begun)),
        out_specs=[ANY] * 3,
        scratch_shapes=[pltpu.VMEM((depth // 2, width), x.dtype) for x in own] * 2
        + [pltpu.SemaphoreType.DMA((3,)), pltpu.SemaphoreType.DMA((3, blocks))],
        input_output_aliases={8 + len(sent) + i: i for i in range(len(begun))},
        compiler_params=pltpu.CompilerParams(vmem_limit_bytes=32 * 1024 * 1024),
        name="adam_half",
    )(winner, other, learn_rate, explore, grad, *own, *sent, *begun)


def in_plane(x, j):
    pairs = [(m * SHARDS + k, m * SHARDS + (k ^ j)) for m in range(PLANES) for k in range(SHARDS)]
    return lax.ppermute(x, "pop", pairs)


def along(x, hops):
    idle = [m for m in range(PLANES) if all(m not in hop for hop in hops)]
    pairs = [(a * SHARDS + k, b * SHARDS + k) for a, b in hops for k in range(SHARDS)]
    pairs += [(m * SHARDS + k, m * SHARDS + (k ^ 1)) for m in idle for k in range(SHARDS)]
    return lax.ppermute(x, "pop", pairs)


def beside(x):
    return lax.ppermute(x, "rep", [(0, 1), (1, 0)])


def after(x, *others):
    return lax.optimization_barrier((x, *others))[0]


def tiles(here, tile_ids, width):
    near0, middle0, (here0, halves) = here
    near = [along(x, ENDS) for x in halves]
    far0 = along(near0, MIDDLE)
    middle = [along(x, MIDDLE) for x in halves]
    far = [along(x, MIDDLE) for x in near]
    pool = [(here0, halves), (near0, near), (middle0, middle), (far0, far)]
    handed = [along(pick_for_end(h, tile_ids, pool), ENDS) for h in range(2)]
    quarter, targets = pick_own(tile_ids, pool, handed, width)
    side = in_plane(quarter, 1)
    cross = in_plane(quarter, 2)
    return (quarter, side, cross, in_plane(cross, 1)), targets


def moved(winner, other, own, ready):
    half = own[0].shape[1] // 2
    last, arrivals, backs = (), [], []
    for t in range(1, 4):
        guest = beside(own[t - 1][0, half:])
        to_ends, to_middle = stage(jnp.full((1,), t, jnp.int32), winner, other, own, guest, last)
        last = (along(to_ends, ENDS), along(to_middle, MIDDLE))
        mine, theirs = arrived(winner, other, *last)
        arrivals.append(mine)
        backs.append(beside(theirs))
    end = last_step(winner, other)

    def more(carry):
        return carry[0] <= end[0]

    def one(carry):
        t, from_ends, from_middle, late_arrivals, late_backs = carry
        to_ends, to_middle = stage(
            t.reshape(1), winner, other, own, None, (from_ends, from_middle)
        )
        from_ends, from_middle = along(to_ends, ENDS), along(to_middle, MIDDLE)
        mine, theirs = arrived(winner, other, from_ends, from_middle)
        late_arrivals = lax.dynamic_update_index_in_dim(late_arrivals, mine, t - 4, 0)
        late_backs = lax.cond(
            end[1] == 1,
            lambda x, y, n: x,
            lambda x, y, n: lax.dynamic_update_index_in_dim(x, beside(y), n, 0),
            late_backs,
            theirs,
            t - 4,
        )
        return t + 1, from_ends, from_middle, late_arrivals, late_backs

    start = after((jnp.int32(4), *last, room(5, last[0]), room(2, last[0])), ready)
    _, _, _, late_arrivals, late_backs = lax.while_loop(more, one, start)
    return (*arrivals, late_arrivals, *backs, late_backs)


def per_device(pool_tokens, pool_targets, weight, first_moment, second_moment, *args):
    winner, learn_rate, explore, task_weight, tile_ids, slot_task, slot_tokens = args
    if winner.shape[0] != PLANES or lax.axis_size("rep") != 2:
        return relayed(pool_tokens, pool_targets, weight, first_moment, second_moment, *args)
    own = (weight, first_moment, second_moment)
    code = route_code(winner)
    other = beside(code)
    parts = pack(code, pool_tokens, pool_targets)
    near0, middle0 = along(parts[0], ENDS), along(parts[0], MIDDLE)
    halves = split_rows([in_plane(parts[j], j) for j in range(1, SHARDS)])
    here = (near0, middle0, (parts[0], halves))
    ins, targets = tiles(here, tile_ids, weight.shape[2])
    sent = moved(winner, other, own, ins[0])
    grad, loss = gradient(
        winner, other, task_weight, slot_task, slot_tokens, ins, targets, weight, sent
    )
    loss = loss + in_plane(loss, 1)
    loss = loss + in_plane(loss, 2)
    ring = [along(loss, [(m, (m + d) % PLANES) for m in range(PLANES)]) for d in range(1, PLANES)]
    loss = loss + ring[0] + ring[1] + ring[2]
    new = adam(0, winner, other, learn_rate, explore, grad, own, sent)
    new = adam(1, winner, other, learn_rate, explore, grad, own, sent, new)
    return (*new, loss[0, :PLANES])


def solution(mesh):
    in_specs = (
        P(("rep", "pop"), None, None),
        P(("rep", "pop"), None, None),
        P(("rep", "pop"), None, None),
        P(("rep", "pop"), None, None),
        P(("rep", "pop"), None, None),
        P("rep"),
        P("rep"),
        P("rep"),
        P("rep", None),
        P("rep", None),
        P("rep", None),
        P("rep", None),
    )
    out_specs = (
        P(("rep", "pop"), None, None),
        P(("rep", "pop"), None, None),
        P(("rep", "pop"), None, None),
        P("rep"),
    )
    return jax.shard_map(
        per_device, mesh=mesh, in_specs=in_specs, out_specs=out_specs, check_vma=False
    )
```

```python
import functools

import jax
import jax.numpy as jnp
from jax import lax
from jax.experimental import pallas as pl
from jax.experimental.pallas import tpu as pltpu
from jax.sharding import PartitionSpec as P

SHARDS = 4
TASKS = 8
SLOTS = 4
PLANES = 4


beta_one = 0.9
beta_two = 0.999
adam_eps = 1e-08
gelu_coef = 0.7978845608028654

SMEM = pl.BlockSpec(memory_space=pltpu.SMEM)
VMEM = pl.BlockSpec(memory_space=pltpu.VMEM)
ANY = pl.BlockSpec(memory_space=pl.ANY)


def gelu_pair(pre):
    inner = jnp.tanh(gelu_coef * (pre + 0.044715 * pre * pre * pre))
    value = 0.5 * pre * (1.0 + inner)
    slope = 0.5 * (1.0 + inner) + 0.5 * pre * (1.0 - inner * inner) * gelu_coef * (
        1.0 + 3.0 * 0.044715 * pre * pre
    )
    return (value, slope)


def for_sending(shard):

    def short(part):
        return part.astype(jnp.bfloat16) if part.dtype == jnp.float32 else part

    return jax.tree.map(short, shard)


def relayed(
    pool_tokens,
    pool_targets,
    weight,
    first_moment,
    second_moment,
    winner,
    learn_rate,
    explore,
    task_weight,
    tile_ids,
    slot_task,
    slot_tokens,
):
    nodes = lax.axis_size("pop")
    place = lax.axis_index("pop")
    member = place // SHARDS
    shard = place % SHARDS
    members = winner.shape[0]
    slots = tile_ids.shape[1]
    tile = pool_tokens.shape[1]
    depth = pool_tokens.shape[2]
    width = weight.shape[2]
    hidden_all = pool_targets.shape[2]
    reach = tile // nodes
    flat_state = (
        weight.reshape(nodes, -1),
        first_moment.reshape(nodes, -1),
        second_moment.reshape(nodes, -1),
    )
    spread = (
        lax.all_to_all(flat_state[0], "pop", split_axis=0, concat_axis=0, tiled=True),
        lax.all_to_all(flat_state[1], "pop", split_axis=0, concat_axis=0, tiled=True),
        lax.all_to_all(flat_state[2], "pop", split_axis=0, concat_axis=0, tiled=True),
    )
    source_rows = (winner[:, None] * SHARDS + jnp.arange(SHARDS, dtype=jnp.int32)[None, :]).reshape(
        -1
    )
    picked_state = tuple((jnp.take(piece, source_rows, axis=0) for piece in spread))
    returned = jax.tree.map(
        lambda part, own: part.astype(own.dtype),
        lax.all_to_all(for_sending(picked_state), "pop", split_axis=0, concat_axis=0, tiled=True),
        picked_state,
    )
    start_weight = returned[0].reshape(depth, width)
    start_first = returned[1].reshape(depth, width)
    start_second = returned[2].reshape(depth, width)
    relay_tokens, relay_targets = (
        lax.all_to_all(pool_tokens, "pop", split_axis=1, concat_axis=0, tiled=True),
        lax.all_to_all(pool_targets, "pop", split_axis=1, concat_axis=0, tiled=True),
    )
    flat_ids = tile_ids.reshape(-1)
    pick_tokens = jnp.take(relay_tokens, flat_ids, axis=0).reshape(members, 1, slots, reach, depth)
    send_tokens = jnp.broadcast_to(pick_tokens, (members, SHARDS, slots, reach, depth)).reshape(
        nodes, slots, reach, depth
    )
    pick_targets = jnp.take(relay_targets, flat_ids, axis=0).reshape(
        members, slots, reach, hidden_all
    )
    send_targets = jnp.broadcast_to(
        pick_targets[:, None], (members, SHARDS, slots, reach, hidden_all)
    ).reshape(nodes, slots, reach, hidden_all)
    got_tokens, got_targets = (
        lax.all_to_all(send_tokens, "pop", split_axis=0, concat_axis=2, tiled=True),
        lax.all_to_all(send_targets, "pop", split_axis=0, concat_axis=2, tiled=True),
    )
    targets = lax.dynamic_slice_in_dim(got_targets[0], shard * width, width, 2).reshape(
        slots * tile, width
    )
    inputs = got_tokens.reshape(slots * tile, depth)
    tasks_here = lax.dynamic_index_in_dim(slot_task, member, 0, keepdims=False)
    lengths = lax.dynamic_index_in_dim(slot_tokens, member, 0, keepdims=False)
    source_member = lax.dynamic_index_in_dim(winner, member, 0, keepdims=False)
    onehot = tasks_here[:, None] == jnp.arange(TASKS, dtype=jnp.int32)[None, :]
    counts = jnp.sum(jnp.where(onehot, lengths[:, None], 0), axis=0)
    weights_here = lax.dynamic_index_in_dim(task_weight, source_member, 0, keepdims=False)
    scale = weights_here / jnp.maximum(counts, 1).astype(jnp.float32)
    per_slot = jnp.sum(jnp.where(onehot, scale[None, :], jnp.float32(0.0)), axis=1)
    live = jnp.arange(tile, dtype=jnp.int32)[None, :] < lengths[:, None]
    coef = jnp.where(live, per_slot[:, None], jnp.float32(0.0)).reshape(-1)
    own_rate = lax.dynamic_index_in_dim(learn_rate, source_member, 0, keepdims=False)
    own_explore = lax.dynamic_index_in_dim(explore, member, 0, keepdims=False)
    step_rate = own_rate * jnp.where(source_member != member, own_explore, jnp.float32(1.0))
    pre = jnp.dot(inputs, start_weight, preferred_element_type=jnp.float32)
    hidden, slope = gelu_pair(pre)
    diff = hidden - targets.astype(jnp.float32)
    part = jnp.sum(coef[:, None] * diff * diff)
    delta = (2.0 * coef[:, None] * diff * slope).astype(jnp.bfloat16)
    grad = lax.dot_general(
        inputs, delta, (((0,), (0,)), ((), ())), preferred_element_type=jnp.float32
    )
    first = beta_one * start_first.astype(jnp.float32) + (1.0 - beta_one) * grad
    second = beta_two * start_second.astype(jnp.float32) + (1.0 - beta_two) * grad * grad
    updated = start_weight.astype(jnp.float32) - step_rate * first / (jnp.sqrt(second) + adam_eps)
    share = jnp.where(jnp.arange(members, dtype=jnp.int32) == member, part, jnp.float32(0.0))
    member_loss = lax.psum(share, "pop")
    return (
        updated.astype(jnp.bfloat16)[None],
        first.astype(jnp.bfloat16)[None],
        second.astype(jnp.bfloat16)[None],
        member_loss,
    )


ENDS = ((0, 1), (1, 0), (2, 3), (3, 2))
MIDDLE = ((1, 2), (2, 1))


def position():
    place = lax.axis_index("pop")
    return place // SHARDS, lax.rem(place, SHARDS)


SHARED, TAKEN, HOPS, BY_ENDS, THEIR_ENDS, TO_ENDS, TO_MIDDLE, EARLY, LAST = range(9)
FOR_END, FOR_OWN, TOKENS, COUNTS = 16, 20, 24, 28
OWN, GUEST, PASSED = range(3)
RATE, TASK = 0, 4


def copied_from(winner):
    loser, source = jnp.int32(0), jnp.int32(0)
    for m in range(PLANES):
        taken = winner[m] != m
        loser = jnp.where(taken, m, loser)
        source = jnp.where(taken, winner[m], source)
    return loser, source


def route_kernel(winner, code):
    loser, source = copied_from(winner)
    code[...] = jnp.full(code.shape, source * PLANES + loser, jnp.int32)


def route_code(winner):
    return pl.pallas_call(
        route_kernel,
        out_shape=jax.ShapeDtypeStruct((8, 128), jnp.int32),
        in_specs=[SMEM],
        out_specs=VMEM,
        name="route_code",
    )(winner)


def on_route(route, m, to):
    source, loser = route
    upward = (to == m + 1) & (source <= m) & (loser >= to)
    return upward | ((to == m - 1) & (source >= m) & (loser <= to))


def by_ends(route):
    source, loser = route
    return jnp.where(source < loser, loser - 1, loser + 1) == (loser ^ 1)


def in_pool(t, m, k):
    ahead = t // SHARDS - m
    ahead = jnp.where(m == 1, ahead, -ahead)
    group = jnp.where(ahead == 0, 0, jnp.where(ahead == -1, 1, ahead + 1))
    return group * SHARDS + (lax.rem(t, SHARDS) ^ k)


def facts_kernel(
    other, winner, learn_rate, explore, task_weight, tile_ids, slot_task, slot_tokens, ints, floats
):
    m, k = position()
    loser, source = copied_from(winner)
    code = other[0, 0]
    mine = source, loser
    theirs = lax.div(code, jnp.int32(PLANES)), lax.rem(code, jnp.int32(PLANES))
    upward = jnp.maximum(mine[0], theirs[0]) < jnp.minimum(mine[1], theirs[1])
    downward = jnp.maximum(mine[1], theirs[1]) < jnp.minimum(mine[0], theirs[0])
    shared = upward | downward
    hops = jnp.abs(mine[0] - mine[1])
    most = jnp.maximum(hops, jnp.abs(theirs[0] - theirs[1]))
    taken = winner[m] != m

    def content(to):
        own = on_route(mine, m, to)
        guest = on_route(theirs, m, to) & jnp.logical_not(shared)
        first = jnp.where(own, jnp.where(m == mine[0], OWN, PASSED), -1)
        return jnp.where(guest, jnp.where(m == theirs[0], GUEST, PASSED), first)

    ints[SHARED] = shared.astype(jnp.int32)
    ints[TAKEN] = taken.astype(jnp.int32)
    ints[HOPS] = hops
    ints[BY_ENDS] = by_ends(mine).astype(jnp.int32)
    ints[THEIR_ENDS] = by_ends(theirs).astype(jnp.int32)
    ints[TO_ENDS] = content(m ^ 1)
    ints[TO_MIDDLE] = content(jnp.where(m == 1, 2, jnp.where(m == 2, 1, -1)))
    ints[EARLY] = jnp.where(shared & (most == PLANES - 1), 4, 3)
    ints[LAST] = jnp.where(shared, 6, 3) + most - 1
    end = jnp.where(m <= 1, 0, PLANES - 1)
    at_end = (m == 0) | (m == PLANES - 1)
    slots = tile_ids.shape[1]
    for s in range(slots):
        task = slot_task[m, s]
        count = jnp.int32(0)
        for o in range(slots):
            count = count + jnp.where(slot_task[m, o] == task, slot_tokens[m, o], 0)
        ints[FOR_END + s] = in_pool(tile_ids[end, s], m, k)
        ints[FOR_OWN + s] = jnp.where(at_end, -1, in_pool(tile_ids[m, s], m, k))
        ints[TOKENS + s] = slot_tokens[m, s]
        ints[COUNTS + s] = jnp.maximum(count, 1)
        floats[TASK + s] = task_weight[winner[m], task]
    floats[RATE] = learn_rate[winner[m]] * jnp.where(taken, explore[m], 1.0)


def gather_facts(other, *small):
    return pl.pallas_call(
        facts_kernel,
        out_shape=[jax.ShapeDtypeStruct((32,), jnp.int32), jax.ShapeDtypeStruct((8,), jnp.float32)],
        in_specs=[SMEM] * 8,
        out_specs=[SMEM, SMEM],
        name="gather_facts",
    )(other, *small)


def stage_kernel(has_guest, has_last, ints, step, *refs):
    state, refs = refs[:3], refs[3:]
    guest = refs[0] if has_guest else None
    from_ends, from_middle = refs[has_guest : has_guest + 2] if has_last else (None, None)
    to_ends, to_middle = refs[has_guest + 2 * has_last :][:2]
    sems = refs[-1]
    t = step[0] if hasattr(step, "shape") else step
    half = to_ends.shape[0]
    shared = ints[SHARED] == 1
    array = jnp.where(shared, lax.div(t - 1, jnp.int32(2)), t - 1)
    start = pl.multiple_of(jnp.where(shared, lax.rem(t - 1, jnp.int32(2)), 0) * half, half)
    sides = ((to_ends, ints[TO_ENDS], from_middle), (to_middle, ints[TO_MIDDLE], from_ends))
    for n, (out, content, _) in enumerate(sides):
        for a, ref in enumerate(state):

            @pl.when((content == OWN) & (array == a))
            def _():
                pltpu.make_async_copy(ref.at[0, pl.ds(start, half)], out, sems.at[n]).start()

    if has_last and has_guest:
        theirs = refs[has_guest + 2 * has_last + 2]

        @pl.when(ints[THEIR_ENDS] == 1)
        def _():
            copy_rows(from_ends, 0, theirs, 0, half)

        @pl.when(ints[THEIR_ENDS] == 0)
        def _():
            copy_rows(from_middle, 0, theirs, 0, half)

    for n, (out, content, passed) in enumerate(sides):
        if guest is not None:

            @pl.when(content == GUEST)
            def _():
                copy_rows(guest, 0, out, 0, half)

        if passed is not None:

            @pl.when(content == PASSED)
            def _():
                copy_rows(passed, 0, out, 0, half)

        @pl.when((content == OWN) & (array < len(state)))
        def _():
            pltpu.make_async_copy(state[0].at[0, pl.ds(0, half)], out, sems.at[n]).wait()


def stage(ints, step, own, guest=None, last=()):
    half, width = own[0].shape[1] // 2, own[0].shape[2]
    guests = () if guest is None else (guest,)
    outs = 3 if guests and last else 2
    kernel = functools.partial(stage_kernel, len(guests), len(last) > 0)
    steps = (step,)
    if isinstance(step, int):
        kernel, steps = (lambda ints, *refs, inner=kernel: inner(ints, step, *refs)), ()
    return pl.pallas_call(
        kernel,
        out_shape=[jax.ShapeDtypeStruct((half, width), own[0].dtype)] * outs,
        in_specs=[SMEM] * (1 + len(steps)) + [ANY] * 3 + [VMEM] * (len(guests) + len(last)),
        out_specs=[VMEM] * outs,
        scratch_shapes=[pltpu.SemaphoreType.DMA((2,))],
        name="stage_chunk",
    )(ints, *steps, *own, *guests, *last)


def theirs_kernel(ints, from_ends, from_middle, theirs):
    @pl.when(ints[THEIR_ENDS] == 1)
    def _():
        copy_rows(from_ends, 0, theirs, 0, theirs.shape[0])

    @pl.when(ints[THEIR_ENDS] == 0)
    def _():
        copy_rows(from_middle, 0, theirs, 0, theirs.shape[0])


def theirs_of(ints, from_ends, from_middle):
    return pl.pallas_call(
        theirs_kernel,
        out_shape=jax.ShapeDtypeStruct(from_ends.shape, from_ends.dtype),
        in_specs=[SMEM] + [VMEM] * 2,
        out_specs=VMEM,
        name="guest_chunk",
    )(ints, from_ends, from_middle)


def keep_kernel(ints, step, from_ends, from_middle, kept, out, sem):
    place = jnp.clip(step[0] - 4, 0, out.shape[0] - 1)

    @pl.when(ints[BY_ENDS] == 1)
    def _():
        pltpu.make_async_copy(from_ends, out.at[place], sem).start()

    @pl.when(ints[BY_ENDS] == 0)
    def _():
        pltpu.make_async_copy(from_middle, out.at[place], sem).start()

    pltpu.make_async_copy(from_ends, out.at[place], sem).wait()


def keep(ints, step, from_ends, from_middle, kept):
    return pl.pallas_call(
        keep_kernel,
        out_shape=jax.ShapeDtypeStruct(kept.shape, kept.dtype),
        in_specs=[SMEM, SMEM, VMEM, VMEM, ANY],
        out_specs=ANY,
        scratch_shapes=[pltpu.SemaphoreType.DMA],
        input_output_aliases={4: 0},
        name="keep_chunk",
    )(ints, step, from_ends, from_middle, kept)


def room(count, like):
    return pl.pallas_call(
        lambda out: None,
        out_shape=jax.ShapeDtypeStruct((count, *like.shape), like.dtype),
        out_specs=ANY,
        name="room_for_chunks",
    )()


EARLY_REFS = 9


def start_copies(ints, a, h, own, sent, out, sem):
    ends, middles, backs, late, late_backs = sent
    shared, taken = ints[SHARED] == 1, ints[TAKEN] == 1
    half = out.shape[0]
    step = jnp.where(shared, 2 * a + h, a) + ints[HOPS]
    direct = taken & shared if h == 1 else taken
    back = taken & jnp.logical_not(shared)

    def copy(ref):
        return pltpu.make_async_copy(ref, out, sem)

    @pl.when(jnp.logical_not(taken))
    def _():
        copy(own.at[0, pl.ds(h * half, half)]).start()

    sides = [
        (ends, direct & (ints[BY_ENDS] == 1)),
        (middles, direct & (ints[BY_ENDS] == 0)),
    ]
    lates = [(late, direct)]
    if h == 1:
        sides.append((backs, back))
        lates.append((late_backs, back))
    for refs, here in sides:
        for n, ref in enumerate(refs):

            @pl.when(here & (step == n + 1))
            def _():
                copy(ref).start()

    for ref, here in lates:

        @pl.when(here & (step > 3))
        def _():
            copy(ref.at[jnp.clip(step - 4, 0, ref.shape[0] - 1)]).start()

    return copy(own.at[0, pl.ds(h * half, half)])


def sent_refs(refs):
    return refs[0:3], refs[3:6], refs[6:9], refs[9], refs[10]


def pack_kernel(code, tokens, targets, *parts):
    _, k = position()
    width = targets.shape[2] // SHARDS
    slim = tokens.shape[2] // SHARDS
    for j, part in enumerate(parts):
        q = k ^ j
        part[:, :width] = targets[0, :, pl.ds(pl.multiple_of(q * width, 128), width)]
        part[:, width:] = tokens[0, :, pl.ds(pl.multiple_of(q * slim, 128), slim)]


def pack(code, tokens, targets):
    tile = tokens.shape[1]
    row = (tokens.shape[2] + targets.shape[2]) // SHARDS
    return pl.pallas_call(
        pack_kernel,
        out_shape=[jax.ShapeDtypeStruct((tile, row), tokens.dtype)] * SHARDS,
        in_specs=[VMEM] * 3,
        out_specs=[VMEM] * SHARDS,
        name="pack_quarters",
    )(code, tokens, targets)


def copy_rows(ref, start, out, at, count, columns=slice(None)):
    step = 32

    def body(i, _):
        rows = pl.ds(pl.multiple_of(at + i * step, step), step)
        out[rows, :] = ref[pl.ds(start + i * step, step), columns]
        return 0

    lax.fori_loop(0, count // step, body, 0, unroll=True if count <= 64 else 4)


def split_kernel(one, two, three, *halves):
    count = one.shape[0] // 2
    for h, half in enumerate(halves):
        for n, part in enumerate((one, two, three)):
            copy_rows(part, h * count, half, n * count, count)


def split_rows(parts):
    tile, row = parts[0].shape
    half = jax.ShapeDtypeStruct((len(parts) * tile // 2, row), parts[0].dtype)
    return pl.pallas_call(
        split_kernel,
        out_shape=[half, half],
        in_specs=[VMEM] * len(parts),
        out_specs=[VMEM, VMEM],
        name="split_rows",
    )(*parts)


def piece(pool, which, h):
    group, j = divmod(which, SHARDS)
    whole, halves = pool[group]
    rows = whole.shape[0] // 2
    return (whole, h * rows, rows) if j == 0 else (halves[h], (j - 1) * rows, rows)


def grouped(refs, halves):
    size = 1 + len(halves)
    pool = []
    for g in range(PLANES):
        group = refs[g * size : (g + 1) * size]
        pool.append((group[0], dict(zip(halves, group[1:]))))
    return pool, refs[PLANES * size :]


def pick_for_end_kernel(h, ints, *refs):
    pool, (out,) = grouped(refs, (h,))

    def slot(s, _):
        place = ints[FOR_END + s]
        for which in range(PLANES * SHARDS):
            ref, start, rows = piece(pool, which, h)

            @pl.when(place == which)
            def _():
                copy_rows(ref, start, out, s * rows, rows)

        return 0

    lax.fori_loop(0, SLOTS, slot, 0)


def pick_for_end(h, ints, pool):
    tile, row = pool[0][0].shape
    operands = [x for whole, halves in pool for x in (whole, halves[h])]
    return pl.pallas_call(
        functools.partial(pick_for_end_kernel, h),
        out_shape=jax.ShapeDtypeStruct((SLOTS * tile // 2, row), operands[0].dtype),
        in_specs=[SMEM] + [VMEM] * len(operands),
        out_specs=VMEM,
        compiler_params=pltpu.CompilerParams(vmem_limit_bytes=32 * 1024 * 1024),
        name="pick_for_end",
    )(ints, *operands)


def pick_own_kernel(ints, *refs):
    pool, (handed_a, handed_b, quarter, targets) = grouped(refs, (0, 1))
    handed = (handed_a, handed_b)
    width = targets.shape[1]
    half = quarter.shape[0] // SLOTS // 2

    def slot(s, _):
        place = ints[FOR_OWN + s]
        for h in range(2):
            at = (2 * s + h) * half

            @pl.when(place < 0)
            def _():
                start = pl.multiple_of(s * half, half)
                copy_rows(handed[h], start, targets, at, half, slice(0, width))
                copy_rows(handed[h], start, quarter, at, half, slice(width, None))

            for which in range(PLANES * SHARDS):
                ref, start, rows = piece(pool, which, h)

                @pl.when(place == which)
                def _():
                    copy_rows(ref, start, targets, at, rows, slice(0, width))
                    copy_rows(ref, start, quarter, at, rows, slice(width, None))

        return 0

    lax.fori_loop(0, SLOTS, slot, 0)


def pick_own(ints, pool, handed, width):
    rows, row = handed[0].shape
    operands = [x for whole, halves in pool for x in (whole, *halves)]
    return pl.pallas_call(
        pick_own_kernel,
        out_shape=[
            jax.ShapeDtypeStruct((2 * rows, row - width), handed[0].dtype),
            jax.ShapeDtypeStruct((2 * rows, width), handed[0].dtype),
        ],
        in_specs=[SMEM] + [VMEM] * (len(operands) + 2),
        out_specs=[VMEM, VMEM],
        compiler_params=pltpu.CompilerParams(vmem_limit_bytes=32 * 1024 * 1024),
        name="pick_own",
    )(ints, *operands, *handed)


def grad_kernel(ints, floats, in0, in1, in2, in3, targets, own_w, *refs):
    sent, (grad, loss, w_buf, delta, sem) = sent_refs(refs[:11]), refs[11:]
    m, k = position()
    half = w_buf.shape[0] // 2
    copies = [
        start_copies(ints, 0, h, own_w, sent, w_buf.at[pl.ds(h * half, half)], sem.at[h])
        for h in range(2)
    ]
    tile = in0.shape[0] // SLOTS
    slim = in0.shape[1]
    ins = (in0, in1, in2, in3)
    for copy in copies:
        copy.wait()

    def slot(s, total):
        span = pl.ds(pl.multiple_of(s * tile, tile), tile)
        pre = None
        for j in range(SHARDS):
            at = pl.ds(pl.multiple_of((k ^ j) * slim, slim), slim)
            one = jnp.dot(ins[j][span, :], w_buf[at, :], preferred_element_type=jnp.float32)
            pre = one if pre is None else pre + one
        live = lax.broadcasted_iota(jnp.int32, pre.shape, 0) < ints[TOKENS + s]
        many = jnp.full(pre.shape, ints[COUNTS + s], jnp.int32).astype(jnp.float32)
        coef = jnp.where(live, floats[TASK + s] / many, 0.0)
        hidden, slope = gelu_pair(pre)
        diff = hidden - targets[span, :].astype(jnp.float32)
        scaled = coef * diff
        delta[span, :] = (2.0 * scaled * slope).astype(jnp.bfloat16)
        return total + jnp.sum(scaled * diff, keepdims=True)

    total = lax.fori_loop(0, SLOTS, slot, jnp.zeros((1, 1), jnp.float32))
    lane = lax.broadcasted_iota(jnp.int32, loss.shape, 1)
    loss[...] = jnp.where(lane == m, total, 0.0)
    for j in range(SHARDS):
        at = pl.ds(pl.multiple_of((k ^ j) * slim, slim), slim)
        grad[at, :] = lax.dot_general(
            ins[j][...], delta[...], (((0,), (0,)), ((), ())), preferred_element_type=jnp.float32
        )


def gradient(ints, floats, ins, targets, own_w, sent):
    rows, width = targets.shape
    depth = own_w.shape[1]
    return pl.pallas_call(
        grad_kernel,
        out_shape=[
            jax.ShapeDtypeStruct((depth, width), jnp.float32),
            jax.ShapeDtypeStruct((8, 128), jnp.float32),
        ],
        in_specs=[SMEM] * 2 + [VMEM] * 5 + [ANY] + [VMEM] * EARLY_REFS + [ANY] * 2,
        out_specs=[VMEM, VMEM],
        scratch_shapes=[
            pltpu.VMEM((depth, width), own_w.dtype),
            pltpu.VMEM((rows, width), jnp.bfloat16),
            pltpu.SemaphoreType.DMA((2,)),
        ],
        compiler_params=pltpu.CompilerParams(vmem_limit_bytes=32 * 1024 * 1024),
        name="forward_and_gradient",
    )(ints, floats, *ins, targets, own_w, *sent)


def adam_kernel(h, ints, floats, grad, *refs):
    own, sent, refs = refs[:3], sent_refs(refs[3:14]), refs[14:]
    new, bufs, outs, (in_sem, out_sem) = refs[-11:-8], refs[-8:-5], refs[-5:-2], refs[-2:]
    blocks = out_sem.shape[1]
    rows = bufs[0].shape[0]
    step = rows // blocks
    here = h * rows

    def result(i, b):
        return pltpu.make_async_copy(
            outs[i].at[pl.ds(b * step, step)],
            new[i].at[0, pl.ds(here + b * step, step)],
            out_sem.at[i, b],
        )

    copies = [
        start_copies(ints, a, h, own[a], sent, bufs[a], in_sem.at[a]) for a in range(3)
    ]
    rate = floats[RATE]
    for copy in copies:
        copy.wait()
    for b in range(blocks):

        def body(n, _):
            at = pl.ds(pl.multiple_of(b * step + n * 16, 16), 16)
            g = grad[pl.ds(pl.multiple_of(here + b * step + n * 16, 16), 16), :]
            first = beta_one * bufs[1][at, :].astype(jnp.float32) + (1.0 - beta_one) * g
            second = beta_two * bufs[2][at, :].astype(jnp.float32) + (1.0 - beta_two) * g * g
            start = bufs[0][at, :].astype(jnp.float32)
            updated = start - rate * first / (jnp.sqrt(second) + adam_eps)
            outs[0][at, :] = updated.astype(outs[0].dtype)
            outs[1][at, :] = first.astype(outs[1].dtype)
            outs[2][at, :] = second.astype(outs[2].dtype)
            return 0

        lax.fori_loop(0, step // 16, body, 0, unroll=2)
        for i in range(3):
            result(i, b).start()
    for b in range(blocks):
        for i in range(3):
            result(i, b).wait()


def adam(h, ints, floats, grad, own, sent, begun=()):
    depth, width = grad.shape
    blocks = 2
    return pl.pallas_call(
        functools.partial(adam_kernel, h),
        out_shape=[jax.ShapeDtypeStruct(x.shape, x.dtype) for x in own],
        in_specs=[SMEM] * 2 + [VMEM] + [ANY] * 3 + [VMEM] * EARLY_REFS + [ANY] * (2 + len(begun)),
        out_specs=[ANY] * 3,
        scratch_shapes=[pltpu.VMEM((depth // 2, width), x.dtype) for x in own] * 2
        + [pltpu.SemaphoreType.DMA((3,)), pltpu.SemaphoreType.DMA((3, blocks))],
        input_output_aliases={6 + len(sent) + i: i for i in range(len(begun))},
        compiler_params=pltpu.CompilerParams(vmem_limit_bytes=32 * 1024 * 1024),
        name="adam_half",
    )(ints, floats, grad, *own, *sent, *begun)


def in_plane(x, j):
    pairs = [(m * SHARDS + k, m * SHARDS + (k ^ j)) for m in range(PLANES) for k in range(SHARDS)]
    return lax.ppermute(x, "pop", pairs)


def along(x, hops):
    idle = [m for m in range(PLANES) if all(m not in hop for hop in hops)]
    pairs = [(a * SHARDS + k, b * SHARDS + k) for a, b in hops for k in range(SHARDS)]
    pairs += [(m * SHARDS + k, m * SHARDS + (k ^ 1)) for m in idle for k in range(SHARDS)]
    return lax.ppermute(x, "pop", pairs)


def beside(x):
    return lax.ppermute(x, "rep", [(0, 1), (1, 0)])


def after(x, *others):
    return lax.optimization_barrier((x, *others))[0]


def tiles(here, ints, width):
    near0, middle0, (here0, halves) = here
    near = [along(x, ENDS) for x in halves]
    far0 = along(near0, MIDDLE)
    middle = [along(x, MIDDLE) for x in halves]
    far = [along(x, MIDDLE) for x in near]
    pool = [(here0, halves), (near0, near), (middle0, middle), (far0, far)]
    handed = [along(pick_for_end(h, ints, pool), ENDS) for h in range(2)]
    quarter, targets = pick_own(ints, pool, handed, width)
    side = in_plane(quarter, 1)
    cross = in_plane(quarter, 2)
    return (quarter, side, cross, in_plane(cross, 1)), targets


def first_steps(ints, own):
    half = own[0].shape[1] // 2
    guests = [beside(after(x[0, half:], ints)) for x in own]
    last, ends, middles, backs = (), [], [], []
    for t in range(1, 4):
        to_ends, to_middle, *theirs = stage(ints, t, own, guests[t - 1], last)
        backs += [beside(x) for x in theirs]
        last = (along(to_ends, ENDS), along(to_middle, MIDDLE))
        ends.append(last[0])
        middles.append(last[1])
    backs.append(beside(theirs_of(ints, *last)))
    return ends, middles, backs


def late_steps(ints, own, until, carry):
    def more(carry):
        return carry[0] <= ints[until]

    def one(carry):
        t, from_ends, from_middle, late, late_backs = carry
        to_ends, to_middle = stage(ints, t.reshape(1), own, None, (from_ends, from_middle))
        from_ends, from_middle = along(to_ends, ENDS), along(to_middle, MIDDLE)
        late = keep(ints, t.reshape(1), from_ends, from_middle, late)
        late_backs = lax.cond(
            ints[SHARED] == 1,
            lambda x, n, e, m: x,
            lambda x, n, e, m: lax.dynamic_update_index_in_dim(
                x, beside(theirs_of(ints, e, m)), n, 0
            ),
            late_backs,
            t - 4,
            from_ends,
            from_middle,
        )
        return t + 1, from_ends, from_middle, late, late_backs

    return lax.while_loop(more, one, carry)


def per_device(pool_tokens, pool_targets, weight, first_moment, second_moment, *args):
    winner, tile_ids = args[0], args[4]
    if winner.shape[0] != PLANES or tile_ids.shape[1] != SLOTS or lax.axis_size("rep") != 2:
        return relayed(pool_tokens, pool_targets, weight, first_moment, second_moment, *args)
    own = (weight, first_moment, second_moment)
    code = route_code(winner)
    ints, floats = gather_facts(beside(code), *args)
    parts = pack(code, pool_tokens, pool_targets)
    near0, middle0 = along(parts[0], ENDS), along(parts[0], MIDDLE)
    halves = split_rows([in_plane(parts[j], j) for j in range(1, SHARDS)])
    here = (near0, middle0, (parts[0], halves))
    ins, targets = tiles(here, ints, weight.shape[2])
    ends, middles, backs = first_steps(ints, own)
    carry = (jnp.int32(4), ends[-1], middles[-1], room(5, ends[-1]), room(2, ends[-1]))
    carry = late_steps(ints, own, EARLY, after(carry, ins))
    grad, loss = gradient(
        ints, floats, ins, targets, weight, (*ends, *middles, *backs, *carry[3:])
    )
    carry = late_steps(ints, own, LAST, after(carry, grad))
    sent = (*ends, *middles, *backs, *carry[3:])
    loss = loss + in_plane(loss, 1)
    new = adam(0, ints, floats, grad, own, sent)
    loss = loss + in_plane(after(loss, new[0]), 2)
    new = adam(1, ints, floats, grad, own, sent, new)
    ring = [along(loss, [(m, (m + d) % PLANES) for m in range(PLANES)]) for d in range(1, PLANES)]
    loss = loss + ring[0] + ring[1] + ring[2]
    return (*new, loss[0, :PLANES])


def solution(mesh):
    in_specs = (
        P(("rep", "pop"), None, None),
        P(("rep", "pop"), None, None),
        P(("rep", "pop"), None, None),
        P(("rep", "pop"), None, None),
        P(("rep", "pop"), None, None),
        P("rep"),
        P("rep"),
        P("rep"),
        P("rep", None),
        P("rep", None),
        P("rep", None),
        P("rep", None),
    )
    out_specs = (
        P(("rep", "pop"), None, None),
        P(("rep", "pop"), None, None),
        P(("rep", "pop"), None, None),
        P("rep"),
    )
    return jax.shard_map(
        per_device, mesh=mesh, in_specs=in_specs, out_specs=out_specs, check_vma=False
    )
```

```python
import functools

import jax
import jax.numpy as jnp
from jax import lax
from jax.experimental import pallas as pl
from jax.experimental.pallas import tpu as pltpu
from jax.sharding import PartitionSpec as P

SHARDS = 4
TASKS = 8
SLOTS = 4
PLANES = 4


beta_one = 0.9
beta_two = 0.999
adam_eps = 1e-08
gelu_coef = 0.7978845608028654

SMEM = pl.BlockSpec(memory_space=pltpu.SMEM)
VMEM = pl.BlockSpec(memory_space=pltpu.VMEM)
ANY = pl.BlockSpec(memory_space=pl.ANY)


def gelu_pair(pre):
    inner = jnp.tanh(gelu_coef * (pre + 0.044715 * pre * pre * pre))
    value = 0.5 * pre * (1.0 + inner)
    slope = 0.5 * (1.0 + inner) + 0.5 * pre * (1.0 - inner * inner) * gelu_coef * (
        1.0 + 3.0 * 0.044715 * pre * pre
    )
    return (value, slope)


def for_sending(shard):

    def short(part):
        return part.astype(jnp.bfloat16) if part.dtype == jnp.float32 else part

    return jax.tree.map(short, shard)


def relayed(
    pool_tokens,
    pool_targets,
    weight,
    first_moment,
    second_moment,
    winner,
    learn_rate,
    explore,
    task_weight,
    tile_ids,
    slot_task,
    slot_tokens,
):
    nodes = lax.axis_size("pop")
    place = lax.axis_index("pop")
    member = place // SHARDS
    shard = place % SHARDS
    members = winner.shape[0]
    slots = tile_ids.shape[1]
    tile = pool_tokens.shape[1]
    depth = pool_tokens.shape[2]
    width = weight.shape[2]
    hidden_all = pool_targets.shape[2]
    reach = tile // nodes
    flat_state = (
        weight.reshape(nodes, -1),
        first_moment.reshape(nodes, -1),
        second_moment.reshape(nodes, -1),
    )
    spread = (
        lax.all_to_all(flat_state[0], "pop", split_axis=0, concat_axis=0, tiled=True),
        lax.all_to_all(flat_state[1], "pop", split_axis=0, concat_axis=0, tiled=True),
        lax.all_to_all(flat_state[2], "pop", split_axis=0, concat_axis=0, tiled=True),
    )
    source_rows = (winner[:, None] * SHARDS + jnp.arange(SHARDS, dtype=jnp.int32)[None, :]).reshape(
        -1
    )
    picked_state = tuple((jnp.take(piece, source_rows, axis=0) for piece in spread))
    returned = jax.tree.map(
        lambda part, own: part.astype(own.dtype),
        lax.all_to_all(for_sending(picked_state), "pop", split_axis=0, concat_axis=0, tiled=True),
        picked_state,
    )
    start_weight = returned[0].reshape(depth, width)
    start_first = returned[1].reshape(depth, width)
    start_second = returned[2].reshape(depth, width)
    relay_tokens, relay_targets = (
        lax.all_to_all(pool_tokens, "pop", split_axis=1, concat_axis=0, tiled=True),
        lax.all_to_all(pool_targets, "pop", split_axis=1, concat_axis=0, tiled=True),
    )
    flat_ids = tile_ids.reshape(-1)
    pick_tokens = jnp.take(relay_tokens, flat_ids, axis=0).reshape(members, 1, slots, reach, depth)
    send_tokens = jnp.broadcast_to(pick_tokens, (members, SHARDS, slots, reach, depth)).reshape(
        nodes, slots, reach, depth
    )
    pick_targets = jnp.take(relay_targets, flat_ids, axis=0).reshape(
        members, slots, reach, hidden_all
    )
    send_targets = jnp.broadcast_to(
        pick_targets[:, None], (members, SHARDS, slots, reach, hidden_all)
    ).reshape(nodes, slots, reach, hidden_all)
    got_tokens, got_targets = (
        lax.all_to_all(send_tokens, "pop", split_axis=0, concat_axis=2, tiled=True),
        lax.all_to_all(send_targets, "pop", split_axis=0, concat_axis=2, tiled=True),
    )
    targets = lax.dynamic_slice_in_dim(got_targets[0], shard * width, width, 2).reshape(
        slots * tile, width
    )
    inputs = got_tokens.reshape(slots * tile, depth)
    tasks_here = lax.dynamic_index_in_dim(slot_task, member, 0, keepdims=False)
    lengths = lax.dynamic_index_in_dim(slot_tokens, member, 0, keepdims=False)
    source_member = lax.dynamic_index_in_dim(winner, member, 0, keepdims=False)
    onehot = tasks_here[:, None] == jnp.arange(TASKS, dtype=jnp.int32)[None, :]
    counts = jnp.sum(jnp.where(onehot, lengths[:, None], 0), axis=0)
    weights_here = lax.dynamic_index_in_dim(task_weight, source_member, 0, keepdims=False)
    scale = weights_here / jnp.maximum(counts, 1).astype(jnp.float32)
    per_slot = jnp.sum(jnp.where(onehot, scale[None, :], jnp.float32(0.0)), axis=1)
    live = jnp.arange(tile, dtype=jnp.int32)[None, :] < lengths[:, None]
    coef = jnp.where(live, per_slot[:, None], jnp.float32(0.0)).reshape(-1)
    own_rate = lax.dynamic_index_in_dim(learn_rate, source_member, 0, keepdims=False)
    own_explore = lax.dynamic_index_in_dim(explore, member, 0, keepdims=False)
    step_rate = own_rate * jnp.where(source_member != member, own_explore, jnp.float32(1.0))
    pre = jnp.dot(inputs, start_weight, preferred_element_type=jnp.float32)
    hidden, slope = gelu_pair(pre)
    diff = hidden - targets.astype(jnp.float32)
    part = jnp.sum(coef[:, None] * diff * diff)
    delta = (2.0 * coef[:, None] * diff * slope).astype(jnp.bfloat16)
    grad = lax.dot_general(
        inputs, delta, (((0,), (0,)), ((), ())), preferred_element_type=jnp.float32
    )
    first = beta_one * start_first.astype(jnp.float32) + (1.0 - beta_one) * grad
    second = beta_two * start_second.astype(jnp.float32) + (1.0 - beta_two) * grad * grad
    updated = start_weight.astype(jnp.float32) - step_rate * first / (jnp.sqrt(second) + adam_eps)
    share = jnp.where(jnp.arange(members, dtype=jnp.int32) == member, part, jnp.float32(0.0))
    member_loss = lax.psum(share, "pop")
    return (
        updated.astype(jnp.bfloat16)[None],
        first.astype(jnp.bfloat16)[None],
        second.astype(jnp.bfloat16)[None],
        member_loss,
    )


ENDS = ((0, 1), (1, 0), (2, 3), (3, 2))
MIDDLE = ((1, 2), (2, 1))


def position():
    place = lax.axis_index("pop")
    return place // SHARDS, lax.rem(place, SHARDS)


SHARED, TAKEN, HOPS, BY_ENDS, THEIR_ENDS, TO_ENDS, TO_MIDDLE, PLAN = range(8)
FOR_END, FOR_OWN, TOKENS, COUNTS = 16, 20, 24, 28
OWN, GUEST, PASSED = range(3)
RATE, TASK = 0, 4


def copied_from(winner):
    loser, source = jnp.int32(0), jnp.int32(0)
    for m in range(PLANES):
        taken = winner[m] != m
        loser = jnp.where(taken, m, loser)
        source = jnp.where(taken, winner[m], source)
    return loser, source


def route_kernel(winner, code):
    loser, source = copied_from(winner)
    code[...] = jnp.full(code.shape, source * PLANES + loser, jnp.int32)


def route_code(winner):
    return pl.pallas_call(
        route_kernel,
        out_shape=jax.ShapeDtypeStruct((8, 128), jnp.int32),
        in_specs=[SMEM],
        out_specs=VMEM,
        name="route_code",
    )(winner)


def on_route(route, m, to):
    source, loser = route
    upward = (to == m + 1) & (source <= m) & (loser >= to)
    return upward | ((to == m - 1) & (source >= m) & (loser <= to))


def by_ends(route):
    source, loser = route
    return jnp.where(source < loser, loser - 1, loser + 1) == (loser ^ 1)


def in_pool(t, m, k):
    ahead = t // SHARDS - m
    ahead = jnp.where(m == 1, ahead, -ahead)
    group = jnp.where(ahead == 0, 0, jnp.where(ahead == -1, 1, ahead + 1))
    return group * SHARDS + (lax.rem(t, SHARDS) ^ k)


def facts_kernel(
    other, winner, learn_rate, explore, task_weight, tile_ids, slot_task, slot_tokens, ints, floats
):
    m, k = position()
    loser, source = copied_from(winner)
    code = other[0, 0]
    mine = source, loser
    theirs = lax.div(code, jnp.int32(PLANES)), lax.rem(code, jnp.int32(PLANES))
    upward = jnp.maximum(mine[0], theirs[0]) < jnp.minimum(mine[1], theirs[1])
    downward = jnp.maximum(mine[1], theirs[1]) < jnp.minimum(mine[0], theirs[0])
    shared = upward | downward
    hops = jnp.abs(mine[0] - mine[1])
    most = jnp.maximum(hops, jnp.abs(theirs[0] - theirs[1]))
    taken = winner[m] != m

    def content(to):
        own = on_route(mine, m, to)
        guest = on_route(theirs, m, to) & jnp.logical_not(shared)
        first = jnp.where(own, jnp.where(m == mine[0], OWN, PASSED), -1)
        return jnp.where(guest, jnp.where(m == theirs[0], GUEST, PASSED), first)

    ints[SHARED] = shared.astype(jnp.int32)
    ints[TAKEN] = taken.astype(jnp.int32)
    ints[HOPS] = hops
    ints[BY_ENDS] = by_ends(mine).astype(jnp.int32)
    ints[THEIR_ENDS] = by_ends(theirs).astype(jnp.int32)
    ints[TO_ENDS] = content(m ^ 1)
    ints[TO_MIDDLE] = content(jnp.where(m == 1, 2, jnp.where(m == 2, 1, -1)))
    ints[PLAN] = jnp.where(most == PLANES - 1, 3, jnp.where(shared, 2, most - 1))
    end = jnp.where(m <= 1, 0, PLANES - 1)
    at_end = (m == 0) | (m == PLANES - 1)
    slots = tile_ids.shape[1]
    for s in range(slots):
        task = slot_task[m, s]
        count = jnp.int32(0)
        for o in range(slots):
            count = count + jnp.where(slot_task[m, o] == task, slot_tokens[m, o], 0)
        ints[FOR_END + s] = in_pool(tile_ids[end, s], m, k)
        ints[FOR_OWN + s] = jnp.where(at_end, -1, in_pool(tile_ids[m, s], m, k))
        ints[TOKENS + s] = slot_tokens[m, s]
        ints[COUNTS + s] = jnp.maximum(count, 1)
        floats[TASK + s] = task_weight[winner[m], task]
    floats[RATE] = learn_rate[winner[m]] * jnp.where(taken, explore[m], 1.0)


def gather_facts(other, *small):
    return pl.pallas_call(
        facts_kernel,
        out_shape=[jax.ShapeDtypeStruct((32,), jnp.int32), jax.ShapeDtypeStruct((8,), jnp.float32)],
        in_specs=[SMEM] * 8,
        out_specs=[SMEM, SMEM],
        name="gather_facts",
    )(other, *small)


def stage_kernel(t, has_guest, has_theirs, has_last, ints, *refs):
    state, refs = refs[:3], refs[3:]
    guest = refs[0] if has_guest else None
    from_ends, from_middle = refs[has_guest : has_guest + 2] if has_last else (None, None)
    to_ends, to_middle = refs[has_guest + 2 * has_last :][:2]
    sems = refs[-1]
    half = to_ends.shape[0]
    shared = ints[SHARED] == 1
    array = jnp.where(shared, (t - 1) // 2, t - 1)
    start = pl.multiple_of(jnp.where(shared, (t - 1) % 2, 0) * half, half)
    sides = ((to_ends, ints[TO_ENDS], from_middle), (to_middle, ints[TO_MIDDLE], from_ends))
    for n, (out, content, _) in enumerate(sides):
        for a, ref in enumerate(state):

            @pl.when((content == OWN) & (array == a))
            def _():
                pltpu.make_async_copy(ref.at[0, pl.ds(start, half)], out, sems.at[n]).start()

    if has_theirs:
        theirs = refs[has_guest + 2 * has_last + 2]

        @pl.when(ints[THEIR_ENDS] == 1)
        def _():
            copy_rows(from_ends, 0, theirs, 0, half)

        @pl.when(ints[THEIR_ENDS] == 0)
        def _():
            copy_rows(from_middle, 0, theirs, 0, half)

    for n, (out, content, passed) in enumerate(sides):
        if guest is not None:

            @pl.when(content == GUEST)
            def _():
                copy_rows(guest, 0, out, 0, half)

        if passed is not None:

            @pl.when(content == PASSED)
            def _():
                copy_rows(passed, 0, out, 0, half)

        @pl.when((content == OWN) & (array < len(state)))
        def _():
            pltpu.make_async_copy(state[0].at[0, pl.ds(0, half)], out, sems.at[n]).wait()


def stage(ints, step, own, guest, last, theirs):
    half, width = own[0].shape[1] // 2, own[0].shape[2]
    guests = () if guest is None else (guest,)
    kernel = functools.partial(stage_kernel, step, len(guests), theirs, len(last) > 0)
    return pl.pallas_call(
        kernel,
        out_shape=[jax.ShapeDtypeStruct((half, width), own[0].dtype)] * (2 + theirs),
        in_specs=[SMEM] + [ANY] * 3 + [VMEM] * (len(guests) + len(last)),
        out_specs=[VMEM] * (2 + theirs),
        scratch_shapes=[pltpu.SemaphoreType.DMA((2,))],
        name="stage_chunk",
    )(ints, *own, *guests, *last)


def theirs_kernel(ints, from_ends, from_middle, theirs):
    @pl.when(ints[THEIR_ENDS] == 1)
    def _():
        copy_rows(from_ends, 0, theirs, 0, theirs.shape[0])

    @pl.when(ints[THEIR_ENDS] == 0)
    def _():
        copy_rows(from_middle, 0, theirs, 0, theirs.shape[0])


def theirs_of(ints, from_ends, from_middle):
    return pl.pallas_call(
        theirs_kernel,
        out_shape=jax.ShapeDtypeStruct(from_ends.shape, from_ends.dtype),
        in_specs=[SMEM] + [VMEM] * 2,
        out_specs=VMEM,
        name="guest_chunk",
    )(ints, from_ends, from_middle)


def start_copies(ints, a, h, own, sent, out, sem):
    ends, middles, backs = sent
    shared, taken = ints[SHARED] == 1, ints[TAKEN] == 1
    half = out.shape[0]
    step = jnp.where(shared, 2 * a + h, a) + ints[HOPS]
    direct = taken & shared if h == 1 else taken

    def copy(ref):
        return pltpu.make_async_copy(ref, out, sem)

    @pl.when(jnp.logical_not(taken))
    def _():
        copy(own.at[0, pl.ds(h * half, half)]).start()

    sides = [
        (ends, direct & (ints[BY_ENDS] == 1)),
        (middles, direct & (ints[BY_ENDS] == 0)),
    ]
    if h == 1:
        sides.append((backs, taken & jnp.logical_not(shared)))
    for refs, here in sides:
        for n, ref in enumerate(refs):

            @pl.when(here & (step == n + 1))
            def _():
                copy(ref).start()

    return copy(own.at[0, pl.ds(h * half, half)])


def counts_of(sent):
    return tuple(len(refs) for refs in sent)


def sent_refs(counts, refs):
    a, b, c = counts
    return (refs[:a], refs[a : a + b], refs[a + b : a + b + c]), refs[a + b + c :]


def pack_kernel(code, tokens, targets, *parts):
    _, k = position()
    width = targets.shape[2] // SHARDS
    slim = tokens.shape[2] // SHARDS
    for j, part in enumerate(parts):
        q = k ^ j
        part[:, :width] = targets[0, :, pl.ds(pl.multiple_of(q * width, 128), width)]
        part[:, width:] = tokens[0, :, pl.ds(pl.multiple_of(q * slim, 128), slim)]


def pack(code, tokens, targets):
    tile = tokens.shape[1]
    row = (tokens.shape[2] + targets.shape[2]) // SHARDS
    return pl.pallas_call(
        pack_kernel,
        out_shape=[jax.ShapeDtypeStruct((tile, row), tokens.dtype)] * SHARDS,
        in_specs=[VMEM] * 3,
        out_specs=[VMEM] * SHARDS,
        name="pack_quarters",
    )(code, tokens, targets)


def copy_rows(ref, start, out, at, count, columns=slice(None)):
    step = 32

    def body(i, _):
        rows = pl.ds(pl.multiple_of(at + i * step, step), step)
        out[rows, :] = ref[pl.ds(pl.multiple_of(start + i * step, step), step), columns]
        return 0

    lax.fori_loop(0, count // step, body, 0, unroll=True if count <= 64 else 4)


def split_kernel(one, two, three, *halves):
    count = one.shape[0] // 2
    for h, half in enumerate(halves):
        for n, part in enumerate((one, two, three)):
            copy_rows(part, h * count, half, n * count, count)


def split_rows(parts):
    tile, row = parts[0].shape
    half = jax.ShapeDtypeStruct((len(parts) * tile // 2, row), parts[0].dtype)
    return pl.pallas_call(
        split_kernel,
        out_shape=[half, half],
        in_specs=[VMEM] * len(parts),
        out_specs=[VMEM, VMEM],
        name="split_rows",
    )(*parts)


def piece(pool, which, h):
    group, j = divmod(which, SHARDS)
    whole, halves = pool[group]
    rows = whole.shape[0] // 2
    return (whole, h * rows, rows) if j == 0 else (halves[h], (j - 1) * rows, rows)


def grouped(refs, halves):
    size = 1 + len(halves)
    pool = []
    for g in range(PLANES):
        group = refs[g * size : (g + 1) * size]
        pool.append((group[0], dict(zip(halves, group[1:]))))
    return pool, refs[PLANES * size :]


def pick_for_end_kernel(h, ints, *refs):
    pool, (out,) = grouped(refs, (h,))

    def slot(s, _):
        place = ints[FOR_END + s]
        for which in range(PLANES * SHARDS):
            ref, start, rows = piece(pool, which, h)

            @pl.when(place == which)
            def _():
                copy_rows(ref, start, out, s * rows, rows)

        return 0

    lax.fori_loop(0, SLOTS, slot, 0)


def pick_for_end(h, ints, pool):
    tile, row = pool[0][0].shape
    operands = [x for whole, halves in pool for x in (whole, halves[h])]
    return pl.pallas_call(
        functools.partial(pick_for_end_kernel, h),
        out_shape=jax.ShapeDtypeStruct((SLOTS * tile // 2, row), operands[0].dtype),
        in_specs=[SMEM] + [VMEM] * len(operands),
        out_specs=VMEM,
        compiler_params=pltpu.CompilerParams(vmem_limit_bytes=16 * 1024 * 1024),
        name="pick_for_end",
    )(ints, *operands)


def pick_own_kernel(ints, *refs):
    pool, (handed_a, handed_b, quarter, targets) = grouped(refs, (0, 1))
    handed = (handed_a, handed_b)
    width = targets.shape[1]
    half = quarter.shape[0] // SLOTS // 2

    def slot(s, _):
        place = ints[FOR_OWN + s]
        for h in range(2):
            at = (2 * s + h) * half

            @pl.when(place < 0)
            def _():
                start = pl.multiple_of(s * half, half)
                copy_rows(handed[h], start, targets, at, half, slice(0, width))
                copy_rows(handed[h], start, quarter, at, half, slice(width, None))

            for which in range(PLANES * SHARDS):
                ref, start, rows = piece(pool, which, h)

                @pl.when(place == which)
                def _():
                    copy_rows(ref, start, targets, at, rows, slice(0, width))
                    copy_rows(ref, start, quarter, at, rows, slice(width, None))

        return 0

    lax.fori_loop(0, SLOTS, slot, 0)


def pick_own(ints, pool, handed, width):
    rows, row = handed[0].shape
    operands = [x for whole, halves in pool for x in (whole, *halves)]
    return pl.pallas_call(
        pick_own_kernel,
        out_shape=[
            jax.ShapeDtypeStruct((2 * rows, row - width), handed[0].dtype),
            jax.ShapeDtypeStruct((2 * rows, width), handed[0].dtype),
        ],
        in_specs=[SMEM] + [VMEM] * (len(operands) + 2),
        out_specs=[VMEM, VMEM],
        compiler_params=pltpu.CompilerParams(vmem_limit_bytes=16 * 1024 * 1024),
        name="pick_own",
    )(ints, *operands, *handed)


def grad_kernel(counts, ints, floats, in0, in1, in2, in3, targets, own_w, *refs):
    sent, (grad, loss, w_buf, delta, sem) = sent_refs(counts, refs)
    m, k = position()
    half = w_buf.shape[0] // 2
    copies = [
        start_copies(ints, 0, h, own_w, sent, w_buf.at[pl.ds(h * half, half)], sem.at[h])
        for h in range(2)
    ]
    tile = in0.shape[0] // SLOTS
    slim = in0.shape[1]
    ins = (in0, in1, in2, in3)
    for copy in copies:
        copy.wait()

    def slot(s, total):
        span = pl.ds(pl.multiple_of(s * tile, tile), tile)
        pre = None
        for j in range(SHARDS):
            at = pl.ds(pl.multiple_of((k ^ j) * slim, slim), slim)
            one = jnp.dot(ins[j][span, :], w_buf[at, :], preferred_element_type=jnp.float32)
            pre = one if pre is None else pre + one
        live = lax.broadcasted_iota(jnp.int32, pre.shape, 0) < ints[TOKENS + s]
        many = jnp.full(pre.shape, ints[COUNTS + s], jnp.int32).astype(jnp.float32)
        coef = jnp.where(live, floats[TASK + s] / many, 0.0)
        hidden, slope = gelu_pair(pre)
        diff = hidden - targets[span, :].astype(jnp.float32)
        scaled = coef * diff
        delta[span, :] = (2.0 * scaled * slope).astype(jnp.bfloat16)
        return total + jnp.sum(scaled * diff, keepdims=True)

    total = lax.fori_loop(0, SLOTS, slot, jnp.zeros((1, 1), jnp.float32))
    lane = lax.broadcasted_iota(jnp.int32, loss.shape, 1)
    loss[...] = jnp.where(lane == m * SHARDS + k, total, 0.0)
    for j in range(SHARDS):
        at = pl.ds(pl.multiple_of((k ^ j) * slim, slim), slim)
        grad[at, :] = lax.dot_general(
            ins[j][...], delta[...], (((0,), (0,)), ((), ())), preferred_element_type=jnp.float32
        )


def gradient(ints, floats, ins, targets, own_w, sent):
    rows, width = targets.shape
    depth = own_w.shape[1]
    return pl.pallas_call(
        functools.partial(grad_kernel, counts_of(sent)),
        out_shape=[
            jax.ShapeDtypeStruct((depth, width), jnp.float32),
            jax.ShapeDtypeStruct((8, 128), jnp.float32),
        ],
        in_specs=[SMEM] * 2 + [VMEM] * 5 + [ANY] + [VMEM] * sum(counts_of(sent)),
        out_specs=[VMEM, VMEM],
        scratch_shapes=[
            pltpu.VMEM((depth, width), own_w.dtype),
            pltpu.VMEM((rows, width), jnp.bfloat16),
            pltpu.SemaphoreType.DMA((2,)),
        ],
        compiler_params=pltpu.CompilerParams(vmem_limit_bytes=16 * 1024 * 1024),
        name="forward_and_gradient",
    )(ints, floats, *ins, targets, own_w, *sent[0], *sent[1], *sent[2])


def adam_kernel(h, counts, ints, floats, grad, *refs):
    own, (sent, refs) = refs[:3], sent_refs(counts, refs[3:])
    new, bufs, outs, (in_sem, out_sem) = refs[-11:-8], refs[-8:-5], refs[-5:-2], refs[-2:]
    blocks = out_sem.shape[1]
    rows = bufs[0].shape[0]
    step = rows // blocks
    here = h * rows

    def result(i, b):
        return pltpu.make_async_copy(
            outs[i].at[pl.ds(b * step, step)],
            new[i].at[0, pl.ds(here + b * step, step)],
            out_sem.at[i, b],
        )

    copies = [
        start_copies(ints, a, h, own[a], sent, bufs[a], in_sem.at[a]) for a in range(3)
    ]
    rate = floats[RATE]
    for copy in copies:
        copy.wait()
    for b in range(blocks):

        def body(n, _):
            at = pl.ds(pl.multiple_of(b * step + n * 16, 16), 16)
            g = grad[pl.ds(pl.multiple_of(here + b * step + n * 16, 16), 16), :]
            first = beta_one * bufs[1][at, :].astype(jnp.float32) + (1.0 - beta_one) * g
            second = beta_two * bufs[2][at, :].astype(jnp.float32) + (1.0 - beta_two) * g * g
            start = bufs[0][at, :].astype(jnp.float32)
            updated = start - rate * first / (jnp.sqrt(second) + adam_eps)
            outs[0][at, :] = updated.astype(outs[0].dtype)
            outs[1][at, :] = first.astype(outs[1].dtype)
            outs[2][at, :] = second.astype(outs[2].dtype)
            return 0

        lax.fori_loop(0, step // 16, body, 0, unroll=2)
        for i in range(3):
            result(i, b).start()
    for b in range(blocks):
        for i in range(3):
            result(i, b).wait()


def adam(h, ints, floats, grad, own, sent, begun=()):
    depth, width = grad.shape
    blocks = 2
    taken = sum(counts_of(sent))
    return pl.pallas_call(
        functools.partial(adam_kernel, h, counts_of(sent)),
        out_shape=[jax.ShapeDtypeStruct(x.shape, x.dtype) for x in own],
        in_specs=[SMEM] * 2 + [VMEM] + [ANY] * 3 + [VMEM] * taken + [ANY] * len(begun),
        out_specs=[ANY] * 3,
        scratch_shapes=[pltpu.VMEM((depth // 2, width), x.dtype) for x in own] * 2
        + [pltpu.SemaphoreType.DMA((3,)), pltpu.SemaphoreType.DMA((3, blocks))],
        input_output_aliases={6 + taken + i: i for i in range(len(begun))},
        compiler_params=pltpu.CompilerParams(vmem_limit_bytes=16 * 1024 * 1024),
        name="adam_half",
    )(ints, floats, grad, *own, *sent[0], *sent[1], *sent[2], *begun)


def in_plane(x, j):
    pairs = [(m * SHARDS + k, m * SHARDS + (k ^ j)) for m in range(PLANES) for k in range(SHARDS)]
    return lax.ppermute(x, "pop", pairs)


def along(x, hops):
    idle = [m for m in range(PLANES) if all(m not in hop for hop in hops)]
    pairs = [(a * SHARDS + k, b * SHARDS + k) for a, b in hops for k in range(SHARDS)]
    pairs += [(m * SHARDS + k, m * SHARDS + (k ^ 1)) for m in idle for k in range(SHARDS)]
    return lax.ppermute(x, "pop", pairs)


def beside(x):
    return lax.ppermute(x, "rep", [(0, 1), (1, 0)])


def after(x, *others):
    return lax.optimization_barrier((x, *others))[0]


def tiles(here, ints, width):
    near0, middle0, (here0, halves) = here
    near = [along(x, ENDS) for x in halves]
    far0 = along(near0, MIDDLE)
    middle = [along(x, MIDDLE) for x in halves]
    far = [along(x, MIDDLE) for x in near]
    pool = [(here0, halves), (near0, near), (middle0, middle), (far0, far)]
    handed = [along(pick_for_end(h, ints, pool), ENDS) for h in range(2)]
    quarter, targets = pick_own(ints, pool, handed, width)
    side = in_plane(quarter, 1)
    cross = in_plane(quarter, 2)
    return (quarter, side, cross, in_plane(cross, 1)), targets


PLANS = ((3, 3), (4, 4), (7, 0), (8, 5))


def state_steps(ints, own, gate, steps, returns):
    half = own[0].shape[1] // 2
    guests = [beside(x[0, half:]) for x in own] if returns else []
    last, ends, middles, backs = (), [], [], []
    for t in range(1, steps + 1):
        guest = guests[t - 1] if t <= len(guests) else None
        if t == 1 and guest is not None:
            guest = after(guest, gate)
        theirs = 1 < t <= returns + 1
        to_ends, to_middle, *brought = stage(ints, t, own, guest, last, theirs)
        backs += [beside(x) for x in brought]
        last = (along(to_ends, ENDS), along(to_middle, MIDDLE))
        ends.append(last[0])
        middles.append(last[1])
    if len(backs) < returns:
        backs.append(beside(theirs_of(ints, *last)))
    return ends, middles, backs


def run(plan, ints, floats, parts, own):
    steps, returns = PLANS[plan]
    near0, middle0 = along(parts[0], ENDS), along(parts[0], MIDDLE)
    halves = split_rows([in_plane(parts[j], j) for j in range(1, SHARDS)])
    here = (near0, middle0, (parts[0], halves))
    ins, targets = tiles(here, ints, own[0].shape[2])
    ends, middles, backs = state_steps(ints, own, halves, steps, returns)
    first = plan + 1
    grad, loss = gradient(
        ints, floats, ins, targets, own[0], (ends[:first], middles[:first], backs[:first])
    )
    round_one = [in_plane(loss, j) for j in range(1, SHARDS)]
    new = adam(0, ints, floats, grad, own, (ends, middles, []))
    loss = loss + round_one[0] + round_one[1] + round_one[2]
    loss = after(loss, new[0])
    ring = [along(loss, [(m, (m + d) % PLANES) for m in range(PLANES)]) for d in range(1, PLANES)]
    direct = (ends, middles) if plan > 1 else ([], [])
    new = adam(1, ints, floats, grad, own, (*direct, backs), new)
    loss = loss + ring[0] + ring[1] + ring[2]
    return (*new, jnp.sum(loss[0, : PLANES * SHARDS].reshape(PLANES, SHARDS), axis=1))


def per_device(pool_tokens, pool_targets, weight, first_moment, second_moment, *args):
    winner, tile_ids = args[0], args[4]
    if winner.shape[0] != PLANES or tile_ids.shape[1] != SLOTS or lax.axis_size("rep") != 2:
        return relayed(pool_tokens, pool_targets, weight, first_moment, second_moment, *args)
    code = route_code(winner)
    parts = pack(code, pool_tokens, pool_targets)
    ints, floats = gather_facts(beside(code), *args)
    plans = [functools.partial(run, plan) for plan in range(len(PLANS))]
    return lax.switch(ints[PLAN], plans, ints, floats, parts, (weight, first_moment, second_moment))


def solution(mesh):
    in_specs = (
        P(("rep", "pop"), None, None),
        P(("rep", "pop"), None, None),
        P(("rep", "pop"), None, None),
        P(("rep", "pop"), None, None),
        P(("rep", "pop"), None, None),
        P("rep"),
        P("rep"),
        P("rep"),
        P("rep", None),
        P("rep", None),
        P("rep", None),
        P("rep", None),
    )
    out_specs = (
        P(("rep", "pop"), None, None),
        P(("rep", "pop"), None, None),
        P(("rep", "pop"), None, None),
        P("rep"),
    )
    return jax.shard_map(
        per_device, mesh=mesh, in_specs=in_specs, out_specs=out_specs, check_vma=False
    )
```

```python
import functools

import jax
import jax.numpy as jnp
from jax import lax
from jax.experimental import pallas as pl
from jax.experimental.pallas import tpu as pltpu
from jax.sharding import PartitionSpec as P

SHARDS = 4
TASKS = 8
SLOTS = 4
PLANES = 4


beta_one = 0.9
beta_two = 0.999
adam_eps = 1e-08
gelu_coef = 0.7978845608028654

SMEM = pl.BlockSpec(memory_space=pltpu.SMEM)
VMEM = pl.BlockSpec(memory_space=pltpu.VMEM)
ANY = pl.BlockSpec(memory_space=pl.ANY)


def gelu_pair(pre):
    inner = jnp.tanh(gelu_coef * (pre + 0.044715 * pre * pre * pre))
    value = 0.5 * pre * (1.0 + inner)
    slope = 0.5 * (1.0 + inner) + 0.5 * pre * (1.0 - inner * inner) * gelu_coef * (
        1.0 + 3.0 * 0.044715 * pre * pre
    )
    return (value, slope)


def for_sending(shard):

    def short(part):
        return part.astype(jnp.bfloat16) if part.dtype == jnp.float32 else part

    return jax.tree.map(short, shard)


def relayed(
    pool_tokens,
    pool_targets,
    weight,
    first_moment,
    second_moment,
    winner,
    learn_rate,
    explore,
    task_weight,
    tile_ids,
    slot_task,
    slot_tokens,
):
    nodes = lax.axis_size("pop")
    place = lax.axis_index("pop")
    member = place // SHARDS
    shard = place % SHARDS
    members = winner.shape[0]
    slots = tile_ids.shape[1]
    tile = pool_tokens.shape[1]
    depth = pool_tokens.shape[2]
    width = weight.shape[2]
    hidden_all = pool_targets.shape[2]
    reach = tile // nodes
    flat_state = (
        weight.reshape(nodes, -1),
        first_moment.reshape(nodes, -1),
        second_moment.reshape(nodes, -1),
    )
    spread = (
        lax.all_to_all(flat_state[0], "pop", split_axis=0, concat_axis=0, tiled=True),
        lax.all_to_all(flat_state[1], "pop", split_axis=0, concat_axis=0, tiled=True),
        lax.all_to_all(flat_state[2], "pop", split_axis=0, concat_axis=0, tiled=True),
    )
    source_rows = (winner[:, None] * SHARDS + jnp.arange(SHARDS, dtype=jnp.int32)[None, :]).reshape(
        -1
    )
    picked_state = tuple((jnp.take(piece, source_rows, axis=0) for piece in spread))
    returned = jax.tree.map(
        lambda part, own: part.astype(own.dtype),
        lax.all_to_all(for_sending(picked_state), "pop", split_axis=0, concat_axis=0, tiled=True),
        picked_state,
    )
    start_weight = returned[0].reshape(depth, width)
    start_first = returned[1].reshape(depth, width)
    start_second = returned[2].reshape(depth, width)
    relay_tokens, relay_targets = (
        lax.all_to_all(pool_tokens, "pop", split_axis=1, concat_axis=0, tiled=True),
        lax.all_to_all(pool_targets, "pop", split_axis=1, concat_axis=0, tiled=True),
    )
    flat_ids = tile_ids.reshape(-1)
    pick_tokens = jnp.take(relay_tokens, flat_ids, axis=0).reshape(members, 1, slots, reach, depth)
    send_tokens = jnp.broadcast_to(pick_tokens, (members, SHARDS, slots, reach, depth)).reshape(
        nodes, slots, reach, depth
    )
    pick_targets = jnp.take(relay_targets, flat_ids, axis=0).reshape(
        members, slots, reach, hidden_all
    )
    send_targets = jnp.broadcast_to(
        pick_targets[:, None], (members, SHARDS, slots, reach, hidden_all)
    ).reshape(nodes, slots, reach, hidden_all)
    got_tokens, got_targets = (
        lax.all_to_all(send_tokens, "pop", split_axis=0, concat_axis=2, tiled=True),
        lax.all_to_all(send_targets, "pop", split_axis=0, concat_axis=2, tiled=True),
    )
    targets = lax.dynamic_slice_in_dim(got_targets[0], shard * width, width, 2).reshape(
        slots * tile, width
    )
    inputs = got_tokens.reshape(slots * tile, depth)
    tasks_here = lax.dynamic_index_in_dim(slot_task, member, 0, keepdims=False)
    lengths = lax.dynamic_index_in_dim(slot_tokens, member, 0, keepdims=False)
    source_member = lax.dynamic_index_in_dim(winner, member, 0, keepdims=False)
    onehot = tasks_here[:, None] == jnp.arange(TASKS, dtype=jnp.int32)[None, :]
    counts = jnp.sum(jnp.where(onehot, lengths[:, None], 0), axis=0)
    weights_here = lax.dynamic_index_in_dim(task_weight, source_member, 0, keepdims=False)
    scale = weights_here / jnp.maximum(counts, 1).astype(jnp.float32)
    per_slot = jnp.sum(jnp.where(onehot, scale[None, :], jnp.float32(0.0)), axis=1)
    live = jnp.arange(tile, dtype=jnp.int32)[None, :] < lengths[:, None]
    coef = jnp.where(live, per_slot[:, None], jnp.float32(0.0)).reshape(-1)
    own_rate = lax.dynamic_index_in_dim(learn_rate, source_member, 0, keepdims=False)
    own_explore = lax.dynamic_index_in_dim(explore, member, 0, keepdims=False)
    step_rate = own_rate * jnp.where(source_member != member, own_explore, jnp.float32(1.0))
    pre = jnp.dot(inputs, start_weight, preferred_element_type=jnp.float32)
    hidden, slope = gelu_pair(pre)
    diff = hidden - targets.astype(jnp.float32)
    part = jnp.sum(coef[:, None] * diff * diff)
    delta = (2.0 * coef[:, None] * diff * slope).astype(jnp.bfloat16)
    grad = lax.dot_general(
        inputs, delta, (((0,), (0,)), ((), ())), preferred_element_type=jnp.float32
    )
    first = beta_one * start_first.astype(jnp.float32) + (1.0 - beta_one) * grad
    second = beta_two * start_second.astype(jnp.float32) + (1.0 - beta_two) * grad * grad
    updated = start_weight.astype(jnp.float32) - step_rate * first / (jnp.sqrt(second) + adam_eps)
    share = jnp.where(jnp.arange(members, dtype=jnp.int32) == member, part, jnp.float32(0.0))
    member_loss = lax.psum(share, "pop")
    return (
        updated.astype(jnp.bfloat16)[None],
        first.astype(jnp.bfloat16)[None],
        second.astype(jnp.bfloat16)[None],
        member_loss,
    )


ENDS = ((0, 1), (1, 0), (2, 3), (3, 2))
MIDDLE = ((1, 2), (2, 1))


def position():
    place = lax.axis_index("pop")
    return place // SHARDS, lax.rem(place, SHARDS)


SHARED, TAKEN, HOPS, BY_ENDS, THEIR_ENDS, TO_ENDS, TO_MIDDLE, LONG = range(8)
FOR_END, FOR_OWN, TOKENS, COUNTS = 16, 20, 24, 28
OWN, GUEST, PASSED = range(3)
RATE, TASK = 0, 4


def copied_from(winner):
    loser, source = jnp.int32(0), jnp.int32(0)
    for m in range(PLANES):
        taken = winner[m] != m
        loser = jnp.where(taken, m, loser)
        source = jnp.where(taken, winner[m], source)
    return loser, source


def route_kernel(winner, code):
    loser, source = copied_from(winner)
    code[...] = jnp.full(code.shape, source * PLANES + loser, jnp.int32)


def route_code(winner):
    return pl.pallas_call(
        route_kernel,
        out_shape=jax.ShapeDtypeStruct((8, 128), jnp.int32),
        in_specs=[SMEM],
        out_specs=VMEM,
        name="route_code",
    )(winner)


def on_route(route, m, to):
    source, loser = route
    upward = (to == m + 1) & (source <= m) & (loser >= to)
    return upward | ((to == m - 1) & (source >= m) & (loser <= to))


def by_ends(route):
    source, loser = route
    return jnp.where(source < loser, loser - 1, loser + 1) == (loser ^ 1)


def in_pool(t, m, k):
    ahead = t // SHARDS - m
    ahead = jnp.where(m == 1, ahead, -ahead)
    group = jnp.where(ahead == 0, 0, jnp.where(ahead == -1, 1, ahead + 1))
    return group * SHARDS + (lax.rem(t, SHARDS) ^ k)


def facts_kernel(
    other, winner, learn_rate, explore, task_weight, tile_ids, slot_task, slot_tokens, ints, floats
):
    m, k = position()
    loser, source = copied_from(winner)
    code = other[0, 0]
    mine = source, loser
    theirs = lax.div(code, jnp.int32(PLANES)), lax.rem(code, jnp.int32(PLANES))
    upward = jnp.maximum(mine[0], theirs[0]) < jnp.minimum(mine[1], theirs[1])
    downward = jnp.maximum(mine[1], theirs[1]) < jnp.minimum(mine[0], theirs[0])
    hops = jnp.abs(mine[0] - mine[1])
    long = jnp.maximum(hops, jnp.abs(theirs[0] - theirs[1])) == PLANES - 1
    shared = upward | downward | long
    taken = winner[m] != m

    def content(to):
        own = on_route(mine, m, to)
        guest = on_route(theirs, m, to) & jnp.logical_not(shared)
        first = jnp.where(own, jnp.where(m == mine[0], OWN, PASSED), -1)
        return jnp.where(guest, jnp.where(m == theirs[0], GUEST, PASSED), first)

    ints[SHARED] = shared.astype(jnp.int32)
    ints[TAKEN] = taken.astype(jnp.int32)
    ints[HOPS] = hops
    ints[BY_ENDS] = by_ends(mine).astype(jnp.int32)
    ints[THEIR_ENDS] = by_ends(theirs).astype(jnp.int32)
    ints[TO_ENDS] = content(m ^ 1)
    ints[TO_MIDDLE] = content(jnp.where(m == 1, 2, jnp.where(m == 2, 1, -1)))
    ints[LONG] = long.astype(jnp.int32)
    end = jnp.where(m <= 1, 0, PLANES - 1)
    at_end = (m == 0) | (m == PLANES - 1)
    slots = tile_ids.shape[1]
    for s in range(slots):
        task = slot_task[m, s]
        count = jnp.int32(0)
        for o in range(slots):
            count = count + jnp.where(slot_task[m, o] == task, slot_tokens[m, o], 0)
        ints[FOR_END + s] = in_pool(tile_ids[end, s], m, k)
        ints[FOR_OWN + s] = jnp.where(at_end, -1, in_pool(tile_ids[m, s], m, k))
        ints[TOKENS + s] = slot_tokens[m, s]
        ints[COUNTS + s] = jnp.maximum(count, 1)
        floats[TASK + s] = task_weight[winner[m], task]
    floats[RATE] = learn_rate[winner[m]] * jnp.where(taken, explore[m], 1.0)


def gather_facts(other, *small):
    return pl.pallas_call(
        facts_kernel,
        out_shape=[jax.ShapeDtypeStruct((32,), jnp.int32), jax.ShapeDtypeStruct((8,), jnp.float32)],
        in_specs=[SMEM] * 8,
        out_specs=[SMEM, SMEM],
        name="gather_facts",
    )(other, *small)


def stage_kernel(t, has_guest, has_theirs, has_last, ints, *refs):
    state, refs = refs[:3], refs[3:]
    guest = refs[0] if has_guest else None
    from_ends, from_middle = refs[has_guest : has_guest + 2] if has_last else (None, None)
    to_ends, to_middle = refs[has_guest + 2 * has_last :][:2]
    sems = refs[-1]
    half = to_ends.shape[0]
    shared = ints[SHARED] == 1
    array = jnp.where(shared, (t - 1) // 2, t - 1)
    start = pl.multiple_of(jnp.where(shared, (t - 1) % 2, 0) * half, half)
    sides = ((to_ends, ints[TO_ENDS], from_middle), (to_middle, ints[TO_MIDDLE], from_ends))
    for n, (out, content, _) in enumerate(sides):
        for a, ref in enumerate(state):

            @pl.when((content == OWN) & (array == a))
            def _():
                pltpu.make_async_copy(ref.at[0, pl.ds(start, half)], out, sems.at[n]).start()

    if has_theirs:
        theirs = refs[has_guest + 2 * has_last + 2]

        @pl.when(ints[THEIR_ENDS] == 1)
        def _():
            copy_rows(from_ends, 0, theirs, 0, half)

        @pl.when(ints[THEIR_ENDS] == 0)
        def _():
            copy_rows(from_middle, 0, theirs, 0, half)

    for n, (out, content, passed) in enumerate(sides):
        if guest is not None:

            @pl.when(content == GUEST)
            def _():
                copy_rows(guest, 0, out, 0, half)

        if passed is not None:

            @pl.when(content == PASSED)
            def _():
                copy_rows(passed, 0, out, 0, half)

        @pl.when((content == OWN) & (array < len(state)))
        def _():
            pltpu.make_async_copy(state[0].at[0, pl.ds(0, half)], out, sems.at[n]).wait()


def stage(ints, step, own, guest, last, theirs):
    half, width = own[0].shape[1] // 2, own[0].shape[2]
    guests = () if guest is None else (guest,)
    kernel = functools.partial(stage_kernel, step, len(guests), theirs, len(last) > 0)
    return pl.pallas_call(
        kernel,
        out_shape=[jax.ShapeDtypeStruct((half, width), own[0].dtype)] * (2 + theirs),
        in_specs=[SMEM] + [ANY] * 3 + [VMEM] * (len(guests) + len(last)),
        out_specs=[VMEM] * (2 + theirs),
        scratch_shapes=[pltpu.SemaphoreType.DMA((2,))],
        name="stage_chunk",
    )(ints, *own, *guests, *last)


def theirs_kernel(ints, from_ends, from_middle, theirs):
    @pl.when(ints[THEIR_ENDS] == 1)
    def _():
        copy_rows(from_ends, 0, theirs, 0, theirs.shape[0])

    @pl.when(ints[THEIR_ENDS] == 0)
    def _():
        copy_rows(from_middle, 0, theirs, 0, theirs.shape[0])


def theirs_of(ints, from_ends, from_middle):
    return pl.pallas_call(
        theirs_kernel,
        out_shape=jax.ShapeDtypeStruct(from_ends.shape, from_ends.dtype),
        in_specs=[SMEM] + [VMEM] * 2,
        out_specs=VMEM,
        name="guest_chunk",
    )(ints, from_ends, from_middle)


def start_copies(ints, a, h, own, sent, out, sem):
    ends, middles, backs = sent
    shared, taken = ints[SHARED] == 1, ints[TAKEN] == 1
    half = out.shape[0]
    step = jnp.where(shared, 2 * a + h, a) + ints[HOPS]
    direct = taken & shared if h == 1 else taken

    def copy(ref):
        return pltpu.make_async_copy(ref, out, sem)

    @pl.when(jnp.logical_not(taken))
    def _():
        copy(own.at[0, pl.ds(h * half, half)]).start()

    sides = [
        (ends, direct & (ints[BY_ENDS] == 1)),
        (middles, direct & (ints[BY_ENDS] == 0)),
    ]
    if h == 1:
        sides.append((backs, taken & jnp.logical_not(shared)))
    for refs, here in sides:
        for n, ref in enumerate(refs):

            @pl.when(here & (step == n + 1))
            def _():
                copy(ref).start()

    return copy(own.at[0, pl.ds(h * half, half)])


def counts_of(sent):
    return tuple(len(refs) for refs in sent)


def sent_refs(counts, refs):
    a, b, c = counts
    return (refs[:a], refs[a : a + b], refs[a + b : a + b + c]), refs[a + b + c :]


def pack_kernel(code, tokens, targets, *parts):
    _, k = position()
    width = targets.shape[2] // SHARDS
    slim = tokens.shape[2] // SHARDS
    for j, part in enumerate(parts):
        q = k ^ j
        part[:, :width] = targets[0, :, pl.ds(pl.multiple_of(q * width, 128), width)]
        part[:, width:] = tokens[0, :, pl.ds(pl.multiple_of(q * slim, 128), slim)]


def pack(code, tokens, targets):
    tile = tokens.shape[1]
    row = (tokens.shape[2] + targets.shape[2]) // SHARDS
    return pl.pallas_call(
        pack_kernel,
        out_shape=[jax.ShapeDtypeStruct((tile, row), tokens.dtype)] * SHARDS,
        in_specs=[VMEM] * 3,
        out_specs=[VMEM] * SHARDS,
        name="pack_quarters",
    )(code, tokens, targets)


def copy_rows(ref, start, out, at, count, columns=slice(None)):
    step = 32

    def body(i, _):
        rows = pl.ds(pl.multiple_of(at + i * step, step), step)
        out[rows, :] = ref[pl.ds(pl.multiple_of(start + i * step, step), step), columns]
        return 0

    lax.fori_loop(0, count // step, body, 0, unroll=True if count <= 64 else 4)


def split_kernel(one, two, three, *halves):
    count = one.shape[0] // 2
    for h, half in enumerate(halves):
        for n, part in enumerate((one, two, three)):
            copy_rows(part, h * count, half, n * count, count)


def split_rows(parts):
    tile, row = parts[0].shape
    half = jax.ShapeDtypeStruct((len(parts) * tile // 2, row), parts[0].dtype)
    return pl.pallas_call(
        split_kernel,
        out_shape=[half, half],
        in_specs=[VMEM] * len(parts),
        out_specs=[VMEM, VMEM],
        name="split_rows",
    )(*parts)


def piece(pool, which, h):
    group, j = divmod(which, SHARDS)
    whole, halves = pool[group]
    rows = whole.shape[0] // 2
    return (whole, h * rows, rows) if j == 0 else (halves[h], (j - 1) * rows, rows)


def grouped(refs, halves):
    size = 1 + len(halves)
    pool = []
    for g in range(PLANES):
        group = refs[g * size : (g + 1) * size]
        pool.append((group[0], dict(zip(halves, group[1:]))))
    return pool, refs[PLANES * size :]


def pick_for_end_kernel(h, ints, *refs):
    pool, (out,) = grouped(refs, (h,))

    def slot(s, _):
        place = ints[FOR_END + s]
        for which in range(PLANES * SHARDS):
            ref, start, rows = piece(pool, which, h)

            @pl.when(place == which)
            def _():
                copy_rows(ref, start, out, s * rows, rows)

        return 0

    lax.fori_loop(0, SLOTS, slot, 0)


def pick_for_end(h, ints, pool):
    tile, row = pool[0][0].shape
    operands = [x for whole, halves in pool for x in (whole, halves[h])]
    return pl.pallas_call(
        functools.partial(pick_for_end_kernel, h),
        out_shape=jax.ShapeDtypeStruct((SLOTS * tile // 2, row), operands[0].dtype),
        in_specs=[SMEM] + [VMEM] * len(operands),
        out_specs=VMEM,
        compiler_params=pltpu.CompilerParams(vmem_limit_bytes=16 * 1024 * 1024),
        name="pick_for_end",
    )(ints, *operands)


def pick_own_kernel(ints, *refs):
    pool, (handed_a, handed_b, quarter, targets) = grouped(refs, (0, 1))
    handed = (handed_a, handed_b)
    width = targets.shape[1]
    half = quarter.shape[0] // SLOTS // 2

    def slot(s, _):
        place = ints[FOR_OWN + s]
        for h in range(2):
            at = (2 * s + h) * half

            @pl.when(place < 0)
            def _():
                start = pl.multiple_of(s * half, half)
                copy_rows(handed[h], start, targets, at, half, slice(0, width))
                copy_rows(handed[h], start, quarter, at, half, slice(width, None))

            for which in range(PLANES * SHARDS):
                ref, start, rows = piece(pool, which, h)

                @pl.when(place == which)
                def _():
                    copy_rows(ref, start, targets, at, rows, slice(0, width))
                    copy_rows(ref, start, quarter, at, rows, slice(width, None))

        return 0

    lax.fori_loop(0, SLOTS, slot, 0)


def pick_own(ints, pool, handed, width):
    rows, row = handed[0].shape
    operands = [x for whole, halves in pool for x in (whole, *halves)]
    return pl.pallas_call(
        pick_own_kernel,
        out_shape=[
            jax.ShapeDtypeStruct((2 * rows, row - width), handed[0].dtype),
            jax.ShapeDtypeStruct((2 * rows, width), handed[0].dtype),
        ],
        in_specs=[SMEM] + [VMEM] * (len(operands) + 2),
        out_specs=[VMEM, VMEM],
        compiler_params=pltpu.CompilerParams(vmem_limit_bytes=16 * 1024 * 1024),
        name="pick_own",
    )(ints, *operands, *handed)


def grad_kernel(counts, ints, floats, in0, in1, in2, in3, targets, own_w, *refs):
    sent, (grad, loss, w_buf, delta, sem) = sent_refs(counts, refs)
    m, k = position()
    half = w_buf.shape[0] // 2
    copies = [
        start_copies(ints, 0, h, own_w, sent, w_buf.at[pl.ds(h * half, half)], sem.at[h])
        for h in range(2)
    ]
    tile = in0.shape[0] // SLOTS
    slim = in0.shape[1]
    ins = (in0, in1, in2, in3)
    for copy in copies:
        copy.wait()

    def slot(s, total):
        span = pl.ds(pl.multiple_of(s * tile, tile), tile)
        pre = None
        for j in range(SHARDS):
            at = pl.ds(pl.multiple_of((k ^ j) * slim, slim), slim)
            one = jnp.dot(ins[j][span, :], w_buf[at, :], preferred_element_type=jnp.float32)
            pre = one if pre is None else pre + one
        live = lax.broadcasted_iota(jnp.int32, pre.shape, 0) < ints[TOKENS + s]
        many = jnp.full(pre.shape, ints[COUNTS + s], jnp.int32).astype(jnp.float32)
        coef = jnp.where(live, floats[TASK + s] / many, 0.0)
        hidden, slope = gelu_pair(pre)
        diff = hidden - targets[span, :].astype(jnp.float32)
        scaled = coef * diff
        delta[span, :] = (2.0 * scaled * slope).astype(jnp.bfloat16)
        return total + jnp.sum(scaled * diff, keepdims=True)

    total = lax.fori_loop(0, SLOTS, slot, jnp.zeros((1, 1), jnp.float32))
    lane = lax.broadcasted_iota(jnp.int32, loss.shape, 1)
    loss[...] = jnp.where(lane == m * SHARDS + k, total, 0.0)
    for j in range(SHARDS):
        at = pl.ds(pl.multiple_of((k ^ j) * slim, slim), slim)
        grad[at, :] = lax.dot_general(
            ins[j][...], delta[...], (((0,), (0,)), ((), ())), preferred_element_type=jnp.float32
        )


def gradient(ints, floats, ins, targets, own_w, sent):
    rows, width = targets.shape
    depth = own_w.shape[1]
    return pl.pallas_call(
        functools.partial(grad_kernel, counts_of(sent)),
        out_shape=[
            jax.ShapeDtypeStruct((depth, width), jnp.float32),
            jax.ShapeDtypeStruct((8, 128), jnp.float32),
        ],
        in_specs=[SMEM] * 2 + [VMEM] * 5 + [ANY] * (1 + sum(counts_of(sent))),
        out_specs=[VMEM, VMEM],
        scratch_shapes=[
            pltpu.VMEM((depth, width), own_w.dtype),
            pltpu.VMEM((rows, width), jnp.bfloat16),
            pltpu.SemaphoreType.DMA((2,)),
        ],
        compiler_params=pltpu.CompilerParams(vmem_limit_bytes=16 * 1024 * 1024),
        name="forward_and_gradient",
    )(ints, floats, *ins, targets, own_w, *sent[0], *sent[1], *sent[2])


def adam_kernel(h, counts, ints, floats, grad, *refs):
    own, (sent, refs) = refs[:3], sent_refs(counts, refs[3:])
    new, bufs, outs, (in_sem, out_sem) = refs[-11:-8], refs[-8:-5], refs[-5:-2], refs[-2:]
    blocks = out_sem.shape[1]
    rows = bufs[0].shape[0]
    step = rows // blocks
    here = h * rows

    def result(i, b):
        return pltpu.make_async_copy(
            outs[i].at[pl.ds(b * step, step)],
            new[i].at[0, pl.ds(here + b * step, step)],
            out_sem.at[i, b],
        )

    copies = [
        start_copies(ints, a, h, own[a], sent, bufs[a], in_sem.at[a]) for a in range(3)
    ]
    rate = floats[RATE]
    for copy in copies:
        copy.wait()
    for b in range(blocks):

        def body(n, _):
            at = pl.ds(pl.multiple_of(b * step + n * 16, 16), 16)
            g = grad[pl.ds(pl.multiple_of(here + b * step + n * 16, 16), 16), :]
            first = beta_one * bufs[1][at, :].astype(jnp.float32) + (1.0 - beta_one) * g
            second = beta_two * bufs[2][at, :].astype(jnp.float32) + (1.0 - beta_two) * g * g
            start = bufs[0][at, :].astype(jnp.float32)
            updated = start - rate * first / (jnp.sqrt(second) + adam_eps)
            outs[0][at, :] = updated.astype(outs[0].dtype)
            outs[1][at, :] = first.astype(outs[1].dtype)
            outs[2][at, :] = second.astype(outs[2].dtype)
            return 0

        lax.fori_loop(0, step // 16, body, 0, unroll=2)
        for i in range(3):
            result(i, b).start()
    for b in range(blocks):
        for i in range(3):
            result(i, b).wait()


def adam(h, ints, floats, grad, own, sent, begun=()):
    depth, width = grad.shape
    blocks = 2
    taken = sum(counts_of(sent))
    return pl.pallas_call(
        functools.partial(adam_kernel, h, counts_of(sent)),
        out_shape=[jax.ShapeDtypeStruct(x.shape, x.dtype) for x in own],
        in_specs=[SMEM] * 2 + [VMEM] + [ANY] * (3 + taken + len(begun)),
        out_specs=[ANY] * 3,
        scratch_shapes=[pltpu.VMEM((depth // 2, width), x.dtype) for x in own] * 2
        + [pltpu.SemaphoreType.DMA((3,)), pltpu.SemaphoreType.DMA((3, blocks))],
        input_output_aliases={6 + taken + i: i for i in range(len(begun))},
        compiler_params=pltpu.CompilerParams(vmem_limit_bytes=16 * 1024 * 1024),
        name="adam_half",
    )(ints, floats, grad, *own, *sent[0], *sent[1], *sent[2], *begun)


def in_plane(x, j):
    pairs = [(m * SHARDS + k, m * SHARDS + (k ^ j)) for m in range(PLANES) for k in range(SHARDS)]
    return lax.ppermute(x, "pop", pairs)


def along(x, hops):
    idle = [m for m in range(PLANES) if all(m not in hop for hop in hops)]
    pairs = [(a * SHARDS + k, b * SHARDS + k) for a, b in hops for k in range(SHARDS)]
    pairs += [(m * SHARDS + k, m * SHARDS + (k ^ 1)) for m in idle for k in range(SHARDS)]
    return lax.ppermute(x, "pop", pairs)


def beside(x):
    return lax.ppermute(x, "rep", [(0, 1), (1, 0)])


def after(x, *others):
    return lax.optimization_barrier((x, *others))[0]


def tiles(here, ints, width):
    near0, middle0, (here0, halves) = here
    near = [along(x, ENDS) for x in halves]
    far0 = along(near0, MIDDLE)
    middle = [along(x, MIDDLE) for x in halves]
    far = [along(x, MIDDLE) for x in near]
    pool = [(here0, halves), (near0, near), (middle0, middle), (far0, far)]
    picked = [pick_for_end(h, ints, pool) for h in range(2)]
    handed = [along(x, ENDS) for x in picked]
    quarter, targets = pick_own(ints, pool, handed, width)
    side = in_plane(quarter, 1)
    cross = in_plane(quarter, 2)
    gates = [halves, (near, middle), picked, handed, quarter]
    return gates, (quarter, side, cross, in_plane(cross, 1)), targets


def state_steps(ints, own, gates, steps, returns):
    half = own[0].shape[1] // 2
    guests = [beside(x[0, half:]) for x in own] if returns else []
    last, ends, middles, backs = (), [], [], []
    for t in range(1, steps + 1):
        guest = guests[t - 1] if t <= len(guests) else None
        theirs = 1 < t <= returns + 1
        gate = (gates[t - 1 : t], backs[t - 4 : t - 3] if t > 3 else [])
        facts = after(ints, gate) if jax.tree.leaves(gate) else ints
        to_ends, to_middle, *brought = stage(facts, t, own, guest, last, theirs)
        backs += [beside(x) for x in brought]
        last = (along(to_ends, ENDS), along(to_middle, MIDDLE))
        ends.append(last[0])
        middles.append(last[1])
    if len(backs) < returns:
        backs.append(beside(theirs_of(ints, *last)))
    return ends, middles, backs


def one_more(ints, own, step, last):
    def go(ints, own, last):
        to_ends, to_middle = stage(ints, step, own, None, last, False)
        return along(to_ends, ENDS), along(to_middle, MIDDLE)

    return lax.cond(ints[LONG] == 1, go, lambda ints, own, last: last, ints, own, last)


def run(by_both, ints, floats, parts, own):
    near0, middle0 = along(parts[0], ENDS), along(parts[0], MIDDLE)
    swapped = [in_plane(parts[j], j) for j in range(1, SHARDS)]
    halves = split_rows(after(swapped, near0, middle0))
    here = (near0, middle0, (parts[0], halves))
    gates, ins, targets = tiles(here, ints, own[0].shape[2])
    if by_both:
        ends, middles, backs = state_steps(ints, own, gates, 4, 4)
        first = 2
    else:
        ends, middles, backs = state_steps(ints, own, gates, 7, 0)
        first = 4
    grad, loss = gradient(
        ints, floats, ins, targets, own[0], (ends[:first], middles[:first], backs[:first])
    )
    round_one = [in_plane(loss, j) for j in range(1, SHARDS)]
    new = adam(0, ints, floats, grad, own, (ends, middles, []))
    loss = loss + round_one[0] + round_one[1] + round_one[2]
    ring = [along(loss, [(m, (m + d) % PLANES) for m in range(PLANES)]) for d in range(1, PLANES)]
    direct = ([], [])
    if not by_both:
        end, middle = one_more(ints, own, 8, (ends[-1], middles[-1]))
        direct = ([*ends, end], [*middles, middle])
    new = adam(1, ints, floats, grad, own, (*direct, backs), new)
    loss = loss + ring[0] + ring[1] + ring[2]
    return (*new, jnp.sum(loss[0, : PLANES * SHARDS].reshape(PLANES, SHARDS), axis=1))


def per_device(pool_tokens, pool_targets, weight, first_moment, second_moment, *args):
    winner, tile_ids = args[0], args[4]
    if winner.shape[0] != PLANES or tile_ids.shape[1] != SLOTS or lax.axis_size("rep") != 2:
        return relayed(pool_tokens, pool_targets, weight, first_moment, second_moment, *args)
    code = route_code(winner)
    parts = pack(code, pool_tokens, pool_targets)
    ints, floats = gather_facts(beside(code), *args)
    own = (weight, first_moment, second_moment)
    plans = [functools.partial(run, by_both) for by_both in (True, False)]
    return lax.switch(ints[SHARED], plans, ints, floats, parts, own)


def solution(mesh):
    in_specs = (
        P(("rep", "pop"), None, None),
        P(("rep", "pop"), None, None),
        P(("rep", "pop"), None, None),
        P(("rep", "pop"), None, None),
        P(("rep", "pop"), None, None),
        P("rep"),
        P("rep"),
        P("rep"),
        P("rep", None),
        P("rep", None),
        P("rep", None),
        P("rep", None),
    )
    out_specs = (
        P(("rep", "pop"), None, None),
        P(("rep", "pop"), None, None),
        P(("rep", "pop"), None, None),
        P("rep"),
    )
    return jax.shard_map(
        per_device, mesh=mesh, in_specs=in_specs, out_specs=out_specs, check_vma=False
    )
```

```python
import functools

import jax
import jax.numpy as jnp
from jax import lax
from jax.experimental import pallas as pl
from jax.experimental.pallas import tpu as pltpu
from jax.sharding import PartitionSpec as P

SHARDS = 4
TASKS = 8
SLOTS = 4
PLANES = 4


beta_one = 0.9
beta_two = 0.999
adam_eps = 1e-08
gelu_coef = 0.7978845608028654

SMEM = pl.BlockSpec(memory_space=pltpu.SMEM)
VMEM = pl.BlockSpec(memory_space=pltpu.VMEM)
ANY = pl.BlockSpec(memory_space=pl.ANY)


def gelu_pair(pre):
    inner = jnp.tanh(gelu_coef * (pre + 0.044715 * pre * pre * pre))
    value = 0.5 * pre * (1.0 + inner)
    slope = 0.5 * (1.0 + inner) + 0.5 * pre * (1.0 - inner * inner) * gelu_coef * (
        1.0 + 3.0 * 0.044715 * pre * pre
    )
    return (value, slope)


def for_sending(shard):

    def short(part):
        return part.astype(jnp.bfloat16) if part.dtype == jnp.float32 else part

    return jax.tree.map(short, shard)


def relayed(
    pool_tokens,
    pool_targets,
    weight,
    first_moment,
    second_moment,
    winner,
    learn_rate,
    explore,
    task_weight,
    tile_ids,
    slot_task,
    slot_tokens,
):
    nodes = lax.axis_size("pop")
    place = lax.axis_index("pop")
    member = place // SHARDS
    shard = place % SHARDS
    members = winner.shape[0]
    slots = tile_ids.shape[1]
    tile = pool_tokens.shape[1]
    depth = pool_tokens.shape[2]
    width = weight.shape[2]
    hidden_all = pool_targets.shape[2]
    reach = tile // nodes
    flat_state = (
        weight.reshape(nodes, -1),
        first_moment.reshape(nodes, -1),
        second_moment.reshape(nodes, -1),
    )
    spread = (
        lax.all_to_all(flat_state[0], "pop", split_axis=0, concat_axis=0, tiled=True),
        lax.all_to_all(flat_state[1], "pop", split_axis=0, concat_axis=0, tiled=True),
        lax.all_to_all(flat_state[2], "pop", split_axis=0, concat_axis=0, tiled=True),
    )
    source_rows = (winner[:, None] * SHARDS + jnp.arange(SHARDS, dtype=jnp.int32)[None, :]).reshape(
        -1
    )
    picked_state = tuple((jnp.take(piece, source_rows, axis=0) for piece in spread))
    returned = jax.tree.map(
        lambda part, own: part.astype(own.dtype),
        lax.all_to_all(for_sending(picked_state), "pop", split_axis=0, concat_axis=0, tiled=True),
        picked_state,
    )
    start_weight = returned[0].reshape(depth, width)
    start_first = returned[1].reshape(depth, width)
    start_second = returned[2].reshape(depth, width)
    relay_tokens, relay_targets = (
        lax.all_to_all(pool_tokens, "pop", split_axis=1, concat_axis=0, tiled=True),
        lax.all_to_all(pool_targets, "pop", split_axis=1, concat_axis=0, tiled=True),
    )
    flat_ids = tile_ids.reshape(-1)
    pick_tokens = jnp.take(relay_tokens, flat_ids, axis=0).reshape(members, 1, slots, reach, depth)
    send_tokens = jnp.broadcast_to(pick_tokens, (members, SHARDS, slots, reach, depth)).reshape(
        nodes, slots, reach, depth
    )
    pick_targets = jnp.take(relay_targets, flat_ids, axis=0).reshape(
        members, slots, reach, hidden_all
    )
    send_targets = jnp.broadcast_to(
        pick_targets[:, None], (members, SHARDS, slots, reach, hidden_all)
    ).reshape(nodes, slots, reach, hidden_all)
    got_tokens, got_targets = (
        lax.all_to_all(send_tokens, "pop", split_axis=0, concat_axis=2, tiled=True),
        lax.all_to_all(send_targets, "pop", split_axis=0, concat_axis=2, tiled=True),
    )
    targets = lax.dynamic_slice_in_dim(got_targets[0], shard * width, width, 2).reshape(
        slots * tile, width
    )
    inputs = got_tokens.reshape(slots * tile, depth)
    tasks_here = lax.dynamic_index_in_dim(slot_task, member, 0, keepdims=False)
    lengths = lax.dynamic_index_in_dim(slot_tokens, member, 0, keepdims=False)
    source_member = lax.dynamic_index_in_dim(winner, member, 0, keepdims=False)
    onehot = tasks_here[:, None] == jnp.arange(TASKS, dtype=jnp.int32)[None, :]
    counts = jnp.sum(jnp.where(onehot, lengths[:, None], 0), axis=0)
    weights_here = lax.dynamic_index_in_dim(task_weight, source_member, 0, keepdims=False)
    scale = weights_here / jnp.maximum(counts, 1).astype(jnp.float32)
    per_slot = jnp.sum(jnp.where(onehot, scale[None, :], jnp.float32(0.0)), axis=1)
    live = jnp.arange(tile, dtype=jnp.int32)[None, :] < lengths[:, None]
    coef = jnp.where(live, per_slot[:, None], jnp.float32(0.0)).reshape(-1)
    own_rate = lax.dynamic_index_in_dim(learn_rate, source_member, 0, keepdims=False)
    own_explore = lax.dynamic_index_in_dim(explore, member, 0, keepdims=False)
    step_rate = own_rate * jnp.where(source_member != member, own_explore, jnp.float32(1.0))
    pre = jnp.dot(inputs, start_weight, preferred_element_type=jnp.float32)
    hidden, slope = gelu_pair(pre)
    diff = hidden - targets.astype(jnp.float32)
    part = jnp.sum(coef[:, None] * diff * diff)
    delta = (2.0 * coef[:, None] * diff * slope).astype(jnp.bfloat16)
    grad = lax.dot_general(
        inputs, delta, (((0,), (0,)), ((), ())), preferred_element_type=jnp.float32
    )
    first = beta_one * start_first.astype(jnp.float32) + (1.0 - beta_one) * grad
    second = beta_two * start_second.astype(jnp.float32) + (1.0 - beta_two) * grad * grad
    updated = start_weight.astype(jnp.float32) - step_rate * first / (jnp.sqrt(second) + adam_eps)
    share = jnp.where(jnp.arange(members, dtype=jnp.int32) == member, part, jnp.float32(0.0))
    member_loss = lax.psum(share, "pop")
    return (
        updated.astype(jnp.bfloat16)[None],
        first.astype(jnp.bfloat16)[None],
        second.astype(jnp.bfloat16)[None],
        member_loss,
    )


ENDS = ((0, 1), (1, 0), (2, 3), (3, 2))
MIDDLE = ((1, 2), (2, 1))


def position():
    place = lax.axis_index("pop")
    return place // SHARDS, lax.rem(place, SHARDS)


SHARED, TAKEN, HOPS, BY_ENDS, THEIR_ENDS, TO_ENDS, TO_MIDDLE, LONG = range(8)
FOR_END, FOR_OWN, TOKENS, COUNTS = 16, 20, 24, 28
OWN, GUEST, PASSED = range(3)
RATE, TASK = 0, 4


def copied_from(winner):
    loser, source = jnp.int32(0), jnp.int32(0)
    for m in range(PLANES):
        taken = winner[m] != m
        loser = jnp.where(taken, m, loser)
        source = jnp.where(taken, winner[m], source)
    return loser, source


def route_kernel(winner, code):
    loser, source = copied_from(winner)
    code[...] = jnp.full(code.shape, source * PLANES + loser, jnp.int32)


def route_code(winner):
    return pl.pallas_call(
        route_kernel,
        out_shape=jax.ShapeDtypeStruct((8, 128), jnp.int32),
        in_specs=[SMEM],
        out_specs=VMEM,
        compiler_params=pltpu.CompilerParams(vmem_limit_bytes=8 * 1024 * 1024),
        name="route_code",
    )(winner)


def on_route(route, m, to):
    source, loser = route
    upward = (to == m + 1) & (source <= m) & (loser >= to)
    return upward | ((to == m - 1) & (source >= m) & (loser <= to))


def by_ends(route):
    source, loser = route
    return jnp.where(source < loser, loser - 1, loser + 1) == (loser ^ 1)


def in_pool(t, m, k):
    ahead = t // SHARDS - m
    ahead = jnp.where(m == 1, ahead, -ahead)
    group = jnp.where(ahead == 0, 0, jnp.where(ahead == -1, 1, ahead + 1))
    return group * SHARDS + (lax.rem(t, SHARDS) ^ k)


def facts_kernel(
    other, winner, learn_rate, explore, task_weight, tile_ids, slot_task, slot_tokens, ints, floats
):
    m, k = position()
    loser, source = copied_from(winner)
    code = other[0, 0]
    mine = source, loser
    theirs = lax.div(code, jnp.int32(PLANES)), lax.rem(code, jnp.int32(PLANES))
    upward = jnp.maximum(mine[0], theirs[0]) < jnp.minimum(mine[1], theirs[1])
    downward = jnp.maximum(mine[1], theirs[1]) < jnp.minimum(mine[0], theirs[0])
    hops = jnp.abs(mine[0] - mine[1])
    long = jnp.maximum(hops, jnp.abs(theirs[0] - theirs[1])) == PLANES - 1
    shared = upward | downward | long
    taken = winner[m] != m

    def content(to):
        own = on_route(mine, m, to)
        guest = on_route(theirs, m, to) & jnp.logical_not(shared)
        first = jnp.where(own, jnp.where(m == mine[0], OWN, PASSED), -1)
        return jnp.where(guest, jnp.where(m == theirs[0], GUEST, PASSED), first)

    ints[SHARED] = shared.astype(jnp.int32)
    ints[TAKEN] = taken.astype(jnp.int32)
    ints[HOPS] = hops
    ints[BY_ENDS] = by_ends(mine).astype(jnp.int32)
    ints[THEIR_ENDS] = by_ends(theirs).astype(jnp.int32)
    ints[TO_ENDS] = content(m ^ 1)
    ints[TO_MIDDLE] = content(jnp.where(m == 1, 2, jnp.where(m == 2, 1, -1)))
    ints[LONG] = long.astype(jnp.int32)
    end = jnp.where(m <= 1, 0, PLANES - 1)
    at_end = (m == 0) | (m == PLANES - 1)
    slots = tile_ids.shape[1]
    for s in range(slots):
        task = slot_task[m, s]
        count = jnp.int32(0)
        for o in range(slots):
            count = count + jnp.where(slot_task[m, o] == task, slot_tokens[m, o], 0)
        ints[FOR_END + s] = in_pool(tile_ids[end, s], m, k)
        ints[FOR_OWN + s] = jnp.where(at_end, -1, in_pool(tile_ids[m, s], m, k))
        ints[TOKENS + s] = slot_tokens[m, s]
        ints[COUNTS + s] = jnp.maximum(count, 1)
        floats[TASK + s] = task_weight[winner[m], task]
    floats[RATE] = learn_rate[winner[m]] * jnp.where(taken, explore[m], 1.0)


def gather_facts(other, *small):
    return pl.pallas_call(
        facts_kernel,
        out_shape=[jax.ShapeDtypeStruct((32,), jnp.int32), jax.ShapeDtypeStruct((8,), jnp.float32)],
        in_specs=[SMEM] * 8,
        out_specs=[SMEM, SMEM],
        compiler_params=pltpu.CompilerParams(vmem_limit_bytes=8 * 1024 * 1024),
        name="gather_facts",
    )(other, *small)


def stage_kernel(t, has_guest, has_theirs, has_last, ints, *refs):
    state, refs = refs[:3], refs[3:]
    guest = refs[0] if has_guest else None
    from_ends, from_middle = refs[has_guest : has_guest + 2] if has_last else (None, None)
    to_ends, to_middle = refs[has_guest + 2 * has_last :][:2]
    sems = refs[-1]
    half = to_ends.shape[0]
    shared = ints[SHARED] == 1
    array = jnp.where(shared, (t - 1) // 2, t - 1)
    start = pl.multiple_of(jnp.where(shared, (t - 1) % 2, 0) * half, half)
    sides = ((to_ends, ints[TO_ENDS], from_middle), (to_middle, ints[TO_MIDDLE], from_ends))
    for n, (out, content, _) in enumerate(sides):
        for a, ref in enumerate(state):

            @pl.when((content == OWN) & (array == a))
            def _():
                pltpu.make_async_copy(ref.at[0, pl.ds(start, half)], out, sems.at[n]).start()

    if has_theirs:
        theirs = refs[has_guest + 2 * has_last + 2]

        @pl.when(ints[THEIR_ENDS] == 1)
        def _():
            copy_rows(from_ends, 0, theirs, 0, half)

        @pl.when(ints[THEIR_ENDS] == 0)
        def _():
            copy_rows(from_middle, 0, theirs, 0, half)

    for n, (out, content, passed) in enumerate(sides):
        if guest is not None:

            @pl.when(content == GUEST)
            def _():
                copy_rows(guest, 0, out, 0, half)

        if passed is not None:

            @pl.when(content == PASSED)
            def _():
                copy_rows(passed, 0, out, 0, half)

        @pl.when((content == OWN) & (array < len(state)))
        def _():
            pltpu.make_async_copy(state[0].at[0, pl.ds(0, half)], out, sems.at[n]).wait()


def stage(ints, step, own, guest, last, theirs):
    half, width = own[0].shape[1] // 2, own[0].shape[2]
    guests = () if guest is None else (guest,)
    kernel = functools.partial(stage_kernel, step, len(guests), theirs, len(last) > 0)
    return pl.pallas_call(
        kernel,
        out_shape=[jax.ShapeDtypeStruct((half, width), own[0].dtype)] * (2 + theirs),
        in_specs=[SMEM] + [ANY] * 3 + [VMEM] * (len(guests) + len(last)),
        out_specs=[VMEM] * (2 + theirs),
        scratch_shapes=[pltpu.SemaphoreType.DMA((2,))],
        compiler_params=pltpu.CompilerParams(vmem_limit_bytes=8 * 1024 * 1024),
        name="stage_chunk",
    )(ints, *own, *guests, *last)


def theirs_kernel(ints, from_ends, from_middle, theirs):
    @pl.when(ints[THEIR_ENDS] == 1)
    def _():
        copy_rows(from_ends, 0, theirs, 0, theirs.shape[0])

    @pl.when(ints[THEIR_ENDS] == 0)
    def _():
        copy_rows(from_middle, 0, theirs, 0, theirs.shape[0])


def theirs_of(ints, from_ends, from_middle):
    return pl.pallas_call(
        theirs_kernel,
        out_shape=jax.ShapeDtypeStruct(from_ends.shape, from_ends.dtype),
        in_specs=[SMEM] + [VMEM] * 2,
        out_specs=VMEM,
        compiler_params=pltpu.CompilerParams(vmem_limit_bytes=8 * 1024 * 1024),
        name="guest_chunk",
    )(ints, from_ends, from_middle)


def start_copies(ints, a, h, own, sent, out, sem):
    ends, middles, backs = sent
    shared, taken = ints[SHARED] == 1, ints[TAKEN] == 1
    half = out.shape[0]
    step = jnp.where(shared, 2 * a + h, a) + ints[HOPS]
    direct = taken & shared if h == 1 else taken

    def copy(ref):
        return pltpu.make_async_copy(ref, out, sem)

    @pl.when(jnp.logical_not(taken))
    def _():
        copy(own.at[0, pl.ds(h * half, half)]).start()

    sides = [
        (ends, direct & (ints[BY_ENDS] == 1)),
        (middles, direct & (ints[BY_ENDS] == 0)),
    ]
    if h == 1:
        sides.append((backs, taken & jnp.logical_not(shared)))
    for refs, here in sides:
        for n, ref in enumerate(refs):

            @pl.when(here & (step == n + 1))
            def _():
                copy(ref).start()

    return copy(own.at[0, pl.ds(h * half, half)])


def counts_of(sent):
    return tuple(len(refs) for refs in sent)


def sent_refs(counts, refs):
    a, b, c = counts
    return (refs[:a], refs[a : a + b], refs[a + b : a + b + c]), refs[a + b + c :]


def pack_kernel(code, tokens, targets, *parts):
    _, k = position()
    width = targets.shape[2] // SHARDS
    slim = tokens.shape[2] // SHARDS
    for j, part in enumerate(parts):
        q = k ^ j
        part[:, :width] = targets[0, :, pl.ds(pl.multiple_of(q * width, 128), width)]
        part[:, width:] = tokens[0, :, pl.ds(pl.multiple_of(q * slim, 128), slim)]


def pack(code, tokens, targets):
    tile = tokens.shape[1]
    row = (tokens.shape[2] + targets.shape[2]) // SHARDS
    return pl.pallas_call(
        pack_kernel,
        out_shape=[jax.ShapeDtypeStruct((tile, row), tokens.dtype)] * SHARDS,
        in_specs=[VMEM] * 3,
        out_specs=[VMEM] * SHARDS,
        compiler_params=pltpu.CompilerParams(vmem_limit_bytes=8 * 1024 * 1024),
        name="pack_quarters",
    )(code, tokens, targets)


def copy_rows(ref, start, out, at, count, columns=slice(None)):
    step = 32

    def body(i, _):
        rows = pl.ds(pl.multiple_of(at + i * step, step), step)
        out[rows, :] = ref[pl.ds(pl.multiple_of(start + i * step, step), step), columns]
        return 0

    lax.fori_loop(0, count // step, body, 0, unroll=True if count <= 64 else 4)


def split_kernel(one, two, three, *halves):
    count = one.shape[0] // 2
    for h, half in enumerate(halves):
        for n, part in enumerate((one, two, three)):
            copy_rows(part, h * count, half, n * count, count)


def split_rows(parts):
    tile, row = parts[0].shape
    half = jax.ShapeDtypeStruct((len(parts) * tile // 2, row), parts[0].dtype)
    return pl.pallas_call(
        split_kernel,
        out_shape=[half, half],
        in_specs=[VMEM] * len(parts),
        out_specs=[VMEM, VMEM],
        compiler_params=pltpu.CompilerParams(vmem_limit_bytes=8 * 1024 * 1024),
        name="split_rows",
    )(*parts)


def piece(pool, which, h):
    group, j = divmod(which, SHARDS)
    whole, halves = pool[group]
    rows = whole.shape[0] // 2
    return (whole, h * rows, rows) if j == 0 else (halves[h], (j - 1) * rows, rows)


def grouped(refs, halves):
    size = 1 + len(halves)
    pool = []
    for g in range(PLANES):
        group = refs[g * size : (g + 1) * size]
        pool.append((group[0], dict(zip(halves, group[1:]))))
    return pool, refs[PLANES * size :]


def pick_for_end_kernel(h, ints, *refs):
    pool, (out,) = grouped(refs, (h,))

    def slot(s, _):
        place = ints[FOR_END + s]
        for which in range(PLANES * SHARDS):
            ref, start, rows = piece(pool, which, h)

            @pl.when(place == which)
            def _():
                copy_rows(ref, start, out, s * rows, rows)

        return 0

    lax.fori_loop(0, SLOTS, slot, 0)


def pick_for_end(h, ints, pool):
    tile, row = pool[0][0].shape
    operands = [x for whole, halves in pool for x in (whole, halves[h])]
    return pl.pallas_call(
        functools.partial(pick_for_end_kernel, h),
        out_shape=jax.ShapeDtypeStruct((SLOTS * tile // 2, row), operands[0].dtype),
        in_specs=[SMEM] + [VMEM] * len(operands),
        out_specs=VMEM,
        compiler_params=pltpu.CompilerParams(vmem_limit_bytes=16 * 1024 * 1024),
        name="pick_for_end",
    )(ints, *operands)


def pick_own_kernel(ints, *refs):
    pool, (handed_a, handed_b, quarter, targets) = grouped(refs, (0, 1))
    handed = (handed_a, handed_b)
    width = targets.shape[1]
    half = quarter.shape[0] // SLOTS // 2

    def slot(s, _):
        place = ints[FOR_OWN + s]
        for h in range(2):
            at = (2 * s + h) * half

            @pl.when(place < 0)
            def _():
                start = pl.multiple_of(s * half, half)
                copy_rows(handed[h], start, targets, at, half, slice(0, width))
                copy_rows(handed[h], start, quarter, at, half, slice(width, None))

            for which in range(PLANES * SHARDS):
                ref, start, rows = piece(pool, which, h)

                @pl.when(place == which)
                def _():
                    copy_rows(ref, start, targets, at, rows, slice(0, width))
                    copy_rows(ref, start, quarter, at, rows, slice(width, None))

        return 0

    lax.fori_loop(0, SLOTS, slot, 0)


def pick_own(ints, pool, handed, width):
    rows, row = handed[0].shape
    operands = [x for whole, halves in pool for x in (whole, *halves)]
    return pl.pallas_call(
        pick_own_kernel,
        out_shape=[
            jax.ShapeDtypeStruct((2 * rows, row - width), handed[0].dtype),
            jax.ShapeDtypeStruct((2 * rows, width), handed[0].dtype),
        ],
        in_specs=[SMEM] + [VMEM] * (len(operands) + 2),
        out_specs=[VMEM, VMEM],
        compiler_params=pltpu.CompilerParams(vmem_limit_bytes=16 * 1024 * 1024),
        name="pick_own",
    )(ints, *operands, *handed)


def grad_kernel(counts, ints, floats, in0, in1, in2, in3, targets, own_w, *refs):
    sent, (grad, loss, w_buf, delta, sem) = sent_refs(counts, refs)
    m, k = position()
    half = w_buf.shape[0] // 2
    copies = [
        start_copies(ints, 0, h, own_w, sent, w_buf.at[pl.ds(h * half, half)], sem.at[h])
        for h in range(2)
    ]
    tile = in0.shape[0] // SLOTS
    slim = in0.shape[1]
    ins = (in0, in1, in2, in3)
    for copy in copies:
        copy.wait()

    def slot(s, total):
        span = pl.ds(pl.multiple_of(s * tile, tile), tile)
        pre = None
        for j in range(SHARDS):
            at = pl.ds(pl.multiple_of((k ^ j) * slim, slim), slim)
            one = jnp.dot(ins[j][span, :], w_buf[at, :], preferred_element_type=jnp.float32)
            pre = one if pre is None else pre + one
        live = lax.broadcasted_iota(jnp.int32, pre.shape, 0) < ints[TOKENS + s]
        many = jnp.full(pre.shape, ints[COUNTS + s], jnp.int32).astype(jnp.float32)
        coef = jnp.where(live, floats[TASK + s] / many, 0.0)
        hidden, slope = gelu_pair(pre)
        diff = hidden - targets[span, :].astype(jnp.float32)
        scaled = coef * diff
        delta[span, :] = (2.0 * scaled * slope).astype(jnp.bfloat16)
        return total + jnp.sum(scaled * diff, keepdims=True)

    total = lax.fori_loop(0, SLOTS, slot, jnp.zeros((1, 1), jnp.float32))
    lane = lax.broadcasted_iota(jnp.int32, loss.shape, 1)
    loss[...] = jnp.where(lane == m * SHARDS + k, total, 0.0)
    for j in range(SHARDS):
        at = pl.ds(pl.multiple_of((k ^ j) * slim, slim), slim)
        grad[at, :] = lax.dot_general(
            ins[j][...], delta[...], (((0,), (0,)), ((), ())), preferred_element_type=jnp.float32
        )


def gradient(ints, floats, ins, targets, own_w, sent):
    rows, width = targets.shape
    depth = own_w.shape[1]
    return pl.pallas_call(
        functools.partial(grad_kernel, counts_of(sent)),
        out_shape=[
            jax.ShapeDtypeStruct((depth, width), jnp.float32),
            jax.ShapeDtypeStruct((8, 128), jnp.float32),
        ],
        in_specs=[SMEM] * 2 + [VMEM] * 5 + [ANY] * (1 + sum(counts_of(sent))),
        out_specs=[VMEM, VMEM],
        scratch_shapes=[
            pltpu.VMEM((depth, width), own_w.dtype),
            pltpu.VMEM((rows, width), jnp.bfloat16),
            pltpu.SemaphoreType.DMA((2,)),
        ],
        compiler_params=pltpu.CompilerParams(vmem_limit_bytes=16 * 1024 * 1024),
        name="forward_and_gradient",
    )(ints, floats, *ins, targets, own_w, *sent[0], *sent[1], *sent[2])


def adam_kernel(h, counts, ints, floats, grad, *refs):
    own, (sent, refs) = refs[:3], sent_refs(counts, refs[3:])
    new, bufs, outs, (in_sem, out_sem) = refs[-11:-8], refs[-8:-5], refs[-5:-2], refs[-2:]
    blocks = out_sem.shape[1]
    rows = bufs[0].shape[0]
    step = rows // blocks
    here = h * rows

    def result(i, b):
        return pltpu.make_async_copy(
            outs[i].at[pl.ds(b * step, step)],
            new[i].at[0, pl.ds(here + b * step, step)],
            out_sem.at[i, b],
        )

    copies = [
        start_copies(ints, a, h, own[a], sent, bufs[a], in_sem.at[a]) for a in range(3)
    ]
    rate = floats[RATE]
    for copy in copies:
        copy.wait()
    for b in range(blocks):

        def body(n, _):
            at = pl.ds(pl.multiple_of(b * step + n * 16, 16), 16)
            g = grad[pl.ds(pl.multiple_of(here + b * step + n * 16, 16), 16), :]
            first = beta_one * bufs[1][at, :].astype(jnp.float32) + (1.0 - beta_one) * g
            second = beta_two * bufs[2][at, :].astype(jnp.float32) + (1.0 - beta_two) * g * g
            start = bufs[0][at, :].astype(jnp.float32)
            updated = start - rate * first / (jnp.sqrt(second) + adam_eps)
            outs[0][at, :] = updated.astype(outs[0].dtype)
            outs[1][at, :] = first.astype(outs[1].dtype)
            outs[2][at, :] = second.astype(outs[2].dtype)
            return 0

        lax.fori_loop(0, step // 16, body, 0, unroll=2)
        for i in range(3):
            result(i, b).start()
    for b in range(blocks):
        for i in range(3):
            result(i, b).wait()


def adam(h, ints, floats, grad, own, sent, begun=()):
    depth, width = grad.shape
    blocks = 2
    taken = sum(counts_of(sent))
    return pl.pallas_call(
        functools.partial(adam_kernel, h, counts_of(sent)),
        out_shape=[jax.ShapeDtypeStruct(x.shape, x.dtype) for x in own],
        in_specs=[SMEM] * 2 + [VMEM] + [ANY] * (3 + taken + len(begun)),
        out_specs=[ANY] * 3,
        scratch_shapes=[pltpu.VMEM((depth // 2, width), x.dtype) for x in own] * 2
        + [pltpu.SemaphoreType.DMA((3,)), pltpu.SemaphoreType.DMA((3, blocks))],
        input_output_aliases={6 + taken + i: i for i in range(len(begun))},
        compiler_params=pltpu.CompilerParams(vmem_limit_bytes=16 * 1024 * 1024),
        name="adam_half",
    )(ints, floats, grad, *own, *sent[0], *sent[1], *sent[2], *begun)


def in_plane(x, j):
    pairs = [(m * SHARDS + k, m * SHARDS + (k ^ j)) for m in range(PLANES) for k in range(SHARDS)]
    return lax.ppermute(x, "pop", pairs)


def along(x, hops):
    idle = [m for m in range(PLANES) if all(m not in hop for hop in hops)]
    pairs = [(a * SHARDS + k, b * SHARDS + k) for a, b in hops for k in range(SHARDS)]
    pairs += [(m * SHARDS + k, m * SHARDS + (k ^ 1)) for m in idle for k in range(SHARDS)]
    return lax.ppermute(x, "pop", pairs)


def beside(x):
    return lax.ppermute(x, "rep", [(0, 1), (1, 0)])


def after(x, *others):
    return lax.optimization_barrier((x, *others))[0]


def tiles(here, ints, width):
    near0, middle0, (here0, halves) = here
    near = [along(x, ENDS) for x in halves]
    far0 = along(near0, MIDDLE)
    middle = [along(x, MIDDLE) for x in halves]
    far = [along(x, MIDDLE) for x in near]
    pool = [(here0, halves), (near0, near), (middle0, middle), (far0, far)]
    picked = [pick_for_end(h, ints, pool) for h in range(2)]
    handed = [along(x, ENDS) for x in picked]
    quarter, targets = pick_own(ints, pool, handed, width)
    side = in_plane(quarter, 1)
    cross = in_plane(quarter, 2)
    gates = [halves, (near, middle), picked, handed, quarter]
    return gates, (quarter, side, cross, in_plane(cross, 1)), targets


def state_steps(ints, own, gates, steps, returns):
    half = own[0].shape[1] // 2
    guests = [beside(x[0, half:]) for x in own] if returns else []
    last, ends, middles, backs = (), [], [], []
    for t in range(1, steps + 1):
        guest = guests[t - 1] if t <= len(guests) else None
        theirs = 1 < t <= returns + 1
        gate = (gates[t - 1 : t], backs[t - 4 : t - 3] if t > 3 else [])
        facts = after(ints, gate) if jax.tree.leaves(gate) else ints
        to_ends, to_middle, *brought = stage(facts, t, own, guest, last, theirs)
        backs += [beside(x) for x in brought]
        last = (along(to_ends, ENDS), along(to_middle, MIDDLE))
        ends.append(last[0])
        middles.append(last[1])
    if len(backs) < returns:
        backs.append(beside(theirs_of(ints, *last)))
    return ends, middles, backs


def one_more(ints, own, step, last):
    def go(ints, own, last):
        to_ends, to_middle = stage(ints, step, own, None, last, False)
        return along(to_ends, ENDS), along(to_middle, MIDDLE)

    return lax.cond(ints[LONG] == 1, go, lambda ints, own, last: last, ints, own, last)


def run(by_both, ints, floats, parts, own):
    near0, middle0 = along(parts[0], ENDS), along(parts[0], MIDDLE)
    swapped = [in_plane(parts[j], j) for j in range(1, SHARDS)]
    halves = split_rows(after(swapped, near0, middle0))
    here = (near0, middle0, (parts[0], halves))
    gates, ins, targets = tiles(here, ints, own[0].shape[2])
    if by_both:
        ends, middles, backs = state_steps(ints, own, gates, 4, 4)
        first = 2
    else:
        ends, middles, backs = state_steps(ints, own, gates, 7, 0)
        first = 4
    grad, loss = gradient(
        ints, floats, ins, targets, own[0], (ends[:first], middles[:first], backs[:first])
    )
    round_one = [in_plane(loss, j) for j in range(1, SHARDS)]
    new = adam(0, ints, floats, grad, own, (ends, middles, []))
    loss = loss + round_one[0] + round_one[1] + round_one[2]
    ring = [along(loss, [(m, (m + d) % PLANES) for m in range(PLANES)]) for d in range(1, PLANES)]
    direct = ([], [])
    if not by_both:
        end, middle = one_more(ints, own, 8, (ends[-1], middles[-1]))
        direct = ([*ends, end], [*middles, middle])
    new = adam(1, ints, floats, grad, own, (*direct, backs), new)
    loss = loss + ring[0] + ring[1] + ring[2]
    return (*new, jnp.sum(loss[0, : PLANES * SHARDS].reshape(PLANES, SHARDS), axis=1))


def per_device(pool_tokens, pool_targets, weight, first_moment, second_moment, *args):
    winner, tile_ids = args[0], args[4]
    if winner.shape[0] != PLANES or tile_ids.shape[1] != SLOTS or lax.axis_size("rep") != 2:
        return relayed(pool_tokens, pool_targets, weight, first_moment, second_moment, *args)
    code = route_code(winner)
    parts = pack(code, pool_tokens, pool_targets)
    ints, floats = gather_facts(beside(code), *args)
    own = (weight, first_moment, second_moment)
    plans = [functools.partial(run, by_both) for by_both in (True, False)]
    return lax.switch(ints[SHARED], plans, ints, floats, parts, own)


def solution(mesh):
    in_specs = (
        P(("rep", "pop"), None, None),
        P(("rep", "pop"), None, None),
        P(("rep", "pop"), None, None),
        P(("rep", "pop"), None, None),
        P(("rep", "pop"), None, None),
        P("rep"),
        P("rep"),
        P("rep"),
        P("rep", None),
        P("rep", None),
        P("rep", None),
        P("rep", None),
    )
    out_specs = (
        P(("rep", "pop"), None, None),
        P(("rep", "pop"), None, None),
        P(("rep", "pop"), None, None),
        P("rep"),
    )
    return jax.shard_map(
        per_device, mesh=mesh, in_specs=in_specs, out_specs=out_specs, check_vma=False
    )
```

```python
import functools

import jax
import jax.numpy as jnp
from jax import lax
from jax.experimental import pallas as pl
from jax.experimental.pallas import tpu as pltpu
from jax.sharding import PartitionSpec as P

SHARDS = 4
TASKS = 8
SLOTS = 4
PLANES = 4


beta_one = 0.9
beta_two = 0.999
adam_eps = 1e-08
gelu_coef = 0.7978845608028654

SMEM = pl.BlockSpec(memory_space=pltpu.SMEM)
VMEM = pl.BlockSpec(memory_space=pltpu.VMEM)
ANY = pl.BlockSpec(memory_space=pl.ANY)
HBM = pl.BlockSpec(memory_space=pltpu.HBM)


def gelu_pair(pre):
    inner = jnp.tanh(gelu_coef * (pre + 0.044715 * pre * pre * pre))
    value = 0.5 * pre * (1.0 + inner)
    slope = 0.5 * (1.0 + inner) + 0.5 * pre * (1.0 - inner * inner) * gelu_coef * (
        1.0 + 3.0 * 0.044715 * pre * pre
    )
    return (value, slope)


def for_sending(shard):

    def short(part):
        return part.astype(jnp.bfloat16) if part.dtype == jnp.float32 else part

    return jax.tree.map(short, shard)


def relayed(
    pool_tokens,
    pool_targets,
    weight,
    first_moment,
    second_moment,
    winner,
    learn_rate,
    explore,
    task_weight,
    tile_ids,
    slot_task,
    slot_tokens,
):
    nodes = lax.axis_size("pop")
    place = lax.axis_index("pop")
    member = place // SHARDS
    shard = place % SHARDS
    members = winner.shape[0]
    slots = tile_ids.shape[1]
    tile = pool_tokens.shape[1]
    depth = pool_tokens.shape[2]
    width = weight.shape[2]
    hidden_all = pool_targets.shape[2]
    reach = tile // nodes
    flat_state = (
        weight.reshape(nodes, -1),
        first_moment.reshape(nodes, -1),
        second_moment.reshape(nodes, -1),
    )
    spread = (
        lax.all_to_all(flat_state[0], "pop", split_axis=0, concat_axis=0, tiled=True),
        lax.all_to_all(flat_state[1], "pop", split_axis=0, concat_axis=0, tiled=True),
        lax.all_to_all(flat_state[2], "pop", split_axis=0, concat_axis=0, tiled=True),
    )
    source_rows = (winner[:, None] * SHARDS + jnp.arange(SHARDS, dtype=jnp.int32)[None, :]).reshape(
        -1
    )
    picked_state = tuple((jnp.take(piece, source_rows, axis=0) for piece in spread))
    returned = jax.tree.map(
        lambda part, own: part.astype(own.dtype),
        lax.all_to_all(for_sending(picked_state), "pop", split_axis=0, concat_axis=0, tiled=True),
        picked_state,
    )
    start_weight = returned[0].reshape(depth, width)
    start_first = returned[1].reshape(depth, width)
    start_second = returned[2].reshape(depth, width)
    relay_tokens, relay_targets = (
        lax.all_to_all(pool_tokens, "pop", split_axis=1, concat_axis=0, tiled=True),
        lax.all_to_all(pool_targets, "pop", split_axis=1, concat_axis=0, tiled=True),
    )
    flat_ids = tile_ids.reshape(-1)
    pick_tokens = jnp.take(relay_tokens, flat_ids, axis=0).reshape(members, 1, slots, reach, depth)
    send_tokens = jnp.broadcast_to(pick_tokens, (members, SHARDS, slots, reach, depth)).reshape(
        nodes, slots, reach, depth
    )
    pick_targets = jnp.take(relay_targets, flat_ids, axis=0).reshape(
        members, slots, reach, hidden_all
    )
    send_targets = jnp.broadcast_to(
        pick_targets[:, None], (members, SHARDS, slots, reach, hidden_all)
    ).reshape(nodes, slots, reach, hidden_all)
    got_tokens, got_targets = (
        lax.all_to_all(send_tokens, "pop", split_axis=0, concat_axis=2, tiled=True),
        lax.all_to_all(send_targets, "pop", split_axis=0, concat_axis=2, tiled=True),
    )
    targets = lax.dynamic_slice_in_dim(got_targets[0], shard * width, width, 2).reshape(
        slots * tile, width
    )
    inputs = got_tokens.reshape(slots * tile, depth)
    tasks_here = lax.dynamic_index_in_dim(slot_task, member, 0, keepdims=False)
    lengths = lax.dynamic_index_in_dim(slot_tokens, member, 0, keepdims=False)
    source_member = lax.dynamic_index_in_dim(winner, member, 0, keepdims=False)
    onehot = tasks_here[:, None] == jnp.arange(TASKS, dtype=jnp.int32)[None, :]
    counts = jnp.sum(jnp.where(onehot, lengths[:, None], 0), axis=0)
    weights_here = lax.dynamic_index_in_dim(task_weight, source_member, 0, keepdims=False)
    scale = weights_here / jnp.maximum(counts, 1).astype(jnp.float32)
    per_slot = jnp.sum(jnp.where(onehot, scale[None, :], jnp.float32(0.0)), axis=1)
    live = jnp.arange(tile, dtype=jnp.int32)[None, :] < lengths[:, None]
    coef = jnp.where(live, per_slot[:, None], jnp.float32(0.0)).reshape(-1)
    own_rate = lax.dynamic_index_in_dim(learn_rate, source_member, 0, keepdims=False)
    own_explore = lax.dynamic_index_in_dim(explore, member, 0, keepdims=False)
    step_rate = own_rate * jnp.where(source_member != member, own_explore, jnp.float32(1.0))
    pre = jnp.dot(inputs, start_weight, preferred_element_type=jnp.float32)
    hidden, slope = gelu_pair(pre)
    diff = hidden - targets.astype(jnp.float32)
    part = jnp.sum(coef[:, None] * diff * diff)
    delta = (2.0 * coef[:, None] * diff * slope).astype(jnp.bfloat16)
    grad = lax.dot_general(
        inputs, delta, (((0,), (0,)), ((), ())), preferred_element_type=jnp.float32
    )
    first = beta_one * start_first.astype(jnp.float32) + (1.0 - beta_one) * grad
    second = beta_two * start_second.astype(jnp.float32) + (1.0 - beta_two) * grad * grad
    updated = start_weight.astype(jnp.float32) - step_rate * first / (jnp.sqrt(second) + adam_eps)
    share = jnp.where(jnp.arange(members, dtype=jnp.int32) == member, part, jnp.float32(0.0))
    member_loss = lax.psum(share, "pop")
    return (
        updated.astype(jnp.bfloat16)[None],
        first.astype(jnp.bfloat16)[None],
        second.astype(jnp.bfloat16)[None],
        member_loss,
    )


ENDS = ((0, 1), (1, 0), (2, 3), (3, 2))
MIDDLE = ((1, 2), (2, 1))


def position():
    place = lax.axis_index("pop")
    return place // SHARDS, lax.rem(place, SHARDS)


SHARED, TAKEN, HOPS, BY_ENDS, THEIR_ENDS, TO_ENDS, TO_MIDDLE = range(7)
FOR_END, FOR_OWN, TOKENS, COUNTS = 16, 20, 24, 28
OWN, GUEST, PASSED = range(3)
RATE, TASK = 0, 4


def copied_from(winner):
    loser, source = jnp.int32(0), jnp.int32(0)
    for m in range(PLANES):
        taken = winner[m] != m
        loser = jnp.where(taken, m, loser)
        source = jnp.where(taken, winner[m], source)
    return loser, source


def route_kernel(winner, code):
    loser, source = copied_from(winner)
    code[...] = jnp.full(code.shape, source * PLANES + loser, jnp.int32)


def route_code(winner):
    return pl.pallas_call(
        route_kernel,
        out_shape=jax.ShapeDtypeStruct((8, 128), jnp.int32),
        in_specs=[SMEM],
        out_specs=VMEM,
        name="route_code",
    )(winner)


def on_route(route, m, to):
    source, loser = route
    upward = (to == m + 1) & (source <= m) & (loser >= to)
    return upward | ((to == m - 1) & (source >= m) & (loser <= to))


def by_ends(route):
    source, loser = route
    return jnp.where(source < loser, loser - 1, loser + 1) == (loser ^ 1)


def in_pool(t, m, k):
    ahead = t // SHARDS - m
    ahead = jnp.where(m == 1, ahead, -ahead)
    group = jnp.where(ahead == 0, 0, jnp.where(ahead == -1, 1, ahead + 1))
    return group * SHARDS + (lax.rem(t, SHARDS) ^ k)


def facts_kernel(
    other, winner, learn_rate, explore, task_weight, tile_ids, slot_task, slot_tokens, ints, floats
):
    m, k = position()
    loser, source = copied_from(winner)
    code = other[0, 0]
    mine = source, loser
    theirs = lax.div(code, jnp.int32(PLANES)), lax.rem(code, jnp.int32(PLANES))
    upward = jnp.maximum(mine[0], theirs[0]) < jnp.minimum(mine[1], theirs[1])
    downward = jnp.maximum(mine[1], theirs[1]) < jnp.minimum(mine[0], theirs[0])
    hops = jnp.abs(mine[0] - mine[1])
    long = jnp.maximum(hops, jnp.abs(theirs[0] - theirs[1])) == PLANES - 1
    shared = upward | downward | long
    taken = winner[m] != m

    def content(to):
        own = on_route(mine, m, to)
        guest = on_route(theirs, m, to) & jnp.logical_not(shared)
        first = jnp.where(own, jnp.where(m == mine[0], OWN, PASSED), -1)
        return jnp.where(guest, jnp.where(m == theirs[0], GUEST, PASSED), first)

    ints[SHARED] = shared.astype(jnp.int32)
    ints[TAKEN] = taken.astype(jnp.int32)
    ints[HOPS] = hops
    ints[BY_ENDS] = by_ends(mine).astype(jnp.int32)
    ints[THEIR_ENDS] = by_ends(theirs).astype(jnp.int32)
    ints[TO_ENDS] = content(m ^ 1)
    ints[TO_MIDDLE] = content(jnp.where(m == 1, 2, jnp.where(m == 2, 1, -1)))
    end = jnp.where(m <= 1, 0, PLANES - 1)
    at_end = (m == 0) | (m == PLANES - 1)
    slots = tile_ids.shape[1]
    for s in range(slots):
        task = slot_task[m, s]
        count = jnp.int32(0)
        for o in range(slots):
            count = count + jnp.where(slot_task[m, o] == task, slot_tokens[m, o], 0)
        ints[FOR_END + s] = in_pool(tile_ids[end, s], m, k)
        ints[FOR_OWN + s] = jnp.where(at_end, -1, in_pool(tile_ids[m, s], m, k))
        ints[TOKENS + s] = slot_tokens[m, s]
        ints[COUNTS + s] = jnp.maximum(count, 1)
        floats[TASK + s] = task_weight[winner[m], task]
    floats[RATE] = learn_rate[winner[m]] * jnp.where(taken, explore[m], 1.0)


def gather_facts(other, *small):
    return pl.pallas_call(
        facts_kernel,
        out_shape=[jax.ShapeDtypeStruct((32,), jnp.int32), jax.ShapeDtypeStruct((8,), jnp.float32)],
        in_specs=[SMEM] * 8,
        out_specs=[SMEM, SMEM],
        name="gather_facts",
    )(other, *small)


def stage_kernel(t, has_guest, has_theirs, has_last, ints, *refs):
    state, refs = refs[:3], refs[3:]
    guest = refs[0] if has_guest else None
    from_ends, from_middle = refs[has_guest : has_guest + 2] if has_last else (None, None)
    to_ends, to_middle = refs[has_guest + 2 * has_last :][:2]
    sems = refs[-1]
    half = to_ends.shape[0]
    shared = ints[SHARED] == 1
    array = jnp.where(shared, (t - 1) // 2, t - 1)
    start = pl.multiple_of(jnp.where(shared, (t - 1) % 2, 0) * half, half)
    sides = ((to_ends, ints[TO_ENDS], from_middle), (to_middle, ints[TO_MIDDLE], from_ends))
    for n, (out, content, _) in enumerate(sides):
        for a, ref in enumerate(state):

            @pl.when((content == OWN) & (array == a))
            def _():
                pltpu.make_async_copy(ref.at[0, pl.ds(start, half)], out, sems.at[n]).start()

    if has_theirs:
        theirs = refs[has_guest + 2 * has_last + 2]

        @pl.when(ints[THEIR_ENDS] == 1)
        def _():
            copy_rows(from_ends, 0, theirs, 0, half)

        @pl.when(ints[THEIR_ENDS] == 0)
        def _():
            copy_rows(from_middle, 0, theirs, 0, half)

    for n, (out, content, passed) in enumerate(sides):
        if guest is not None:

            @pl.when(content == GUEST)
            def _():
                copy_rows(guest, 0, out, 0, half)

        if passed is not None:

            @pl.when(content == PASSED)
            def _():
                copy_rows(passed, 0, out, 0, half)

        @pl.when((content == OWN) & (array < len(state)))
        def _():
            pltpu.make_async_copy(state[0].at[0, pl.ds(0, half)], out, sems.at[n]).wait()


def stage(ints, step, own, guest, last, theirs):
    half, width = own[0].shape[1] // 2, own[0].shape[2]
    guests = () if guest is None else (guest,)
    kernel = functools.partial(stage_kernel, step, len(guests), theirs, len(last) > 0)
    return pl.pallas_call(
        kernel,
        out_shape=[jax.ShapeDtypeStruct((half, width), own[0].dtype)] * (2 + theirs),
        in_specs=[SMEM] + [ANY] * 3 + [VMEM] * (len(guests) + len(last)),
        out_specs=[VMEM] * (2 + theirs),
        scratch_shapes=[pltpu.SemaphoreType.DMA((2,))],
        compiler_params=pltpu.CompilerParams(vmem_limit_bytes=8 * 1024 * 1024),
        name="stage_chunk",
    )(ints, *own, *guests, *last)


def theirs_kernel(ints, from_ends, from_middle, theirs):
    @pl.when(ints[THEIR_ENDS] == 1)
    def _():
        copy_rows(from_ends, 0, theirs, 0, theirs.shape[0])

    @pl.when(ints[THEIR_ENDS] == 0)
    def _():
        copy_rows(from_middle, 0, theirs, 0, theirs.shape[0])


def theirs_of(ints, from_ends, from_middle):
    return pl.pallas_call(
        theirs_kernel,
        out_shape=jax.ShapeDtypeStruct(from_ends.shape, from_ends.dtype),
        in_specs=[SMEM] + [VMEM] * 2,
        out_specs=VMEM,
        compiler_params=pltpu.CompilerParams(vmem_limit_bytes=8 * 1024 * 1024),
        name="guest_chunk",
    )(ints, from_ends, from_middle)


def start_copies(ints, a, h, own, sent, out, sem):
    ends, middles, backs = sent
    shared, taken = ints[SHARED] == 1, ints[TAKEN] == 1
    half = out.shape[0]
    step = jnp.where(shared, 2 * a + h, a) + ints[HOPS]
    direct = taken & shared if h == 1 else taken

    def copy(ref):
        return pltpu.make_async_copy(ref, out, sem)

    @pl.when(jnp.logical_not(taken))
    def _():
        copy(own.at[0, pl.ds(h * half, half)]).start()

    sides = [
        (ends, direct & (ints[BY_ENDS] == 1)),
        (middles, direct & (ints[BY_ENDS] == 0)),
    ]
    if h == 1:
        sides.append((backs, taken & jnp.logical_not(shared)))
    for refs, here in sides:
        for n, ref in enumerate(refs):

            @pl.when(here & (step == n + 1))
            def _():
                copy(ref).start()

    return copy(own.at[0, pl.ds(h * half, half)])


def counts_of(sent):
    return tuple(len(refs) for refs in sent)


def sent_refs(counts, refs):
    a, b, c = counts
    return (refs[:a], refs[a : a + b], refs[a + b : a + b + c]), refs[a + b + c :]


def pack_kernel(code, tokens, targets, *parts):
    _, k = position()
    width = targets.shape[2] // SHARDS
    slim = tokens.shape[2] // SHARDS
    for j, part in enumerate(parts):
        q = k ^ j
        part[:, :width] = targets[0, :, pl.ds(pl.multiple_of(q * width, 128), width)]
        part[:, width:] = tokens[0, :, pl.ds(pl.multiple_of(q * slim, 128), slim)]


def pack(code, tokens, targets):
    tile = tokens.shape[1]
    row = (tokens.shape[2] + targets.shape[2]) // SHARDS
    return pl.pallas_call(
        pack_kernel,
        out_shape=[jax.ShapeDtypeStruct((tile, row), tokens.dtype)] * SHARDS,
        in_specs=[VMEM] * 3,
        out_specs=[VMEM] * SHARDS,
        name="pack_quarters",
    )(code, tokens, targets)


def copy_rows(ref, start, out, at, count, columns=slice(None)):
    step = 32

    def body(i, _):
        rows = pl.ds(pl.multiple_of(at + i * step, step), step)
        out[rows, :] = ref[pl.ds(pl.multiple_of(start + i * step, step), step), columns]
        return 0

    lax.fori_loop(0, count // step, body, 0, unroll=True if count <= 64 else 4)


def split_kernel(one, two, three, *halves):
    count = one.shape[0] // 2
    for h, half in enumerate(halves):
        for n, part in enumerate((one, two, three)):
            copy_rows(part, h * count, half, n * count, count)


def split_rows(parts):
    tile, row = parts[0].shape
    half = jax.ShapeDtypeStruct((len(parts) * tile // 2, row), parts[0].dtype)
    return pl.pallas_call(
        split_kernel,
        out_shape=[half, half],
        in_specs=[VMEM] * len(parts),
        out_specs=[VMEM, VMEM],
        compiler_params=pltpu.CompilerParams(vmem_limit_bytes=8 * 1024 * 1024),
        name="split_rows",
    )(*parts)


def piece(pool, which, h):
    group, j = divmod(which, SHARDS)
    whole, halves = pool[group]
    rows = whole.shape[0] // 2
    return (whole, h * rows, rows) if j == 0 else (halves[h], (j - 1) * rows, rows)


def grouped(refs, halves):
    size = 1 + len(halves)
    pool = []
    for g in range(PLANES):
        group = refs[g * size : (g + 1) * size]
        pool.append((group[0], dict(zip(halves, group[1:]))))
    return pool, refs[PLANES * size :]


def pick_for_end_kernel(h, ints, *refs):
    pool, (out,) = grouped(refs, (h,))

    def slot(s, _):
        place = ints[FOR_END + s]
        for which in range(PLANES * SHARDS):
            ref, start, rows = piece(pool, which, h)

            @pl.when(place == which)
            def _():
                copy_rows(ref, start, out, s * rows, rows)

        return 0

    lax.fori_loop(0, SLOTS, slot, 0)


def pick_for_end(h, ints, pool):
    tile, row = pool[0][0].shape
    operands = [x for whole, halves in pool for x in (whole, halves[h])]
    return pl.pallas_call(
        functools.partial(pick_for_end_kernel, h),
        out_shape=jax.ShapeDtypeStruct((SLOTS * tile // 2, row), operands[0].dtype),
        in_specs=[SMEM] + [VMEM] * len(operands),
        out_specs=VMEM,
        compiler_params=pltpu.CompilerParams(vmem_limit_bytes=16 * 1024 * 1024),
        name="pick_for_end",
    )(ints, *operands)


def pick_own_kernel(ints, *refs):
    pool, (handed_a, handed_b, quarter, targets) = grouped(refs, (0, 1))
    handed = (handed_a, handed_b)
    width = targets.shape[1]
    half = quarter.shape[0] // SLOTS // 2

    def slot(s, _):
        place = ints[FOR_OWN + s]
        for h in range(2):
            at = (2 * s + h) * half

            @pl.when(place < 0)
            def _():
                start = pl.multiple_of(s * half, half)
                copy_rows(handed[h], start, targets, at, half, slice(0, width))
                copy_rows(handed[h], start, quarter, at, half, slice(width, None))

            for which in range(PLANES * SHARDS):
                ref, start, rows = piece(pool, which, h)

                @pl.when(place == which)
                def _():
                    copy_rows(ref, start, targets, at, rows, slice(0, width))
                    copy_rows(ref, start, quarter, at, rows, slice(width, None))

        return 0

    lax.fori_loop(0, SLOTS, slot, 0)


def pick_own(ints, pool, handed, width):
    rows, row = handed[0].shape
    operands = [x for whole, halves in pool for x in (whole, *halves)]
    return pl.pallas_call(
        pick_own_kernel,
        out_shape=[
            jax.ShapeDtypeStruct((2 * rows, row - width), handed[0].dtype),
            jax.ShapeDtypeStruct((2 * rows, width), handed[0].dtype),
        ],
        in_specs=[SMEM] + [VMEM] * (len(operands) + 2),
        out_specs=[VMEM, VMEM],
        compiler_params=pltpu.CompilerParams(vmem_limit_bytes=16 * 1024 * 1024),
        name="pick_own",
    )(ints, *operands, *handed)


def grad_kernel(counts, ints, floats, in0, in1, in2, in3, targets, own_w, *refs):
    sent, (grad, loss, w_buf, delta, sem) = sent_refs(counts, refs)
    m, k = position()
    half = w_buf.shape[0] // 2
    copies = [
        start_copies(ints, 0, h, own_w, sent, w_buf.at[pl.ds(h * half, half)], sem.at[h])
        for h in range(2)
    ]
    tile = in0.shape[0] // SLOTS
    slim = in0.shape[1]
    ins = (in0, in1, in2, in3)
    for copy in copies:
        copy.wait()

    def slot(s, total):
        span = pl.ds(pl.multiple_of(s * tile, tile), tile)
        pre = None
        for j in range(SHARDS):
            at = pl.ds(pl.multiple_of((k ^ j) * slim, slim), slim)
            one = jnp.dot(ins[j][span, :], w_buf[at, :], preferred_element_type=jnp.float32)
            pre = one if pre is None else pre + one
        live = lax.broadcasted_iota(jnp.int32, pre.shape, 0) < ints[TOKENS + s]
        many = jnp.full(pre.shape, ints[COUNTS + s], jnp.int32).astype(jnp.float32)
        coef = jnp.where(live, floats[TASK + s] / many, 0.0)
        hidden, slope = gelu_pair(pre)
        diff = hidden - targets[span, :].astype(jnp.float32)
        scaled = coef * diff
        delta[span, :] = (2.0 * scaled * slope).astype(jnp.bfloat16)
        return total + jnp.sum(scaled * diff, keepdims=True)

    total = lax.fori_loop(0, SLOTS, slot, jnp.zeros((1, 1), jnp.float32))
    lane = lax.broadcasted_iota(jnp.int32, loss.shape, 1)
    loss[...] = jnp.where(lane == m * SHARDS + k, total, 0.0)
    for j in range(SHARDS):
        at = pl.ds(pl.multiple_of((k ^ j) * slim, slim), slim)
        grad[at, :] = lax.dot_general(
            ins[j][...], delta[...], (((0,), (0,)), ((), ())), preferred_element_type=jnp.float32
        )


def gradient(ints, floats, ins, targets, own_w, sent):
    rows, width = targets.shape
    depth = own_w.shape[1]
    return pl.pallas_call(
        functools.partial(grad_kernel, counts_of(sent)),
        out_shape=[
            jax.ShapeDtypeStruct((depth, width), jnp.float32),
            jax.ShapeDtypeStruct((8, 128), jnp.float32),
        ],
        in_specs=[SMEM] * 2 + [VMEM] * 5 + [ANY] * (1 + sum(counts_of(sent))),
        out_specs=[VMEM, VMEM],
        scratch_shapes=[
            pltpu.VMEM((depth, width), own_w.dtype),
            pltpu.VMEM((rows, width), jnp.bfloat16),
            pltpu.SemaphoreType.DMA((2,)),
        ],
        compiler_params=pltpu.CompilerParams(vmem_limit_bytes=16 * 1024 * 1024),
        name="forward_and_gradient",
    )(ints, floats, *ins, targets, own_w, *sent[0], *sent[1], *sent[2])


def adam_kernel(h, counts, ints, floats, grad, *refs):
    own, (sent, refs) = refs[:3], sent_refs(counts, refs[3:])
    new, bufs, outs, (in_sem, out_sem) = refs[-11:-8], refs[-8:-5], refs[-5:-2], refs[-2:]
    blocks = out_sem.shape[1]
    rows = bufs[0].shape[0]
    step = rows // blocks
    here = h * rows

    def result(i, b):
        return pltpu.make_async_copy(
            outs[i].at[pl.ds(b * step, step)],
            new[i].at[0, pl.ds(here + b * step, step)],
            out_sem.at[i, b],
        )

    copies = [
        start_copies(ints, a, h, own[a], sent, bufs[a], in_sem.at[a]) for a in range(3)
    ]
    rate = floats[RATE]
    for copy in copies:
        copy.wait()
    for b in range(blocks):

        def body(n, _):
            at = pl.ds(pl.multiple_of(b * step + n * 16, 16), 16)
            g = grad[pl.ds(pl.multiple_of(here + b * step + n * 16, 16), 16), :]
            first = beta_one * bufs[1][at, :].astype(jnp.float32) + (1.0 - beta_one) * g
            second = beta_two * bufs[2][at, :].astype(jnp.float32) + (1.0 - beta_two) * g * g
            start = bufs[0][at, :].astype(jnp.float32)
            updated = start - rate * first / (jnp.sqrt(second) + adam_eps)
            outs[0][at, :] = updated.astype(outs[0].dtype)
            outs[1][at, :] = first.astype(outs[1].dtype)
            outs[2][at, :] = second.astype(outs[2].dtype)
            return 0

        lax.fori_loop(0, step // 16, body, 0, unroll=2)
        for i in range(3):
            result(i, b).start()
    for b in range(blocks):
        for i in range(3):
            result(i, b).wait()


def adam(h, ints, floats, grad, own, sent, begun=()):
    depth, width = grad.shape
    blocks = 2
    taken = sum(counts_of(sent))
    return pl.pallas_call(
        functools.partial(adam_kernel, h, counts_of(sent)),
        out_shape=[jax.ShapeDtypeStruct(x.shape, x.dtype) for x in own],
        in_specs=[SMEM] * 2 + [VMEM] + [ANY] * (3 + taken) + [HBM] * len(begun),
        out_specs=[HBM] * 3,
        scratch_shapes=[pltpu.VMEM((depth // 2, width), x.dtype) for x in own] * 2
        + [pltpu.SemaphoreType.DMA((3,)), pltpu.SemaphoreType.DMA((3, blocks))],
        input_output_aliases={6 + taken + i: i for i in range(len(begun))},
        compiler_params=pltpu.CompilerParams(vmem_limit_bytes=16 * 1024 * 1024),
        name="adam_half",
    )(ints, floats, grad, *own, *sent[0], *sent[1], *sent[2], *begun)


def in_plane(x, j):
    pairs = [(m * SHARDS + k, m * SHARDS + (k ^ j)) for m in range(PLANES) for k in range(SHARDS)]
    return lax.ppermute(x, "pop", pairs)


def along(x, hops):
    idle = [m for m in range(PLANES) if all(m not in hop for hop in hops)]
    pairs = [(a * SHARDS + k, b * SHARDS + k) for a, b in hops for k in range(SHARDS)]
    pairs += [(m * SHARDS + k, m * SHARDS + (k ^ 1)) for m in idle for k in range(SHARDS)]
    return lax.ppermute(x, "pop", pairs)


def beside(x):
    return lax.ppermute(x, "rep", [(0, 1), (1, 0)])


def after(x, *others):
    return lax.optimization_barrier((x, *others))[0]


def tiles(here, ints, width):
    near0, middle0, (here0, halves) = here
    near = [along(x, ENDS) for x in halves]
    far0 = along(near0, MIDDLE)
    middle = [along(x, MIDDLE) for x in halves]
    far_a = along(near[0], MIDDLE)
    far = [far_a, along(after(near[1], far_a), MIDDLE)]
    pool = [(here0, halves), (near0, near), (middle0, middle), (far0, far)]
    picked = [pick_for_end(h, ints, pool) for h in range(2)]
    handed = [along(picked[0], ENDS), along(picked[1], ENDS)]
    quarter, targets = pick_own(ints, pool, handed, width)
    side = in_plane(quarter, 1)
    cross = in_plane(quarter, 2)
    gates = [halves, (near, middle), picked[0], (picked[1], handed[0]), handed[1]]
    return gates, (quarter, side, cross, in_plane(cross, 1)), targets


def state_steps(ints, own, gates, steps, returns):
    half = own[0].shape[1] // 2
    guests = [beside(x[0, half:]) for x in own] if returns else []
    last, ends, middles, backs = (), [], [], []
    for t in range(1, steps + 1):
        guest = guests[t - 1] if t <= len(guests) else None
        theirs = 1 < t <= returns + 1
        gate = (gates[t - 1 : t], backs)
        facts = after(ints, gate) if jax.tree.leaves(gate) else ints
        to_ends, to_middle, *brought = stage(facts, t, own, guest, last, theirs)
        backs += [beside(x) for x in brought]
        last = (along(to_ends, ENDS), along(to_middle, MIDDLE))
        ends.append(last[0])
        middles.append(last[1])
    if len(backs) < returns:
        backs.append(beside(theirs_of(after(ints, backs), *last)))
    return ends, middles, backs


def run(by_both, ints, floats, parts, own):
    near0, middle0 = along(parts[0], ENDS), along(parts[0], MIDDLE)
    swapped = [in_plane(parts[j], j) for j in range(1, SHARDS)]
    halves = split_rows(after(swapped, near0, middle0))
    here = (near0, middle0, (parts[0], halves))
    gates, ins, targets = tiles(here, ints, own[0].shape[2])
    if by_both:
        ends, middles, backs = state_steps(ints, own, gates, 4, 4)
        first = 2
    else:
        ends, middles, backs = state_steps(ints, own, [(), *gates], 8, 0)
        first = 4
    grad, loss = gradient(
        ints, floats, ins, targets, own[0], (ends[:first], middles[:first], backs[:first])
    )
    round_one = [in_plane(loss, j) for j in range(1, SHARDS)]
    early = slice(None) if by_both else slice(-1)
    new = adam(0, ints, floats, grad, own, (ends[early], middles[early], []))
    loss = loss + round_one[0] + round_one[1] + round_one[2]
    ring = [along(loss, [(m, (m + d) % PLANES) for m in range(PLANES)]) for d in range(1, PLANES)]
    direct = ([], []) if by_both else (ends, middles)
    new = adam(1, ints, floats, grad, own, (*direct, backs), new)
    loss = loss + ring[0] + ring[1] + ring[2]
    return (*new, jnp.sum(loss[0, : PLANES * SHARDS].reshape(PLANES, SHARDS), axis=1))


def per_device(pool_tokens, pool_targets, weight, first_moment, second_moment, *args):
    winner, tile_ids = args[0], args[4]
    if winner.shape[0] != PLANES or tile_ids.shape[1] != SLOTS or lax.axis_size("rep") != 2:
        return relayed(pool_tokens, pool_targets, weight, first_moment, second_moment, *args)
    code = route_code(winner)
    parts = pack(code, pool_tokens, pool_targets)
    ints, floats = gather_facts(beside(code), *args)
    own = (weight, first_moment, second_moment)
    plans = [functools.partial(run, by_both) for by_both in (True, False)]
    return lax.switch(ints[SHARED], plans, ints, floats, parts, own)


def solution(mesh):
    in_specs = (
        P(("rep", "pop"), None, None),
        P(("rep", "pop"), None, None),
        P(("rep", "pop"), None, None),
        P(("rep", "pop"), None, None),
        P(("rep", "pop"), None, None),
        P("rep"),
        P("rep"),
        P("rep"),
        P("rep", None),
        P("rep", None),
        P("rep", None),
        P("rep", None),
    )
    out_specs = (
        P(("rep", "pop"), None, None),
        P(("rep", "pop"), None, None),
        P(("rep", "pop"), None, None),
        P("rep"),
    )
    return jax.shard_map(
        per_device, mesh=mesh, in_specs=in_specs, out_specs=out_specs, check_vma=False
    )
```

```python
import functools

import jax
import jax.numpy as jnp
from jax import lax
from jax.experimental import pallas as pl
from jax.experimental.pallas import tpu as pltpu
from jax.sharding import PartitionSpec as P

SHARDS = 4
TASKS = 8
SLOTS = 4
PLANES = 4


beta_one = 0.9
beta_two = 0.999
adam_eps = 1e-08
gelu_coef = 0.7978845608028654

SMEM = pl.BlockSpec(memory_space=pltpu.SMEM)
VMEM = pl.BlockSpec(memory_space=pltpu.VMEM)
ANY = pl.BlockSpec(memory_space=pl.ANY)
HBM = pl.BlockSpec(memory_space=pltpu.HBM)


def gelu_pair(pre):
    inner = jnp.tanh(gelu_coef * (pre + 0.044715 * pre * pre * pre))
    value = 0.5 * pre * (1.0 + inner)
    slope = 0.5 * (1.0 + inner) + 0.5 * pre * (1.0 - inner * inner) * gelu_coef * (
        1.0 + 3.0 * 0.044715 * pre * pre
    )
    return (value, slope)


def for_sending(shard):

    def short(part):
        return part.astype(jnp.bfloat16) if part.dtype == jnp.float32 else part

    return jax.tree.map(short, shard)


def relayed(
    pool_tokens,
    pool_targets,
    weight,
    first_moment,
    second_moment,
    winner,
    learn_rate,
    explore,
    task_weight,
    tile_ids,
    slot_task,
    slot_tokens,
):
    nodes = lax.axis_size("pop")
    place = lax.axis_index("pop")
    member = place // SHARDS
    shard = place % SHARDS
    members = winner.shape[0]
    slots = tile_ids.shape[1]
    tile = pool_tokens.shape[1]
    depth = pool_tokens.shape[2]
    width = weight.shape[2]
    hidden_all = pool_targets.shape[2]
    reach = tile // nodes
    flat_state = (
        weight.reshape(nodes, -1),
        first_moment.reshape(nodes, -1),
        second_moment.reshape(nodes, -1),
    )
    spread = (
        lax.all_to_all(flat_state[0], "pop", split_axis=0, concat_axis=0, tiled=True),
        lax.all_to_all(flat_state[1], "pop", split_axis=0, concat_axis=0, tiled=True),
        lax.all_to_all(flat_state[2], "pop", split_axis=0, concat_axis=0, tiled=True),
    )
    source_rows = (winner[:, None] * SHARDS + jnp.arange(SHARDS, dtype=jnp.int32)[None, :]).reshape(
        -1
    )
    picked_state = tuple((jnp.take(piece, source_rows, axis=0) for piece in spread))
    returned = jax.tree.map(
        lambda part, own: part.astype(own.dtype),
        lax.all_to_all(for_sending(picked_state), "pop", split_axis=0, concat_axis=0, tiled=True),
        picked_state,
    )
    start_weight = returned[0].reshape(depth, width)
    start_first = returned[1].reshape(depth, width)
    start_second = returned[2].reshape(depth, width)
    relay_tokens, relay_targets = (
        lax.all_to_all(pool_tokens, "pop", split_axis=1, concat_axis=0, tiled=True),
        lax.all_to_all(pool_targets, "pop", split_axis=1, concat_axis=0, tiled=True),
    )
    flat_ids = tile_ids.reshape(-1)
    pick_tokens = jnp.take(relay_tokens, flat_ids, axis=0).reshape(members, 1, slots, reach, depth)
    send_tokens = jnp.broadcast_to(pick_tokens, (members, SHARDS, slots, reach, depth)).reshape(
        nodes, slots, reach, depth
    )
    pick_targets = jnp.take(relay_targets, flat_ids, axis=0).reshape(
        members, slots, reach, hidden_all
    )
    send_targets = jnp.broadcast_to(
        pick_targets[:, None], (members, SHARDS, slots, reach, hidden_all)
    ).reshape(nodes, slots, reach, hidden_all)
    got_tokens, got_targets = (
        lax.all_to_all(send_tokens, "pop", split_axis=0, concat_axis=2, tiled=True),
        lax.all_to_all(send_targets, "pop", split_axis=0, concat_axis=2, tiled=True),
    )
    targets = lax.dynamic_slice_in_dim(got_targets[0], shard * width, width, 2).reshape(
        slots * tile, width
    )
    inputs = got_tokens.reshape(slots * tile, depth)
    tasks_here = lax.dynamic_index_in_dim(slot_task, member, 0, keepdims=False)
    lengths = lax.dynamic_index_in_dim(slot_tokens, member, 0, keepdims=False)
    source_member = lax.dynamic_index_in_dim(winner, member, 0, keepdims=False)
    onehot = tasks_here[:, None] == jnp.arange(TASKS, dtype=jnp.int32)[None, :]
    counts = jnp.sum(jnp.where(onehot, lengths[:, None], 0), axis=0)
    weights_here = lax.dynamic_index_in_dim(task_weight, source_member, 0, keepdims=False)
    scale = weights_here / jnp.maximum(counts, 1).astype(jnp.float32)
    per_slot = jnp.sum(jnp.where(onehot, scale[None, :], jnp.float32(0.0)), axis=1)
    live = jnp.arange(tile, dtype=jnp.int32)[None, :] < lengths[:, None]
    coef = jnp.where(live, per_slot[:, None], jnp.float32(0.0)).reshape(-1)
    own_rate = lax.dynamic_index_in_dim(learn_rate, source_member, 0, keepdims=False)
    own_explore = lax.dynamic_index_in_dim(explore, member, 0, keepdims=False)
    step_rate = own_rate * jnp.where(source_member != member, own_explore, jnp.float32(1.0))
    pre = jnp.dot(inputs, start_weight, preferred_element_type=jnp.float32)
    hidden, slope = gelu_pair(pre)
    diff = hidden - targets.astype(jnp.float32)
    part = jnp.sum(coef[:, None] * diff * diff)
    delta = (2.0 * coef[:, None] * diff * slope).astype(jnp.bfloat16)
    grad = lax.dot_general(
        inputs, delta, (((0,), (0,)), ((), ())), preferred_element_type=jnp.float32
    )
    first = beta_one * start_first.astype(jnp.float32) + (1.0 - beta_one) * grad
    second = beta_two * start_second.astype(jnp.float32) + (1.0 - beta_two) * grad * grad
    updated = start_weight.astype(jnp.float32) - step_rate * first / (jnp.sqrt(second) + adam_eps)
    share = jnp.where(jnp.arange(members, dtype=jnp.int32) == member, part, jnp.float32(0.0))
    member_loss = lax.psum(share, "pop")
    return (
        updated.astype(jnp.bfloat16)[None],
        first.astype(jnp.bfloat16)[None],
        second.astype(jnp.bfloat16)[None],
        member_loss,
    )


ENDS = ((0, 1), (1, 0), (2, 3), (3, 2))
MIDDLE = ((1, 2), (2, 1))


def position():
    place = lax.axis_index("pop")
    return place // SHARDS, lax.rem(place, SHARDS)


SHARED, TAKEN, HOPS, BY_ENDS, THEIR_ENDS, TO_ENDS, TO_MIDDLE = range(7)
FOR_END, FOR_OWN, TOKENS, COUNTS = 16, 20, 24, 28
OWN, GUEST, PASSED = range(3)
RATE, TASK = 0, 4


def copied_from(winner):
    loser, source = jnp.int32(0), jnp.int32(0)
    for m in range(PLANES):
        taken = winner[m] != m
        loser = jnp.where(taken, m, loser)
        source = jnp.where(taken, winner[m], source)
    return loser, source


def route_kernel(winner, code):
    loser, source = copied_from(winner)
    code[...] = jnp.full(code.shape, source * PLANES + loser, jnp.int32)


def route_code(winner):
    return pl.pallas_call(
        route_kernel,
        out_shape=jax.ShapeDtypeStruct((8, 128), jnp.int32),
        in_specs=[SMEM],
        out_specs=VMEM,
        name="route_code",
    )(winner)


def on_route(route, m, to):
    source, loser = route
    upward = (to == m + 1) & (source <= m) & (loser >= to)
    return upward | ((to == m - 1) & (source >= m) & (loser <= to))


def by_ends(route):
    source, loser = route
    return jnp.where(source < loser, loser - 1, loser + 1) == (loser ^ 1)


def in_pool(t, m, k):
    ahead = t // SHARDS - m
    ahead = jnp.where(m == 1, ahead, -ahead)
    group = jnp.where(ahead == 0, 0, jnp.where(ahead == -1, 1, ahead + 1))
    return group * SHARDS + (lax.rem(t, SHARDS) ^ k)


def facts_kernel(
    other, winner, learn_rate, explore, task_weight, tile_ids, slot_task, slot_tokens, ints, floats
):
    m, k = position()
    loser, source = copied_from(winner)
    code = other[0, 0]
    mine = source, loser
    theirs = lax.div(code, jnp.int32(PLANES)), lax.rem(code, jnp.int32(PLANES))
    upward = jnp.maximum(mine[0], theirs[0]) < jnp.minimum(mine[1], theirs[1])
    downward = jnp.maximum(mine[1], theirs[1]) < jnp.minimum(mine[0], theirs[0])
    hops = jnp.abs(mine[0] - mine[1])
    long = jnp.maximum(hops, jnp.abs(theirs[0] - theirs[1])) == PLANES - 1
    shared = upward | downward | long
    taken = winner[m] != m

    def content(to):
        own = on_route(mine, m, to)
        guest = on_route(theirs, m, to) & jnp.logical_not(shared)
        first = jnp.where(own, jnp.where(m == mine[0], OWN, PASSED), -1)
        return jnp.where(guest, jnp.where(m == theirs[0], GUEST, PASSED), first)

    ints[SHARED] = shared.astype(jnp.int32)
    ints[TAKEN] = taken.astype(jnp.int32)
    ints[HOPS] = hops
    ints[BY_ENDS] = by_ends(mine).astype(jnp.int32)
    ints[THEIR_ENDS] = by_ends(theirs).astype(jnp.int32)
    ints[TO_ENDS] = content(m ^ 1)
    ints[TO_MIDDLE] = content(jnp.where(m == 1, 2, jnp.where(m == 2, 1, -1)))
    end = jnp.where(m <= 1, 0, PLANES - 1)
    at_end = (m == 0) | (m == PLANES - 1)
    slots = tile_ids.shape[1]
    for s in range(slots):
        task = slot_task[m, s]
        count = jnp.int32(0)
        for o in range(slots):
            count = count + jnp.where(slot_task[m, o] == task, slot_tokens[m, o], 0)
        ints[FOR_END + s] = in_pool(tile_ids[end, s], m, k)
        ints[FOR_OWN + s] = jnp.where(at_end, -1, in_pool(tile_ids[m, s], m, k))
        ints[TOKENS + s] = slot_tokens[m, s]
        ints[COUNTS + s] = jnp.maximum(count, 1)
        floats[TASK + s] = task_weight[winner[m], task]
    floats[RATE] = learn_rate[winner[m]] * jnp.where(taken, explore[m], 1.0)


def gather_facts(other, *small):
    return pl.pallas_call(
        facts_kernel,
        out_shape=[jax.ShapeDtypeStruct((32,), jnp.int32), jax.ShapeDtypeStruct((8,), jnp.float32)],
        in_specs=[SMEM] * 8,
        out_specs=[SMEM, SMEM],
        name="gather_facts",
    )(other, *small)


def stage_kernel(t, has_guest, has_theirs, has_last, ints, *refs):
    state, refs = refs[:3], refs[3:]
    guest = refs[0] if has_guest else None
    from_ends, from_middle = refs[has_guest : has_guest + 2] if has_last else (None, None)
    to_ends, to_middle = refs[has_guest + 2 * has_last :][:2]
    sems = refs[-1]
    half = to_ends.shape[0]
    shared = ints[SHARED] == 1
    array = jnp.where(shared, (t - 1) // 2, t - 1)
    start = pl.multiple_of(jnp.where(shared, (t - 1) % 2, 0) * half, half)
    sides = ((to_ends, ints[TO_ENDS], from_middle), (to_middle, ints[TO_MIDDLE], from_ends))
    for n, (out, content, _) in enumerate(sides):
        for a, ref in enumerate(state):

            @pl.when((content == OWN) & (array == a))
            def _():
                pltpu.make_async_copy(ref.at[0, pl.ds(start, half)], out, sems.at[n]).start()

    if has_theirs:
        theirs = refs[has_guest + 2 * has_last + 2]

        @pl.when(ints[THEIR_ENDS] == 1)
        def _():
            copy_rows(from_ends, 0, theirs, 0, half)

        @pl.when(ints[THEIR_ENDS] == 0)
        def _():
            copy_rows(from_middle, 0, theirs, 0, half)

    for n, (out, content, passed) in enumerate(sides):
        if guest is not None:

            @pl.when(content == GUEST)
            def _():
                copy_rows(guest, 0, out, 0, half)

        if passed is not None:

            @pl.when(content == PASSED)
            def _():
                copy_rows(passed, 0, out, 0, half)

        @pl.when((content == OWN) & (array < len(state)))
        def _():
            pltpu.make_async_copy(state[0].at[0, pl.ds(0, half)], out, sems.at[n]).wait()


def stage(ints, step, own, guest, last, theirs):
    half, width = own[0].shape[1] // 2, own[0].shape[2]
    guests = () if guest is None else (guest,)
    kernel = functools.partial(stage_kernel, step, len(guests), theirs, len(last) > 0)
    return pl.pallas_call(
        kernel,
        out_shape=[jax.ShapeDtypeStruct((half, width), own[0].dtype)] * (2 + theirs),
        in_specs=[SMEM] + [ANY] * 3 + [VMEM] * (len(guests) + len(last)),
        out_specs=[VMEM] * (2 + theirs),
        scratch_shapes=[pltpu.SemaphoreType.DMA((2,))],
        compiler_params=pltpu.CompilerParams(vmem_limit_bytes=8 * 1024 * 1024),
        name="stage_chunk",
    )(ints, *own, *guests, *last)


def theirs_kernel(ints, from_ends, from_middle, theirs):
    @pl.when(ints[THEIR_ENDS] == 1)
    def _():
        copy_rows(from_ends, 0, theirs, 0, theirs.shape[0])

    @pl.when(ints[THEIR_ENDS] == 0)
    def _():
        copy_rows(from_middle, 0, theirs, 0, theirs.shape[0])


def theirs_of(ints, from_ends, from_middle):
    return pl.pallas_call(
        theirs_kernel,
        out_shape=jax.ShapeDtypeStruct(from_ends.shape, from_ends.dtype),
        in_specs=[SMEM] + [VMEM] * 2,
        out_specs=VMEM,
        compiler_params=pltpu.CompilerParams(vmem_limit_bytes=8 * 1024 * 1024),
        name="guest_chunk",
    )(ints, from_ends, from_middle)


def start_copies(ints, a, h, own, sent, out, sem):
    ends, middles, backs = sent
    shared, taken = ints[SHARED] == 1, ints[TAKEN] == 1
    half = out.shape[0]
    step = jnp.where(shared, 2 * a + h, a) + ints[HOPS]
    direct = taken & shared if h == 1 else taken

    def copy(ref):
        return pltpu.make_async_copy(ref, out, sem)

    @pl.when(jnp.logical_not(taken))
    def _():
        copy(own.at[0, pl.ds(h * half, half)]).start()

    sides = [
        (ends, direct & (ints[BY_ENDS] == 1)),
        (middles, direct & (ints[BY_ENDS] == 0)),
    ]
    if h == 1:
        sides.append((backs, taken & jnp.logical_not(shared)))
    for refs, here in sides:
        for n, ref in enumerate(refs):

            @pl.when(here & (step == n + 1))
            def _():
                copy(ref).start()

    return copy(own.at[0, pl.ds(h * half, half)])


def counts_of(sent):
    return tuple(len(refs) for refs in sent)


def sent_refs(counts, refs):
    a, b, c = counts
    return (refs[:a], refs[a : a + b], refs[a + b : a + b + c]), refs[a + b + c :]


def pack_kernel(code, tokens, targets, *parts):
    _, k = position()
    width = targets.shape[2] // SHARDS
    slim = tokens.shape[2] // SHARDS
    for j, part in enumerate(parts):
        q = k ^ j
        part[:, :width] = targets[0, :, pl.ds(pl.multiple_of(q * width, 128), width)]
        part[:, width:] = tokens[0, :, pl.ds(pl.multiple_of(q * slim, 128), slim)]


def pack(code, tokens, targets):
    tile = tokens.shape[1]
    row = (tokens.shape[2] + targets.shape[2]) // SHARDS
    return pl.pallas_call(
        pack_kernel,
        out_shape=[jax.ShapeDtypeStruct((tile, row), tokens.dtype)] * SHARDS,
        in_specs=[VMEM] * 3,
        out_specs=[VMEM] * SHARDS,
        name="pack_quarters",
    )(code, tokens, targets)


def copy_rows(ref, start, out, at, count, columns=slice(None)):
    step = 32

    def body(i, _):
        rows = pl.ds(pl.multiple_of(at + i * step, step), step)
        out[rows, :] = ref[pl.ds(pl.multiple_of(start + i * step, step), step), columns]
        return 0

    lax.fori_loop(0, count // step, body, 0, unroll=True if count <= 64 else 4)


def split_kernel(one, two, three, *halves):
    count = one.shape[0] // 2
    for h, half in enumerate(halves):
        for n, part in enumerate((one, two, three)):
            copy_rows(part, h * count, half, n * count, count)


def split_rows(parts):
    tile, row = parts[0].shape
    half = jax.ShapeDtypeStruct((len(parts) * tile // 2, row), parts[0].dtype)
    return pl.pallas_call(
        split_kernel,
        out_shape=[half, half],
        in_specs=[VMEM] * len(parts),
        out_specs=[VMEM, VMEM],
        compiler_params=pltpu.CompilerParams(vmem_limit_bytes=8 * 1024 * 1024),
        name="split_rows",
    )(*parts)


def piece(pool, which, h):
    group, j = divmod(which, SHARDS)
    whole, halves = pool[group]
    rows = whole.shape[0] // 2
    return (whole, h * rows, rows) if j == 0 else (halves[h], (j - 1) * rows, rows)


def grouped(refs, halves):
    size = 1 + len(halves)
    pool = []
    for g in range(PLANES):
        group = refs[g * size : (g + 1) * size]
        pool.append((group[0], dict(zip(halves, group[1:]))))
    return pool, refs[PLANES * size :]


def pick_for_end_kernel(h, ints, *refs):
    pool, (out,) = grouped(refs, (h,))

    def slot(s, _):
        place = ints[FOR_END + s]
        for which in range(PLANES * SHARDS):
            ref, start, rows = piece(pool, which, h)

            @pl.when(place == which)
            def _():
                copy_rows(ref, start, out, s * rows, rows)

        return 0

    lax.fori_loop(0, SLOTS, slot, 0)


def pick_for_end(h, ints, pool):
    tile, row = pool[0][0].shape
    operands = [x for whole, halves in pool for x in (whole, halves[h])]
    return pl.pallas_call(
        functools.partial(pick_for_end_kernel, h),
        out_shape=jax.ShapeDtypeStruct((SLOTS * tile // 2, row), operands[0].dtype),
        in_specs=[SMEM] + [VMEM] * len(operands),
        out_specs=VMEM,
        compiler_params=pltpu.CompilerParams(vmem_limit_bytes=16 * 1024 * 1024),
        name="pick_for_end",
    )(ints, *operands)


def pick_own_kernel(ints, *refs):
    pool, (handed_a, handed_b, quarter, targets) = grouped(refs, (0, 1))
    handed = (handed_a, handed_b)
    width = targets.shape[1]
    half = quarter.shape[0] // SLOTS // 2

    def slot(s, _):
        place = ints[FOR_OWN + s]
        for h in range(2):
            at = (2 * s + h) * half

            @pl.when(place < 0)
            def _():
                start = pl.multiple_of(s * half, half)
                copy_rows(handed[h], start, targets, at, half, slice(0, width))
                copy_rows(handed[h], start, quarter, at, half, slice(width, None))

            for which in range(PLANES * SHARDS):
                ref, start, rows = piece(pool, which, h)

                @pl.when(place == which)
                def _():
                    copy_rows(ref, start, targets, at, rows, slice(0, width))
                    copy_rows(ref, start, quarter, at, rows, slice(width, None))

        return 0

    lax.fori_loop(0, SLOTS, slot, 0)


def pick_own(ints, pool, handed, width):
    rows, row = handed[0].shape
    operands = [x for whole, halves in pool for x in (whole, *halves)]
    return pl.pallas_call(
        pick_own_kernel,
        out_shape=[
            jax.ShapeDtypeStruct((2 * rows, row - width), handed[0].dtype),
            jax.ShapeDtypeStruct((2 * rows, width), handed[0].dtype),
        ],
        in_specs=[SMEM] + [VMEM] * (len(operands) + 2),
        out_specs=[VMEM, VMEM],
        compiler_params=pltpu.CompilerParams(vmem_limit_bytes=16 * 1024 * 1024),
        name="pick_own",
    )(ints, *operands, *handed)


def grad_kernel(counts, ints, floats, in0, in1, in2, in3, targets, own_w, *refs):
    sent, (grad, loss, w_buf, delta, sem) = sent_refs(counts, refs)
    m, k = position()
    half = w_buf.shape[0] // 2
    copies = [
        start_copies(ints, 0, h, own_w, sent, w_buf.at[pl.ds(h * half, half)], sem.at[h])
        for h in range(2)
    ]
    tile = in0.shape[0] // SLOTS
    slim = in0.shape[1]
    ins = (in0, in1, in2, in3)
    for copy in copies:
        copy.wait()

    def slot(s, total):
        span = pl.ds(pl.multiple_of(s * tile, tile), tile)
        pre = None
        for j in range(SHARDS):
            at = pl.ds(pl.multiple_of((k ^ j) * slim, slim), slim)
            one = jnp.dot(ins[j][span, :], w_buf[at, :], preferred_element_type=jnp.float32)
            pre = one if pre is None else pre + one
        live = lax.broadcasted_iota(jnp.int32, pre.shape, 0) < ints[TOKENS + s]
        many = jnp.full(pre.shape, ints[COUNTS + s], jnp.int32).astype(jnp.float32)
        coef = jnp.where(live, floats[TASK + s] / many, 0.0)
        hidden, slope = gelu_pair(pre)
        diff = hidden - targets[span, :].astype(jnp.float32)
        scaled = coef * diff
        delta[span, :] = (2.0 * scaled * slope).astype(jnp.bfloat16)
        return total + jnp.sum(scaled * diff, keepdims=True)

    total = lax.fori_loop(0, SLOTS, slot, jnp.zeros((1, 1), jnp.float32))
    lane = lax.broadcasted_iota(jnp.int32, loss.shape, 1)
    loss[...] = jnp.where(lane == m * SHARDS + k, total, 0.0)
    for j in range(SHARDS):
        at = pl.ds(pl.multiple_of((k ^ j) * slim, slim), slim)
        grad[at, :] = lax.dot_general(
            ins[j][...], delta[...], (((0,), (0,)), ((), ())), preferred_element_type=jnp.float32
        )


def gradient(ints, floats, ins, targets, own_w, sent):
    rows, width = targets.shape
    depth = own_w.shape[1]
    return pl.pallas_call(
        functools.partial(grad_kernel, counts_of(sent)),
        out_shape=[
            jax.ShapeDtypeStruct((depth, width), jnp.float32),
            jax.ShapeDtypeStruct((8, 128), jnp.float32),
        ],
        in_specs=[SMEM] * 2 + [VMEM] * 5 + [ANY] * (1 + sum(counts_of(sent))),
        out_specs=[VMEM, VMEM],
        scratch_shapes=[
            pltpu.VMEM((depth, width), own_w.dtype),
            pltpu.VMEM((rows, width), jnp.bfloat16),
            pltpu.SemaphoreType.DMA((2,)),
        ],
        compiler_params=pltpu.CompilerParams(vmem_limit_bytes=16 * 1024 * 1024),
        name="forward_and_gradient",
    )(ints, floats, *ins, targets, own_w, *sent[0], *sent[1], *sent[2])


def adam_kernel(h, counts, ints, floats, grad, *refs):
    own, (sent, refs) = refs[:3], sent_refs(counts, refs[3:])
    new, bufs, outs, (in_sem, out_sem) = refs[-11:-8], refs[-8:-5], refs[-5:-2], refs[-2:]
    blocks = out_sem.shape[1]
    rows = bufs[0].shape[0]
    step = rows // blocks
    here = h * rows

    def result(i, b):
        return pltpu.make_async_copy(
            outs[i].at[pl.ds(b * step, step)],
            new[i].at[0, pl.ds(here + b * step, step)],
            out_sem.at[i, b],
        )

    copies = [
        start_copies(ints, a, h, own[a], sent, bufs[a], in_sem.at[a]) for a in range(3)
    ]
    rate = floats[RATE]
    for copy in copies:
        copy.wait()
    for b in range(blocks):

        def body(n, _):
            at = pl.ds(pl.multiple_of(b * step + n * 16, 16), 16)
            g = grad[pl.ds(pl.multiple_of(here + b * step + n * 16, 16), 16), :]
            first = beta_one * bufs[1][at, :].astype(jnp.float32) + (1.0 - beta_one) * g
            second = beta_two * bufs[2][at, :].astype(jnp.float32) + (1.0 - beta_two) * g * g
            start = bufs[0][at, :].astype(jnp.float32)
            updated = start - rate * first / (jnp.sqrt(second) + adam_eps)
            outs[0][at, :] = updated.astype(outs[0].dtype)
            outs[1][at, :] = first.astype(outs[1].dtype)
            outs[2][at, :] = second.astype(outs[2].dtype)
            return 0

        lax.fori_loop(0, step // 16, body, 0, unroll=2)
        for i in range(3):
            result(i, b).start()
    for b in range(blocks):
        for i in range(3):
            result(i, b).wait()


def adam(h, ints, floats, grad, own, sent, begun=()):
    depth, width = grad.shape
    blocks = 2
    taken = sum(counts_of(sent))
    own = [pltpu.with_memory_space_constraint(x, pltpu.HBM) for x in own]
    sent = [
        [pltpu.with_memory_space_constraint(x, pltpu.HBM) for x in refs[:-1]] + list(refs[-1:])
        for refs in sent
    ]
    return pl.pallas_call(
        functools.partial(adam_kernel, h, counts_of(sent)),
        out_shape=[pltpu.HBM(x.shape, x.dtype) for x in own],
        in_specs=[SMEM] * 2 + [VMEM] + [ANY] * (3 + taken) + [HBM] * len(begun),
        out_specs=[HBM] * 3,
        scratch_shapes=[pltpu.VMEM((depth // 2, width), x.dtype) for x in own] * 2
        + [pltpu.SemaphoreType.DMA((3,)), pltpu.SemaphoreType.DMA((3, blocks))],
        input_output_aliases={6 + taken + i: i for i in range(len(begun))},
        compiler_params=pltpu.CompilerParams(vmem_limit_bytes=16 * 1024 * 1024),
        name="adam_half",
    )(ints, floats, grad, *own, *sent[0], *sent[1], *sent[2], *begun)


def in_plane(x, j):
    pairs = [(m * SHARDS + k, m * SHARDS + (k ^ j)) for m in range(PLANES) for k in range(SHARDS)]
    return lax.ppermute(x, "pop", pairs)


def along(x, hops):
    idle = [m for m in range(PLANES) if all(m not in hop for hop in hops)]
    pairs = [(a * SHARDS + k, b * SHARDS + k) for a, b in hops for k in range(SHARDS)]
    pairs += [(m * SHARDS + k, m * SHARDS + (k ^ 1)) for m in idle for k in range(SHARDS)]
    return lax.ppermute(x, "pop", pairs)


def beside(x):
    return lax.ppermute(x, "rep", [(0, 1), (1, 0)])


def after(x, *others):
    return lax.optimization_barrier((x, *others))[0]


def tiles(here, ints, width):
    near0, middle0, (here0, halves) = here
    near = [along(x, ENDS) for x in halves]
    far0 = along(near0, MIDDLE)
    middle = [along(x, MIDDLE) for x in halves]
    far_a = along(near[0], MIDDLE)
    far = [far_a, along(after(near[1], far_a), MIDDLE)]
    pool = [(here0, halves), (near0, near), (middle0, middle), (far0, far)]
    picked = [pick_for_end(h, ints, pool) for h in range(2)]
    handed = [along(picked[0], ENDS), along(picked[1], ENDS)]
    quarter, targets = pick_own(ints, pool, handed, width)
    side = in_plane(quarter, 1)
    cross = in_plane(quarter, 2)
    gates = [halves, (near, middle), picked[0], (picked[1], handed[0]), handed[1]]
    return gates, (quarter, side, cross, in_plane(cross, 1)), targets


def state_steps(ints, own, gates, steps, returns):
    half = own[0].shape[1] // 2
    guests = [beside(x[0, half:]) for x in own] if returns else []
    last, ends, middles, backs = (), [], [], []
    for t in range(1, steps + 1):
        guest = guests[t - 1] if t <= len(guests) else None
        theirs = 1 < t <= returns + 1
        gate = (gates[t - 1 : t], backs)
        facts = after(ints, gate) if jax.tree.leaves(gate) else ints
        to_ends, to_middle, *brought = stage(facts, t, own, guest, last, theirs)
        backs += [beside(x) for x in brought]
        last = (along(to_ends, ENDS), along(to_middle, MIDDLE))
        ends.append(last[0])
        middles.append(last[1])
    if len(backs) < returns:
        backs.append(beside(theirs_of(after(ints, backs), *last)))
    return ends, middles, backs


def run(by_both, ints, floats, parts, own):
    near0, middle0 = along(parts[0], ENDS), along(parts[0], MIDDLE)
    swapped = [in_plane(parts[j], j) for j in range(1, SHARDS)]
    halves = split_rows(after(swapped, near0, middle0))
    here = (near0, middle0, (parts[0], halves))
    gates, ins, targets = tiles(here, ints, own[0].shape[2])
    if by_both:
        ends, middles, backs = state_steps(ints, own, gates, 4, 4)
        first = 2
    else:
        ends, middles, backs = state_steps(ints, own, [(), *gates], 8, 0)
        first = 4
    grad, loss = gradient(
        ints, floats, ins, targets, own[0], (ends[:first], middles[:first], backs[:first])
    )
    round_one = [in_plane(loss, j) for j in range(1, SHARDS)]
    early = slice(None) if by_both else slice(-1)
    new = adam(0, ints, floats, grad, own, (ends[early], middles[early], []))
    loss = after(loss, new[0])
    loss = loss + round_one[0] + round_one[1] + round_one[2]
    ring = [along(loss, [(m, (m + d) % PLANES) for m in range(PLANES)]) for d in range(1, PLANES)]
    direct = ([], []) if by_both else (ends, middles)
    new = adam(1, ints, floats, grad, own, (*direct, backs), new)
    loss = after(loss, new[0]) + ring[0] + ring[1] + ring[2]
    return (*new, jnp.sum(loss[0, : PLANES * SHARDS].reshape(PLANES, SHARDS), axis=1))


def per_device(pool_tokens, pool_targets, weight, first_moment, second_moment, *args):
    winner, tile_ids = args[0], args[4]
    if winner.shape[0] != PLANES or tile_ids.shape[1] != SLOTS or lax.axis_size("rep") != 2:
        return relayed(pool_tokens, pool_targets, weight, first_moment, second_moment, *args)
    code = route_code(winner)
    parts = pack(code, pool_tokens, pool_targets)
    ints, floats = gather_facts(beside(code), *args)
    own = (weight, first_moment, second_moment)
    plans = [functools.partial(run, by_both) for by_both in (True, False)]
    return lax.switch(ints[SHARED], plans, ints, floats, parts, own)


def solution(mesh):
    in_specs = (
        P(("rep", "pop"), None, None),
        P(("rep", "pop"), None, None),
        P(("rep", "pop"), None, None),
        P(("rep", "pop"), None, None),
        P(("rep", "pop"), None, None),
        P("rep"),
        P("rep"),
        P("rep"),
        P("rep", None),
        P("rep", None),
        P("rep", None),
        P("rep", None),
    )
    out_specs = (
        P(("rep", "pop"), None, None),
        P(("rep", "pop"), None, None),
        P(("rep", "pop"), None, None),
        P("rep"),
    )
    return jax.shard_map(
        per_device, mesh=mesh, in_specs=in_specs, out_specs=out_specs, check_vma=False
    )
```

```python
import functools

import jax
import jax.numpy as jnp
from jax import lax
from jax.experimental import pallas as pl
from jax.experimental.pallas import tpu as pltpu
from jax.sharding import PartitionSpec as P

SHARDS = 4
TASKS = 8
SLOTS = 4
PLANES = 4


beta_one = 0.9
beta_two = 0.999
adam_eps = 1e-08
gelu_coef = 0.7978845608028654

SMEM = pl.BlockSpec(memory_space=pltpu.SMEM)
VMEM = pl.BlockSpec(memory_space=pltpu.VMEM)
ANY = pl.BlockSpec(memory_space=pl.ANY)
HBM = pl.BlockSpec(memory_space=pltpu.HBM)


def gelu_pair(pre):
    inner = jnp.tanh(gelu_coef * (pre + 0.044715 * pre * pre * pre))
    value = 0.5 * pre * (1.0 + inner)
    slope = 0.5 * (1.0 + inner) + 0.5 * pre * (1.0 - inner * inner) * gelu_coef * (
        1.0 + 3.0 * 0.044715 * pre * pre
    )
    return (value, slope)


def for_sending(shard):

    def short(part):
        return part.astype(jnp.bfloat16) if part.dtype == jnp.float32 else part

    return jax.tree.map(short, shard)


def relayed(
    pool_tokens,
    pool_targets,
    weight,
    first_moment,
    second_moment,
    winner,
    learn_rate,
    explore,
    task_weight,
    tile_ids,
    slot_task,
    slot_tokens,
):
    nodes = lax.axis_size("pop")
    place = lax.axis_index("pop")
    member = place // SHARDS
    shard = place % SHARDS
    members = winner.shape[0]
    slots = tile_ids.shape[1]
    tile = pool_tokens.shape[1]
    depth = pool_tokens.shape[2]
    width = weight.shape[2]
    hidden_all = pool_targets.shape[2]
    reach = tile // nodes
    flat_state = (
        weight.reshape(nodes, -1),
        first_moment.reshape(nodes, -1),
        second_moment.reshape(nodes, -1),
    )
    spread = (
        lax.all_to_all(flat_state[0], "pop", split_axis=0, concat_axis=0, tiled=True),
        lax.all_to_all(flat_state[1], "pop", split_axis=0, concat_axis=0, tiled=True),
        lax.all_to_all(flat_state[2], "pop", split_axis=0, concat_axis=0, tiled=True),
    )
    source_rows = (winner[:, None] * SHARDS + jnp.arange(SHARDS, dtype=jnp.int32)[None, :]).reshape(
        -1
    )
    picked_state = tuple((jnp.take(piece, source_rows, axis=0) for piece in spread))
    returned = jax.tree.map(
        lambda part, own: part.astype(own.dtype),
        lax.all_to_all(for_sending(picked_state), "pop", split_axis=0, concat_axis=0, tiled=True),
        picked_state,
    )
    start_weight = returned[0].reshape(depth, width)
    start_first = returned[1].reshape(depth, width)
    start_second = returned[2].reshape(depth, width)
    relay_tokens, relay_targets = (
        lax.all_to_all(pool_tokens, "pop", split_axis=1, concat_axis=0, tiled=True),
        lax.all_to_all(pool_targets, "pop", split_axis=1, concat_axis=0, tiled=True),
    )
    flat_ids = tile_ids.reshape(-1)
    pick_tokens = jnp.take(relay_tokens, flat_ids, axis=0).reshape(members, 1, slots, reach, depth)
    send_tokens = jnp.broadcast_to(pick_tokens, (members, SHARDS, slots, reach, depth)).reshape(
        nodes, slots, reach, depth
    )
    pick_targets = jnp.take(relay_targets, flat_ids, axis=0).reshape(
        members, slots, reach, hidden_all
    )
    send_targets = jnp.broadcast_to(
        pick_targets[:, None], (members, SHARDS, slots, reach, hidden_all)
    ).reshape(nodes, slots, reach, hidden_all)
    got_tokens, got_targets = (
        lax.all_to_all(send_tokens, "pop", split_axis=0, concat_axis=2, tiled=True),
        lax.all_to_all(send_targets, "pop", split_axis=0, concat_axis=2, tiled=True),
    )
    targets = lax.dynamic_slice_in_dim(got_targets[0], shard * width, width, 2).reshape(
        slots * tile, width
    )
    inputs = got_tokens.reshape(slots * tile, depth)
    tasks_here = lax.dynamic_index_in_dim(slot_task, member, 0, keepdims=False)
    lengths = lax.dynamic_index_in_dim(slot_tokens, member, 0, keepdims=False)
    source_member = lax.dynamic_index_in_dim(winner, member, 0, keepdims=False)
    onehot = tasks_here[:, None] == jnp.arange(TASKS, dtype=jnp.int32)[None, :]
    counts = jnp.sum(jnp.where(onehot, lengths[:, None], 0), axis=0)
    weights_here = lax.dynamic_index_in_dim(task_weight, source_member, 0, keepdims=False)
    scale = weights_here / jnp.maximum(counts, 1).astype(jnp.float32)
    per_slot = jnp.sum(jnp.where(onehot, scale[None, :], jnp.float32(0.0)), axis=1)
    live = jnp.arange(tile, dtype=jnp.int32)[None, :] < lengths[:, None]
    coef = jnp.where(live, per_slot[:, None], jnp.float32(0.0)).reshape(-1)
    own_rate = lax.dynamic_index_in_dim(learn_rate, source_member, 0, keepdims=False)
    own_explore = lax.dynamic_index_in_dim(explore, member, 0, keepdims=False)
    step_rate = own_rate * jnp.where(source_member != member, own_explore, jnp.float32(1.0))
    pre = jnp.dot(inputs, start_weight, preferred_element_type=jnp.float32)
    hidden, slope = gelu_pair(pre)
    diff = hidden - targets.astype(jnp.float32)
    part = jnp.sum(coef[:, None] * diff * diff)
    delta = (2.0 * coef[:, None] * diff * slope).astype(jnp.bfloat16)
    grad = lax.dot_general(
        inputs, delta, (((0,), (0,)), ((), ())), preferred_element_type=jnp.float32
    )
    first = beta_one * start_first.astype(jnp.float32) + (1.0 - beta_one) * grad
    second = beta_two * start_second.astype(jnp.float32) + (1.0 - beta_two) * grad * grad
    updated = start_weight.astype(jnp.float32) - step_rate * first / (jnp.sqrt(second) + adam_eps)
    share = jnp.where(jnp.arange(members, dtype=jnp.int32) == member, part, jnp.float32(0.0))
    member_loss = lax.psum(share, "pop")
    return (
        updated.astype(jnp.bfloat16)[None],
        first.astype(jnp.bfloat16)[None],
        second.astype(jnp.bfloat16)[None],
        member_loss,
    )


ENDS = ((0, 1), (1, 0), (2, 3), (3, 2))
MIDDLE = ((1, 2), (2, 1))


def position():
    place = lax.axis_index("pop")
    return place // SHARDS, lax.rem(place, SHARDS)


SHARED, TAKEN, HOPS, BY_ENDS, THEIR_ENDS, TO_ENDS, TO_MIDDLE, PLAN = range(8)
FOR_END, FOR_OWN, TOKENS, COUNTS = 16, 20, 24, 28
OWN, GUEST, PASSED = range(3)
RATE, TASK = 0, 4


def copied_from(winner):
    loser, source = jnp.int32(0), jnp.int32(0)
    for m in range(PLANES):
        taken = winner[m] != m
        loser = jnp.where(taken, m, loser)
        source = jnp.where(taken, winner[m], source)
    return loser, source


def route_kernel(winner, code):
    loser, source = copied_from(winner)
    code[...] = jnp.full(code.shape, source * PLANES + loser, jnp.int32)


def route_code(winner):
    return pl.pallas_call(
        route_kernel,
        out_shape=jax.ShapeDtypeStruct((8, 128), jnp.int32),
        in_specs=[SMEM],
        out_specs=VMEM,
        name="route_code",
    )(winner)


def on_route(route, m, to):
    source, loser = route
    upward = (to == m + 1) & (source <= m) & (loser >= to)
    return upward | ((to == m - 1) & (source >= m) & (loser <= to))


def by_ends(route):
    source, loser = route
    return jnp.where(source < loser, loser - 1, loser + 1) == (loser ^ 1)


def in_pool(t, m, k):
    ahead = t // SHARDS - m
    ahead = jnp.where(m == 1, ahead, -ahead)
    group = jnp.where(ahead == 0, 0, jnp.where(ahead == -1, 1, ahead + 1))
    return group * SHARDS + (lax.rem(t, SHARDS) ^ k)


def facts_kernel(
    other, winner, learn_rate, explore, task_weight, tile_ids, slot_task, slot_tokens, ints, floats
):
    m, k = position()
    loser, source = copied_from(winner)
    code = other[0, 0]
    mine = source, loser
    theirs = lax.div(code, jnp.int32(PLANES)), lax.rem(code, jnp.int32(PLANES))
    upward = jnp.maximum(mine[0], theirs[0]) < jnp.minimum(mine[1], theirs[1])
    downward = jnp.maximum(mine[1], theirs[1]) < jnp.minimum(mine[0], theirs[0])
    hops = jnp.abs(mine[0] - mine[1])
    long = jnp.maximum(hops, jnp.abs(theirs[0] - theirs[1])) == PLANES - 1
    shared = upward | downward | long
    taken = winner[m] != m

    def content(to):
        own = on_route(mine, m, to)
        guest = on_route(theirs, m, to) & jnp.logical_not(shared)
        first = jnp.where(own, jnp.where(m == mine[0], OWN, PASSED), -1)
        return jnp.where(guest, jnp.where(m == theirs[0], GUEST, PASSED), first)

    ints[SHARED] = shared.astype(jnp.int32)
    ints[TAKEN] = taken.astype(jnp.int32)
    ints[HOPS] = hops
    ints[PLAN] = jnp.where(long, 2, shared.astype(jnp.int32))
    ints[BY_ENDS] = by_ends(mine).astype(jnp.int32)
    ints[THEIR_ENDS] = by_ends(theirs).astype(jnp.int32)
    ints[TO_ENDS] = content(m ^ 1)
    ints[TO_MIDDLE] = content(jnp.where(m == 1, 2, jnp.where(m == 2, 1, -1)))
    end = jnp.where(m <= 1, 0, PLANES - 1)
    at_end = (m == 0) | (m == PLANES - 1)
    slots = tile_ids.shape[1]
    for s in range(slots):
        task = slot_task[m, s]
        count = jnp.int32(0)
        for o in range(slots):
            count = count + jnp.where(slot_task[m, o] == task, slot_tokens[m, o], 0)
        ints[FOR_END + s] = in_pool(tile_ids[end, s], m, k)
        ints[FOR_OWN + s] = jnp.where(at_end, -1, in_pool(tile_ids[m, s], m, k))
        ints[TOKENS + s] = slot_tokens[m, s]
        ints[COUNTS + s] = jnp.maximum(count, 1)
        floats[TASK + s] = task_weight[winner[m], task]
    floats[RATE] = learn_rate[winner[m]] * jnp.where(taken, explore[m], 1.0)


def gather_facts(other, *small):
    return pl.pallas_call(
        facts_kernel,
        out_shape=[jax.ShapeDtypeStruct((32,), jnp.int32), jax.ShapeDtypeStruct((8,), jnp.float32)],
        in_specs=[SMEM] * 8,
        out_specs=[SMEM, SMEM],
        name="gather_facts",
    )(other, *small)


def stage_kernel(t, has_guest, has_theirs, has_last, ints, *refs):
    state, refs = refs[:3], refs[3:]
    guest = refs[0] if has_guest else None
    from_ends, from_middle = refs[has_guest : has_guest + 2] if has_last else (None, None)
    to_ends, to_middle = refs[has_guest + 2 * has_last :][:2]
    sems = refs[-1]
    half = to_ends.shape[0]
    shared = ints[SHARED] == 1
    array = jnp.where(shared, (t - 1) // 2, t - 1)
    start = pl.multiple_of(jnp.where(shared, (t - 1) % 2, 0) * half, half)
    sides = ((to_ends, ints[TO_ENDS], from_middle), (to_middle, ints[TO_MIDDLE], from_ends))
    for n, (out, content, _) in enumerate(sides):
        for a, ref in enumerate(state):

            @pl.when((content == OWN) & (array == a))
            def _():
                pltpu.make_async_copy(ref.at[0, pl.ds(start, half)], out, sems.at[n]).start()

    if has_theirs:
        theirs = refs[has_guest + 2 * has_last + 2]

        @pl.when(ints[THEIR_ENDS] == 1)
        def _():
            copy_rows(from_ends, 0, theirs, 0, half)

        @pl.when(ints[THEIR_ENDS] == 0)
        def _():
            copy_rows(from_middle, 0, theirs, 0, half)

    for n, (out, content, passed) in enumerate(sides):
        if guest is not None:

            @pl.when(content == GUEST)
            def _():
                copy_rows(guest, 0, out, 0, half)

        if passed is not None:

            @pl.when(content == PASSED)
            def _():
                copy_rows(passed, 0, out, 0, half)

        @pl.when((content == OWN) & (array < len(state)))
        def _():
            pltpu.make_async_copy(state[0].at[0, pl.ds(0, half)], out, sems.at[n]).wait()


def stage(ints, step, own, guest, last, theirs):
    half, width = own[0].shape[1] // 2, own[0].shape[2]
    guests = () if guest is None else (guest,)
    kernel = functools.partial(stage_kernel, step, len(guests), theirs, len(last) > 0)
    return pl.pallas_call(
        kernel,
        out_shape=[jax.ShapeDtypeStruct((half, width), own[0].dtype)] * (2 + theirs),
        in_specs=[SMEM] + [ANY] * 3 + [VMEM] * (len(guests) + len(last)),
        out_specs=[VMEM] * (2 + theirs),
        scratch_shapes=[pltpu.SemaphoreType.DMA((2,))],
        compiler_params=pltpu.CompilerParams(vmem_limit_bytes=8 * 1024 * 1024),
        name="stage_chunk",
    )(ints, *own, *guests, *last)


def theirs_kernel(ints, from_ends, from_middle, theirs):
    @pl.when(ints[THEIR_ENDS] == 1)
    def _():
        copy_rows(from_ends, 0, theirs, 0, theirs.shape[0])

    @pl.when(ints[THEIR_ENDS] == 0)
    def _():
        copy_rows(from_middle, 0, theirs, 0, theirs.shape[0])


def theirs_of(ints, from_ends, from_middle):
    return pl.pallas_call(
        theirs_kernel,
        out_shape=jax.ShapeDtypeStruct(from_ends.shape, from_ends.dtype),
        in_specs=[SMEM] + [VMEM] * 2,
        out_specs=VMEM,
        compiler_params=pltpu.CompilerParams(vmem_limit_bytes=8 * 1024 * 1024),
        name="guest_chunk",
    )(ints, from_ends, from_middle)


def start_copies(ints, a, h, own, sent, out, sem):
    ends, middles, backs = sent
    shared, taken = ints[SHARED] == 1, ints[TAKEN] == 1
    half = out.shape[0]
    step = jnp.where(shared, 2 * a + h, a) + ints[HOPS]
    direct = taken & shared if h == 1 else taken

    def copy(ref):
        return pltpu.make_async_copy(ref, out, sem)

    @pl.when(jnp.logical_not(taken))
    def _():
        copy(own.at[0, pl.ds(h * half, half)]).start()

    sides = [
        (ends, direct & (ints[BY_ENDS] == 1)),
        (middles, direct & (ints[BY_ENDS] == 0)),
    ]
    if h == 1:
        sides.append((backs, taken & jnp.logical_not(shared)))
    for refs, here in sides:
        for n, ref in enumerate(refs):

            @pl.when(here & (step == n + 1))
            def _():
                copy(ref).start()

    return copy(own.at[0, pl.ds(h * half, half)])


def counts_of(sent):
    return tuple(len(refs) for refs in sent)


def sent_refs(counts, refs):
    a, b, c = counts
    return (refs[:a], refs[a : a + b], refs[a + b : a + b + c]), refs[a + b + c :]


def pack_kernel(code, tokens, targets, *parts):
    _, k = position()
    width = targets.shape[2] // SHARDS
    slim = tokens.shape[2] // SHARDS
    for j, part in enumerate(parts):
        q = k ^ j
        part[:, :width] = targets[0, :, pl.ds(pl.multiple_of(q * width, 128), width)]
        part[:, width:] = tokens[0, :, pl.ds(pl.multiple_of(q * slim, 128), slim)]


def pack(code, tokens, targets):
    tile = tokens.shape[1]
    row = (tokens.shape[2] + targets.shape[2]) // SHARDS
    return pl.pallas_call(
        pack_kernel,
        out_shape=[jax.ShapeDtypeStruct((tile, row), tokens.dtype)] * SHARDS,
        in_specs=[VMEM] * 3,
        out_specs=[VMEM] * SHARDS,
        name="pack_quarters",
    )(code, tokens, targets)


def copy_rows(ref, start, out, at, count, columns=slice(None)):
    step = 32

    def body(i, _):
        rows = pl.ds(pl.multiple_of(at + i * step, step), step)
        out[rows, :] = ref[pl.ds(pl.multiple_of(start + i * step, step), step), columns]
        return 0

    lax.fori_loop(0, count // step, body, 0, unroll=True if count <= 64 else 4)


def split_kernel(one, two, three, *halves):
    count = one.shape[0] // 2
    for h, half in enumerate(halves):
        for n, part in enumerate((one, two, three)):
            copy_rows(part, h * count, half, n * count, count)


def split_rows(parts):
    tile, row = parts[0].shape
    half = jax.ShapeDtypeStruct((len(parts) * tile // 2, row), parts[0].dtype)
    return pl.pallas_call(
        split_kernel,
        out_shape=[half, half],
        in_specs=[VMEM] * len(parts),
        out_specs=[VMEM, VMEM],
        compiler_params=pltpu.CompilerParams(vmem_limit_bytes=8 * 1024 * 1024),
        name="split_rows",
    )(*parts)


def piece(pool, which, h):
    group, j = divmod(which, SHARDS)
    whole, halves = pool[group]
    rows = whole.shape[0] // 2
    return (whole, h * rows, rows) if j == 0 else (halves[h], (j - 1) * rows, rows)


def grouped(refs, halves):
    size = 1 + len(halves)
    pool = []
    for g in range(PLANES):
        group = refs[g * size : (g + 1) * size]
        pool.append((group[0], dict(zip(halves, group[1:]))))
    return pool, refs[PLANES * size :]


def pick_for_end_kernel(h, ints, *refs):
    pool, (out,) = grouped(refs, (h,))

    def slot(s, _):
        place = ints[FOR_END + s]
        for which in range(PLANES * SHARDS):
            ref, start, rows = piece(pool, which, h)

            @pl.when(place == which)
            def _():
                copy_rows(ref, start, out, s * rows, rows)

        return 0

    lax.fori_loop(0, SLOTS, slot, 0)


def pick_for_end(h, ints, pool):
    tile, row = pool[0][0].shape
    operands = [x for whole, halves in pool for x in (whole, halves[h])]
    return pl.pallas_call(
        functools.partial(pick_for_end_kernel, h),
        out_shape=jax.ShapeDtypeStruct((SLOTS * tile // 2, row), operands[0].dtype),
        in_specs=[SMEM] + [VMEM] * len(operands),
        out_specs=VMEM,
        compiler_params=pltpu.CompilerParams(vmem_limit_bytes=16 * 1024 * 1024),
        name="pick_for_end",
    )(ints, *operands)


def pick_own_kernel(ints, *refs):
    pool, (handed_a, handed_b, quarter, targets) = grouped(refs, (0, 1))
    handed = (handed_a, handed_b)
    width = targets.shape[1]
    half = quarter.shape[0] // SLOTS // 2

    def slot(s, _):
        place = ints[FOR_OWN + s]
        for h in range(2):
            at = (2 * s + h) * half

            @pl.when(place < 0)
            def _():
                start = pl.multiple_of(s * half, half)
                copy_rows(handed[h], start, targets, at, half, slice(0, width))
                copy_rows(handed[h], start, quarter, at, half, slice(width, None))

            for which in range(PLANES * SHARDS):
                ref, start, rows = piece(pool, which, h)

                @pl.when(place == which)
                def _():
                    copy_rows(ref, start, targets, at, rows, slice(0, width))
                    copy_rows(ref, start, quarter, at, rows, slice(width, None))

        return 0

    lax.fori_loop(0, SLOTS, slot, 0)


def pick_own(ints, pool, handed, width):
    rows, row = handed[0].shape
    operands = [x for whole, halves in pool for x in (whole, *halves)]
    return pl.pallas_call(
        pick_own_kernel,
        out_shape=[
            jax.ShapeDtypeStruct((2 * rows, row - width), handed[0].dtype),
            jax.ShapeDtypeStruct((2 * rows, width), handed[0].dtype),
        ],
        in_specs=[SMEM] + [VMEM] * (len(operands) + 2),
        out_specs=[VMEM, VMEM],
        compiler_params=pltpu.CompilerParams(vmem_limit_bytes=16 * 1024 * 1024),
        name="pick_own",
    )(ints, *operands, *handed)


def grad_kernel(counts, ints, floats, in0, in1, in2, in3, targets, own_w, *refs):
    sent, (grad, loss, w_buf, delta, sem) = sent_refs(counts, refs)
    m, k = position()
    half = w_buf.shape[0] // 2
    copies = [
        start_copies(ints, 0, h, own_w, sent, w_buf.at[pl.ds(h * half, half)], sem.at[h])
        for h in range(2)
    ]
    tile = in0.shape[0] // SLOTS
    slim = in0.shape[1]
    ins = (in0, in1, in2, in3)
    for copy in copies:
        copy.wait()

    def slot(s, total):
        span = pl.ds(pl.multiple_of(s * tile, tile), tile)
        pre = None
        for j in range(SHARDS):
            at = pl.ds(pl.multiple_of((k ^ j) * slim, slim), slim)
            one = jnp.dot(ins[j][span, :], w_buf[at, :], preferred_element_type=jnp.float32)
            pre = one if pre is None else pre + one
        live = lax.broadcasted_iota(jnp.int32, pre.shape, 0) < ints[TOKENS + s]
        many = jnp.full(pre.shape, ints[COUNTS + s], jnp.int32).astype(jnp.float32)
        coef = jnp.where(live, floats[TASK + s] / many, 0.0)
        hidden, slope = gelu_pair(pre)
        diff = hidden - targets[span, :].astype(jnp.float32)
        scaled = coef * diff
        delta[span, :] = (2.0 * scaled * slope).astype(jnp.bfloat16)
        return total + jnp.sum(scaled * diff, keepdims=True)

    total = lax.fori_loop(0, SLOTS, slot, jnp.zeros((1, 1), jnp.float32))
    lane = lax.broadcasted_iota(jnp.int32, loss.shape, 1)
    loss[...] = jnp.where(lane == m * SHARDS + k, total, 0.0)
    for j in range(SHARDS):
        at = pl.ds(pl.multiple_of((k ^ j) * slim, slim), slim)
        grad[at, :] = lax.dot_general(
            ins[j][...], delta[...], (((0,), (0,)), ((), ())), preferred_element_type=jnp.float32
        )


def gradient(ints, floats, ins, targets, own_w, sent):
    rows, width = targets.shape
    depth = own_w.shape[1]
    return pl.pallas_call(
        functools.partial(grad_kernel, counts_of(sent)),
        out_shape=[
            jax.ShapeDtypeStruct((depth, width), jnp.float32),
            jax.ShapeDtypeStruct((8, 128), jnp.float32),
        ],
        in_specs=[SMEM] * 2 + [VMEM] * 5 + [ANY] * (1 + sum(counts_of(sent))),
        out_specs=[VMEM, VMEM],
        scratch_shapes=[
            pltpu.VMEM((depth, width), own_w.dtype),
            pltpu.VMEM((rows, width), jnp.bfloat16),
            pltpu.SemaphoreType.DMA((2,)),
        ],
        compiler_params=pltpu.CompilerParams(vmem_limit_bytes=16 * 1024 * 1024),
        name="forward_and_gradient",
    )(ints, floats, *ins, targets, own_w, *sent[0], *sent[1], *sent[2])


def adam_kernel(h, counts, ints, floats, grad, *refs):
    own, (sent, refs) = refs[:3], sent_refs(counts, refs[3:])
    new, bufs, outs, (in_sem, out_sem) = refs[-11:-8], refs[-8:-5], refs[-5:-2], refs[-2:]
    blocks = out_sem.shape[1]
    rows = bufs[0].shape[0]
    step = rows // blocks
    here = h * rows

    def result(i, b):
        return pltpu.make_async_copy(
            outs[i].at[pl.ds(b * step, step)],
            new[i].at[0, pl.ds(here + b * step, step)],
            out_sem.at[i, b],
        )

    copies = [
        start_copies(ints, a, h, own[a], sent, bufs[a], in_sem.at[a]) for a in range(3)
    ]
    rate = floats[RATE]
    for copy in copies:
        copy.wait()
    for b in range(blocks):

        def body(n, _):
            at = pl.ds(pl.multiple_of(b * step + n * 16, 16), 16)
            g = grad[pl.ds(pl.multiple_of(here + b * step + n * 16, 16), 16), :]
            first = beta_one * bufs[1][at, :].astype(jnp.float32) + (1.0 - beta_one) * g
            second = beta_two * bufs[2][at, :].astype(jnp.float32) + (1.0 - beta_two) * g * g
            start = bufs[0][at, :].astype(jnp.float32)
            updated = start - rate * first / (jnp.sqrt(second) + adam_eps)
            outs[0][at, :] = updated.astype(outs[0].dtype)
            outs[1][at, :] = first.astype(outs[1].dtype)
            outs[2][at, :] = second.astype(outs[2].dtype)
            return 0

        lax.fori_loop(0, step // 16, body, 0, unroll=2)
        for i in range(3):
            result(i, b).start()
    for b in range(blocks):
        for i in range(3):
            result(i, b).wait()


def adam(h, ints, floats, grad, own, sent, begun=()):
    depth, width = grad.shape
    blocks = 2
    taken = sum(counts_of(sent))
    own = [pltpu.with_memory_space_constraint(x, pltpu.HBM) for x in own]
    sent = [
        [pltpu.with_memory_space_constraint(x, pltpu.HBM) for x in refs[:-1]] + list(refs[-1:])
        for refs in sent
    ]
    return pl.pallas_call(
        functools.partial(adam_kernel, h, counts_of(sent)),
        out_shape=[pltpu.HBM(x.shape, x.dtype) for x in own],
        in_specs=[SMEM] * 2 + [VMEM] + [ANY] * (3 + taken) + [HBM] * len(begun),
        out_specs=[HBM] * 3,
        scratch_shapes=[pltpu.VMEM((depth // 2, width), x.dtype) for x in own] * 2
        + [pltpu.SemaphoreType.DMA((3,)), pltpu.SemaphoreType.DMA((3, blocks))],
        input_output_aliases={6 + taken + i: i for i in range(len(begun))},
        compiler_params=pltpu.CompilerParams(vmem_limit_bytes=16 * 1024 * 1024),
        name="adam_half",
    )(ints, floats, grad, *own, *sent[0], *sent[1], *sent[2], *begun)


def in_plane(x, j):
    pairs = [(m * SHARDS + k, m * SHARDS + (k ^ j)) for m in range(PLANES) for k in range(SHARDS)]
    return lax.ppermute(x, "pop", pairs)


def along(x, hops):
    idle = [m for m in range(PLANES) if all(m not in hop for hop in hops)]
    pairs = [(a * SHARDS + k, b * SHARDS + k) for a, b in hops for k in range(SHARDS)]
    pairs += [(m * SHARDS + k, m * SHARDS + (k ^ 1)) for m in idle for k in range(SHARDS)]
    return lax.ppermute(x, "pop", pairs)


def beside(x):
    return lax.ppermute(x, "rep", [(0, 1), (1, 0)])


def after(x, *others):
    return lax.optimization_barrier((x, *others))[0]


def tiles(here, ints, width):
    near0, middle0, (here0, halves) = here
    near = [along(x, ENDS) for x in halves]
    far0 = along(near0, MIDDLE)
    middle = [along(x, MIDDLE) for x in halves]
    far_a = along(near[0], MIDDLE)
    far = [far_a, along(after(near[1], far_a), MIDDLE)]
    pool = [(here0, halves), (near0, near), (middle0, middle), (far0, far)]
    picked = [pick_for_end(h, ints, pool) for h in range(2)]
    handed = [along(picked[0], ENDS), along(picked[1], ENDS)]
    quarter, targets = pick_own(ints, pool, handed, width)
    side = in_plane(quarter, 1)
    cross = in_plane(quarter, 2)
    gates = [halves, (near, middle, near0, middle0), picked[0], (picked[1], handed[0]), handed[1], quarter]
    return gates, (quarter, side, cross, in_plane(cross, 1)), targets


def state_steps(ints, own, gates, steps, returns):
    half = own[0].shape[1] // 2
    guests = [beside(x[0, half:]) for x in own] if returns else []
    last, ends, middles, backs = (), [], [], []
    for t in range(1, steps + 1):
        guest = guests[t - 1] if t <= len(guests) else None
        theirs = 1 < t <= returns + 1
        gate = (gates[t - 1 : t], backs)
        facts = after(ints, gate) if jax.tree.leaves(gate) else ints
        to_ends, to_middle, *brought = stage(facts, t, own, guest, last, theirs)
        backs += [beside(x) for x in brought]
        last = (along(to_ends, ENDS), along(to_middle, MIDDLE))
        ends.append(last[0])
        middles.append(last[1])
    if len(backs) < returns:
        backs.append(beside(theirs_of(after(ints, (backs, gates[-1])), *last)))
    return ends, middles, backs


def run(plan, ints, floats, parts, own):
    near0, middle0 = along(parts[0], ENDS), along(parts[0], MIDDLE)
    swapped = [in_plane(parts[j], j) for j in range(1, SHARDS)]
    by_both = plan == 0
    halves = split_rows(after(swapped, near0, middle0) if by_both else swapped)
    here = (near0, middle0, (parts[0], halves))
    gates, ins, targets = tiles(here, ints, own[0].shape[2])
    if by_both:
        ends, middles, backs = state_steps(ints, own, gates, 4, 4)
        first = 2
    else:
        ends, middles, backs = state_steps(ints, own, [(), *gates], 6 + plan, 0)
        first = 2 + plan
    grad, loss = gradient(
        ints, floats, ins, targets, own[0], (ends[:first], middles[:first], backs[:first])
    )
    round_one = [in_plane(loss, j) for j in range(1, SHARDS)]
    early = slice(None) if by_both else slice(-1)
    new = adam(0, ints, floats, grad, own, (ends[early], middles[early], []))
    loss = after(loss, new[0])
    loss = loss + round_one[0] + round_one[1] + round_one[2]
    ring = [along(loss, [(m, (m + d) % PLANES) for m in range(PLANES)]) for d in range(1, PLANES)]
    direct = ([], []) if by_both else (ends, middles)
    new = adam(1, ints, floats, grad, own, (*direct, backs), new)
    loss = after(loss, new[0]) + ring[0] + ring[1] + ring[2]
    return (*new, jnp.sum(loss[0, : PLANES * SHARDS].reshape(PLANES, SHARDS), axis=1))


def per_device(pool_tokens, pool_targets, weight, first_moment, second_moment, *args):
    winner, tile_ids = args[0], args[4]
    if winner.shape[0] != PLANES or tile_ids.shape[1] != SLOTS or lax.axis_size("rep") != 2:
        return relayed(pool_tokens, pool_targets, weight, first_moment, second_moment, *args)
    code = route_code(winner)
    parts = pack(code, pool_tokens, pool_targets)
    ints, floats = gather_facts(beside(code), *args)
    own = (weight, first_moment, second_moment)
    plans = [functools.partial(run, plan) for plan in range(3)]
    return lax.switch(ints[PLAN], plans, ints, floats, parts, own)


def solution(mesh):
    in_specs = (
        P(("rep", "pop"), None, None),
        P(("rep", "pop"), None, None),
        P(("rep", "pop"), None, None),
        P(("rep", "pop"), None, None),
        P(("rep", "pop"), None, None),
        P("rep"),
        P("rep"),
        P("rep"),
        P("rep", None),
        P("rep", None),
        P("rep", None),
        P("rep", None),
    )
    out_specs = (
        P(("rep", "pop"), None, None),
        P(("rep", "pop"), None, None),
        P(("rep", "pop"), None, None),
        P("rep"),
    )
    return jax.shard_map(
        per_device, mesh=mesh, in_specs=in_specs, out_specs=out_specs, check_vma=False
    )
```

```python
import functools

import jax
import jax.numpy as jnp
from jax import lax
from jax.experimental import pallas as pl
from jax.experimental.pallas import tpu as pltpu
from jax.sharding import PartitionSpec as P

SHARDS = 4
TASKS = 8
SLOTS = 4
PLANES = 4


beta_one = 0.9
beta_two = 0.999
adam_eps = 1e-08
gelu_coef = 0.7978845608028654

SMEM = pl.BlockSpec(memory_space=pltpu.SMEM)
VMEM = pl.BlockSpec(memory_space=pltpu.VMEM)
ANY = pl.BlockSpec(memory_space=pl.ANY)
HBM = pl.BlockSpec(memory_space=pltpu.HBM)


def gelu_pair(pre):
    inner = jnp.tanh(gelu_coef * (pre + 0.044715 * pre * pre * pre))
    value = 0.5 * pre * (1.0 + inner)
    slope = 0.5 * (1.0 + inner) + 0.5 * pre * (1.0 - inner * inner) * gelu_coef * (
        1.0 + 3.0 * 0.044715 * pre * pre
    )
    return (value, slope)


def for_sending(shard):

    def short(part):
        return part.astype(jnp.bfloat16) if part.dtype == jnp.float32 else part

    return jax.tree.map(short, shard)


def relayed(
    pool_tokens,
    pool_targets,
    weight,
    first_moment,
    second_moment,
    winner,
    learn_rate,
    explore,
    task_weight,
    tile_ids,
    slot_task,
    slot_tokens,
):
    nodes = lax.axis_size("pop")
    place = lax.axis_index("pop")
    member = place // SHARDS
    shard = place % SHARDS
    members = winner.shape[0]
    slots = tile_ids.shape[1]
    tile = pool_tokens.shape[1]
    depth = pool_tokens.shape[2]
    width = weight.shape[2]
    hidden_all = pool_targets.shape[2]
    reach = tile // nodes
    flat_state = (
        weight.reshape(nodes, -1),
        first_moment.reshape(nodes, -1),
        second_moment.reshape(nodes, -1),
    )
    spread = (
        lax.all_to_all(flat_state[0], "pop", split_axis=0, concat_axis=0, tiled=True),
        lax.all_to_all(flat_state[1], "pop", split_axis=0, concat_axis=0, tiled=True),
        lax.all_to_all(flat_state[2], "pop", split_axis=0, concat_axis=0, tiled=True),
    )
    source_rows = (winner[:, None] * SHARDS + jnp.arange(SHARDS, dtype=jnp.int32)[None, :]).reshape(
        -1
    )
    picked_state = tuple((jnp.take(piece, source_rows, axis=0) for piece in spread))
    returned = jax.tree.map(
        lambda part, own: part.astype(own.dtype),
        lax.all_to_all(for_sending(picked_state), "pop", split_axis=0, concat_axis=0, tiled=True),
        picked_state,
    )
    start_weight = returned[0].reshape(depth, width)
    start_first = returned[1].reshape(depth, width)
    start_second = returned[2].reshape(depth, width)
    relay_tokens, relay_targets = (
        lax.all_to_all(pool_tokens, "pop", split_axis=1, concat_axis=0, tiled=True),
        lax.all_to_all(pool_targets, "pop", split_axis=1, concat_axis=0, tiled=True),
    )
    flat_ids = tile_ids.reshape(-1)
    pick_tokens = jnp.take(relay_tokens, flat_ids, axis=0).reshape(members, 1, slots, reach, depth)
    send_tokens = jnp.broadcast_to(pick_tokens, (members, SHARDS, slots, reach, depth)).reshape(
        nodes, slots, reach, depth
    )
    pick_targets = jnp.take(relay_targets, flat_ids, axis=0).reshape(
        members, slots, reach, hidden_all
    )
    send_targets = jnp.broadcast_to(
        pick_targets[:, None], (members, SHARDS, slots, reach, hidden_all)
    ).reshape(nodes, slots, reach, hidden_all)
    got_tokens, got_targets = (
        lax.all_to_all(send_tokens, "pop", split_axis=0, concat_axis=2, tiled=True),
        lax.all_to_all(send_targets, "pop", split_axis=0, concat_axis=2, tiled=True),
    )
    targets = lax.dynamic_slice_in_dim(got_targets[0], shard * width, width, 2).reshape(
        slots * tile, width
    )
    inputs = got_tokens.reshape(slots * tile, depth)
    tasks_here = lax.dynamic_index_in_dim(slot_task, member, 0, keepdims=False)
    lengths = lax.dynamic_index_in_dim(slot_tokens, member, 0, keepdims=False)
    source_member = lax.dynamic_index_in_dim(winner, member, 0, keepdims=False)
    onehot = tasks_here[:, None] == jnp.arange(TASKS, dtype=jnp.int32)[None, :]
    counts = jnp.sum(jnp.where(onehot, lengths[:, None], 0), axis=0)
    weights_here = lax.dynamic_index_in_dim(task_weight, source_member, 0, keepdims=False)
    scale = weights_here / jnp.maximum(counts, 1).astype(jnp.float32)
    per_slot = jnp.sum(jnp.where(onehot, scale[None, :], jnp.float32(0.0)), axis=1)
    live = jnp.arange(tile, dtype=jnp.int32)[None, :] < lengths[:, None]
    coef = jnp.where(live, per_slot[:, None], jnp.float32(0.0)).reshape(-1)
    own_rate = lax.dynamic_index_in_dim(learn_rate, source_member, 0, keepdims=False)
    own_explore = lax.dynamic_index_in_dim(explore, member, 0, keepdims=False)
    step_rate = own_rate * jnp.where(source_member != member, own_explore, jnp.float32(1.0))
    pre = jnp.dot(inputs, start_weight, preferred_element_type=jnp.float32)
    hidden, slope = gelu_pair(pre)
    diff = hidden - targets.astype(jnp.float32)
    part = jnp.sum(coef[:, None] * diff * diff)
    delta = (2.0 * coef[:, None] * diff * slope).astype(jnp.bfloat16)
    grad = lax.dot_general(
        inputs, delta, (((0,), (0,)), ((), ())), preferred_element_type=jnp.float32
    )
    first = beta_one * start_first.astype(jnp.float32) + (1.0 - beta_one) * grad
    second = beta_two * start_second.astype(jnp.float32) + (1.0 - beta_two) * grad * grad
    updated = start_weight.astype(jnp.float32) - step_rate * first / (jnp.sqrt(second) + adam_eps)
    share = jnp.where(jnp.arange(members, dtype=jnp.int32) == member, part, jnp.float32(0.0))
    member_loss = lax.psum(share, "pop")
    return (
        updated.astype(jnp.bfloat16)[None],
        first.astype(jnp.bfloat16)[None],
        second.astype(jnp.bfloat16)[None],
        member_loss,
    )


ENDS = ((0, 1), (1, 0), (2, 3), (3, 2))
MIDDLE = ((1, 2), (2, 1))


def position():
    place = lax.axis_index("pop")
    return place // SHARDS, lax.rem(place, SHARDS)


SHARED, TAKEN, HOPS, BY_ENDS, THEIR_ENDS, TO_ENDS, TO_MIDDLE, PLAN = range(8)
FOR_END, FOR_OWN, TOKENS, COUNTS = 16, 20, 24, 28
OWN, GUEST, PASSED = range(3)
RATE, TASK = 0, 4


def copied_from(winner):
    loser, source = jnp.int32(0), jnp.int32(0)
    for m in range(PLANES):
        taken = winner[m] != m
        loser = jnp.where(taken, m, loser)
        source = jnp.where(taken, winner[m], source)
    return loser, source


def route_kernel(winner, code):
    loser, source = copied_from(winner)
    code[...] = jnp.full(code.shape, source * PLANES + loser, jnp.int32)


def route_code(winner):
    return pl.pallas_call(
        route_kernel,
        out_shape=jax.ShapeDtypeStruct((8, 128), jnp.int32),
        in_specs=[SMEM],
        out_specs=VMEM,
        name="route_code",
    )(winner)


def on_route(route, m, to):
    source, loser = route
    upward = (to == m + 1) & (source <= m) & (loser >= to)
    return upward | ((to == m - 1) & (source >= m) & (loser <= to))


def by_ends(route):
    source, loser = route
    return jnp.where(source < loser, loser - 1, loser + 1) == (loser ^ 1)


def in_pool(t, m, k):
    ahead = t // SHARDS - m
    ahead = jnp.where(m == 1, ahead, -ahead)
    group = jnp.where(ahead == 0, 0, jnp.where(ahead == -1, 1, ahead + 1))
    return group * SHARDS + (lax.rem(t, SHARDS) ^ k)


def facts_kernel(
    other, winner, learn_rate, explore, task_weight, tile_ids, slot_task, slot_tokens, ints, floats
):
    m, k = position()
    loser, source = copied_from(winner)
    code = other[0, 0]
    mine = source, loser
    theirs = lax.div(code, jnp.int32(PLANES)), lax.rem(code, jnp.int32(PLANES))
    upward = jnp.maximum(mine[0], theirs[0]) < jnp.minimum(mine[1], theirs[1])
    downward = jnp.maximum(mine[1], theirs[1]) < jnp.minimum(mine[0], theirs[0])
    hops = jnp.abs(mine[0] - mine[1])
    long = jnp.maximum(hops, jnp.abs(theirs[0] - theirs[1])) == PLANES - 1
    shared = upward | downward | long
    taken = winner[m] != m

    def content(to):
        own = on_route(mine, m, to)
        guest = on_route(theirs, m, to) & jnp.logical_not(shared)
        first = jnp.where(own, jnp.where(m == mine[0], OWN, PASSED), -1)
        return jnp.where(guest, jnp.where(m == theirs[0], GUEST, PASSED), first)

    ints[SHARED] = shared.astype(jnp.int32)
    ints[TAKEN] = taken.astype(jnp.int32)
    ints[HOPS] = hops
    ints[PLAN] = jnp.where(long, 2, shared.astype(jnp.int32))
    ints[BY_ENDS] = by_ends(mine).astype(jnp.int32)
    ints[THEIR_ENDS] = by_ends(theirs).astype(jnp.int32)
    ints[TO_ENDS] = content(m ^ 1)
    ints[TO_MIDDLE] = content(jnp.where(m == 1, 2, jnp.where(m == 2, 1, -1)))
    end = jnp.where(m <= 1, 0, PLANES - 1)
    at_end = (m == 0) | (m == PLANES - 1)
    slots = tile_ids.shape[1]
    for s in range(slots):
        task = slot_task[m, s]
        count = jnp.int32(0)
        for o in range(slots):
            count = count + jnp.where(slot_task[m, o] == task, slot_tokens[m, o], 0)
        ints[FOR_END + s] = in_pool(tile_ids[end, s], m, k)
        ints[FOR_OWN + s] = jnp.where(at_end, -1, in_pool(tile_ids[m, s], m, k))
        ints[TOKENS + s] = slot_tokens[m, s]
        ints[COUNTS + s] = jnp.maximum(count, 1)
        floats[TASK + s] = task_weight[winner[m], task]
    floats[RATE] = learn_rate[winner[m]] * jnp.where(taken, explore[m], 1.0)


def gather_facts(other, *small):
    return pl.pallas_call(
        facts_kernel,
        out_shape=[jax.ShapeDtypeStruct((32,), jnp.int32), jax.ShapeDtypeStruct((8,), jnp.float32)],
        in_specs=[SMEM] * 8,
        out_specs=[SMEM, SMEM],
        name="gather_facts",
    )(other, *small)


def stage_kernel(t, has_guest, has_theirs, has_last, ints, *refs):
    state, refs = refs[:3], refs[3:]
    guest = refs[0] if has_guest else None
    from_ends, from_middle = refs[has_guest : has_guest + 2] if has_last else (None, None)
    to_ends, to_middle = refs[has_guest + 2 * has_last :][:2]
    sems = refs[-1]
    half = to_ends.shape[0]
    shared = ints[SHARED] == 1
    array = jnp.where(shared, (t - 1) // 2, t - 1)
    start = pl.multiple_of(jnp.where(shared, (t - 1) % 2, 0) * half, half)
    sides = ((to_ends, ints[TO_ENDS], from_middle), (to_middle, ints[TO_MIDDLE], from_ends))
    for n, (out, content, _) in enumerate(sides):
        for a, ref in enumerate(state):

            @pl.when((content == OWN) & (array == a))
            def _():
                pltpu.make_async_copy(ref.at[0, pl.ds(start, half)], out, sems.at[n]).start()

    if has_theirs:
        theirs = refs[has_guest + 2 * has_last + 2]

        @pl.when(ints[THEIR_ENDS] == 1)
        def _():
            copy_rows(from_ends, 0, theirs, 0, half)

        @pl.when(ints[THEIR_ENDS] == 0)
        def _():
            copy_rows(from_middle, 0, theirs, 0, half)

    for n, (out, content, passed) in enumerate(sides):
        if guest is not None:

            @pl.when(content == GUEST)
            def _():
                copy_rows(guest, 0, out, 0, half)

        if passed is not None:

            @pl.when(content == PASSED)
            def _():
                copy_rows(passed, 0, out, 0, half)

        @pl.when((content == OWN) & (array < len(state)))
        def _():
            pltpu.make_async_copy(state[0].at[0, pl.ds(0, half)], out, sems.at[n]).wait()


def stage(ints, step, own, guest, last, theirs):
    half, width = own[0].shape[1] // 2, own[0].shape[2]
    guests = () if guest is None else (guest,)
    kernel = functools.partial(stage_kernel, step, len(guests), theirs, len(last) > 0)
    return pl.pallas_call(
        kernel,
        out_shape=[jax.ShapeDtypeStruct((half, width), own[0].dtype)] * (2 + theirs),
        in_specs=[SMEM] + [ANY] * 3 + [VMEM] * (len(guests) + len(last)),
        out_specs=[VMEM] * (2 + theirs),
        scratch_shapes=[pltpu.SemaphoreType.DMA((2,))],
        compiler_params=pltpu.CompilerParams(vmem_limit_bytes=8 * 1024 * 1024),
        name="stage_chunk",
    )(ints, *own, *guests, *last)


def theirs_kernel(ints, from_ends, from_middle, theirs):
    @pl.when(ints[THEIR_ENDS] == 1)
    def _():
        copy_rows(from_ends, 0, theirs, 0, theirs.shape[0])

    @pl.when(ints[THEIR_ENDS] == 0)
    def _():
        copy_rows(from_middle, 0, theirs, 0, theirs.shape[0])


def theirs_of(ints, from_ends, from_middle):
    return pl.pallas_call(
        theirs_kernel,
        out_shape=jax.ShapeDtypeStruct(from_ends.shape, from_ends.dtype),
        in_specs=[SMEM] + [VMEM] * 2,
        out_specs=VMEM,
        compiler_params=pltpu.CompilerParams(vmem_limit_bytes=8 * 1024 * 1024),
        name="guest_chunk",
    )(ints, from_ends, from_middle)


def start_copies(ints, a, h, own, sent, out, sem):
    ends, middles, backs = sent
    shared, taken = ints[SHARED] == 1, ints[TAKEN] == 1
    half = out.shape[0]
    step = jnp.where(shared, 2 * a + h, a) + ints[HOPS]
    direct = taken & shared if h == 1 else taken

    def copy(ref):
        return pltpu.make_async_copy(ref, out, sem)

    @pl.when(jnp.logical_not(taken))
    def _():
        copy(own.at[0, pl.ds(h * half, half)]).start()

    sides = [
        (ends, direct & (ints[BY_ENDS] == 1)),
        (middles, direct & (ints[BY_ENDS] == 0)),
    ]
    if h == 1:
        sides.append((backs, taken & jnp.logical_not(shared)))
    for refs, here in sides:
        for n, ref in enumerate(refs):

            @pl.when(here & (step == n + 1))
            def _():
                copy(ref).start()

    return copy(own.at[0, pl.ds(h * half, half)])


def counts_of(sent):
    return tuple(len(refs) for refs in sent)


def sent_refs(counts, refs):
    a, b, c = counts
    return (refs[:a], refs[a : a + b], refs[a + b : a + b + c]), refs[a + b + c :]


def pack_kernel(code, tokens, targets, *parts):
    _, k = position()
    width = targets.shape[2] // SHARDS
    slim = tokens.shape[2] // SHARDS
    for j, part in enumerate(parts):
        q = k ^ j
        part[:, :width] = targets[0, :, pl.ds(pl.multiple_of(q * width, 128), width)]
        part[:, width:] = tokens[0, :, pl.ds(pl.multiple_of(q * slim, 128), slim)]


def pack(code, tokens, targets):
    tile = tokens.shape[1]
    row = (tokens.shape[2] + targets.shape[2]) // SHARDS
    return pl.pallas_call(
        pack_kernel,
        out_shape=[jax.ShapeDtypeStruct((tile, row), tokens.dtype)] * SHARDS,
        in_specs=[VMEM] * 3,
        out_specs=[VMEM] * SHARDS,
        name="pack_quarters",
    )(code, tokens, targets)


def copy_rows(ref, start, out, at, count, columns=slice(None)):
    step = 32

    def body(i, _):
        rows = pl.ds(pl.multiple_of(at + i * step, step), step)
        out[rows, :] = ref[pl.ds(pl.multiple_of(start + i * step, step), step), columns]
        return 0

    lax.fori_loop(0, count // step, body, 0, unroll=True if count <= 64 else 4)


def split_kernel(one, two, three, *halves):
    count = one.shape[0] // 2
    for h, half in enumerate(halves):
        for n, part in enumerate((one, two, three)):
            copy_rows(part, h * count, half, n * count, count)


def split_rows(parts):
    tile, row = parts[0].shape
    half = jax.ShapeDtypeStruct((len(parts) * tile // 2, row), parts[0].dtype)
    return pl.pallas_call(
        split_kernel,
        out_shape=[half, half],
        in_specs=[VMEM] * len(parts),
        out_specs=[VMEM, VMEM],
        compiler_params=pltpu.CompilerParams(vmem_limit_bytes=8 * 1024 * 1024),
        name="split_rows",
    )(*parts)


def piece(pool, which, h):
    group, j = divmod(which, SHARDS)
    whole, halves = pool[group]
    rows = whole.shape[0] // 2
    return (whole, h * rows, rows) if j == 0 else (halves[h], (j - 1) * rows, rows)


def grouped(refs, halves):
    size = 1 + len(halves)
    pool = []
    for g in range(PLANES):
        group = refs[g * size : (g + 1) * size]
        pool.append((group[0], dict(zip(halves, group[1:]))))
    return pool, refs[PLANES * size :]


def pick_for_end_kernel(h, ints, *refs):
    pool, (out,) = grouped(refs, (h,))

    def slot(s, _):
        place = ints[FOR_END + s]
        for which in range(PLANES * SHARDS):
            ref, start, rows = piece(pool, which, h)

            @pl.when(place == which)
            def _():
                copy_rows(ref, start, out, s * rows, rows)

        return 0

    lax.fori_loop(0, SLOTS, slot, 0)


def pick_for_end(h, ints, pool):
    tile, row = pool[0][0].shape
    operands = [x for whole, halves in pool for x in (whole, halves[h])]
    return pl.pallas_call(
        functools.partial(pick_for_end_kernel, h),
        out_shape=jax.ShapeDtypeStruct((SLOTS * tile // 2, row), operands[0].dtype),
        in_specs=[SMEM] + [VMEM] * len(operands),
        out_specs=VMEM,
        compiler_params=pltpu.CompilerParams(vmem_limit_bytes=16 * 1024 * 1024),
        name="pick_for_end",
    )(ints, *operands)


def pick_own_kernel(ints, *refs):
    pool, (handed_a, handed_b, quarter, targets) = grouped(refs, (0, 1))
    handed = (handed_a, handed_b)
    width = targets.shape[1]
    half = quarter.shape[0] // SLOTS // 2

    def slot(s, _):
        place = ints[FOR_OWN + s]
        for h in range(2):
            at = (2 * s + h) * half

            @pl.when(place < 0)
            def _():
                start = pl.multiple_of(s * half, half)
                copy_rows(handed[h], start, targets, at, half, slice(0, width))
                copy_rows(handed[h], start, quarter, at, half, slice(width, None))

            for which in range(PLANES * SHARDS):
                ref, start, rows = piece(pool, which, h)

                @pl.when(place == which)
                def _():
                    copy_rows(ref, start, targets, at, rows, slice(0, width))
                    copy_rows(ref, start, quarter, at, rows, slice(width, None))

        return 0

    lax.fori_loop(0, SLOTS, slot, 0)


def pick_own(ints, pool, handed, width):
    rows, row = handed[0].shape
    operands = [x for whole, halves in pool for x in (whole, *halves)]
    return pl.pallas_call(
        pick_own_kernel,
        out_shape=[
            jax.ShapeDtypeStruct((2 * rows, row - width), handed[0].dtype),
            jax.ShapeDtypeStruct((2 * rows, width), handed[0].dtype),
        ],
        in_specs=[SMEM] + [VMEM] * (len(operands) + 2),
        out_specs=[VMEM, VMEM],
        compiler_params=pltpu.CompilerParams(vmem_limit_bytes=16 * 1024 * 1024),
        name="pick_own",
    )(ints, *operands, *handed)


def grad_kernel(counts, ints, floats, in0, in1, in2, in3, targets, own_w, *refs):
    sent, (grad, loss, w_buf, delta, sem) = sent_refs(counts, refs)
    m, k = position()
    half = w_buf.shape[0] // 2
    copies = [
        start_copies(ints, 0, h, own_w, sent, w_buf.at[pl.ds(h * half, half)], sem.at[h])
        for h in range(2)
    ]
    tile = in0.shape[0] // SLOTS
    slim = in0.shape[1]
    ins = (in0, in1, in2, in3)
    for copy in copies:
        copy.wait()

    def slot(s, total):
        span = pl.ds(pl.multiple_of(s * tile, tile), tile)
        pre = None
        for j in range(SHARDS):
            at = pl.ds(pl.multiple_of((k ^ j) * slim, slim), slim)
            one = jnp.dot(ins[j][span, :], w_buf[at, :], preferred_element_type=jnp.float32)
            pre = one if pre is None else pre + one
        live = lax.broadcasted_iota(jnp.int32, pre.shape, 0) < ints[TOKENS + s]
        many = jnp.full(pre.shape, ints[COUNTS + s], jnp.int32).astype(jnp.float32)
        coef = jnp.where(live, floats[TASK + s] / many, 0.0)
        hidden, slope = gelu_pair(pre)
        diff = hidden - targets[span, :].astype(jnp.float32)
        scaled = coef * diff
        delta[span, :] = (2.0 * scaled * slope).astype(jnp.bfloat16)
        return total + jnp.sum(scaled * diff, keepdims=True)

    total = lax.fori_loop(0, SLOTS, slot, jnp.zeros((1, 1), jnp.float32))
    lane = lax.broadcasted_iota(jnp.int32, loss.shape, 1)
    loss[...] = jnp.where(lane == m * SHARDS + k, total, 0.0)
    for j in range(SHARDS):
        at = pl.ds(pl.multiple_of((k ^ j) * slim, slim), slim)
        grad[at, :] = lax.dot_general(
            ins[j][...], delta[...], (((0,), (0,)), ((), ())), preferred_element_type=jnp.float32
        )


def gradient(ints, floats, ins, targets, own_w, sent):
    rows, width = targets.shape
    depth = own_w.shape[1]
    return pl.pallas_call(
        functools.partial(grad_kernel, counts_of(sent)),
        out_shape=[
            jax.ShapeDtypeStruct((depth, width), jnp.float32),
            jax.ShapeDtypeStruct((8, 128), jnp.float32),
        ],
        in_specs=[SMEM] * 2 + [VMEM] * 5 + [ANY] * (1 + sum(counts_of(sent))),
        out_specs=[VMEM, VMEM],
        scratch_shapes=[
            pltpu.VMEM((depth, width), own_w.dtype),
            pltpu.VMEM((rows, width), jnp.bfloat16),
            pltpu.SemaphoreType.DMA((2,)),
        ],
        compiler_params=pltpu.CompilerParams(vmem_limit_bytes=16 * 1024 * 1024),
        name="forward_and_gradient",
    )(ints, floats, *ins, targets, own_w, *sent[0], *sent[1], *sent[2])


def adam_kernel(h, counts, ints, floats, grad, *refs):
    own, (sent, refs) = refs[:3], sent_refs(counts, refs[3:])
    new, bufs, outs, (in_sem, out_sem) = refs[-11:-8], refs[-8:-5], refs[-5:-2], refs[-2:]
    blocks = out_sem.shape[1]
    rows = bufs[0].shape[0]
    step = rows // blocks
    here = h * rows

    def result(i, b):
        return pltpu.make_async_copy(
            outs[i].at[pl.ds(b * step, step)],
            new[i].at[0, pl.ds(here + b * step, step)],
            out_sem.at[i, b],
        )

    copies = [
        start_copies(ints, a, h, own[a], sent, bufs[a], in_sem.at[a]) for a in range(3)
    ]
    rate = floats[RATE]
    for copy in copies:
        copy.wait()
    for b in range(blocks):

        def body(n, _):
            at = pl.ds(pl.multiple_of(b * step + n * 16, 16), 16)
            g = grad[pl.ds(pl.multiple_of(here + b * step + n * 16, 16), 16), :]
            first = beta_one * bufs[1][at, :].astype(jnp.float32) + (1.0 - beta_one) * g
            second = beta_two * bufs[2][at, :].astype(jnp.float32) + (1.0 - beta_two) * g * g
            start = bufs[0][at, :].astype(jnp.float32)
            updated = start - rate * first / (jnp.sqrt(second) + adam_eps)
            outs[0][at, :] = updated.astype(outs[0].dtype)
            outs[1][at, :] = first.astype(outs[1].dtype)
            outs[2][at, :] = second.astype(outs[2].dtype)
            return 0

        lax.fori_loop(0, step // 16, body, 0, unroll=2)
        for i in range(3):
            result(i, b).start()
    for b in range(blocks):
        for i in range(3):
            result(i, b).wait()


def adam(h, ints, floats, grad, own, sent, begun=()):
    depth, width = grad.shape
    blocks = 2
    taken = sum(counts_of(sent))
    own = [pltpu.with_memory_space_constraint(x, pltpu.HBM) for x in own]
    sent = [
        [pltpu.with_memory_space_constraint(x, pltpu.HBM) for x in refs[:-1]] + list(refs[-1:])
        for refs in sent
    ]
    return pl.pallas_call(
        functools.partial(adam_kernel, h, counts_of(sent)),
        out_shape=[pltpu.HBM(x.shape, x.dtype) for x in own],
        in_specs=[SMEM] * 2 + [VMEM] + [ANY] * (3 + taken) + [HBM] * len(begun),
        out_specs=[HBM] * 3,
        scratch_shapes=[pltpu.VMEM((depth // 2, width), x.dtype) for x in own] * 2
        + [pltpu.SemaphoreType.DMA((3,)), pltpu.SemaphoreType.DMA((3, blocks))],
        input_output_aliases={6 + taken + i: i for i in range(len(begun))},
        compiler_params=pltpu.CompilerParams(vmem_limit_bytes=16 * 1024 * 1024),
        name="adam_half",
    )(ints, floats, grad, *own, *sent[0], *sent[1], *sent[2], *begun)


def in_plane(x, j):
    pairs = [(m * SHARDS + k, m * SHARDS + (k ^ j)) for m in range(PLANES) for k in range(SHARDS)]
    return lax.ppermute(x, "pop", pairs)


def along(x, hops):
    idle = [m for m in range(PLANES) if all(m not in hop for hop in hops)]
    pairs = [(a * SHARDS + k, b * SHARDS + k) for a, b in hops for k in range(SHARDS)]
    pairs += [(m * SHARDS + k, m * SHARDS + (k ^ 1)) for m in idle for k in range(SHARDS)]
    return lax.ppermute(x, "pop", pairs)


def beside(x):
    return lax.ppermute(x, "rep", [(0, 1), (1, 0)])


def after(x, *others):
    return lax.optimization_barrier((x, *others))[0]


def tiles(here, ints, width):
    near0, middle0, (here0, halves) = here
    near = [along(x, ENDS) for x in halves]
    middle = [along(x, MIDDLE) for x in halves]
    far0 = along(near0, MIDDLE)
    far_a = along(near[0], MIDDLE)
    far = [far_a, along(after(near[1], far_a), MIDDLE)]
    pool = [(here0, halves), (near0, near), (middle0, middle), (far0, far)]
    picked = [pick_for_end(h, ints, pool) for h in range(2)]
    handed = [along(picked[0], ENDS), along(picked[1], ENDS)]
    quarter, targets = pick_own(ints, pool, handed, width)
    side = in_plane(quarter, 1)
    cross = in_plane(quarter, 2)
    gates = [halves, (near, middle), picked[0], (picked[1], handed[0]), handed[1], quarter]
    return gates, (quarter, side, cross, in_plane(cross, 1)), targets


def state_steps(ints, own, gates, steps, returns, grad_step, gradient_of):
    half = own[0].shape[1] // 2
    guests = [beside(x[0, half:]) for x in own] if returns else []
    last, ends, middles, backs = (), [], [], []
    grad = None
    for t in range(1, steps + 1):
        if t == grad_step:
            grad = gradient_of(ends, middles, backs)
            gates = [*gates[: t - 1], grad[0]]
        guest = guests[t - 1] if t <= len(guests) else None
        theirs = 1 < t <= returns + 1
        gate = (gates[t - 1 : t], backs)
        facts = after(ints, gate) if jax.tree.leaves(gate) else ints
        to_ends, to_middle, *brought = stage(facts, t, own, guest, last, theirs)
        backs += [beside(x) for x in brought]
        last = (along(to_ends, ENDS), along(to_middle, MIDDLE))
        ends.append(last[0])
        middles.append(last[1])
    if len(backs) < returns:
        backs.append(beside(theirs_of(after(ints, (backs, gates[-1])), *last)))
    return ends, middles, backs, gradient_of(ends, middles, backs) if grad is None else grad


def run(plan, ints, floats, parts, own):
    near0, middle0 = along(parts[0], ENDS), along(parts[0], MIDDLE)
    swapped = [in_plane(parts[j], j) for j in range(1, SHARDS)]
    by_both = plan == 0
    halves = split_rows(after(swapped, near0, middle0) if by_both else swapped)
    here = (near0, middle0, (parts[0], halves))
    gates, ins, targets = tiles(here, ints, own[0].shape[2])
    first = 2 + plan

    def gradient_of(ends, middles, backs):
        sent = (ends[:first], middles[:first], backs[:first])
        return gradient(ints, floats, ins, targets, own[0], sent)

    if by_both:
        moved = state_steps(ints, own, gates, 4, 4, 0, gradient_of)
    else:
        gates = [(), (near0, middle0, halves), *gates[1:]]
        moved = state_steps(ints, own, gates, 6 + plan, 0, 7, gradient_of)
    ends, middles, backs, (grad, loss) = moved
    round_one = [in_plane(loss, j) for j in range(1, SHARDS)]
    early = slice(None) if by_both else slice(-1)
    new = adam(0, ints, floats, grad, own, (ends[early], middles[early], []))
    loss = after(loss, new[0])
    loss = loss + round_one[0] + round_one[1] + round_one[2]
    ring = [along(loss, [(m, (m + d) % PLANES) for m in range(PLANES)]) for d in range(1, PLANES)]
    direct = ([], []) if by_both else (ends, middles)
    new = adam(1, ints, floats, grad, own, (*direct, backs), new)
    loss = after(loss, new[0]) + ring[0] + ring[1] + ring[2]
    return (*new, jnp.sum(loss[0, : PLANES * SHARDS].reshape(PLANES, SHARDS), axis=1))


def per_device(pool_tokens, pool_targets, weight, first_moment, second_moment, *args):
    winner, tile_ids = args[0], args[4]
    if winner.shape[0] != PLANES or tile_ids.shape[1] != SLOTS or lax.axis_size("rep") != 2:
        return relayed(pool_tokens, pool_targets, weight, first_moment, second_moment, *args)
    code = route_code(winner)
    parts = pack(code, pool_tokens, pool_targets)
    ints, floats = gather_facts(beside(code), *args)
    own = (weight, first_moment, second_moment)
    plans = [functools.partial(run, plan) for plan in range(3)]
    return lax.switch(ints[PLAN], plans, ints, floats, parts, own)


def solution(mesh):
    in_specs = (
        P(("rep", "pop"), None, None),
        P(("rep", "pop"), None, None),
        P(("rep", "pop"), None, None),
        P(("rep", "pop"), None, None),
        P(("rep", "pop"), None, None),
        P("rep"),
        P("rep"),
        P("rep"),
        P("rep", None),
        P("rep", None),
        P("rep", None),
        P("rep", None),
    )
    out_specs = (
        P(("rep", "pop"), None, None),
        P(("rep", "pop"), None, None),
        P(("rep", "pop"), None, None),
        P("rep"),
    )
    return jax.shard_map(
        per_device, mesh=mesh, in_specs=in_specs, out_specs=out_specs, check_vma=False
    )
```

```python
import functools

import jax
import jax.numpy as jnp
from jax import lax
from jax.experimental import pallas as pl
from jax.experimental.pallas import tpu as pltpu
from jax.sharding import PartitionSpec as P

SHARDS = 4
TASKS = 8
SLOTS = 4
PLANES = 4


beta_one = 0.9
beta_two = 0.999
adam_eps = 1e-08
gelu_coef = 0.7978845608028654

SMEM = pl.BlockSpec(memory_space=pltpu.SMEM)
VMEM = pl.BlockSpec(memory_space=pltpu.VMEM)
ANY = pl.BlockSpec(memory_space=pl.ANY)
HBM = pl.BlockSpec(memory_space=pltpu.HBM)


def gelu_pair(pre):
    inner = jnp.tanh(gelu_coef * (pre + 0.044715 * pre * pre * pre))
    value = 0.5 * pre * (1.0 + inner)
    slope = 0.5 * (1.0 + inner) + 0.5 * pre * (1.0 - inner * inner) * gelu_coef * (
        1.0 + 3.0 * 0.044715 * pre * pre
    )
    return (value, slope)


def for_sending(shard):

    def short(part):
        return part.astype(jnp.bfloat16) if part.dtype == jnp.float32 else part

    return jax.tree.map(short, shard)


def relayed(
    pool_tokens,
    pool_targets,
    weight,
    first_moment,
    second_moment,
    winner,
    learn_rate,
    explore,
    task_weight,
    tile_ids,
    slot_task,
    slot_tokens,
):
    nodes = lax.axis_size("pop")
    place = lax.axis_index("pop")
    member = place // SHARDS
    shard = place % SHARDS
    members = winner.shape[0]
    slots = tile_ids.shape[1]
    tile = pool_tokens.shape[1]
    depth = pool_tokens.shape[2]
    width = weight.shape[2]
    hidden_all = pool_targets.shape[2]
    reach = tile // nodes
    flat_state = (
        weight.reshape(nodes, -1),
        first_moment.reshape(nodes, -1),
        second_moment.reshape(nodes, -1),
    )
    spread = (
        lax.all_to_all(flat_state[0], "pop", split_axis=0, concat_axis=0, tiled=True),
        lax.all_to_all(flat_state[1], "pop", split_axis=0, concat_axis=0, tiled=True),
        lax.all_to_all(flat_state[2], "pop", split_axis=0, concat_axis=0, tiled=True),
    )
    source_rows = (winner[:, None] * SHARDS + jnp.arange(SHARDS, dtype=jnp.int32)[None, :]).reshape(
        -1
    )
    picked_state = tuple((jnp.take(piece, source_rows, axis=0) for piece in spread))
    returned = jax.tree.map(
        lambda part, own: part.astype(own.dtype),
        lax.all_to_all(for_sending(picked_state), "pop", split_axis=0, concat_axis=0, tiled=True),
        picked_state,
    )
    start_weight = returned[0].reshape(depth, width)
    start_first = returned[1].reshape(depth, width)
    start_second = returned[2].reshape(depth, width)
    relay_tokens, relay_targets = (
        lax.all_to_all(pool_tokens, "pop", split_axis=1, concat_axis=0, tiled=True),
        lax.all_to_all(pool_targets, "pop", split_axis=1, concat_axis=0, tiled=True),
    )
    flat_ids = tile_ids.reshape(-1)
    pick_tokens = jnp.take(relay_tokens, flat_ids, axis=0).reshape(members, 1, slots, reach, depth)
    send_tokens = jnp.broadcast_to(pick_tokens, (members, SHARDS, slots, reach, depth)).reshape(
        nodes, slots, reach, depth
    )
    pick_targets = jnp.take(relay_targets, flat_ids, axis=0).reshape(
        members, slots, reach, hidden_all
    )
    send_targets = jnp.broadcast_to(
        pick_targets[:, None], (members, SHARDS, slots, reach, hidden_all)
    ).reshape(nodes, slots, reach, hidden_all)
    got_tokens, got_targets = (
        lax.all_to_all(send_tokens, "pop", split_axis=0, concat_axis=2, tiled=True),
        lax.all_to_all(send_targets, "pop", split_axis=0, concat_axis=2, tiled=True),
    )
    targets = lax.dynamic_slice_in_dim(got_targets[0], shard * width, width, 2).reshape(
        slots * tile, width
    )
    inputs = got_tokens.reshape(slots * tile, depth)
    tasks_here = lax.dynamic_index_in_dim(slot_task, member, 0, keepdims=False)
    lengths = lax.dynamic_index_in_dim(slot_tokens, member, 0, keepdims=False)
    source_member = lax.dynamic_index_in_dim(winner, member, 0, keepdims=False)
    onehot = tasks_here[:, None] == jnp.arange(TASKS, dtype=jnp.int32)[None, :]
    counts = jnp.sum(jnp.where(onehot, lengths[:, None], 0), axis=0)
    weights_here = lax.dynamic_index_in_dim(task_weight, source_member, 0, keepdims=False)
    scale = weights_here / jnp.maximum(counts, 1).astype(jnp.float32)
    per_slot = jnp.sum(jnp.where(onehot, scale[None, :], jnp.float32(0.0)), axis=1)
    live = jnp.arange(tile, dtype=jnp.int32)[None, :] < lengths[:, None]
    coef = jnp.where(live, per_slot[:, None], jnp.float32(0.0)).reshape(-1)
    own_rate = lax.dynamic_index_in_dim(learn_rate, source_member, 0, keepdims=False)
    own_explore = lax.dynamic_index_in_dim(explore, member, 0, keepdims=False)
    step_rate = own_rate * jnp.where(source_member != member, own_explore, jnp.float32(1.0))
    pre = jnp.dot(inputs, start_weight, preferred_element_type=jnp.float32)
    hidden, slope = gelu_pair(pre)
    diff = hidden - targets.astype(jnp.float32)
    part = jnp.sum(coef[:, None] * diff * diff)
    delta = (2.0 * coef[:, None] * diff * slope).astype(jnp.bfloat16)
    grad = lax.dot_general(
        inputs, delta, (((0,), (0,)), ((), ())), preferred_element_type=jnp.float32
    )
    first = beta_one * start_first.astype(jnp.float32) + (1.0 - beta_one) * grad
    second = beta_two * start_second.astype(jnp.float32) + (1.0 - beta_two) * grad * grad
    updated = start_weight.astype(jnp.float32) - step_rate * first / (jnp.sqrt(second) + adam_eps)
    share = jnp.where(jnp.arange(members, dtype=jnp.int32) == member, part, jnp.float32(0.0))
    member_loss = lax.psum(share, "pop")
    return (
        updated.astype(jnp.bfloat16)[None],
        first.astype(jnp.bfloat16)[None],
        second.astype(jnp.bfloat16)[None],
        member_loss,
    )


ENDS = ((0, 1), (1, 0), (2, 3), (3, 2))
MIDDLE = ((1, 2), (2, 1))


def position():
    place = lax.axis_index("pop")
    return place // SHARDS, lax.rem(place, SHARDS)


SHARED, TAKEN, HOPS, BY_ENDS, THEIR_ENDS, TO_ENDS, TO_MIDDLE, PLAN = range(8)
FOR_END, FOR_OWN, TOKENS, COUNTS = 16, 20, 24, 28
OWN, GUEST, PASSED = range(3)
RATE, TASK = 0, 4


def copied_from(winner):
    loser, source = jnp.int32(0), jnp.int32(0)
    for m in range(PLANES):
        taken = winner[m] != m
        loser = jnp.where(taken, m, loser)
        source = jnp.where(taken, winner[m], source)
    return loser, source


def route_kernel(winner, code):
    loser, source = copied_from(winner)
    code[...] = jnp.full(code.shape, source * PLANES + loser, jnp.int32)


def route_code(winner):
    return pl.pallas_call(
        route_kernel,
        out_shape=jax.ShapeDtypeStruct((8, 128), jnp.int32),
        in_specs=[SMEM],
        out_specs=VMEM,
        name="route_code",
    )(winner)


def on_route(route, m, to):
    source, loser = route
    upward = (to == m + 1) & (source <= m) & (loser >= to)
    return upward | ((to == m - 1) & (source >= m) & (loser <= to))


def by_ends(route):
    source, loser = route
    return jnp.where(source < loser, loser - 1, loser + 1) == (loser ^ 1)


def in_pool(t, m, k):
    ahead = t // SHARDS - m
    ahead = jnp.where(m == 1, ahead, -ahead)
    group = jnp.where(ahead == 0, 0, jnp.where(ahead == -1, 1, ahead + 1))
    return group * SHARDS + (lax.rem(t, SHARDS) ^ k)


def facts_kernel(
    other, winner, learn_rate, explore, task_weight, tile_ids, slot_task, slot_tokens, ints, floats
):
    m, k = position()
    loser, source = copied_from(winner)
    code = other[0, 0]
    mine = source, loser
    theirs = lax.div(code, jnp.int32(PLANES)), lax.rem(code, jnp.int32(PLANES))
    upward = jnp.maximum(mine[0], theirs[0]) < jnp.minimum(mine[1], theirs[1])
    downward = jnp.maximum(mine[1], theirs[1]) < jnp.minimum(mine[0], theirs[0])
    hops = jnp.abs(mine[0] - mine[1])
    long = jnp.maximum(hops, jnp.abs(theirs[0] - theirs[1])) == PLANES - 1
    shared = upward | downward | long
    taken = winner[m] != m

    def content(to):
        own = on_route(mine, m, to)
        guest = on_route(theirs, m, to) & jnp.logical_not(shared)
        first = jnp.where(own, jnp.where(m == mine[0], OWN, PASSED), -1)
        return jnp.where(guest, jnp.where(m == theirs[0], GUEST, PASSED), first)

    ints[SHARED] = shared.astype(jnp.int32)
    ints[TAKEN] = taken.astype(jnp.int32)
    ints[HOPS] = hops
    ints[PLAN] = jnp.where(long, 2, shared.astype(jnp.int32))
    ints[BY_ENDS] = by_ends(mine).astype(jnp.int32)
    ints[THEIR_ENDS] = by_ends(theirs).astype(jnp.int32)
    ints[TO_ENDS] = content(m ^ 1)
    ints[TO_MIDDLE] = content(jnp.where(m == 1, 2, jnp.where(m == 2, 1, -1)))
    end = jnp.where(m <= 1, 0, PLANES - 1)
    at_end = (m == 0) | (m == PLANES - 1)
    slots = tile_ids.shape[1]
    for s in range(slots):
        task = slot_task[m, s]
        count = jnp.int32(0)
        for o in range(slots):
            count = count + jnp.where(slot_task[m, o] == task, slot_tokens[m, o], 0)
        ints[FOR_END + s] = in_pool(tile_ids[end, s], m, k)
        ints[FOR_OWN + s] = jnp.where(at_end, -1, in_pool(tile_ids[m, s], m, k))
        ints[TOKENS + s] = slot_tokens[m, s]
        ints[COUNTS + s] = jnp.maximum(count, 1)
        floats[TASK + s] = task_weight[winner[m], task]
    floats[RATE] = learn_rate[winner[m]] * jnp.where(taken, explore[m], 1.0)


def gather_facts(other, *small):
    return pl.pallas_call(
        facts_kernel,
        out_shape=[jax.ShapeDtypeStruct((32,), jnp.int32), jax.ShapeDtypeStruct((8,), jnp.float32)],
        in_specs=[SMEM] * 8,
        out_specs=[SMEM, SMEM],
        name="gather_facts",
    )(other, *small)


def stage_kernel(t, has_guest, has_theirs, has_last, ints, *refs):
    state, refs = refs[:3], refs[3:]
    guest = refs[0] if has_guest else None
    from_ends, from_middle = refs[has_guest : has_guest + 2] if has_last else (None, None)
    to_ends, to_middle = refs[has_guest + 2 * has_last :][:2]
    sems = refs[-1]
    half = to_ends.shape[0]
    shared = ints[SHARED] == 1
    array = jnp.where(shared, (t - 1) // 2, t - 1)
    start = pl.multiple_of(jnp.where(shared, (t - 1) % 2, 0) * half, half)
    sides = ((to_ends, ints[TO_ENDS], from_middle), (to_middle, ints[TO_MIDDLE], from_ends))
    for n, (out, content, _) in enumerate(sides):
        for a, ref in enumerate(state):

            @pl.when((content == OWN) & (array == a))
            def _():
                pltpu.make_async_copy(ref.at[0, pl.ds(start, half)], out, sems.at[n]).start()

    if has_theirs:
        theirs = refs[has_guest + 2 * has_last + 2]

        @pl.when(ints[THEIR_ENDS] == 1)
        def _():
            copy_rows(from_ends, 0, theirs, 0, half)

        @pl.when(ints[THEIR_ENDS] == 0)
        def _():
            copy_rows(from_middle, 0, theirs, 0, half)

    for n, (out, content, passed) in enumerate(sides):
        if guest is not None:

            @pl.when(content == GUEST)
            def _():
                copy_rows(guest, 0, out, 0, half)

        if passed is not None:

            @pl.when(content == PASSED)
            def _():
                copy_rows(passed, 0, out, 0, half)

        @pl.when((content == OWN) & (array < len(state)))
        def _():
            pltpu.make_async_copy(state[0].at[0, pl.ds(0, half)], out, sems.at[n]).wait()


def stage(ints, step, own, guest, last, theirs):
    half, width = own[0].shape[1] // 2, own[0].shape[2]
    guests = () if guest is None else (guest,)
    kernel = functools.partial(stage_kernel, step, len(guests), theirs, len(last) > 0)
    return pl.pallas_call(
        kernel,
        out_shape=[jax.ShapeDtypeStruct((half, width), own[0].dtype)] * (2 + theirs),
        in_specs=[SMEM] + [ANY] * 3 + [VMEM] * (len(guests) + len(last)),
        out_specs=[VMEM] * (2 + theirs),
        scratch_shapes=[pltpu.SemaphoreType.DMA((2,))],
        compiler_params=pltpu.CompilerParams(vmem_limit_bytes=8 * 1024 * 1024),
        name="stage_chunk",
    )(ints, *own, *guests, *last)


def theirs_kernel(ints, from_ends, from_middle, theirs):
    @pl.when(ints[THEIR_ENDS] == 1)
    def _():
        copy_rows(from_ends, 0, theirs, 0, theirs.shape[0])

    @pl.when(ints[THEIR_ENDS] == 0)
    def _():
        copy_rows(from_middle, 0, theirs, 0, theirs.shape[0])


def theirs_of(ints, from_ends, from_middle):
    return pl.pallas_call(
        theirs_kernel,
        out_shape=jax.ShapeDtypeStruct(from_ends.shape, from_ends.dtype),
        in_specs=[SMEM] + [VMEM] * 2,
        out_specs=VMEM,
        compiler_params=pltpu.CompilerParams(vmem_limit_bytes=8 * 1024 * 1024),
        name="guest_chunk",
    )(ints, from_ends, from_middle)


def start_copies(ints, a, h, own, sent, out, sem):
    ends, middles, backs = sent
    shared, taken = ints[SHARED] == 1, ints[TAKEN] == 1
    half = out.shape[0]
    step = jnp.where(shared, 2 * a + h, a) + ints[HOPS]
    direct = taken & shared if h == 1 else taken

    def copy(ref):
        return pltpu.make_async_copy(ref, out, sem)

    @pl.when(jnp.logical_not(taken))
    def _():
        copy(own.at[0, pl.ds(h * half, half)]).start()

    sides = [
        (ends, direct & (ints[BY_ENDS] == 1)),
        (middles, direct & (ints[BY_ENDS] == 0)),
    ]
    if h == 1:
        sides.append((backs, taken & jnp.logical_not(shared)))
    for refs, here in sides:
        for n, ref in enumerate(refs):

            @pl.when(here & (step == n + 1))
            def _():
                copy(ref).start()

    return copy(own.at[0, pl.ds(h * half, half)])


def counts_of(sent):
    return tuple(len(refs) for refs in sent)


def sent_refs(counts, refs):
    a, b, c = counts
    return (refs[:a], refs[a : a + b], refs[a + b : a + b + c]), refs[a + b + c :]


def pack_kernel(code, tokens, targets, *parts):
    _, k = position()
    width = targets.shape[2] // SHARDS
    slim = tokens.shape[2] // SHARDS
    for j, part in enumerate(parts):
        q = k ^ j
        part[:, :width] = targets[0, :, pl.ds(pl.multiple_of(q * width, 128), width)]
        part[:, width:] = tokens[0, :, pl.ds(pl.multiple_of(q * slim, 128), slim)]


def pack(code, tokens, targets):
    tile = tokens.shape[1]
    row = (tokens.shape[2] + targets.shape[2]) // SHARDS
    return pl.pallas_call(
        pack_kernel,
        out_shape=[jax.ShapeDtypeStruct((tile, row), tokens.dtype)] * SHARDS,
        in_specs=[VMEM] * 3,
        out_specs=[VMEM] * SHARDS,
        name="pack_quarters",
    )(code, tokens, targets)


def copy_rows(ref, start, out, at, count, columns=slice(None)):
    step = 32

    def body(i, _):
        rows = pl.ds(pl.multiple_of(at + i * step, step), step)
        out[rows, :] = ref[pl.ds(pl.multiple_of(start + i * step, step), step), columns]
        return 0

    lax.fori_loop(0, count // step, body, 0, unroll=True if count <= 64 else 4)


def split_kernel(one, two, three, *halves):
    count = one.shape[0] // 2
    for h, half in enumerate(halves):
        for n, part in enumerate((one, two, three)):
            copy_rows(part, h * count, half, n * count, count)


def split_rows(parts):
    tile, row = parts[0].shape
    half = jax.ShapeDtypeStruct((len(parts) * tile // 2, row), parts[0].dtype)
    return pl.pallas_call(
        split_kernel,
        out_shape=[half, half],
        in_specs=[VMEM] * len(parts),
        out_specs=[VMEM, VMEM],
        compiler_params=pltpu.CompilerParams(vmem_limit_bytes=8 * 1024 * 1024),
        name="split_rows",
    )(*parts)


def piece(pool, which, h):
    group, j = divmod(which, SHARDS)
    whole, halves = pool[group]
    rows = whole.shape[0] // 2
    return (whole, h * rows, rows) if j == 0 else (halves[h], (j - 1) * rows, rows)


def grouped(refs, halves):
    size = 1 + len(halves)
    pool = []
    for g in range(PLANES):
        group = refs[g * size : (g + 1) * size]
        pool.append((group[0], dict(zip(halves, group[1:]))))
    return pool, refs[PLANES * size :]


def pick_for_end_kernel(h, ints, *refs):
    pool, (out,) = grouped(refs, (h,))

    def slot(s, _):
        place = ints[FOR_END + s]
        for which in range(PLANES * SHARDS):
            ref, start, rows = piece(pool, which, h)

            @pl.when(place == which)
            def _():
                copy_rows(ref, start, out, s * rows, rows)

        return 0

    lax.fori_loop(0, SLOTS, slot, 0)


def pick_for_end(h, ints, pool):
    tile, row = pool[0][0].shape
    operands = [x for whole, halves in pool for x in (whole, halves[h])]
    return pl.pallas_call(
        functools.partial(pick_for_end_kernel, h),
        out_shape=jax.ShapeDtypeStruct((SLOTS * tile // 2, row), operands[0].dtype),
        in_specs=[SMEM] + [VMEM] * len(operands),
        out_specs=VMEM,
        compiler_params=pltpu.CompilerParams(vmem_limit_bytes=16 * 1024 * 1024),
        name="pick_for_end",
    )(ints, *operands)


def pick_own_kernel(ints, *refs):
    pool, (handed_a, handed_b, quarter, targets) = grouped(refs, (0, 1))
    handed = (handed_a, handed_b)
    width = targets.shape[1]
    half = quarter.shape[0] // SLOTS // 2

    def slot(s, _):
        place = ints[FOR_OWN + s]
        for h in range(2):
            at = (2 * s + h) * half

            @pl.when(place < 0)
            def _():
                start = pl.multiple_of(s * half, half)
                copy_rows(handed[h], start, targets, at, half, slice(0, width))
                copy_rows(handed[h], start, quarter, at, half, slice(width, None))

            for which in range(PLANES * SHARDS):
                ref, start, rows = piece(pool, which, h)

                @pl.when(place == which)
                def _():
                    copy_rows(ref, start, targets, at, rows, slice(0, width))
                    copy_rows(ref, start, quarter, at, rows, slice(width, None))

        return 0

    lax.fori_loop(0, SLOTS, slot, 0)


def pick_own(ints, pool, handed, width):
    rows, row = handed[0].shape
    operands = [x for whole, halves in pool for x in (whole, *halves)]
    return pl.pallas_call(
        pick_own_kernel,
        out_shape=[
            jax.ShapeDtypeStruct((2 * rows, row - width), handed[0].dtype),
            jax.ShapeDtypeStruct((2 * rows, width), handed[0].dtype),
        ],
        in_specs=[SMEM] + [VMEM] * (len(operands) + 2),
        out_specs=[VMEM, VMEM],
        compiler_params=pltpu.CompilerParams(vmem_limit_bytes=16 * 1024 * 1024),
        name="pick_own",
    )(ints, *operands, *handed)


def grad_kernel(counts, ints, floats, in0, in1, in2, in3, targets, own_w, *refs):
    sent, (grad, loss, w_buf, delta, sem) = sent_refs(counts, refs)
    m, k = position()
    half = w_buf.shape[0] // 2
    copies = [
        start_copies(ints, 0, h, own_w, sent, w_buf.at[pl.ds(h * half, half)], sem.at[h])
        for h in range(2)
    ]
    tile = in0.shape[0] // SLOTS
    slim = in0.shape[1]
    ins = (in0, in1, in2, in3)
    for copy in copies:
        copy.wait()

    def slot(s, total):
        span = pl.ds(pl.multiple_of(s * tile, tile), tile)
        pre = None
        for j in range(SHARDS):
            at = pl.ds(pl.multiple_of((k ^ j) * slim, slim), slim)
            one = jnp.dot(ins[j][span, :], w_buf[at, :], preferred_element_type=jnp.float32)
            pre = one if pre is None else pre + one
        live = lax.broadcasted_iota(jnp.int32, pre.shape, 0) < ints[TOKENS + s]
        many = jnp.full(pre.shape, ints[COUNTS + s], jnp.int32).astype(jnp.float32)
        coef = jnp.where(live, floats[TASK + s] / many, 0.0)
        hidden, slope = gelu_pair(pre)
        diff = hidden - targets[span, :].astype(jnp.float32)
        scaled = coef * diff
        delta[span, :] = (2.0 * scaled * slope).astype(jnp.bfloat16)
        return total + jnp.sum(scaled * diff, keepdims=True)

    total = lax.fori_loop(0, SLOTS, slot, jnp.zeros((1, 1), jnp.float32))
    lane = lax.broadcasted_iota(jnp.int32, loss.shape, 1)
    loss[...] = jnp.where(lane == m * SHARDS + k, total, 0.0)
    for j in range(SHARDS):
        at = pl.ds(pl.multiple_of((k ^ j) * slim, slim), slim)
        grad[at, :] = lax.dot_general(
            ins[j][...], delta[...], (((0,), (0,)), ((), ())), preferred_element_type=jnp.float32
        )


def gradient(ints, floats, ins, targets, own_w, sent):
    rows, width = targets.shape
    depth = own_w.shape[1]
    return pl.pallas_call(
        functools.partial(grad_kernel, counts_of(sent)),
        out_shape=[
            jax.ShapeDtypeStruct((depth, width), jnp.float32),
            jax.ShapeDtypeStruct((8, 128), jnp.float32),
        ],
        in_specs=[SMEM] * 2 + [VMEM] * 5 + [ANY] * (1 + sum(counts_of(sent))),
        out_specs=[VMEM, VMEM],
        scratch_shapes=[
            pltpu.VMEM((depth, width), own_w.dtype),
            pltpu.VMEM((rows, width), jnp.bfloat16),
            pltpu.SemaphoreType.DMA((2,)),
        ],
        compiler_params=pltpu.CompilerParams(vmem_limit_bytes=16 * 1024 * 1024),
        name="forward_and_gradient",
    )(ints, floats, *ins, targets, own_w, *sent[0], *sent[1], *sent[2])


def adam_kernel(h, counts, ints, floats, grad, *refs):
    own, (sent, refs) = refs[:3], sent_refs(counts, refs[3:])
    new, bufs, outs, (in_sem, out_sem) = refs[-11:-8], refs[-8:-5], refs[-5:-2], refs[-2:]
    blocks = out_sem.shape[1]
    rows = bufs[0].shape[0]
    step = rows // blocks
    here = h * rows

    def result(i, b):
        return pltpu.make_async_copy(
            outs[i].at[pl.ds(b * step, step)],
            new[i].at[0, pl.ds(here + b * step, step)],
            out_sem.at[i, b],
        )

    copies = [
        start_copies(ints, a, h, own[a], sent, bufs[a], in_sem.at[a]) for a in range(3)
    ]
    rate = floats[RATE]
    for copy in copies:
        copy.wait()
    for b in range(blocks):

        def body(n, _):
            at = pl.ds(pl.multiple_of(b * step + n * 16, 16), 16)
            g = grad[pl.ds(pl.multiple_of(here + b * step + n * 16, 16), 16), :]
            first = beta_one * bufs[1][at, :].astype(jnp.float32) + (1.0 - beta_one) * g
            second = beta_two * bufs[2][at, :].astype(jnp.float32) + (1.0 - beta_two) * g * g
            start = bufs[0][at, :].astype(jnp.float32)
            updated = start - rate * first / (jnp.sqrt(second) + adam_eps)
            outs[0][at, :] = updated.astype(outs[0].dtype)
            outs[1][at, :] = first.astype(outs[1].dtype)
            outs[2][at, :] = second.astype(outs[2].dtype)
            return 0

        lax.fori_loop(0, step // 16, body, 0, unroll=2)
        for i in range(3):
            result(i, b).start()
    for b in range(blocks):
        for i in range(3):
            result(i, b).wait()


def adam(h, ints, floats, grad, own, sent, begun=()):
    depth, width = grad.shape
    blocks = 2
    taken = sum(counts_of(sent))
    own = [pltpu.with_memory_space_constraint(x, pltpu.HBM) for x in own]
    sent = [
        [pltpu.with_memory_space_constraint(x, pltpu.HBM) for x in refs[:-1]] + list(refs[-1:])
        for refs in sent
    ]
    return pl.pallas_call(
        functools.partial(adam_kernel, h, counts_of(sent)),
        out_shape=[pltpu.HBM(x.shape, x.dtype) for x in own],
        in_specs=[SMEM] * 2 + [VMEM] + [ANY] * (3 + taken) + [HBM] * len(begun),
        out_specs=[HBM] * 3,
        scratch_shapes=[pltpu.VMEM((depth // 2, width), x.dtype) for x in own] * 2
        + [pltpu.SemaphoreType.DMA((3,)), pltpu.SemaphoreType.DMA((3, blocks))],
        input_output_aliases={6 + taken + i: i for i in range(len(begun))},
        compiler_params=pltpu.CompilerParams(vmem_limit_bytes=16 * 1024 * 1024),
        name="adam_half",
    )(ints, floats, grad, *own, *sent[0], *sent[1], *sent[2], *begun)


def in_plane(x, j):
    pairs = [(m * SHARDS + k, m * SHARDS + (k ^ j)) for m in range(PLANES) for k in range(SHARDS)]
    return lax.ppermute(x, "pop", pairs)


def along(x, hops):
    idle = [m for m in range(PLANES) if all(m not in hop for hop in hops)]
    pairs = [(a * SHARDS + k, b * SHARDS + k) for a, b in hops for k in range(SHARDS)]
    pairs += [(m * SHARDS + k, m * SHARDS + (k ^ 1)) for m in idle for k in range(SHARDS)]
    return lax.ppermute(x, "pop", pairs)


def beside(x):
    return lax.ppermute(x, "rep", [(0, 1), (1, 0)])


def after(x, *others):
    return lax.optimization_barrier((x, *others))[0]


def tiles(here, ints, width):
    near0, middle0, (here0, halves) = here
    middle = [along(x, MIDDLE) for x in halves]
    near = [along(halves[0], ENDS), along(after(halves[1], middle[0]), ENDS)]
    far0 = along(near0, MIDDLE)
    far_a = along(near[0], MIDDLE)
    far = [far_a, along(after(near[1], far_a), MIDDLE)]
    pool = [(here0, halves), (near0, near), (middle0, middle), (far0, far)]
    picked = [pick_for_end(h, ints, pool) for h in range(2)]
    handed = [along(picked[0], ENDS), along(picked[1], ENDS)]
    quarter, targets = pick_own(ints, pool, handed, width)
    side = in_plane(quarter, 1)
    cross = in_plane(quarter, 2)
    gates = [halves, (near, middle), picked[0], (picked[1], handed[0]), handed[1], quarter]
    return gates, (quarter, side, cross, in_plane(cross, 1)), targets


def state_steps(ints, own, gates, steps, returns, grad_step, gradient_of):
    half = own[0].shape[1] // 2
    guests = [beside(x[0, half:]) for x in own] if returns else []
    last, ends, middles, backs = (), [], [], []
    grad = None
    for t in range(1, steps + 1):
        if t == grad_step:
            grad = gradient_of(ends, middles, backs)
            gates = [*gates[: t - 1], grad[0]]
        guest = guests[t - 1] if t <= len(guests) else None
        theirs = 1 < t <= returns + 1
        gate = (gates[t - 1 : t], backs)
        facts = after(ints, gate) if jax.tree.leaves(gate) else ints
        to_ends, to_middle, *brought = stage(facts, t, own, guest, last, theirs)
        backs += [beside(x) for x in brought]
        last = (along(to_ends, ENDS), along(to_middle, MIDDLE))
        ends.append(last[0])
        middles.append(last[1])
    if len(backs) < returns:
        backs.append(beside(theirs_of(after(ints, (backs, gates[-1])), *last)))
    return ends, middles, backs, gradient_of(ends, middles, backs) if grad is None else grad


def run(plan, ints, floats, parts, own):
    near0, middle0 = along(parts[0], ENDS), along(parts[0], MIDDLE)
    swapped = [in_plane(parts[j], j) for j in range(1, SHARDS)]
    by_both = plan == 0
    halves = split_rows(after(swapped, near0, middle0) if by_both else swapped)
    here = (near0, middle0, (parts[0], halves))
    gates, ins, targets = tiles(here, ints, own[0].shape[2])
    first = 2 + plan

    def gradient_of(ends, middles, backs):
        sent = (ends[:first], middles[:first], backs[:first])
        return gradient(ints, floats, ins, targets, own[0], sent)

    if by_both:
        gates = [*gates[:3], (gates[3], gates[4]), gates[5]]
        moved = state_steps(ints, own, gates, 4, 4, 0, gradient_of)
    else:
        gates = [(), (near0, middle0, halves), *gates[1:]]
        moved = state_steps(ints, own, gates, 6 + plan, 0, 7, gradient_of)
    ends, middles, backs, (grad, loss) = moved
    round_one = [in_plane(loss, j) for j in range(1, SHARDS)]
    early = slice(None) if by_both else slice(-1)
    new = adam(0, ints, floats, grad, own, (ends[early], middles[early], []))
    loss = after(loss, new[0])
    loss = loss + round_one[0] + round_one[1] + round_one[2]
    ring = [along(loss, [(m, (m + d) % PLANES) for m in range(PLANES)]) for d in range(1, PLANES)]
    direct = ([], []) if by_both else (ends, middles)
    new = adam(1, ints, floats, grad, own, (*direct, backs), new)
    loss = after(loss, new[0]) + ring[0] + ring[1] + ring[2]
    return (*new, jnp.sum(loss[0, : PLANES * SHARDS].reshape(PLANES, SHARDS), axis=1))


def per_device(pool_tokens, pool_targets, weight, first_moment, second_moment, *args):
    winner, tile_ids = args[0], args[4]
    if winner.shape[0] != PLANES or tile_ids.shape[1] != SLOTS or lax.axis_size("rep") != 2:
        return relayed(pool_tokens, pool_targets, weight, first_moment, second_moment, *args)
    code = route_code(winner)
    parts = pack(code, pool_tokens, pool_targets)
    ints, floats = gather_facts(beside(code), *args)
    own = (weight, first_moment, second_moment)
    plans = [functools.partial(run, plan) for plan in range(3)]
    return lax.switch(ints[PLAN], plans, ints, floats, parts, own)


def solution(mesh):
    in_specs = (
        P(("rep", "pop"), None, None),
        P(("rep", "pop"), None, None),
        P(("rep", "pop"), None, None),
        P(("rep", "pop"), None, None),
        P(("rep", "pop"), None, None),
        P("rep"),
        P("rep"),
        P("rep"),
        P("rep", None),
        P("rep", None),
        P("rep", None),
        P("rep", None),
    )
    out_specs = (
        P(("rep", "pop"), None, None),
        P(("rep", "pop"), None, None),
        P(("rep", "pop"), None, None),
        P("rep"),
    )
    return jax.shard_map(
        per_device, mesh=mesh, in_specs=in_specs, out_specs=out_specs, check_vma=False
    )
```

```python
import functools

import jax
import jax.numpy as jnp
from jax import lax
from jax.experimental import pallas as pl
from jax.experimental.pallas import tpu as pltpu
from jax.sharding import PartitionSpec as P

SHARDS = 4
TASKS = 8
SLOTS = 4
PLANES = 4


beta_one = 0.9
beta_two = 0.999
adam_eps = 1e-08
gelu_coef = 0.7978845608028654

SMEM = pl.BlockSpec(memory_space=pltpu.SMEM)
VMEM = pl.BlockSpec(memory_space=pltpu.VMEM)
ANY = pl.BlockSpec(memory_space=pl.ANY)
HBM = pl.BlockSpec(memory_space=pltpu.HBM)


def gelu_pair(pre):
    inner = jnp.tanh(gelu_coef * (pre + 0.044715 * pre * pre * pre))
    value = 0.5 * pre * (1.0 + inner)
    slope = 0.5 * (1.0 + inner) + 0.5 * pre * (1.0 - inner * inner) * gelu_coef * (
        1.0 + 3.0 * 0.044715 * pre * pre
    )
    return (value, slope)


def for_sending(shard):

    def short(part):
        return part.astype(jnp.bfloat16) if part.dtype == jnp.float32 else part

    return jax.tree.map(short, shard)


def relayed(
    pool_tokens,
    pool_targets,
    weight,
    first_moment,
    second_moment,
    winner,
    learn_rate,
    explore,
    task_weight,
    tile_ids,
    slot_task,
    slot_tokens,
):
    nodes = lax.axis_size("pop")
    place = lax.axis_index("pop")
    member = place // SHARDS
    shard = place % SHARDS
    members = winner.shape[0]
    slots = tile_ids.shape[1]
    tile = pool_tokens.shape[1]
    depth = pool_tokens.shape[2]
    width = weight.shape[2]
    hidden_all = pool_targets.shape[2]
    reach = tile // nodes
    flat_state = (
        weight.reshape(nodes, -1),
        first_moment.reshape(nodes, -1),
        second_moment.reshape(nodes, -1),
    )
    spread = (
        lax.all_to_all(flat_state[0], "pop", split_axis=0, concat_axis=0, tiled=True),
        lax.all_to_all(flat_state[1], "pop", split_axis=0, concat_axis=0, tiled=True),
        lax.all_to_all(flat_state[2], "pop", split_axis=0, concat_axis=0, tiled=True),
    )
    source_rows = (winner[:, None] * SHARDS + jnp.arange(SHARDS, dtype=jnp.int32)[None, :]).reshape(
        -1
    )
    picked_state = tuple((jnp.take(piece, source_rows, axis=0) for piece in spread))
    returned = jax.tree.map(
        lambda part, own: part.astype(own.dtype),
        lax.all_to_all(for_sending(picked_state), "pop", split_axis=0, concat_axis=0, tiled=True),
        picked_state,
    )
    start_weight = returned[0].reshape(depth, width)
    start_first = returned[1].reshape(depth, width)
    start_second = returned[2].reshape(depth, width)
    relay_tokens, relay_targets = (
        lax.all_to_all(pool_tokens, "pop", split_axis=1, concat_axis=0, tiled=True),
        lax.all_to_all(pool_targets, "pop", split_axis=1, concat_axis=0, tiled=True),
    )
    flat_ids = tile_ids.reshape(-1)
    pick_tokens = jnp.take(relay_tokens, flat_ids, axis=0).reshape(members, 1, slots, reach, depth)
    send_tokens = jnp.broadcast_to(pick_tokens, (members, SHARDS, slots, reach, depth)).reshape(
        nodes, slots, reach, depth
    )
    pick_targets = jnp.take(relay_targets, flat_ids, axis=0).reshape(
        members, slots, reach, hidden_all
    )
    send_targets = jnp.broadcast_to(
        pick_targets[:, None], (members, SHARDS, slots, reach, hidden_all)
    ).reshape(nodes, slots, reach, hidden_all)
    got_tokens, got_targets = (
        lax.all_to_all(send_tokens, "pop", split_axis=0, concat_axis=2, tiled=True),
        lax.all_to_all(send_targets, "pop", split_axis=0, concat_axis=2, tiled=True),
    )
    targets = lax.dynamic_slice_in_dim(got_targets[0], shard * width, width, 2).reshape(
        slots * tile, width
    )
    inputs = got_tokens.reshape(slots * tile, depth)
    tasks_here = lax.dynamic_index_in_dim(slot_task, member, 0, keepdims=False)
    lengths = lax.dynamic_index_in_dim(slot_tokens, member, 0, keepdims=False)
    source_member = lax.dynamic_index_in_dim(winner, member, 0, keepdims=False)
    onehot = tasks_here[:, None] == jnp.arange(TASKS, dtype=jnp.int32)[None, :]
    counts = jnp.sum(jnp.where(onehot, lengths[:, None], 0), axis=0)
    weights_here = lax.dynamic_index_in_dim(task_weight, source_member, 0, keepdims=False)
    scale = weights_here / jnp.maximum(counts, 1).astype(jnp.float32)
    per_slot = jnp.sum(jnp.where(onehot, scale[None, :], jnp.float32(0.0)), axis=1)
    live = jnp.arange(tile, dtype=jnp.int32)[None, :] < lengths[:, None]
    coef = jnp.where(live, per_slot[:, None], jnp.float32(0.0)).reshape(-1)
    own_rate = lax.dynamic_index_in_dim(learn_rate, source_member, 0, keepdims=False)
    own_explore = lax.dynamic_index_in_dim(explore, member, 0, keepdims=False)
    step_rate = own_rate * jnp.where(source_member != member, own_explore, jnp.float32(1.0))
    pre = jnp.dot(inputs, start_weight, preferred_element_type=jnp.float32)
    hidden, slope = gelu_pair(pre)
    diff = hidden - targets.astype(jnp.float32)
    part = jnp.sum(coef[:, None] * diff * diff)
    delta = (2.0 * coef[:, None] * diff * slope).astype(jnp.bfloat16)
    grad = lax.dot_general(
        inputs, delta, (((0,), (0,)), ((), ())), preferred_element_type=jnp.float32
    )
    first = beta_one * start_first.astype(jnp.float32) + (1.0 - beta_one) * grad
    second = beta_two * start_second.astype(jnp.float32) + (1.0 - beta_two) * grad * grad
    updated = start_weight.astype(jnp.float32) - step_rate * first / (jnp.sqrt(second) + adam_eps)
    share = jnp.where(jnp.arange(members, dtype=jnp.int32) == member, part, jnp.float32(0.0))
    member_loss = lax.psum(share, "pop")
    return (
        updated.astype(jnp.bfloat16)[None],
        first.astype(jnp.bfloat16)[None],
        second.astype(jnp.bfloat16)[None],
        member_loss,
    )


ENDS = ((0, 1), (1, 0), (2, 3), (3, 2))
MIDDLE = ((1, 2), (2, 1))


def position():
    place = lax.axis_index("pop")
    return place // SHARDS, lax.rem(place, SHARDS)


SHARED, TAKEN, HOPS, BY_ENDS, THEIR_ENDS, TO_ENDS, TO_MIDDLE, PLAN = range(8)
FOR_END, FOR_OWN, TOKENS, COUNTS = 16, 20, 24, 28
OWN, GUEST, PASSED = range(3)
RATE, TASK = 0, 4


def copied_from(winner):
    loser, source = jnp.int32(0), jnp.int32(0)
    for m in range(PLANES):
        taken = winner[m] != m
        loser = jnp.where(taken, m, loser)
        source = jnp.where(taken, winner[m], source)
    return loser, source


def route_kernel(winner, code):
    loser, source = copied_from(winner)
    code[...] = jnp.full(code.shape, source * PLANES + loser, jnp.int32)


def route_code(winner):
    return pl.pallas_call(
        route_kernel,
        out_shape=jax.ShapeDtypeStruct((8, 128), jnp.int32),
        in_specs=[SMEM],
        out_specs=VMEM,
        name="route_code",
    )(winner)


def on_route(route, m, to):
    source, loser = route
    upward = (to == m + 1) & (source <= m) & (loser >= to)
    return upward | ((to == m - 1) & (source >= m) & (loser <= to))


def by_ends(route):
    source, loser = route
    return jnp.where(source < loser, loser - 1, loser + 1) == (loser ^ 1)


def in_pool(t, m, k):
    ahead = t // SHARDS - m
    ahead = jnp.where(m == 1, ahead, -ahead)
    group = jnp.where(ahead == 0, 0, jnp.where(ahead == -1, 1, ahead + 1))
    return group * SHARDS + (lax.rem(t, SHARDS) ^ k)


def facts_kernel(
    other, winner, learn_rate, explore, task_weight, tile_ids, slot_task, slot_tokens, ints, floats
):
    m, k = position()
    loser, source = copied_from(winner)
    code = other[0, 0]
    mine = source, loser
    theirs = lax.div(code, jnp.int32(PLANES)), lax.rem(code, jnp.int32(PLANES))
    upward = jnp.maximum(mine[0], theirs[0]) < jnp.minimum(mine[1], theirs[1])
    downward = jnp.maximum(mine[1], theirs[1]) < jnp.minimum(mine[0], theirs[0])
    hops = jnp.abs(mine[0] - mine[1])
    long = jnp.maximum(hops, jnp.abs(theirs[0] - theirs[1])) == PLANES - 1
    shared = upward | downward | long
    taken = winner[m] != m

    def content(to):
        own = on_route(mine, m, to)
        guest = on_route(theirs, m, to) & jnp.logical_not(shared)
        first = jnp.where(own, jnp.where(m == mine[0], OWN, PASSED), -1)
        return jnp.where(guest, jnp.where(m == theirs[0], GUEST, PASSED), first)

    ints[SHARED] = shared.astype(jnp.int32)
    ints[TAKEN] = taken.astype(jnp.int32)
    ints[HOPS] = hops
    ints[PLAN] = jnp.where(long, 2, shared.astype(jnp.int32))
    ints[BY_ENDS] = by_ends(mine).astype(jnp.int32)
    ints[THEIR_ENDS] = by_ends(theirs).astype(jnp.int32)
    ints[TO_ENDS] = content(m ^ 1)
    ints[TO_MIDDLE] = content(jnp.where(m == 1, 2, jnp.where(m == 2, 1, -1)))
    end = jnp.where(m <= 1, 0, PLANES - 1)
    at_end = (m == 0) | (m == PLANES - 1)
    slots = tile_ids.shape[1]
    for s in range(slots):
        task = slot_task[m, s]
        count = jnp.int32(0)
        for o in range(slots):
            count = count + jnp.where(slot_task[m, o] == task, slot_tokens[m, o], 0)
        ints[FOR_END + s] = in_pool(tile_ids[end, s], m, k)
        ints[FOR_OWN + s] = jnp.where(at_end, -1, in_pool(tile_ids[m, s], m, k))
        ints[TOKENS + s] = slot_tokens[m, s]
        ints[COUNTS + s] = jnp.maximum(count, 1)
        floats[TASK + s] = task_weight[winner[m], task]
    floats[RATE] = learn_rate[winner[m]] * jnp.where(taken, explore[m], 1.0)


def gather_facts(other, *small):
    return pl.pallas_call(
        facts_kernel,
        out_shape=[jax.ShapeDtypeStruct((32,), jnp.int32), jax.ShapeDtypeStruct((8,), jnp.float32)],
        in_specs=[SMEM] * 8,
        out_specs=[SMEM, SMEM],
        name="gather_facts",
    )(other, *small)


def stage_kernel(t, has_guest, has_theirs, has_last, ints, *refs):
    state, refs = refs[:3], refs[3:]
    guest = refs[0] if has_guest else None
    from_ends, from_middle = refs[has_guest : has_guest + 2] if has_last else (None, None)
    to_ends, to_middle = refs[has_guest + 2 * has_last :][:2]
    sems = refs[-1]
    half = to_ends.shape[0]
    shared = ints[SHARED] == 1
    array = jnp.where(shared, (t - 1) // 2, t - 1)
    start = pl.multiple_of(jnp.where(shared, (t - 1) % 2, 0) * half, half)
    sides = ((to_ends, ints[TO_ENDS], from_middle), (to_middle, ints[TO_MIDDLE], from_ends))
    for n, (out, content, _) in enumerate(sides):
        for a, ref in enumerate(state):

            @pl.when((content == OWN) & (array == a))
            def _():
                pltpu.make_async_copy(ref.at[0, pl.ds(start, half)], out, sems.at[n]).start()

    if has_theirs:
        theirs = refs[has_guest + 2 * has_last + 2]

        @pl.when(ints[THEIR_ENDS] == 1)
        def _():
            copy_rows(from_ends, 0, theirs, 0, half)

        @pl.when(ints[THEIR_ENDS] == 0)
        def _():
            copy_rows(from_middle, 0, theirs, 0, half)

    for n, (out, content, passed) in enumerate(sides):
        if guest is not None:

            @pl.when(content == GUEST)
            def _():
                copy_rows(guest, 0, out, 0, half)

        if passed is not None:

            @pl.when(content == PASSED)
            def _():
                copy_rows(passed, 0, out, 0, half)

        @pl.when((content == OWN) & (array < len(state)))
        def _():
            pltpu.make_async_copy(state[0].at[0, pl.ds(0, half)], out, sems.at[n]).wait()


def stage(ints, step, own, guest, last, theirs):
    half, width = own[0].shape[1] // 2, own[0].shape[2]
    guests = () if guest is None else (guest,)
    kernel = functools.partial(stage_kernel, step, len(guests), theirs, len(last) > 0)
    return pl.pallas_call(
        kernel,
        out_shape=[jax.ShapeDtypeStruct((half, width), own[0].dtype)] * (2 + theirs),
        in_specs=[SMEM] + [ANY] * 3 + [VMEM] * (len(guests) + len(last)),
        out_specs=[VMEM] * (2 + theirs),
        scratch_shapes=[pltpu.SemaphoreType.DMA((2,))],
        compiler_params=pltpu.CompilerParams(vmem_limit_bytes=8 * 1024 * 1024),
        name="stage_chunk",
    )(ints, *own, *guests, *last)


def theirs_kernel(ints, from_ends, from_middle, theirs):
    @pl.when(ints[THEIR_ENDS] == 1)
    def _():
        copy_rows(from_ends, 0, theirs, 0, theirs.shape[0])

    @pl.when(ints[THEIR_ENDS] == 0)
    def _():
        copy_rows(from_middle, 0, theirs, 0, theirs.shape[0])


def theirs_of(ints, from_ends, from_middle):
    return pl.pallas_call(
        theirs_kernel,
        out_shape=jax.ShapeDtypeStruct(from_ends.shape, from_ends.dtype),
        in_specs=[SMEM] + [VMEM] * 2,
        out_specs=VMEM,
        compiler_params=pltpu.CompilerParams(vmem_limit_bytes=8 * 1024 * 1024),
        name="guest_chunk",
    )(ints, from_ends, from_middle)


def start_copies(ints, a, h, own, sent, out, sem):
    ends, middles, backs = sent
    shared, taken = ints[SHARED] == 1, ints[TAKEN] == 1
    half = out.shape[0]
    step = jnp.where(shared, 2 * a + h, a) + ints[HOPS]
    direct = taken & shared if h == 1 else taken

    def copy(ref):
        return pltpu.make_async_copy(ref, out, sem)

    @pl.when(jnp.logical_not(taken))
    def _():
        copy(own.at[0, pl.ds(h * half, half)]).start()

    sides = [
        (ends, direct & (ints[BY_ENDS] == 1)),
        (middles, direct & (ints[BY_ENDS] == 0)),
    ]
    if h == 1:
        sides.append((backs, taken & jnp.logical_not(shared)))
    for refs, here in sides:
        for n, ref in enumerate(refs):

            @pl.when(here & (step == n + 1))
            def _():
                copy(ref).start()

    return copy(own.at[0, pl.ds(h * half, half)])


def counts_of(sent):
    return tuple(len(refs) for refs in sent)


def sent_refs(counts, refs):
    a, b, c = counts
    return (refs[:a], refs[a : a + b], refs[a + b : a + b + c]), refs[a + b + c :]


def pack_kernel(code, tokens, targets, *parts):
    _, k = position()
    width = targets.shape[2] // SHARDS
    slim = tokens.shape[2] // SHARDS
    for j, part in enumerate(parts):
        q = k ^ j
        part[:, :width] = targets[0, :, pl.ds(pl.multiple_of(q * width, 128), width)]
        part[:, width:] = tokens[0, :, pl.ds(pl.multiple_of(q * slim, 128), slim)]


def pack(code, tokens, targets):
    tile = tokens.shape[1]
    row = (tokens.shape[2] + targets.shape[2]) // SHARDS
    return pl.pallas_call(
        pack_kernel,
        out_shape=[jax.ShapeDtypeStruct((tile, row), tokens.dtype)] * SHARDS,
        in_specs=[VMEM] * 3,
        out_specs=[VMEM] * SHARDS,
        name="pack_quarters",
    )(code, tokens, targets)


def copy_rows(ref, start, out, at, count, columns=slice(None)):
    step = 32

    def body(i, _):
        rows = pl.ds(pl.multiple_of(at + i * step, step), step)
        out[rows, :] = ref[pl.ds(pl.multiple_of(start + i * step, step), step), columns]
        return 0

    lax.fori_loop(0, count // step, body, 0, unroll=True if count <= 64 else 4)


def split_kernel(one, two, three, *halves):
    count = one.shape[0] // 2
    for h, half in enumerate(halves):
        for n, part in enumerate((one, two, three)):
            copy_rows(part, h * count, half, n * count, count)


def split_rows(parts):
    tile, row = parts[0].shape
    half = jax.ShapeDtypeStruct((len(parts) * tile // 2, row), parts[0].dtype)
    return pl.pallas_call(
        split_kernel,
        out_shape=[half, half],
        in_specs=[VMEM] * len(parts),
        out_specs=[VMEM, VMEM],
        compiler_params=pltpu.CompilerParams(vmem_limit_bytes=8 * 1024 * 1024),
        name="split_rows",
    )(*parts)


def piece(pool, which, h):
    group, j = divmod(which, SHARDS)
    whole, halves = pool[group]
    rows = whole.shape[0] // 2
    return (whole, h * rows, rows) if j == 0 else (halves[h], (j - 1) * rows, rows)


def grouped(refs, halves):
    size = 1 + len(halves)
    pool = []
    for g in range(PLANES):
        group = refs[g * size : (g + 1) * size]
        pool.append((group[0], dict(zip(halves, group[1:]))))
    return pool, refs[PLANES * size :]


def pick_for_end_kernel(h, ints, *refs):
    pool, (out,) = grouped(refs, (h,))

    def slot(s, _):
        place = ints[FOR_END + s]
        for which in range(PLANES * SHARDS):
            ref, start, rows = piece(pool, which, h)

            @pl.when(place == which)
            def _():
                copy_rows(ref, start, out, s * rows, rows)

        return 0

    lax.fori_loop(0, SLOTS, slot, 0)


def pick_for_end(h, ints, pool):
    tile, row = pool[0][0].shape
    operands = [x for whole, halves in pool for x in (whole, halves[h])]
    return pl.pallas_call(
        functools.partial(pick_for_end_kernel, h),
        out_shape=jax.ShapeDtypeStruct((SLOTS * tile // 2, row), operands[0].dtype),
        in_specs=[SMEM] + [VMEM] * len(operands),
        out_specs=VMEM,
        compiler_params=pltpu.CompilerParams(vmem_limit_bytes=16 * 1024 * 1024),
        name="pick_for_end",
    )(ints, *operands)


def pick_own_kernel(ints, *refs):
    pool, (handed_a, handed_b, quarter, targets) = grouped(refs, (0, 1))
    handed = (handed_a, handed_b)
    width = targets.shape[1]
    half = quarter.shape[0] // SLOTS // 2

    def slot(s, _):
        place = ints[FOR_OWN + s]
        for h in range(2):
            at = (2 * s + h) * half

            @pl.when(place < 0)
            def _():
                start = pl.multiple_of(s * half, half)
                copy_rows(handed[h], start, targets, at, half, slice(0, width))
                copy_rows(handed[h], start, quarter, at, half, slice(width, None))

            for which in range(PLANES * SHARDS):
                ref, start, rows = piece(pool, which, h)

                @pl.when(place == which)
                def _():
                    copy_rows(ref, start, targets, at, rows, slice(0, width))
                    copy_rows(ref, start, quarter, at, rows, slice(width, None))

        return 0

    lax.fori_loop(0, SLOTS, slot, 0)


def pick_own(ints, pool, handed, width):
    rows, row = handed[0].shape
    operands = [x for whole, halves in pool for x in (whole, *halves)]
    return pl.pallas_call(
        pick_own_kernel,
        out_shape=[
            jax.ShapeDtypeStruct((2 * rows, row - width), handed[0].dtype),
            jax.ShapeDtypeStruct((2 * rows, width), handed[0].dtype),
        ],
        in_specs=[SMEM] + [VMEM] * (len(operands) + 2),
        out_specs=[VMEM, VMEM],
        compiler_params=pltpu.CompilerParams(vmem_limit_bytes=16 * 1024 * 1024),
        name="pick_own",
    )(ints, *operands, *handed)


def grad_kernel(counts, ints, floats, in0, in1, in2, in3, targets, own_w, *refs):
    sent, (grad, loss, w_buf, delta, sem) = sent_refs(counts, refs)
    m, k = position()
    half = w_buf.shape[0] // 2
    copies = [
        start_copies(ints, 0, h, own_w, sent, w_buf.at[pl.ds(h * half, half)], sem.at[h])
        for h in range(2)
    ]
    tile = in0.shape[0] // SLOTS
    slim = in0.shape[1]
    ins = (in0, in1, in2, in3)
    for copy in copies:
        copy.wait()

    def slot(s, total):
        span = pl.ds(pl.multiple_of(s * tile, tile), tile)
        pre = None
        for j in range(SHARDS):
            at = pl.ds(pl.multiple_of((k ^ j) * slim, slim), slim)
            one = jnp.dot(ins[j][span, :], w_buf[at, :], preferred_element_type=jnp.float32)
            pre = one if pre is None else pre + one
        live = lax.broadcasted_iota(jnp.int32, pre.shape, 0) < ints[TOKENS + s]
        many = jnp.full(pre.shape, ints[COUNTS + s], jnp.int32).astype(jnp.float32)
        coef = jnp.where(live, floats[TASK + s] / many, 0.0)
        hidden, slope = gelu_pair(pre)
        diff = hidden - targets[span, :].astype(jnp.float32)
        scaled = coef * diff
        delta[span, :] = (2.0 * scaled * slope).astype(jnp.bfloat16)
        return total + jnp.sum(scaled * diff, keepdims=True)

    total = lax.fori_loop(0, SLOTS, slot, jnp.zeros((1, 1), jnp.float32))
    lane = lax.broadcasted_iota(jnp.int32, loss.shape, 1)
    loss[...] = jnp.where(lane == m * SHARDS + k, total, 0.0)
    for j in range(SHARDS):
        at = pl.ds(pl.multiple_of((k ^ j) * slim, slim), slim)
        grad[at, :] = lax.dot_general(
            ins[j][...], delta[...], (((0,), (0,)), ((), ())), preferred_element_type=jnp.float32
        )


def gradient(ints, floats, ins, targets, own_w, sent):
    rows, width = targets.shape
    depth = own_w.shape[1]
    return pl.pallas_call(
        functools.partial(grad_kernel, counts_of(sent)),
        out_shape=[
            jax.ShapeDtypeStruct((depth, width), jnp.float32),
            jax.ShapeDtypeStruct((8, 128), jnp.float32),
        ],
        in_specs=[SMEM] * 2 + [VMEM] * 5 + [ANY] * (1 + sum(counts_of(sent))),
        out_specs=[VMEM, VMEM],
        scratch_shapes=[
            pltpu.VMEM((depth, width), own_w.dtype),
            pltpu.VMEM((rows, width), jnp.bfloat16),
            pltpu.SemaphoreType.DMA((2,)),
        ],
        compiler_params=pltpu.CompilerParams(vmem_limit_bytes=16 * 1024 * 1024),
        name="forward_and_gradient",
    )(ints, floats, *ins, targets, own_w, *sent[0], *sent[1], *sent[2])


def adam_kernel(h, counts, ints, floats, grad, *refs):
    own, (sent, refs) = refs[:3], sent_refs(counts, refs[3:])
    new, bufs, outs, (in_sem, out_sem) = refs[-11:-8], refs[-8:-5], refs[-5:-2], refs[-2:]
    blocks = out_sem.shape[1]
    rows = bufs[0].shape[0]
    step = rows // blocks
    here = h * rows

    def result(i, b):
        return pltpu.make_async_copy(
            outs[i].at[pl.ds(b * step, step)],
            new[i].at[0, pl.ds(here + b * step, step)],
            out_sem.at[i, b],
        )

    copies = [
        start_copies(ints, a, h, own[a], sent, bufs[a], in_sem.at[a]) for a in range(3)
    ]
    rate = floats[RATE]
    for copy in copies:
        copy.wait()
    for b in range(blocks):

        def body(n, _):
            at = pl.ds(pl.multiple_of(b * step + n * 16, 16), 16)
            g = grad[pl.ds(pl.multiple_of(here + b * step + n * 16, 16), 16), :]
            first = beta_one * bufs[1][at, :].astype(jnp.float32) + (1.0 - beta_one) * g
            second = beta_two * bufs[2][at, :].astype(jnp.float32) + (1.0 - beta_two) * g * g
            start = bufs[0][at, :].astype(jnp.float32)
            updated = start - rate * first / (jnp.sqrt(second) + adam_eps)
            outs[0][at, :] = updated.astype(outs[0].dtype)
            outs[1][at, :] = first.astype(outs[1].dtype)
            outs[2][at, :] = second.astype(outs[2].dtype)
            return 0

        lax.fori_loop(0, step // 16, body, 0, unroll=2)
        for i in range(3):
            result(i, b).start()
    for b in range(blocks):
        for i in range(3):
            result(i, b).wait()


def adam(h, ints, floats, grad, own, sent, begun=()):
    depth, width = grad.shape
    blocks = 2
    taken = sum(counts_of(sent))
    own = [pltpu.with_memory_space_constraint(x, pltpu.HBM) for x in own]
    sent = [
        [pltpu.with_memory_space_constraint(x, pltpu.HBM) for x in refs[:-1]] + list(refs[-1:])
        for refs in sent
    ]
    return pl.pallas_call(
        functools.partial(adam_kernel, h, counts_of(sent)),
        out_shape=[pltpu.HBM(x.shape, x.dtype) for x in own],
        in_specs=[SMEM] * 2 + [VMEM] + [ANY] * (3 + taken) + [HBM] * len(begun),
        out_specs=[HBM] * 3,
        scratch_shapes=[pltpu.VMEM((depth // 2, width), x.dtype) for x in own] * 2
        + [pltpu.SemaphoreType.DMA((3,)), pltpu.SemaphoreType.DMA((3, blocks))],
        input_output_aliases={6 + taken + i: i for i in range(len(begun))},
        compiler_params=pltpu.CompilerParams(vmem_limit_bytes=16 * 1024 * 1024),
        name="adam_half",
    )(ints, floats, grad, *own, *sent[0], *sent[1], *sent[2], *begun)


def in_plane(x, j):
    pairs = [(m * SHARDS + k, m * SHARDS + (k ^ j)) for m in range(PLANES) for k in range(SHARDS)]
    return lax.ppermute(x, "pop", pairs)


def along(x, hops):
    idle = [m for m in range(PLANES) if all(m not in hop for hop in hops)]
    pairs = [(a * SHARDS + k, b * SHARDS + k) for a, b in hops for k in range(SHARDS)]
    pairs += [(m * SHARDS + k, m * SHARDS + (k ^ 1)) for m in idle for k in range(SHARDS)]
    return lax.ppermute(x, "pop", pairs)


def beside(x):
    return lax.ppermute(x, "rep", [(0, 1), (1, 0)])


def after(x, *others):
    return lax.optimization_barrier((x, *others))[0]


def tiles(here, ints, width):
    near0, middle0, (here0, halves) = here
    middle = [along(x, MIDDLE) for x in halves]
    near = [along(halves[0], ENDS), along(after(halves[1], middle[0]), ENDS)]
    far0 = along(near0, MIDDLE)
    far_a = along(near[0], MIDDLE)
    far = [far_a, along(after(near[1], far_a), MIDDLE)]
    pool = [(here0, halves), (near0, near), (middle0, middle), (far0, far)]
    picked = [pick_for_end(h, ints, pool) for h in range(2)]
    handed = [along(picked[0], ENDS), along(picked[1], ENDS)]
    quarter, targets = pick_own(ints, pool, handed, width)
    side = in_plane(quarter, 1)
    cross = in_plane(quarter, 2)
    ins = (quarter, side, cross, in_plane(cross, 1))
    gates = [halves, (near, middle), picked[0], (picked[1], handed[0]), handed[1], ins]
    return gates, ins, targets


def state_steps(ints, own, gates, steps, returns, grad_step, gradient_of):
    half = own[0].shape[1] // 2
    guests = [beside(x[0, half:]) for x in own] if returns else []
    last, ends, middles, backs = (), [], [], []
    grad = None
    for t in range(1, steps + 1):
        if t == grad_step:
            grad = gradient_of(ends, middles, backs)
            gates = [*gates[: t - 1], grad[0]]
        guest = guests[t - 1] if t <= len(guests) else None
        theirs = 1 < t <= returns + 1
        gate = (gates[t - 1 : t], backs)
        facts = after(ints, gate) if jax.tree.leaves(gate) else ints
        to_ends, to_middle, *brought = stage(facts, t, own, guest, last, theirs)
        backs += [beside(x) for x in brought]
        last = (along(to_ends, ENDS), along(to_middle, MIDDLE))
        ends.append(last[0])
        middles.append(last[1])
    if len(backs) < returns:
        backs.append(beside(theirs_of(after(ints, (backs, gates[-1])), *last)))
    return ends, middles, backs, gradient_of(ends, middles, backs) if grad is None else grad


def run(plan, ints, floats, parts, own):
    near0, middle0 = along(parts[0], ENDS), along(parts[0], MIDDLE)
    swapped = [in_plane(parts[j], j) for j in range(1, SHARDS)]
    by_both = plan == 0
    halves = split_rows(after(swapped, near0, middle0) if by_both else swapped)
    here = (near0, middle0, (parts[0], halves))
    gates, ins, targets = tiles(here, ints, own[0].shape[2])
    first = 2 + plan

    def gradient_of(ends, middles, backs):
        sent = (ends[:first], middles[:first], backs[:first])
        return gradient(ints, floats, ins, targets, own[0], sent)

    if by_both:
        gates = [*gates[:3], (gates[3], gates[4]), gates[5]]
        moved = state_steps(ints, own, gates, 4, 4, 0, gradient_of)
    else:
        gates = [(), (near0, middle0, halves), *gates[1:]]
        moved = state_steps(ints, own, gates, 6 + plan, 0, 7, gradient_of)
    ends, middles, backs, (grad, loss) = moved
    round_one = [in_plane(loss, j) for j in range(1, SHARDS)]
    early = slice(None) if by_both else slice(-1)
    new = adam(0, ints, floats, grad, own, (ends[early], middles[early], []))
    loss = after(loss, new[0])
    loss = loss + round_one[0] + round_one[1] + round_one[2]
    ring = [along(loss, [(m, (m + d) % PLANES) for m in range(PLANES)]) for d in range(1, PLANES)]
    direct = ([], []) if by_both else (ends, middles)
    new = adam(1, ints, floats, grad, own, (*direct, backs), new)
    loss = after(loss, new[0]) + ring[0] + ring[1] + ring[2]
    return (*new, jnp.sum(loss[0, : PLANES * SHARDS].reshape(PLANES, SHARDS), axis=1))


def per_device(pool_tokens, pool_targets, weight, first_moment, second_moment, *args):
    winner, tile_ids = args[0], args[4]
    if winner.shape[0] != PLANES or tile_ids.shape[1] != SLOTS or lax.axis_size("rep") != 2:
        return relayed(pool_tokens, pool_targets, weight, first_moment, second_moment, *args)
    code = route_code(winner)
    parts = pack(code, pool_tokens, pool_targets)
    ints, floats = gather_facts(beside(code), *args)
    own = (weight, first_moment, second_moment)
    plans = [functools.partial(run, plan) for plan in range(3)]
    return lax.switch(ints[PLAN], plans, ints, floats, parts, own)


def solution(mesh):
    in_specs = (
        P(("rep", "pop"), None, None),
        P(("rep", "pop"), None, None),
        P(("rep", "pop"), None, None),
        P(("rep", "pop"), None, None),
        P(("rep", "pop"), None, None),
        P("rep"),
        P("rep"),
        P("rep"),
        P("rep", None),
        P("rep", None),
        P("rep", None),
        P("rep", None),
    )
    out_specs = (
        P(("rep", "pop"), None, None),
        P(("rep", "pop"), None, None),
        P(("rep", "pop"), None, None),
        P("rep"),
    )
    return jax.shard_map(
        per_device, mesh=mesh, in_specs=in_specs, out_specs=out_specs, check_vma=False
    )
```
